32 devices in a mesh: rows: 8 (over y, x, core), chan: 4 (over z).
Axes of the slice: x: 2, y: 2, z: 4, core: 2. Of those that a mesh axis runs over, the one named last changes fastest.
Arguments:
- features: bfloat16 [128, 64, 512], P('rows', None, 'chan'), may hold values from -6 to 6
- embedding: bfloat16 [2, 2048], replicated, may hold values from -6 to 6
- context: bfloat16 [2, 132, 2048], replicated, may hold values from -6 to 6
- image_offset: int32 [1], replicated, may hold values from 0 to 63
- first_gain: float32 [512], P('chan'), may hold values from 0.25 to 1.75
- first_shift: float32 [512], P('chan'), may hold values from -2 to 2
- conv_first: bfloat16 [3, 3, 512, 512], P(None, None, 'chan'), may hold values from -0.09375 to 0.09375
- conv_first_bias: float32 [512], P('chan'), may hold values from -2 to 2
- embed_weight: bfloat16 [2048, 2, 512], P(None, None, 'chan'), may hold values from -0.125 to 0.125
- embed_bias: float32 [2, 512], P(None, 'chan'), may hold values from -2 to 2
- second_gain: float32 [512], P('chan'), may hold values from 0.25 to 1.75
- second_shift: float32 [512], P('chan'), may hold values from -2 to 2
- conv_second: bfloat16 [3, 3, 512, 512], P(None, None, 'chan'), may hold values from -0.09375 to 0.09375
- conv_second_bias: float32 [512], P('chan'), may hold values from -2 to 2
- attend_gain: float32 [512], P('chan'), may hold values from 0.25 to 1.75
- attend_shift: float32 [512], P('chan'), may hold values from -2 to 2
- attend_weight: bfloat16 [512, 3, 512], P(None, None, 'chan'), may hold values from -0.25 to 0.25
- attend_bias: float32 [2, 512], P(None, 'chan'), may hold values from -0.6 to 0.6
- context_weight: bfloat16 [2048, 2, 512], P(None, None, 'chan'), may hold values from -0.125 to 0.125
- context_bias: float32 [2, 512], P(None, 'chan'), may hold values from -2 to 2
- output_weight: bfloat16 [512, 512], P('chan'), may hold values from -4 to 4
- output_bias: float32 [512], P('chan'), may hold values from -2 to 2
- cotangent: bfloat16 [128, 64, 512], P('rows', None, 'chan'), may hold values from -6 to 6
Outputs:
- result: bfloat16 [128, 64, 512], P('rows', None, 'chan')
- features_grad: bfloat16 [128, 64, 512], P('rows', None, 'chan')
- first_gain_grad: float32 [512], P('chan')
- first_shift_grad: float32 [512], P('chan')
- conv_first_grad: float32 [3, 3, 512, 512], P(None, None, 'chan')
- conv_first_bias_grad: float32 [512], P('chan')
- embed_weight_grad: float32 [2048, 2, 512], P(None, None, 'chan')
- embed_bias_grad: float32 [2, 512], P(None, 'chan')
- second_gain_grad: float32 [512], P('chan')
- second_shift_grad: float32 [512], P('chan')
- conv_second_grad: float32 [3, 3, 512, 512], P(None, None, 'chan')
- conv_second_bias_grad: float32 [512], P('chan')
- attend_gain_grad: float32 [512], P('chan')
- attend_shift_grad: float32 [512], P('chan')
- attend_weight_grad: float32 [512, 3, 512], P(None, None, 'chan')
- attend_bias_grad: float32 [2, 512], P(None, 'chan')
- context_weight_grad: float32 [2048, 2, 512], P(None, None, 'chan')
- context_bias_grad: float32 [2, 512], P(None, 'chan')
- output_weight_grad: float32 [512, 512], P('chan')
- output_bias_grad: float32 [512], P('chan')
The draws below stay inside these ranges and needn't reach their ends.
Inputs may be any that keep to these rules, and one draw needn't show every extreme that they name: Image k, for k = 0 to 1, occupies the 64 rows that start at row image_offset + k * 64, counted modulo 128, so the last image may continue at row 0.
All inputs are finite; a program needn't handle non-finite values.
Results may differ from the reference program's by a relative error of at most 0.018.
Values may be sent and summed in bfloat16 or wider, within the bound.
A program may use at most 256 MiB of HBM per device.

```python
import jax
import jax.numpy as jnp
from jax import lax

C = 512
HEADS = 8
HEAD_DIM = 64
GROUPS = 32
EMBED = 2048
ENC = 2048
CTX = 132
IMG_H = 64
IMG_W = 64
TOTAL_ROWS = 128
IMAGES = 2


def level_of(stream_key, extent, pieces, smallest, largest):
    level = 1.0
    for axis_at, shards_of in pieces:
        steps = jax.random.uniform(jax.random.fold_in(jax.random.fold_in(stream_key, 6), axis_at), (shards_of,), jnp.float32, smallest / len(pieces), largest / len(pieces))
        level = level * jnp.repeat(jnp.exp(steps), extent[axis_at] // shards_of).reshape((-1,) + (1,) * (len(extent) - 1 - axis_at))
    return level


def centred(own_key, dims, scale, bound, shards=(), kind=jnp.bfloat16):
    drawn = jax.random.normal(own_key, dims, jnp.float32) * scale
    if len(shards) > 0:
        drawn = level_of(own_key, dims, shards, -0.22, 0.18) * drawn
    return jnp.clip(drawn, min=-bound, max=bound).astype(kind)


def setup_inputs(seed: int = 0) -> dict:
    key_list = jax.random.split(jax.random.key(seed), 24)
    features = centred(key_list[0], (TOTAL_ROWS, IMG_W, C), 1.0, 6.0, ((0, 8), (2, 4)))
    embedding = centred(key_list[1], (IMAGES, EMBED), 1.0, 6.0)
    context = centred(key_list[2], (IMAGES, CTX, ENC), 1.0, 6.0)
    image_offset = jax.random.randint(key_list[3], (1,), 0, IMG_H).astype(jnp.int32)
    first_gain = jnp.clip(1.0 + 0.15 * jax.random.normal(key_list[4], (C,), jnp.float32), 0.25, 1.75)
    first_shift = centred(key_list[5], (C,), 0.3, 2.0, ((0, 4),), jnp.float32)
    conv_first = centred(key_list[6], (3, 3, C, C), (9 * C) ** -0.5, 0.09375, ((2, 4),))
    conv_first_bias = centred(key_list[7], (C,), 0.3, 2.0, ((0, 4),), jnp.float32)
    embed_weight = centred(key_list[8], (EMBED, 2, C), EMBED ** -0.5, 0.125, ((2, 4),))
    embed_bias = centred(key_list[9], (2, C), 0.3, 2.0, ((1, 4),), jnp.float32)
    second_gain = jnp.clip(1.0 + 0.15 * jax.random.normal(key_list[10], (C,), jnp.float32), 0.25, 1.75)
    second_shift = centred(key_list[11], (C,), 0.3, 2.0, ((0, 4),), jnp.float32)
    conv_second = centred(key_list[12], (3, 3, C, C), (9 * C) ** -0.5, 0.09375, ((2, 4),))
    conv_second_bias = centred(key_list[13], (C,), 0.3, 2.0, ((0, 4),), jnp.float32)
    attend_gain = jnp.clip(1.0 + 0.15 * jax.random.normal(key_list[14], (C,), jnp.float32), 0.25, 1.75)
    attend_shift = centred(key_list[15], (C,), 0.3, 2.0, ((0, 4),), jnp.float32)
    attend_weight = centred(key_list[16], (C, 3, C), C ** -0.5, 0.25, ((2, 4),))
    attend_bias = centred(key_list[17], (2, C), 0.1, 0.6, ((1, 4),), jnp.float32)
    context_weight = centred(key_list[18], (ENC, 2, C), ENC ** -0.5, 0.125, ((2, 4),))
    context_bias = centred(key_list[19], (2, C), 0.3, 2.0, ((1, 4),), jnp.float32)
    output_weight = centred(key_list[20], (C, C), (max(2, C // 256)) ** -0.5, 4.0, ((0, 4),))
    output_bias = centred(key_list[21], (C,), 0.3, 2.0, ((0, 4),), jnp.float32)
    cotangent = centred(key_list[22], (TOTAL_ROWS, IMG_W, C), 1.0, 6.0, ((0, 8), (2, 4)))
    return {"features": features, "embedding": embedding, "context": context, "image_offset": image_offset, "first_gain": first_gain, "first_shift": first_shift, "conv_first": conv_first, "conv_first_bias": conv_first_bias, "embed_weight": embed_weight, "embed_bias": embed_bias, "second_gain": second_gain, "second_shift": second_shift, "conv_second": conv_second, "conv_second_bias": conv_second_bias, "attend_gain": attend_gain, "attend_shift": attend_shift, "attend_weight": attend_weight, "attend_bias": attend_bias, "context_weight": context_weight, "context_bias": context_bias, "output_weight": output_weight, "output_bias": output_bias, "cotangent": cotangent}


EPSILON = 1e-05
HIGH = lax.Precision.HIGHEST

@jax.custom_vjp
def low(v):
    return lax.optimization_barrier(v.astype(jnp.bfloat16)).astype(jnp.float32)

@jax.custom_vjp
def low_back(v):
    return v

def low_keep(v):
    return (low(v), None)

def low_pass(kept, grad):
    return (grad,)

def back_keep(v):
    return (v, None)

def back_low(kept, grad):
    return (low(grad),)
low.defvjp(low_keep, low_pass)
low_back.defvjp(back_keep, back_low)

def group_norm(values, gain, shift):
    images, height, columns, channels = values.shape
    grouped = values.reshape(images, height, columns, GROUPS, channels // GROUPS)
    center = lax.optimization_barrier(jnp.mean(grouped, axis=(1, 2, 4), keepdims=True))
    spread = lax.optimization_barrier(jnp.mean(grouped * grouped, axis=(1, 2, 4), keepdims=True)) - center * center
    normed = (grouped - center) * lax.rsqrt(spread + EPSILON)
    return normed.reshape(values.shape) * gain + shift

def convolve(values, kernel):
    return lax.conv_general_dilated(values, kernel, (1, 1), 'SAME', dimension_numbers=('NHWC', 'HWIO', 'NHWC'), precision=HIGH)

def split_heads(array_in):
    return array_in.reshape(array_in.shape[0], HEADS, HEAD_DIM).transpose(1, 0, 2)

def one_head(head_parts):
    queries, key_rows, value_rows = head_parts
    scores = low_back(jnp.einsum('qd,kd->qk', queries, key_rows, precision=HIGH) * HEAD_DIM ** (-0.5))
    softmax_out = jax.nn.softmax(scores, axis=-1)
    return jnp.dot(low(softmax_out), value_rows, precision=HIGH)

def one_image(image_parts):
    queries, image_keys, image_values, context_keys, context_values = image_parts
    key_rows = jnp.concatenate([image_keys, context_keys], axis=0)
    value_rows = jnp.concatenate([image_values, context_values], axis=0)
    heads_out = lax.map(jax.checkpoint(one_head), (split_heads(queries), split_heads(key_rows), split_heads(value_rows)))
    return heads_out.transpose(1, 0, 2).reshape(queries.shape[0], HEADS * HEAD_DIM)

def reference(features, embedding, context, image_offset, first_gain, first_shift, conv_first, conv_first_bias, embed_weight, embed_bias, second_gain, second_shift, conv_second, conv_second_bias, attend_gain, attend_shift, attend_weight, attend_bias, context_weight, context_bias, output_weight, output_bias, cotangent):
    total_rows = features.shape[0]
    images = total_rows // IMG_H
    pixels = IMG_H * IMG_W
    channels = HEADS * HEAD_DIM
    first_row = image_offset[0]

    def stacked(array_in):
        return jnp.roll(array_in.astype(jnp.float32), -first_row, axis=0).reshape(images, IMG_H, IMG_W, array_in.shape[-1])

    def unstacked(array_in):
        return jnp.roll(array_in.reshape(total_rows, IMG_W, array_in.shape[-1]), first_row, axis=0)
    embed_in = embedding.astype(jnp.float32)
    context_in = context.astype(jnp.float32)
    params = tuple((weight_in.astype(jnp.float32) for weight_in in (first_gain, first_shift, conv_first, conv_first_bias, embed_weight, embed_bias, second_gain, second_shift, conv_second, conv_second_bias, attend_gain, attend_shift, attend_weight, attend_bias, context_weight, context_bias, output_weight, output_bias)))

    def forward(x_img, weights):
        gain_one, shift_one, kernel_one, kbias_one, embed_w, embed_b, gain_two, shift_two, kernel_two, kbias_two, gain_three, shift_three, attend_w, attend_b, context_w, context_b, output_w, output_b = weights
        normed_one = group_norm(x_img, gain_one, shift_one)
        act_one = low(jax.nn.silu(normed_one))
        middle = low_back(convolve(act_one, kernel_one)) + kbias_one
        modulate = jnp.dot(embed_in, embed_w.reshape(embed_w.shape[0], 2 * channels), precision=HIGH).reshape(images, 2, channels) + embed_b
        normed_two = group_norm(middle, gain_two, shift_two)
        hidden = normed_two * (1.0 + modulate[:, 0][:, None, None, :]) + modulate[:, 1][:, None, None, :]
        act_two = low(jax.nn.silu(hidden))
        inner = x_img + low_back(convolve(act_two, kernel_two)) + kbias_two
        normed_three = low(group_norm(inner, gain_three, shift_three))
        projected = jnp.einsum('ihwc,cto->ihwto', normed_three, attend_w, precision=HIGH)
        queries = low(low_back(projected[:, :, :, 0, :]) + attend_b[0])
        key_rows = low(low_back(projected[:, :, :, 1, :]))
        value_rows = low(low_back(projected[:, :, :, 2, :]) + attend_b[1])
        context_proj = jnp.einsum('inc,cto->into', context_in, context_w, precision=HIGH) + context_b
        context_keys = low(context_proj[:, :, 0, :])
        context_values = low(context_proj[:, :, 1, :])
        attended = lax.map(jax.checkpoint(one_image), (queries.reshape(images, pixels, channels), key_rows.reshape(images, pixels, channels), value_rows.reshape(images, pixels, channels), context_keys, context_values))
        attended = low(low_back(attended))
        projected_out = jnp.einsum('ipc,co->ipo', attended, output_w, precision=HIGH) + output_b
        return inner + projected_out.reshape(images, IMG_H, IMG_W, channels)
    output, pullback = jax.vjp(forward, stacked(features), params)
    grad_x, grads = pullback(stacked(cotangent))
    return (unstacked(output).astype(jnp.bfloat16), unstacked(grad_x).astype(jnp.bfloat16), grads[0], grads[1], grads[2], grads[3], grads[4], grads[5], grads[6], grads[7], grads[8], grads[9], grads[10], grads[11], grads[12], grads[13], grads[14], grads[15], grads[16], grads[17])
```

```python
import functools

import jax
import jax.numpy as jnp
from jax import lax
from jax.experimental import pallas as pl
from jax.experimental.pallas import tpu as pltpu
from jax.sharding import PartitionSpec as P

C = 512
HEAD_DIM = 64
GROUPS = 32
IMG_H = 64


EPSILON = 1e-05
HIGH = lax.Precision.HIGHEST
NEG = -1e30
bf16, f32 = jnp.bfloat16, jnp.float32
def from_behind(block, axis, distance):
    devices = range(lax.axis_size(axis))
    route = [((i - distance) % len(devices), i) for i in devices]
    return lax.ppermute(block, axis, route)


def dot(a, b, ca, cb):
    return lax.dot_general(a, b, (((ca,), (cb,)), ((), ())), preferred_element_type=f32)

def attend_kernel(tiles, tile_rows, cols, width, image_rows, total_rows, ctx_count, images,
                  info, q_ref, do_ref, kv_ref, ctx_ref,
                  o_ref, dq_ref, dkv_ref, dctx_ref,
                  kv, kt, vt, qt, dot_, s_buf, p_buf, dk, dv, oacc, qacc, sem):
    split, start_a, start_b = info[0], info[1], info[2]
    slab_rows = tiles * tile_rows
    tq = tile_rows * cols
    main = image_rows * cols
    tail = kv.shape[1] - main
    heads = width // HEAD_DIM
    straddle = split < slab_rows

    def row_copy(img, j, start):
        src = lax.rem(start + j, total_rows)
        return pltpu.make_async_copy(kv_ref.at[src], kv.at[img, pl.ds(pl.multiple_of(j * cols, cols), cols)], sem.at[img])

    def load(img, start):
        @pl.loop(0, image_rows)
        def _(j):
            row_copy(img, j, start).start()

    def finish(img, start):
        @pl.loop(0, image_rows)
        def _(j):
            row_copy(img, j, start).wait()
        kv[img, pl.ds(main, tail)] = ctx_ref[img]
        @pl.loop(0, kv.shape[1] // 256)
        def _(c):
            at = pl.ds(pl.multiple_of(c * 256, 256), 256)
            kt[img, :, at] = kv[img, at, :width].T
            vt[img, :, at] = kv[img, at, width:].T
        dk[img] = jnp.zeros(dk.shape[1:], f32)
        dv[img] = jnp.zeros(dv.shape[1:], f32)

    load(0, start_a)
    @pl.when(straddle)
    def _():
        load(1, start_b)
    for t in range(tiles):
        qt[t] = (q_ref[pl.ds(t * tq, tq)] * jnp.asarray(HEAD_DIM ** -0.5, bf16)).T
        dot_[t] = do_ref[pl.ds(t * tq, tq)].T
    finish(0, start_a)
    @pl.when(straddle)
    def _():
        finish(1, start_b)

    count_a = (split + tile_rows - 1) // tile_rows
    first_b = split // tile_rows
    count = count_a + jnp.where(straddle, tiles - first_b, 0)
    feature = lax.broadcasted_iota(jnp.int32, (width, 1), 0) // HEAD_DIM
    lane_row = lax.broadcasted_iota(jnp.int32, (1, tq), 1) // cols
    tail_ok = lax.broadcasted_iota(jnp.int32, (tail, 1), 0) < ctx_count
    chunks = 1
    CH = main

    @pl.loop(0, count)
    def _(item):
        is_b = (item >= count_a).astype(jnp.int32)
        t = jnp.where(is_b == 1, first_b + item - count_a, item)
        row = t * tile_rows + lane_row
        low = jnp.where(is_b == 1, split, 0)
        high = jnp.where(is_b == 1, slab_rows, split)
        mine = jnp.logical_and(row >= low, row < high)
        q_t = qt[t].astype(f32)
        do_t = dot_[t].astype(f32)
        qh = [jnp.where(feature == h, q_t, 0.0).astype(bf16) for h in range(heads)]

        def score(at, size, m, masked):
            keys = kv[is_b, at, :width]
            out = []
            for h in range(heads):
                s = dot(keys, qh[h], 1, 0)
                if masked:
                    s = jnp.where(tail_ok, s, NEG)
                s_buf[h, at] = s
                out.append(jnp.maximum(m[h], jnp.max(s.reshape(size // 8, 8, tq), axis=0)))
            return tuple(out)

        m = tuple(jnp.full((8, tq), NEG, f32) for _ in range(heads))
        m = lax.fori_loop(0, chunks, lambda c, m: score(pl.ds(pl.multiple_of(c * CH, CH), CH), CH, m, False), m)
        m = score(pl.ds(main, tail), tail, m, True)
        m = tuple(jnp.max(v, axis=0, keepdims=True) for v in m)

        def prob(at, size, carry):
            l, o = carry
            lo, oo = [], []
            for h in range(heads):
                p = jnp.exp(s_buf[h, at] - m[h])
                lo.append(l[h] + jnp.sum(p.reshape(size // 8, 8, tq), axis=0))
                pb = p.astype(bf16)
                p_buf[at, pl.ds(h * tq, tq)] = pb
                oo.append(o[h] + dot(vt[is_b, pl.ds(h * HEAD_DIM, HEAD_DIM), at], pb, 1, 0))
            return tuple(lo), tuple(oo)

        l = tuple(jnp.zeros((8, tq), f32) for _ in range(heads))
        o = tuple(jnp.zeros((HEAD_DIM, tq), f32) for _ in range(heads))
        l, o = lax.fori_loop(0, chunks, lambda c, x: prob(pl.ds(pl.multiple_of(c * CH, CH), CH), CH, x), (l, o))
        l, o = prob(pl.ds(main, tail), tail, (l, o))
        inv = [1.0 / jnp.sum(v, axis=0, keepdims=True) for v in l]
        o = [o[h] * inv[h] for h in range(heads)]
        o_all = jnp.concatenate(o, axis=0)
        do_h, delta = [], []
        for h in range(heads):
            scaled = jnp.where(mine, do_t * inv[h], 0.0)
            scaled = jnp.where(feature == h, scaled, 0.0).astype(bf16)
            do_h.append(scaled)
            delta.append(jnp.sum(scaled.astype(f32) * o_all, axis=0, keepdims=True))

        do_cat = jnp.concatenate(do_h, axis=1)
        q_cat = jnp.concatenate(qh, axis=1)

        def back(at, size, dq):
            keys = kv[is_b, at, :width]
            vals = kv[is_b, at, width:]
            out = []
            pbs, dss = [], []
            for h in range(heads):
                dp = dot(vals, do_h[h], 1, 0)
                pb = p_buf[at, pl.ds(h * tq, tq)]
                pbs.append(pb)
                ds = (pb.astype(f32) * (dp - delta[h])).astype(bf16)
                out.append(dq[h] + dot(kt[is_b, pl.ds(h * HEAD_DIM, HEAD_DIM), at], ds, 1, 0))
                dss.append(ds)
            dv_sum = dot(jnp.concatenate(pbs, axis=1), do_cat, 1, 1)
            dk_sum = dot(jnp.concatenate(dss, axis=1), q_cat, 1, 1)
            dv[is_b, at] = dv[is_b, at] + dv_sum
            dk[is_b, at] = dk[is_b, at] + dk_sum
            return tuple(out)

        dq = tuple(jnp.zeros((HEAD_DIM, tq), f32) for _ in range(heads))
        dq = lax.fori_loop(0, chunks, lambda c, x: back(pl.ds(pl.multiple_of(c * CH, CH), CH), CH, x), dq)
        dq = back(pl.ds(main, tail), tail, dq)
        oacc[t] = jnp.where(mine, o_all, oacc[t])
        qacc[t] = jnp.where(mine, jnp.concatenate(dq, axis=0) * (HEAD_DIM ** -0.5), qacc[t])

    for t in range(tiles):
        o_ref[pl.ds(t * tq, tq)] = oacc[t].T.astype(bf16)
        dq_ref[pl.ds(t * tq, tq)] = qacc[t].T

    dkv_ref[...] = jnp.zeros(dkv_ref.shape, dkv_ref.dtype)
    dctx_ref[...] = jnp.zeros(dctx_ref.shape, dctx_ref.dtype)
    share_rows = dctx_ref.shape[0] // images

    def put(img, start):
        @pl.loop(0, image_rows)
        def _(j):
            row = lax.rem(start + j, total_rows)
            at = pl.ds(pl.multiple_of(j * cols, cols), cols)
            dkv_ref[row, :, :width] = dk[img, at].astype(bf16)
            dkv_ref[row, :, width:] = dv[img, at].astype(bf16)
        at = pl.ds(pl.multiple_of(info[3 + img] * share_rows, 16), share_rows)
        dctx_ref[at, :width] = dk[img, pl.ds(main, share_rows)].astype(bf16)
        dctx_ref[at, width:] = dv[img, pl.ds(main, share_rows)].astype(bf16)
    put(0, start_a)
    @pl.when(straddle)
    def _():
        put(1, start_b)

def attend(info, q, do, kv_window, ctx, total_rows, image_rows, ctx_count, images, share_rows, tile_rows=4):
    tokens, width = q.shape
    rows, cols, _ = kv_window.shape
    tiles = tokens // (tile_rows * cols)
    tq = tile_rows * cols
    tail = ctx.shape[1]
    keys = image_rows * cols + tail
    heads = width // HEAD_DIM
    kern = functools.partial(attend_kernel, tiles, tile_rows, cols, width, image_rows, total_rows, ctx_count, images)
    vm = pl.BlockSpec(memory_space=pltpu.VMEM)
    return pl.pallas_call(
        kern, name="attend",
        out_shape=(jax.ShapeDtypeStruct((tokens, width), bf16), jax.ShapeDtypeStruct((tokens, width), f32),
                   jax.ShapeDtypeStruct(kv_window.shape, bf16), jax.ShapeDtypeStruct((images * share_rows, 2 * width), bf16)),
        in_specs=[pl.BlockSpec(memory_space=pltpu.SMEM), vm, vm, pl.BlockSpec(memory_space=pl.ANY), vm],
        out_specs=(vm, vm, vm, vm),
        scratch_shapes=[
            pltpu.VMEM((2, keys, 2 * width), bf16),
            pltpu.VMEM((2, width, keys), bf16), pltpu.VMEM((2, width, keys), bf16),
            pltpu.VMEM((tiles, width, tq), bf16), pltpu.VMEM((tiles, width, tq), bf16),
            pltpu.VMEM((heads, keys, tq), f32), pltpu.VMEM((keys, heads * tq), bf16),
            pltpu.VMEM((2, keys, width), f32), pltpu.VMEM((2, keys, width), f32),
            pltpu.VMEM((tiles, width, tq), f32), pltpu.VMEM((tiles, width, tq), f32),
            pltpu.SemaphoreType.DMA((2,)),
        ],
        cost_estimate=pl.CostEstimate(flops=12 * tokens * keys * width, bytes_accessed=8 * 2**20, transcendentals=heads * tokens * keys),
        compiler_params=pltpu.CompilerParams(vmem_limit_bytes=60 * 2**20),
    )(info, q, do, kv_window, ctx)


MESH = pl.DeviceIdType.MESH


def vmem(shape, dtype=f32):
    return pltpu.VMEM(shape, dtype)


def greet(devices):
    barrier = pltpu.get_barrier_semaphore()
    for device in devices:
        pl.semaphore_signal(barrier, inc=1, device_id=device, device_id_type=MESH)
    pl.semaphore_wait(barrier, len(devices))


def row_peers(count):
    r, z = lax.axis_index("rows"), lax.axis_index("chan")
    return [(lax.rem(r + d, count), z) for d in range(1, count)]


def chan_peers(count):
    r, z = lax.axis_index("rows"), lax.axis_index("chan")
    return [(r, lax.rem(z + d, count)) for d in range(1, count)]


def push(src, dst, send_sem, recv_sem, device):
    copy = pltpu.make_async_remote_copy(
        src_ref=src, dst_ref=dst, send_sem=send_sem, recv_sem=recv_sem, device_id=device, device_id_type=MESH
    )
    copy.start()
    return copy


def share(buf, sends, recvs, count, pieces):
    me = lax.axis_index("rows")
    for index, piece in enumerate(pieces):
        buf[me, pl.ds(index, 1), :] = piece
    copies = [
        push(buf.at[me], buf.at[me], sends.at[d], recvs.at[d], device) for d, device in enumerate(row_peers(count))
    ]
    return copies


def share_total(buf, copies):
    for copy in copies:
        copy.wait()
    total = buf[0]
    for index in range(1, buf.shape[0]):
        total = total + buf[index]
    return total


def group_sum(values, per_group):
    width = values.shape[1]
    one = lax.broadcasted_iota(jnp.int32, (width, width), 0) // per_group
    two = lax.broadcasted_iota(jnp.int32, (width, width), 1) // per_group
    same = (one == two).astype(f32)
    return jnp.dot(values, same, precision=HIGH, preferred_element_type=f32)


def image_sums(values, member):
    by_row = jnp.sum(values, axis=1, keepdims=True)
    return [jnp.sum(by_row * member[i], axis=0) for i in range(member.shape[0])]


def to_rows(per_image, member):
    total = None
    for i, value in enumerate(per_image):
        term = member[i] * value[None]
        total = term if total is None else total + term
    return total


def norm_rows(total, member, entries, per_group):
    images = member.shape[0]
    grouped = group_sum(total, per_group) * (1.0 / entries)
    centers, scales = [], []
    for i in range(images):
        center = grouped[2 * i : 2 * i + 1]
        square = grouped[2 * i + 1 : 2 * i + 2]
        centers.append(center)
        scales.append(lax.rsqrt(square - center * center + EPSILON))
    return to_rows(centers, member), to_rows(scales, member)


def taps(pad, upper, lower, x9):
    rows, cols, width = pad.shape
    rows = rows - 2
    tokens = rows * cols
    col = lax.rem(lax.broadcasted_iota(jnp.int32, (tokens, 1), 0), cols)
    for a in range(3):
        v = pad[pl.ds(a, rows)].astype(f32)
        if a == 0:
            v = v * upper[...]
        if a == 2:
            v = v * lower[...]
        v = v.reshape(tokens, width)
        left = jnp.where(col == 0, 0.0, pltpu.roll(v, 1, 0))
        right = jnp.where(col == cols - 1, 0.0, pltpu.roll(v, tokens - 1, 0))
        for b, part in enumerate((left, v, right)):
            x9[:, pl.ds((3 * a + b) * width, width)] = part.astype(bf16)


def scatter_sum(lhs, weight, out, recv, sends, recvs, count, width):
    z = lax.axis_index("chan")
    copies = []
    for d, device in enumerate(chan_peers(count)):
        at = pl.ds(pl.multiple_of(device[1] * width, width), width)
        out[d] = jnp.dot(lhs[...], weight[:, at], preferred_element_type=f32).astype(bf16)
        copies.append(push(out.at[d], recv.at[d], sends.at[d], recvs.at[d], device))
    at = pl.ds(pl.multiple_of(z * width, width), width)
    return jnp.dot(lhs[...], weight[:, at], preferred_element_type=f32), copies


def forward_kernel(row_count, chan_count, per_group, entries,
                   x_ref, member, upper, lower, vec, mod, w1, w2, w_att,
                   x9_1, x9_2, c1_ref, x1_ref, row_ref, a3_ref, q_ref, kv_ref,
                   pad1, pad2, send1, recv1, send2, recv2, stat, stat_s, stat_r, halo_s, halo_r, z_s, z_r):
    rows, cols, width = x_ref.shape
    tokens = rows * cols
    r, z = lax.axis_index("rows"), lax.axis_index("chan")
    greet(row_peers(row_count) + chan_peers(chan_count))
    up = (lax.rem(r + row_count - 1, row_count), z)
    down = (lax.rem(r + 1, row_count), z)
    pending = []

    def vector(i):
        return vec[i : i + 1, :][None]

    def stats(phase, values):
        pieces = []
        for a, b in zip(image_sums(values, member), image_sums(values * values, member)):
            pieces += [a, b]
        copies = share(stat.at[phase], stat_s.at[phase], stat_r.at[phase], row_count, pieces)
        center, scale = norm_rows(share_total(stat.at[phase], copies), member, entries, per_group)
        row_ref[2 * phase] = center
        row_ref[2 * phase + 1] = scale
        return (values - center) * scale

    def rims(phase, pad):
        one = push(pad.at[1], pad.at[rows + 1], halo_s.at[phase, 0], halo_r.at[phase, 0], up)
        two = push(pad.at[rows], pad.at[0], halo_s.at[phase, 1], halo_r.at[phase, 1], down)
        one.wait()
        two.wait()

    def collect(own, recv, copies):
        total = own
        for d, copy in enumerate(copies):
            copy.wait_recv()
            total = total + recv[d].astype(f32)
        pending.extend(copies)
        return total

    x = x_ref[...].astype(f32)
    n1 = stats(0, x) * vector(0) + vector(1)
    pad1[pl.ds(1, rows)] = (n1 * jax.nn.sigmoid(n1)).astype(bf16)
    rims(0, pad1)
    taps(pad1, upper, lower, x9_1)
    own, copies = scatter_sum(x9_1, w1, send1, recv1, z_s.at[0], z_r.at[0], chan_count, width)
    c1 = collect(own, recv1, copies).reshape(rows, cols, width) + vector(2)
    c1_ref[...] = c1
    n2 = stats(1, c1) * vector(3) + vector(4)
    images = member.shape[0]
    mod_scale = to_rows([mod[i, 0:1, :] for i in range(images)], member)
    mod_shift = to_rows([mod[i, 1:2, :] for i in range(images)], member)
    h2 = n2 * (1.0 + mod_scale) + mod_shift
    pad2[pl.ds(1, rows)] = (h2 * jax.nn.sigmoid(h2)).astype(bf16)
    rims(1, pad2)
    taps(pad2, upper, lower, x9_2)
    own, copies = scatter_sum(x9_2, w2, send2, recv2, z_s.at[1], z_r.at[1], chan_count, width)
    x1 = x_ref[...].astype(f32) + (collect(own, recv2, copies).reshape(rows, cols, width) + vector(5))
    x1_ref[...] = x1
    a3 = stats(2, x1) * vector(6) + vector(7)
    a3_ref[z] = a3.astype(bf16).reshape(tokens, width)
    copies = [
        push(a3_ref.at[z], a3_ref.at[z], z_s.at[2, d], z_r.at[2, d], device)
        for d, device in enumerate(chan_peers(chan_count))
    ]
    for copy in copies:
        copy.wait_recv()
    pending.extend(copies)
    qkv = None
    for i in range(chan_count):
        term = jnp.dot(a3_ref[i], w_att[pl.ds(i * width, width), :], preferred_element_type=f32)
        qkv = term if qkv is None else qkv + term
    q_ref[...] = (qkv[:, :width] + vec[8:9, :]).astype(bf16)
    kv_ref[:, :width] = qkv[:, width : 2 * width].astype(bf16)
    kv_ref[:, width:] = (qkv[:, 2 * width :] + vec[9:10, :]).astype(bf16)
    for copy in pending:
        copy.wait_send()


def forward_block(row_count, chan_count, per_group, entries, x, member, upper, lower, vec, mod, w1, w2, w_att):
    rows, cols, width = x.shape
    tokens = rows * cols
    images = member.shape[0]
    message = -(-2 * images // 8) * 8
    vm = pl.BlockSpec(memory_space=pltpu.VMEM)
    S = jax.ShapeDtypeStruct
    peers = max(chan_count - 1, 1)
    return pl.pallas_call(
        functools.partial(forward_kernel, row_count, chan_count, per_group, entries),
        name="forward_block",
        out_shape=(
            S((tokens, 9 * width), bf16),
            S((tokens, 9 * width), bf16),
            S((rows, cols, width), f32),
            S((rows, cols, width), f32),
            S((6, rows, 1, width), f32),
            S((chan_count, tokens, width), bf16),
            S((tokens, width), bf16),
            S((tokens, 2 * width), bf16),
        ),
        in_specs=[vm] * 9,
        out_specs=(vm,) * 8,
        scratch_shapes=[
            vmem((rows + 2, cols, width), bf16),
            vmem((rows + 2, cols, width), bf16),
            vmem((peers, tokens, width), bf16),
            vmem((peers, tokens, width), bf16),
            vmem((peers, tokens, width), bf16),
            vmem((peers, tokens, width), bf16),
            vmem((3, row_count, message, width), f32),
            pltpu.SemaphoreType.DMA((3, row_count - 1)),
            pltpu.SemaphoreType.DMA((3, row_count - 1)),
            pltpu.SemaphoreType.DMA((2, 2)),
            pltpu.SemaphoreType.DMA((2, 2)),
            pltpu.SemaphoreType.DMA((3, peers)),
            pltpu.SemaphoreType.DMA((3, peers)),
        ],
        cost_estimate=pl.CostEstimate(flops=2 * 4 * 9 * tokens * width * width * 4, bytes_accessed=16 * 2**20, transcendentals=4 * tokens * width),
        compiler_params=pltpu.CompilerParams(collective_id=0, has_side_effects=True, vmem_limit_bytes=56 * 2**20),
    )(x, member, upper, lower, vec, mod, w1, w2, w_att)


def gather_kernel(row_count, chan_count, kv_ref, g_ref, wo_ref, all_ref, gall_ref, do_ref, one_s, one_r, z_s, z_r):
    r, z = lax.axis_index("rows"), lax.axis_index("chan")
    window = all_ref.shape[0]
    tokens, width = g_ref.shape
    half = tokens // 2
    pending = []
    if window == row_count == 8:
        x_dev = r + 2 - 4 * lax.rem(r // 2, 2)
        y_dev = r + 4 - 8 * (r // 4)
        core = r + 1 - 2 * lax.rem(r, 2)
        greet([(x_dev, z), (y_dev, z), (core, z)] + chan_peers(chan_count))
    else:
        greet(row_peers(row_count) + chan_peers(chan_count))
    gall_ref[z] = g_ref[...]
    z_copies = [
        push(g_ref, gall_ref.at[z], z_s.at[d], z_r.at[d], device) for d, device in enumerate(chan_peers(chan_count))
    ]
    if window == row_count == 8:
        first, second = pl.ds(0, half), pl.ds(half, half)
        all_ref[r] = kv_ref[...]

        def send(i, slab, part, device):
            copy = push(all_ref.at[slab, part], all_ref.at[slab, part], one_s.at[i], one_r.at[i], (device, z))
            pending.append(copy)
            return copy

        x1 = send(0, r, first, x_dev)
        y2 = send(1, r, second, y_dev)
        x2 = send(2, r, second, x_dev)
        y1 = send(3, r, first, y_dev)
        c0 = send(4, r, pl.ds(0, tokens), core)
        x1.wait_recv()
        f1 = send(5, x_dev, first, y_dev)
        g1 = send(6, x_dev, first, core)
        y2.wait_recv()
        f2 = send(7, y_dev, second, x_dev)
        g2 = send(8, y_dev, second, core)
        x2.wait_recv()
        g3 = send(9, x_dev, second, core)
        y1.wait_recv()
        g4 = send(10, y_dev, first, core)
        diag = x_dev + y_dev - r
        f1.wait_recv()
        g5 = send(11, diag, first, core)
        f2.wait_recv()
        g6 = send(12, diag, second, core)
        waits = [c0, g1, g2, g3, g4, g5, g6]
    else:
        base = r - (window // 2) if window < row_count else 0
        own = window // 2 if window < row_count else r
        all_ref[own] = kv_ref[...]
        for i in range(1, row_count):
            place = window // 2 - i if i <= window // 2 else window // 2 + row_count - i
            if window < row_count and (place < 0 or place >= window):
                continue
            slot = place if window < row_count else r
            pending.append(push(kv_ref, all_ref.at[slot], one_s.at[i], one_r.at[i], (lax.rem(r + i, row_count), z)))
        waits = list(pending)
    do = None
    order = [z] + [lax.rem(z - d + chan_count, chan_count) for d in range(1, chan_count)]
    for i, block in enumerate(order):
        if i > 0:
            z_copies[i - 1].wait_recv()
        at = pl.ds(pl.multiple_of(block * width, width), width)
        term = lax.dot_general(gall_ref[block], wo_ref[:, at], (((1,), (1,)), ((), ())), preferred_element_type=f32)
        do = term if do is None else do + term
    do_ref[...] = do.astype(bf16)
    for copy in waits:
        copy.wait_recv()
    for copy in pending + z_copies:
        copy.wait_send()


def gather_block(row_count, chan_count, window, kv, g, wo):
    tokens, width = g.shape
    vm = pl.BlockSpec(memory_space=pltpu.VMEM)
    S = jax.ShapeDtypeStruct
    copies = max(16, row_count)
    return pl.pallas_call(
        functools.partial(gather_kernel, row_count, chan_count),
        name="gather_block",
        out_shape=(S((window, tokens, 2 * width), bf16), S((chan_count, tokens, width), bf16), S((tokens, width), bf16)),
        in_specs=[vm] * 3,
        out_specs=(vm,) * 3,
        scratch_shapes=[
            pltpu.SemaphoreType.DMA((copies,)),
            pltpu.SemaphoreType.DMA((copies,)),
            pltpu.SemaphoreType.DMA((max(chan_count - 1, 1),)),
            pltpu.SemaphoreType.DMA((max(chan_count - 1, 1),)),
        ],
        cost_estimate=pl.CostEstimate(flops=2 * tokens * width * width * chan_count, bytes_accessed=8 * 2**20, transcendentals=0),
        compiler_params=pltpu.CompilerParams(collective_id=1, has_side_effects=True, vmem_limit_bytes=56 * 2**20),
    )(kv, g, wo)


def contract(a, b, a_dim, b_dim):
    return lax.dot_general(a, b, (((a_dim,), (b_dim,)), ((), ())), preferred_element_type=f32)


def plane(count):
    r = lax.axis_index("rows")
    core = r + 1 - 2 * lax.rem(r, 2)
    x_dev = r + 2 - 4 * lax.rem(r // 2, 2)
    y_dev = r + 4 - 8 * (r // 4)
    return core, x_dev, y_dev, x_dev + y_dev - r


class Total:
    def __init__(self, part, half, quarters, out, sends, recvs):
        self.part, self.half, self.quarters, self.out = part, half, quarters, out
        self.sends, self.recvs = sends, recvs
        self.r, self.z = lax.axis_index("rows"), lax.axis_index("chan")
        self.core, self.x, self.y, self.d = plane(8)
        self.n = part.shape[0] // 8
        self.copies = []

    def rows(self, device, size=1):
        return pl.ds(pl.multiple_of((lax.rem(device, 2) * 4 + device // 2) * self.n, 16), self.n)

    def half_rows(self, device):
        return pl.ds(pl.multiple_of(lax.rem(device, 2) * 4 * self.n, 16), 4 * self.n)

    def send(self, i, src, dst, device):
        copy = push(src, dst, self.sends.at[i], self.recvs.at[i], (device, self.z))
        self.copies.append(copy)
        return copy

    def one(self):
        self.a = self.send(0, self.part.at[self.half_rows(self.core)], self.half, self.core)

    def two(self):
        self.a.wait_recv()
        mine = self.half_rows(self.r)
        self.half[...] = (self.part[mine, :].astype(f32) + self.half[...].astype(f32)).astype(bf16)
        self.b = []
        for i, device in enumerate((self.d, self.x, self.y)):
            at = pl.ds(pl.multiple_of((device // 2) * self.n, 16), self.n)
            self.b.append(self.send(1 + i, self.half.at[at], self.quarters.at[i], device))

    def three(self):
        at = pl.ds(pl.multiple_of((self.r // 2) * self.n, 16), self.n)
        total = self.half[at, :].astype(f32)
        for i, copy in enumerate(self.b):
            copy.wait_recv()
            total = total + self.quarters[i].astype(f32)
        mine = self.rows(self.r)
        self.out[mine, :] = total.astype(bf16)
        self.c = []
        for i, device in enumerate((self.d, self.x, self.y, self.core)):
            self.c.append(self.send(4 + i, self.out.at[mine], self.out.at[mine], device))

    def four(self):
        self.e = [self.c[3]]
        for i, device in ((1, self.x), (2, self.y), (0, self.d)):
            self.c[i].wait_recv()
            at = self.rows(device)
            self.e.append(self.send(8 + i, self.out.at[at], self.out.at[at], self.core))

    def finish(self):
        for copy in self.e:
            copy.wait_recv()
        for copy in self.copies:
            copy.wait_send()


def total_scratch(n, width):
    return [vmem((n // 2, width), bf16), vmem((3, n // 8, width), bf16), pltpu.SemaphoreType.DMA((11,)), pltpu.SemaphoreType.DMA((11,))]


def backward_kernel(row_count, chan_count, per_group, entries, fast, *refs):
    names = (
        "x", "dq", "dkv", "o", "g_all", "a3_all", "x1", "c1", "rows_in", "member", "upper", "lower", "vec", "mod",
        "x9_1", "x9_2", "w1", "w2", "w_att", "wo", "dctx", "result", "dfeat", "sums", "g_conv1", "g_conv2", "g_att",
        "g_out", "g_ctx", "part1", "part2", "part_att", "part_out", "half1", "quar1", "s_1", "r_1", "half2", "quar2",
        "s_2", "r_2", "half_att", "quar_att", "s_att", "r_att", "half_out", "quar_out", "s_out", "r_out", "half_ctx",
        "quar_ctx", "s_ctx", "r_ctx", "vx9_1", "vx9_2", "vw1", "vw2", "vc1", "va3", "load_s", "core_buf", "send_kv",
        "recv_kv", "relay", "kv_s", "kv_r", "zsend", "zrecv", "z_s", "z_r", "d3", "own", "gpad", "halo_s", "halo_r",
        "zh_s", "zh_r", "stat", "stat_s", "stat_r", "dx1",
    )
    k = dict(zip(names, refs))
    assert len(names) == len(refs)
    rows, cols, width = k["x"].shape
    tokens = rows * cols
    r, z = lax.axis_index("rows"), lax.axis_index("chan")
    member, vec, mod, upper, lower = k["member"], k["vec"], k["mod"], k["upper"], k["lower"]
    images = member.shape[0]
    up = (lax.rem(r + row_count - 1, row_count), z)
    down = (lax.rem(r + 1, row_count), z)
    z_peers = chan_peers(chan_count)
    loads = {}
    for i, (src, dst) in enumerate((("a3_all", "va3"), ("x9_2", "vx9_2"), ("w2", "vw2"), ("c1", "vc1"), ("x9_1", "vx9_1"), ("w1", "vw1"))):
        loads[dst] = pltpu.make_async_copy(k[src], k[dst], k["load_s"].at[i])
        loads[dst].start()
    greet(row_peers(row_count) + z_peers)
    pending = []

    def shaped(values):
        return values.reshape(rows, cols, width)

    def vector(i):
        return vec[i : i + 1, :][None]

    def scatter(phase, block):
        copies = []
        for d, device in enumerate(z_peers):
            k["zsend"][phase, d] = block(device[1]).astype(bf16)
            copies.append(push(k["zsend"].at[phase, d], k["zrecv"].at[phase, d], k["z_s"].at[phase, d], k["z_r"].at[phase, d], device))
        pending.extend(copies)
        k["own"][phase] = block(z)
        return copies

    def collect(phase, copies):
        total = k["own"][phase]
        for d, copy in enumerate(copies):
            copy.wait_recv()
            total = total + k["zrecv"][phase, d].astype(f32)
        return shaped(total)

    def exchange(phase, pieces):
        buf = k["stat"].at[phase]
        copies = share(buf, k["stat_s"].at[phase], k["stat_r"].at[phase], row_count, pieces)
        return share_total(buf, copies)

    def norm_back(phase, total, dxh, xhat, scale):
        grouped = group_sum(total[: 2 * images], per_group) * (1.0 / entries)
        first = to_rows([grouped[2 * i : 2 * i + 1] for i in range(images)], member)
        second = to_rows([grouped[2 * i + 1 : 2 * i + 2] for i in range(images)], member)
        return scale * (dxh - first - xhat * second)

    def norm_pieces(dxh, xhat):
        pieces = []
        for a, b in zip(image_sums(dxh, member), image_sums(dxh * xhat, member)):
            pieces += [a, b]
        return pieces

    def channel_total(values):
        return jnp.sum(jnp.sum(values, axis=1, keepdims=True), axis=0)

    def gather_grad(phase, values):
        pad = k["gpad"].at[phase]
        pad[z, pl.ds(1, rows)] = values
        one = push(pad.at[z, 1], pad.at[z, rows + 1], k["halo_s"].at[phase, 0], k["halo_r"].at[phase, 0], up)
        two = push(pad.at[z, rows], pad.at[z, 0], k["halo_s"].at[phase, 1], k["halo_r"].at[phase, 1], down)
        inner = pl.ds(1, rows)
        copies = [
            push(pad.at[z, inner], pad.at[z, inner], k["zh_s"].at[phase, 0, d], k["zh_r"].at[phase, 0, d], device)
            for d, device in enumerate(z_peers)
        ]
        one.wait_recv()
        two.wait_recv()
        for j, row in enumerate((0, rows + 1)):
            copies += [
                push(pad.at[z, row], pad.at[z, row], k["zh_s"].at[phase, 1 + j, d], k["zh_r"].at[phase, 1 + j, d], device)
                for d, device in enumerate(z_peers)
            ]
        pending.extend(copies + [one, two])
        return copies

    def grad_rows(phase, start, mask):
        parts = []
        for i in range(chan_count):
            part = k["gpad"][phase, i, pl.ds(start, rows)]
            if mask is not None:
                part = (part.astype(f32) * mask[...]).astype(bf16)
            parts.append(part.reshape(tokens, width))
        return jnp.concatenate(parts, axis=1)

    def conv_grads(phase, x9, part):
        grad = grad_rows(phase, 1, None)
        for a in range(3):
            at = pl.ds(a * 3 * width, 3 * width)
            part[at, :] = contract(x9[:, at], grad, 0, 0).astype(bf16)

    def conv_back(phase, weight):
        total = None
        for a, mask in enumerate((lower, None, upper)):
            grad = grad_rows(phase, 2 - a, mask)
            term = contract(grad, weight[pl.ds(a * 3 * width, 3 * width), :], 1, 1)
            total = term if total is None else total + term
        col = lax.rem(lax.broadcasted_iota(jnp.int32, (tokens, 1), 0), cols)
        before = jnp.where(col == cols - 1, 0.0, pltpu.roll(total[:, :width], tokens - 1, 0))
        after = jnp.where(col == 0, 0.0, pltpu.roll(total[:, 2 * width :], 1, 0))
        return shaped(before + total[:, width : 2 * width] + after)

    def silu_slope(values):
        gate = jax.nn.sigmoid(values)
        return gate * (1.0 + values * (1.0 - gate))

    if fast:
        core, x_dev, y_dev, diag = plane(row_count)
        half = tokens // 2
        first, second = pl.ds(0, half), pl.ds(half, half)
        kv_copies = []

        def send(i, src, dst, device):
            copy = push(src, dst, k["kv_s"].at[i], k["kv_r"].at[i], (device, z))
            kv_copies.append(copy)
            return copy

        step = core - r
        to_core = [
            send(i, k["dkv"].at[device + step], k["core_buf"].at[i], core)
            for i, device in enumerate((diag, x_dev, y_dev, r))
        ]

    result_copies = scatter(0, lambda j: jnp.dot(k["o"][...], k["wo"][:, pl.ds(pl.multiple_of(j * width, width), width)], preferred_element_type=f32))

    if fast:
        def chip_sum(i, device, part):
            return k["dkv"][device, part].astype(f32) + k["core_buf"][i, part].astype(f32)

        to_core[0].wait_recv()
        k["send_kv"][0, first] = chip_sum(0, diag, first).astype(bf16)
        relay_x = send(4, k["send_kv"].at[0, first], k["relay"].at[0], x_dev)
        k["send_kv"][0, second] = chip_sum(0, diag, second).astype(bf16)
        relay_y = send(5, k["send_kv"].at[0, second], k["relay"].at[1], y_dev)
        to_core[1].wait_recv()
        k["send_kv"][1, first] = chip_sum(1, x_dev, first).astype(bf16)
        plain_x = send(6, k["send_kv"].at[1, first], k["recv_kv"].at[0, first], x_dev)
        to_core[2].wait_recv()
        k["send_kv"][2, second] = chip_sum(2, y_dev, second).astype(bf16)
        plain_y = send(7, k["send_kv"].at[2, second], k["recv_kv"].at[1, second], y_dev)

    g_cat = jnp.concatenate([k["g_all"][i] for i in range(chan_count)], axis=1)
    out_grad = contract(k["o"][...], g_cat, 0, 0)
    k["part_out"][...] = out_grad.astype(bf16)

    if fast:
        relay_x.wait_recv()
        k["send_kv"][2, first] = (chip_sum(2, y_dev, first) + k["relay"][0].astype(f32)).astype(bf16)
        merged_y = send(8, k["send_kv"].at[2, first], k["recv_kv"].at[1, first], y_dev)
        relay_y.wait_recv()
        k["send_kv"][1, second] = (chip_sum(1, x_dev, second) + k["relay"][1].astype(f32)).astype(bf16)
        merged_x = send(9, k["send_kv"].at[1, second], k["recv_kv"].at[0, second], x_dev)
        to_core[3].wait_recv()
        dkv = chip_sum(3, r, pl.ds(0, tokens))
        for copy in (plain_x, plain_y, merged_y, merged_x):
            copy.wait_recv()
        dkv = dkv + k["recv_kv"][0].astype(f32) + k["recv_kv"][1].astype(f32)
        pending.extend(kv_copies)
    else:
        dkv = k["dkv"][...]
    dq = k["dq"][...]
    k["d3"][:, :width] = dq.astype(bf16)
    k["d3"][:, width:] = dkv.astype(bf16)
    bias_q = jnp.sum(dq, axis=0, keepdims=True)
    bias_v = jnp.sum(dkv[:, width:], axis=0, keepdims=True)

    da3_copies = scatter(1, lambda j: contract(k["d3"][...], k["w_att"][pl.ds(pl.multiple_of(j * width, width), width), :], 1, 1))
    loads["va3"].wait()
    for i in range(chan_count):
        k["part_att"][pl.ds(i * width, width), :] = contract(k["va3"][i], k["d3"][...], 0, 0).astype(bf16)
    totals = {}
    if fast:
        for name, part, out in (("att", "part_att", "g_att"), ("out", "part_out", "g_out"), ("ctx", "dctx", "g_ctx")):
            totals[name] = Total(k[part], k["half_" + name], k["quar_" + name], k[out], k["s_" + name], k["r_" + name])
            totals[name].one()

    x1 = k["x1"][...]
    k["result"][...] = (x1 + collect(0, result_copies) + vector(10)).astype(bf16)
    for t in totals.values():
        t.two()
    g = shaped(k["g_all"][z].astype(f32))
    da3 = collect(1, da3_copies)
    for t in totals.values():
        t.three()
    center, scale = k["rows_in"][4], k["rows_in"][5]
    xhat = (x1 - center) * scale
    dxh = da3 * vector(6)
    total = exchange(
        0,
        norm_pieces(dxh, xhat) + [channel_total(da3 * xhat), channel_total(da3), bias_q, bias_v, channel_total(g)],
    )
    k["sums"][0:5, :] = total[2 * images : 2 * images + 5]
    dx1 = g + norm_back(0, total, dxh, xhat, scale)
    k["dx1"][...] = dx1
    bias_2 = channel_total(dx1)
    copies = gather_grad(0, dx1.astype(bf16))
    for t in totals.values():
        t.four()
    for i in ("vc1", "vx9_2", "vw2"):
        loads[i].wait()
    center, scale = k["rows_in"][2], k["rows_in"][3]
    xhat = (k["vc1"][...] - center) * scale
    n2 = xhat * vector(3) + vector(4)
    mod_scale = 1.0 + to_rows([mod[i, 0:1, :] for i in range(images)], member)
    mod_shift = to_rows([mod[i, 1:2, :] for i in range(images)], member)
    slope = silu_slope(n2 * mod_scale + mod_shift)
    for copy in copies:
        copy.wait_recv()
    dh2 = conv_back(0, k["vw2"]) * slope
    dn2 = dh2 * mod_scale
    dxh = dn2 * vector(3)
    conv_grads(0, k["vx9_2"], k["part2"])
    if fast:
        for t in totals.values():
            t.finish()
        totals = {"2": Total(k["part2"], k["half2"], k["quar2"], k["g_conv2"], k["s_2"], k["r_2"])}
        totals["2"].one()
    dss = []
    for a, b in zip(image_sums(dh2 * n2, member), image_sums(dh2, member)):
        dss += [a, b]
    total = exchange(1, norm_pieces(dxh, xhat) + [channel_total(dn2 * xhat), channel_total(dn2), bias_2] + dss)
    k["sums"][5 : 8 + 2 * images, :] = total[2 * images : 4 * images + 3]
    dc1 = norm_back(1, total, dxh, xhat, scale)
    bias_1 = channel_total(dc1)
    copies = gather_grad(1, dc1.astype(bf16))
    for t in totals.values():
        t.two()
    for i in ("vx9_1", "vw1"):
        loads[i].wait()
    center, scale = k["rows_in"][0], k["rows_in"][1]
    xhat = (k["x"][...].astype(f32) - center) * scale
    slope = silu_slope(xhat * vector(0) + vector(1))
    for t in totals.values():
        t.three()
    for t in totals.values():
        t.four()
    for copy in copies:
        copy.wait_recv()
    conv_grads(1, k["vx9_1"], k["part1"])
    if fast:
        last = Total(k["part1"], k["half1"], k["quar1"], k["g_conv1"], k["s_1"], k["r_1"])
        last.one()
        for t in totals.values():
            t.finish()
    dn1 = conv_back(1, k["vw1"]) * slope
    dxh = dn1 * vector(0)
    if fast:
        last.two()
    total = exchange(2, norm_pieces(dxh, xhat) + [channel_total(dn1 * xhat), channel_total(dn1), bias_1])
    if fast:
        last.three()
    k["sums"][8 + 2 * images : 11 + 2 * images, :] = total[2 * images : 2 * images + 3]
    k["dfeat"][...] = (k["dx1"][...] + norm_back(2, total, dxh, xhat, scale)).astype(bf16)
    if fast:
        last.four()
        last.finish()
    else:
        k["g_conv1"][...] = k["part1"][...]
        k["g_conv2"][...] = k["part2"][...]
        k["g_att"][...] = k["part_att"][...]
        k["g_out"][...] = k["part_out"][...]
        k["g_ctx"][...] = k["dctx"][...]
    for copy in pending:
        copy.wait_send()


def backward_block(row_count, chan_count, per_group, entries, fast, x, dq, dkv, o, g_all, a3_all, x1, c1, rows_in, member,
                   upper, lower, vec, mod, x9_1, x9_2, w1, w2, w_att, wo, dctx):
    rows, cols, width = x.shape
    tokens = rows * cols
    images = member.shape[0]
    full = chan_count * width
    taps_n = 9 * width
    message = -(-(4 * images + 5) // 8) * 8
    vm = pl.BlockSpec(memory_space=pltpu.VMEM)
    hbm = pl.BlockSpec(memory_space=pl.ANY)
    S = jax.ShapeDtypeStruct
    sem = pltpu.SemaphoreType.DMA
    peers = max(chan_count - 1, 1)
    late = {"a3_all", "c1", "x9_1", "x9_2", "w1", "w2"}
    order = (
        "x", "dq", "dkv", "o", "g_all", "a3_all", "x1", "c1", "rows_in", "member", "upper", "lower", "vec", "mod",
        "x9_1", "x9_2", "w1", "w2", "w_att", "wo", "dctx",
    )
    ctx_n, ctx_w = dctx.shape
    total_rows = -(-(11 + 2 * images) // 8) * 8
    return pl.pallas_call(
        functools.partial(backward_kernel, row_count, chan_count, per_group, entries, fast),
        name="backward_block",
        out_shape=(
            S((rows, cols, width), bf16), S((rows, cols, width), bf16), S((total_rows, width), f32),
            S((taps_n, full), bf16), S((taps_n, full), bf16), S((full, 3 * width), bf16), S((width, full), bf16),
            S((ctx_n, ctx_w), bf16),
        ),
        in_specs=[hbm if name in late else vm for name in order],
        out_specs=(vm,) * 8,
        scratch_shapes=[
            vmem((taps_n, full), bf16), vmem((taps_n, full), bf16), vmem((full, 3 * width), bf16), vmem((width, full), bf16),
            *total_scratch(taps_n, full), *total_scratch(taps_n, full), *total_scratch(full, 3 * width),
            *total_scratch(width, full), *total_scratch(ctx_n, ctx_w),
            vmem((tokens, taps_n), bf16), vmem((tokens, taps_n), bf16), vmem((taps_n, full), bf16), vmem((taps_n, full), bf16),
            vmem((rows, cols, width), f32), vmem((chan_count, tokens, width), bf16), sem((6,)),
            vmem((4, tokens, 2 * width), bf16), vmem((3, tokens, 2 * width), bf16), vmem((2, tokens, 2 * width), bf16),
            vmem((2, tokens // 2, 2 * width), bf16), sem((10,)), sem((10,)),
            vmem((2, peers, tokens, width), bf16), vmem((2, peers, tokens, width), bf16), sem((2, peers)), sem((2, peers)),
            vmem((tokens, 3 * width), bf16), vmem((2, tokens, width), f32),
            vmem((2, chan_count, rows + 2, cols, width), bf16), sem((2, 2)), sem((2, 2)),
            sem((2, 3, peers)), sem((2, 3, peers)),
            vmem((3, row_count, message, width), f32), sem((3, row_count - 1)), sem((3, row_count - 1)),
            vmem((rows, cols, width), f32),
        ],
        cost_estimate=pl.CostEstimate(flops=2 * 6 * 9 * tokens * width * full, bytes_accessed=24 * 2**20, transcendentals=4 * tokens * width),
        compiler_params=pltpu.CompilerParams(collective_id=2, has_side_effects=True, vmem_limit_bytes=60 * 2**20),
    )(x, dq, dkv, o, g_all, a3_all, x1, c1, rows_in, member, upper, lower, vec, mod, x9_1, x9_2, w1, w2, w_att, wo, dctx)


def local(
    features,
    embedding,
    context,
    image_offset,
    first_gain,
    first_shift,
    conv_first,
    conv_first_bias,
    embed_weight,
    embed_bias,
    second_gain,
    second_shift,
    conv_second,
    conv_second_bias,
    attend_gain,
    attend_shift,
    attend_weight,
    attend_bias,
    context_weight,
    context_bias,
    output_weight,
    output_bias,
    cotangent,
):
    slab_rows, columns, channels = features.shape
    devices = lax.axis_size("rows")
    total_rows = slab_rows * devices
    images = total_rows // IMG_H
    per_group = C // GROUPS
    groups = channels // per_group
    group_count = IMG_H * columns * per_group
    my_index = lax.axis_index("rows")
    first_raw = image_offset[0]
    image_span = IMG_H // slab_rows

    def image_of(global_rows):
        return jnp.mod(global_rows - first_raw, total_rows) // IMG_H

    own_rows = my_index * slab_rows + jnp.arange(slab_rows, dtype=jnp.int32)
    own_image = image_of(own_rows)
    upper_mask = (jnp.mod(own_rows - first_raw, IMG_H) != 0).astype(jnp.bfloat16)
    lower_mask = (jnp.mod(own_rows + 1 - first_raw, IMG_H) != 0).astype(jnp.bfloat16)
    member = (own_image[:, None] == jnp.arange(images, dtype=jnp.int32)[None, :]).astype(
        jnp.float32
    )

    def per_image(row_values):
        return jnp.dot(member.T, row_values, precision=HIGH)

    def per_row(image_values):
        return jnp.dot(member, image_values, precision=HIGH)

    modulate = (
        jnp.einsum("ie,eto->ito", embedding, embed_weight, preferred_element_type=jnp.float32)
        + embed_bias
    )
    tokens = slab_rows * columns
    chan = lax.axis_size("chan")
    member_rows = jnp.broadcast_to(member.T[:, :, None, None], (images, slab_rows, 1, channels))
    upper_rows = jnp.broadcast_to(upper_mask.astype(f32)[:, None, None], (slab_rows, 1, channels))
    lower_rows = jnp.broadcast_to(lower_mask.astype(f32)[:, None, None], (slab_rows, 1, channels))
    vectors = jnp.stack(
        [first_gain, first_shift, conv_first_bias, second_gain, second_shift, conv_second_bias, attend_gain,
         attend_shift, attend_bias[0], attend_bias[1], output_bias]
        + [jnp.zeros_like(first_gain)] * 5
    )
    x9_one, x9_two, middle, inner, row_stats, attend_blocks, queries, key_value = forward_block(
        devices, chan, per_group, group_count, features, member_rows, upper_rows, lower_rows, vectors, modulate,
        conv_first.reshape(9 * channels, C), conv_second.reshape(9 * channels, C), attend_weight.reshape(C, 3 * channels)
    )
    window = min(devices, 2 * image_span + 1)
    base = (my_index - window // 2) * slab_rows if window < devices else 0
    kv_all, grad_blocks, grad_attended = gather_block(
        devices, chan, window, key_value, cotangent.reshape(tokens, channels), output_weight
    )
    first_image = own_image[0]
    last_image = own_image[slab_rows - 1]
    context_count = context.shape[1]
    tail = 256
    chosen = jnp.stack([first_image, last_image])
    context_pair = jnp.take(context, chosen, axis=0)
    context_proj = (
        jnp.einsum("snc,cto->snto", context_pair, context_weight, preferred_element_type=jnp.float32)
        + context_bias
    )
    context_rows = jnp.pad(
        context_proj.reshape(2, context_count, 2 * channels).astype(bf16), ((0, 0), (0, tail - context_count), (0, 0))
    )
    split = jnp.sum((own_image == first_image).astype(jnp.int32))
    starts = jnp.mod(first_raw + chosen * IMG_H - base, total_rows)
    info = jnp.concatenate([split[None], starts, chosen]).astype(jnp.int32)
    share_rows = -(-context_count // 64) * 64
    attended_low, query_grad, window_grad, context_part = attend(
        info, queries, grad_attended, kv_all.reshape(window * slab_rows, columns, 2 * channels), context_rows,
        total_rows, IMG_H, context_count, images, share_rows,
    )
    fast = devices == 8 and window == devices
    if fast:
        key_value_grad = window_grad.reshape(devices, tokens, 2 * channels)
    else:
        window_grad = window_grad.reshape(window, tokens, 2 * channels)
        key_value_grad = jnp.zeros((tokens, 2 * channels), f32)
        for position in range(window):
            shift_by = position - window // 2
            piece = window_grad[position]
            if shift_by != 0:
                piece = from_behind(piece, "rows", shift_by)
            key_value_grad = key_value_grad + piece.astype(f32)
    result, features_grad, sums, conv_first_grad, conv_second_grad, attend_grad, output_weight_grad, context_sum = backward_block(
        devices, chan, per_group, group_count, fast, features, query_grad, key_value_grad, attended_low, grad_blocks,
        attend_blocks, inner, middle, row_stats, member_rows, upper_rows, lower_rows, vectors, modulate, x9_one, x9_two,
        conv_first.reshape(9 * channels, C), conv_second.reshape(9 * channels, C), attend_weight.reshape(C, 3 * channels),
        output_weight, context_part,
    )
    if not fast:
        conv_first_grad, conv_second_grad, attend_grad, output_weight_grad, context_sum = lax.psum(
            (conv_first_grad, conv_second_grad, attend_grad, output_weight_grad, context_sum), "rows"
        )
    grad_mod = sums[8 : 8 + 2 * images].reshape(images, 2, channels)
    rest = 8 + 2 * images
    context_grad = context_sum.astype(f32).reshape(images, share_rows, 2, channels)[:, :context_count]
    return (
        result,
        features_grad,
        sums[rest],
        sums[rest + 1],
        conv_first_grad.astype(f32).reshape(3, 3, channels, C),
        sums[rest + 2],
        jnp.einsum("ie,ito->eto", embedding.astype(f32), grad_mod, precision=HIGH),
        jnp.sum(grad_mod, axis=0),
        sums[5],
        sums[6],
        conv_second_grad.astype(f32).reshape(3, 3, channels, C),
        sums[7],
        sums[0],
        sums[1],
        attend_grad.astype(f32).reshape(C, 3, channels),
        sums[2:4],
        jnp.einsum("inc,into->cto", context, context_sum.reshape(images, share_rows, 2, channels)[:, :context_count], preferred_element_type=f32),
        jnp.sum(context_grad, axis=(0, 1)),
        output_weight_grad.astype(f32),
        sums[4],
    )


def solution(mesh):
    placed = (
        P("rows", None, "chan"),
        P(),
        P(),
        P(),
        P("chan"),
        P("chan"),
        P(None, None, "chan", None),
        P("chan"),
        P(None, None, "chan"),
        P(None, "chan"),
        P("chan"),
        P("chan"),
        P(None, None, "chan", None),
        P("chan"),
        P("chan"),
        P("chan"),
        P(None, None, "chan"),
        P(None, "chan"),
        P(None, None, "chan"),
        P(None, "chan"),
        P("chan", None),
        P("chan"),
        P("rows", None, "chan"),
    )
    return jax.shard_map(
        local,
        mesh=mesh,
        in_specs=placed,
        out_specs=(
            P("rows", None, "chan"),
            P("rows", None, "chan"),
            P("chan"),
            P("chan"),
            P(None, None, "chan", None),
            P("chan"),
            P(None, None, "chan"),
            P(None, "chan"),
            P("chan"),
            P("chan"),
            P(None, None, "chan", None),
            P("chan"),
            P("chan"),
            P("chan"),
            P(None, None, "chan"),
            P(None, "chan"),
            P(None, None, "chan"),
            P(None, "chan"),
            P("chan", None),
            P("chan"),
        ),
        check_vma=False,
    )
```

```python
import functools

import jax
import jax.numpy as jnp
from jax import lax
from jax.experimental import pallas as pl
from jax.experimental.pallas import tpu as pltpu
from jax.sharding import PartitionSpec as P

C = 512
HEAD_DIM = 64
GROUPS = 32
IMG_H = 64


EPSILON = 1e-05
HIGH = lax.Precision.HIGHEST
NEG = -1e30
bf16, f32 = jnp.bfloat16, jnp.float32


def from_behind(block, axis, distance):
    devices = range(lax.axis_size(axis))
    route = [((i - distance) % len(devices), i) for i in devices]
    return lax.ppermute(block, axis, route)


def dot(a, b, ca, cb):
    return lax.dot_general(a, b, (((ca,), (cb,)), ((), ())), preferred_element_type=f32)

def attend_kernel(tiles, tile_rows, cols, width, image_rows, total_rows, ctx_count, images,
                  window, row_count, offset, q_ref, do_ref, kv_ref, ctx_ref,
                  o_ref, dq_ref, dkv_ref, dctx_ref,
                  kv, kt, vt, qt, dot_, s_buf, p_buf, dk, dv, oacc, qacc, sem):
    slab_rows = tiles * tile_rows
    me = lax.axis_index("rows")
    base = (me - window // 2) * slab_rows if window < row_count else 0
    place = lax.rem(me * slab_rows - offset[0] + total_rows, total_rows)
    image_a = place // image_rows
    split = jnp.minimum(slab_rows, image_rows - lax.rem(place, image_rows))
    image_b = lax.rem(image_a + jnp.where(split < slab_rows, 1, 0), images)
    start_a = lax.rem(offset[0] + image_a * image_rows - base + 2 * total_rows, total_rows)
    start_b = lax.rem(offset[0] + image_b * image_rows - base + 2 * total_rows, total_rows)
    ids = (image_a, image_b)
    tq = tile_rows * cols
    main = image_rows * cols
    tail = kv.shape[1] - main
    heads = width // HEAD_DIM
    straddle = split < slab_rows

    def row_copy(img, j, start):
        src = lax.rem(start + j, total_rows)
        return pltpu.make_async_copy(kv_ref.at[src], kv.at[img, pl.ds(pl.multiple_of(j * cols, cols), cols)], sem.at[img])

    def load(img, start):
        @pl.loop(0, image_rows)
        def _(j):
            row_copy(img, j, start).start()

    def finish(img, start):
        @pl.loop(0, image_rows)
        def _(j):
            row_copy(img, j, start).wait()
        kv[img, pl.ds(main, tail)] = ctx_ref[ids[img]]
        @pl.loop(0, kv.shape[1] // 256)
        def _(c):
            at = pl.ds(pl.multiple_of(c * 256, 256), 256)
            kt[img, :, at] = kv[img, at, :width].T
            vt[img, :, at] = kv[img, at, width:].T
        dk[img] = jnp.zeros(dk.shape[1:], f32)
        dv[img] = jnp.zeros(dv.shape[1:], f32)

    load(0, start_a)
    @pl.when(straddle)
    def _():
        load(1, start_b)
    for t in range(tiles):
        qt[t] = (q_ref[pl.ds(t * tq, tq)] * jnp.asarray(HEAD_DIM ** -0.5, bf16)).T
        dot_[t] = do_ref[pl.ds(t * tq, tq)].T
    finish(0, start_a)
    @pl.when(straddle)
    def _():
        finish(1, start_b)

    count_a = (split + tile_rows - 1) // tile_rows
    first_b = split // tile_rows
    count = count_a + jnp.where(straddle, tiles - first_b, 0)
    feature = lax.broadcasted_iota(jnp.int32, (width, 1), 0) // HEAD_DIM
    lane_row = lax.broadcasted_iota(jnp.int32, (1, tq), 1) // cols
    tail_ok = lax.broadcasted_iota(jnp.int32, (tail, 1), 0) < ctx_count
    chunks = 1
    CH = main

    @pl.loop(0, count)
    def _(item):
        is_b = (item >= count_a).astype(jnp.int32)
        t = jnp.where(is_b == 1, first_b + item - count_a, item)
        row = t * tile_rows + lane_row
        low = jnp.where(is_b == 1, split, 0)
        high = jnp.where(is_b == 1, slab_rows, split)
        mine = jnp.logical_and(row >= low, row < high)
        q_t = qt[t].astype(f32)
        do_t = dot_[t].astype(f32)
        qh = [jnp.where(feature == h, q_t, 0.0).astype(bf16) for h in range(heads)]

        def score(at, size, m, masked):
            keys = kv[is_b, at, :width]
            out = []
            for h in range(heads):
                s = dot(keys, qh[h], 1, 0)
                if masked:
                    s = jnp.where(tail_ok, s, NEG)
                s_buf[h, at] = s
                out.append(jnp.maximum(m[h], jnp.max(s.reshape(size // 8, 8, tq), axis=0)))
            return tuple(out)

        m = tuple(jnp.full((8, tq), NEG, f32) for _ in range(heads))
        m = lax.fori_loop(0, chunks, lambda c, m: score(pl.ds(pl.multiple_of(c * CH, CH), CH), CH, m, False), m)
        m = score(pl.ds(main, tail), tail, m, True)
        m = tuple(jnp.max(v, axis=0, keepdims=True) for v in m)

        def prob(at, size, carry):
            l, o = carry
            lo, oo = [], []
            for h in range(heads):
                p = jnp.exp(s_buf[h, at] - m[h])
                lo.append(l[h] + jnp.sum(p.reshape(size // 8, 8, tq), axis=0))
                pb = p.astype(bf16)
                p_buf[at, pl.ds(h * tq, tq)] = pb
                oo.append(o[h] + dot(vt[is_b, pl.ds(h * HEAD_DIM, HEAD_DIM), at], pb, 1, 0))
            return tuple(lo), tuple(oo)

        l = tuple(jnp.zeros((8, tq), f32) for _ in range(heads))
        o = tuple(jnp.zeros((HEAD_DIM, tq), f32) for _ in range(heads))
        l, o = lax.fori_loop(0, chunks, lambda c, x: prob(pl.ds(pl.multiple_of(c * CH, CH), CH), CH, x), (l, o))
        l, o = prob(pl.ds(main, tail), tail, (l, o))
        inv = [1.0 / jnp.sum(v, axis=0, keepdims=True) for v in l]
        o = [o[h] * inv[h] for h in range(heads)]
        o_all = jnp.concatenate(o, axis=0)
        do_h, delta = [], []
        for h in range(heads):
            scaled = jnp.where(mine, do_t * inv[h], 0.0)
            scaled = jnp.where(feature == h, scaled, 0.0).astype(bf16)
            do_h.append(scaled)
            delta.append(jnp.sum(scaled.astype(f32) * o_all, axis=0, keepdims=True))

        do_cat = jnp.concatenate(do_h, axis=1)
        q_cat = jnp.concatenate(qh, axis=1)

        def back(at, size, dq):
            keys = kv[is_b, at, :width]
            vals = kv[is_b, at, width:]
            out = []
            pbs, dss = [], []
            for h in range(heads):
                dp = dot(vals, do_h[h], 1, 0)
                pb = p_buf[at, pl.ds(h * tq, tq)]
                pbs.append(pb)
                ds = (pb.astype(f32) * (dp - delta[h])).astype(bf16)
                out.append(dq[h] + dot(kt[is_b, pl.ds(h * HEAD_DIM, HEAD_DIM), at], ds, 1, 0))
                dss.append(ds)
            dv_sum = dot(jnp.concatenate(pbs, axis=1), do_cat, 1, 1)
            dk_sum = dot(jnp.concatenate(dss, axis=1), q_cat, 1, 1)
            dv[is_b, at] = dv[is_b, at] + dv_sum
            dk[is_b, at] = dk[is_b, at] + dk_sum
            return tuple(out)

        dq = tuple(jnp.zeros((HEAD_DIM, tq), f32) for _ in range(heads))
        dq = lax.fori_loop(0, chunks, lambda c, x: back(pl.ds(pl.multiple_of(c * CH, CH), CH), CH, x), dq)
        dq = back(pl.ds(main, tail), tail, dq)
        oacc[t] = jnp.where(mine, o_all, oacc[t])
        qacc[t] = jnp.where(mine, jnp.concatenate(dq, axis=0) * (HEAD_DIM ** -0.5), qacc[t])

    for t in range(tiles):
        o_ref[pl.ds(t * tq, tq)] = oacc[t].T.astype(bf16)
        dq_ref[pl.ds(t * tq, tq)] = qacc[t].T

    dkv_ref[...] = jnp.zeros(dkv_ref.shape, dkv_ref.dtype)
    dctx_ref[...] = jnp.zeros(dctx_ref.shape, dctx_ref.dtype)
    share_rows = dctx_ref.shape[0] // images

    def put(img, start):
        @pl.loop(0, image_rows)
        def _(j):
            row = lax.rem(start + j, total_rows)
            at = pl.ds(pl.multiple_of(j * cols, cols), cols)
            dkv_ref[row, :, :width] = dk[img, at].astype(bf16)
            dkv_ref[row, :, width:] = dv[img, at].astype(bf16)
        at = pl.ds(pl.multiple_of(ids[img] * share_rows, 16), share_rows)
        dctx_ref[at, :width] = dk[img, pl.ds(main, share_rows)].astype(bf16)
        dctx_ref[at, width:] = dv[img, pl.ds(main, share_rows)].astype(bf16)
    put(0, start_a)
    @pl.when(straddle)
    def _():
        put(1, start_b)

def attend(row_count, slab, offset, q, do, kv_window, ctx, total_rows, image_rows, ctx_count, images, share_rows, tile_rows=4):
    tokens, width = q.shape
    rows, cols, _ = kv_window.shape
    tiles = tokens // (tile_rows * cols)
    tq = tile_rows * cols
    tail = ctx.shape[1]
    assert tokens == slab * cols
    keys = image_rows * cols + tail
    heads = width // HEAD_DIM
    kern = functools.partial(attend_kernel, tiles, tile_rows, cols, width, image_rows, total_rows, ctx_count, images, rows // slab, row_count)
    vm = pl.BlockSpec(memory_space=pltpu.VMEM)
    return pl.pallas_call(
        kern, name="attend",
        out_shape=(jax.ShapeDtypeStruct((tokens, width), bf16), jax.ShapeDtypeStruct((tokens, width), f32),
                   jax.ShapeDtypeStruct(kv_window.shape, bf16), jax.ShapeDtypeStruct((images * share_rows, 2 * width), bf16)),
        in_specs=[pl.BlockSpec(memory_space=pltpu.SMEM), vm, vm, pl.BlockSpec(memory_space=pl.ANY), vm],
        out_specs=(vm, vm, vm, vm),
        scratch_shapes=[
            pltpu.VMEM((2, keys, 2 * width), bf16),
            pltpu.VMEM((2, width, keys), bf16), pltpu.VMEM((2, width, keys), bf16),
            pltpu.VMEM((tiles, width, tq), bf16), pltpu.VMEM((tiles, width, tq), bf16),
            pltpu.VMEM((heads, keys, tq), f32), pltpu.VMEM((keys, heads * tq), bf16),
            pltpu.VMEM((2, keys, width), f32), pltpu.VMEM((2, keys, width), f32),
            pltpu.VMEM((tiles, width, tq), f32), pltpu.VMEM((tiles, width, tq), f32),
            pltpu.SemaphoreType.DMA((2,)),
        ],
        cost_estimate=pl.CostEstimate(flops=12 * tokens * keys * width, bytes_accessed=8 * 2**20, transcendentals=heads * tokens * keys),
        compiler_params=pltpu.CompilerParams(vmem_limit_bytes=60 * 2**20),
    )(offset, q, do, kv_window, ctx)


MESH = pl.DeviceIdType.MESH


def vmem(shape, dtype=f32):
    return pltpu.VMEM(shape, dtype)


def greet(devices):
    barrier = pltpu.get_barrier_semaphore()
    for device in devices:
        pl.semaphore_signal(barrier, inc=1, device_id=device, device_id_type=MESH)
    pl.semaphore_wait(barrier, len(devices))


def row_peers(count):
    r, z = lax.axis_index("rows"), lax.axis_index("chan")
    return [(lax.rem(r + d, count), z) for d in range(1, count)]


def chan_peers(count):
    r, z = lax.axis_index("rows"), lax.axis_index("chan")
    return [(r, lax.rem(z + d, count)) for d in range(1, count)]


def push(src, dst, send_sem, recv_sem, device):
    copy = pltpu.make_async_remote_copy(
        src_ref=src, dst_ref=dst, send_sem=send_sem, recv_sem=recv_sem, device_id=device, device_id_type=MESH
    )
    copy.start()
    return copy


def share(buf, sends, recvs, count, pieces):
    me = lax.axis_index("rows")
    for index, piece in enumerate(pieces):
        buf[me, pl.ds(index, 1), :] = piece
    copies = [
        push(buf.at[me], buf.at[me], sends.at[d], recvs.at[d], device) for d, device in enumerate(row_peers(count))
    ]
    return copies


def share_total(buf, copies):
    for copy in copies:
        copy.wait()
    total = buf[0]
    for index in range(1, buf.shape[0]):
        total = total + buf[index]
    return total


def image_masks(offset, rows, width, total_rows):
    images = total_rows // IMG_H
    row = lax.axis_index("rows") * rows + lax.broadcasted_iota(jnp.int32, (rows, 1, width), 0) - offset
    row = jnp.where(row < 0, row + total_rows, row)
    one, zero = jnp.ones((rows, 1, width), f32), jnp.zeros((rows, 1, width), f32)
    member, upper, lower = [], one, one
    for i in range(images):
        inside = jnp.logical_and(row >= i * IMG_H, row < (i + 1) * IMG_H)
        member.append(jnp.where(inside, one, zero))
        upper = jnp.where(row == i * IMG_H, zero, upper)
        lower = jnp.where(row == (i + 1) * IMG_H - 1, zero, lower)
    return member, upper, lower


def group_sum(values, per_group):
    width = values.shape[1]
    one = lax.broadcasted_iota(jnp.int32, (width, width), 0) // per_group
    two = lax.broadcasted_iota(jnp.int32, (width, width), 1) // per_group
    same = (one == two).astype(f32)
    return jnp.dot(values, same, precision=HIGH, preferred_element_type=f32)


def image_sums(values, member):
    by_row = jnp.sum(values, axis=1, keepdims=True)
    return [jnp.sum(by_row * member[i], axis=0) for i in range(len(member))]


def to_rows(per_image, member):
    total = None
    for i, value in enumerate(per_image):
        term = member[i] * value[None]
        total = term if total is None else total + term
    return total


def norm_rows(total, member, entries, per_group):
    images = len(member)
    grouped = group_sum(total, per_group) * (1.0 / entries)
    centers, scales = [], []
    for i in range(images):
        center = grouped[2 * i : 2 * i + 1]
        square = grouped[2 * i + 1 : 2 * i + 2]
        centers.append(center)
        scales.append(lax.rsqrt(square - center * center + EPSILON))
    return to_rows(centers, member), to_rows(scales, member)


def taps(pad, upper, lower, x9):
    rows, cols, width = pad.shape
    rows = rows - 2
    tokens = rows * cols
    col = lax.rem(lax.broadcasted_iota(jnp.int32, (tokens, 1), 0), cols)
    for a in range(3):
        v = pad[pl.ds(a, rows)].astype(f32)
        if a == 0:
            v = v * upper
        if a == 2:
            v = v * lower
        v = v.reshape(tokens, width)
        left = jnp.where(col == 0, 0.0, pltpu.roll(v, 1, 0))
        right = jnp.where(col == cols - 1, 0.0, pltpu.roll(v, tokens - 1, 0))
        for b, part in enumerate((left, v, right)):
            x9[:, pl.ds((3 * a + b) * width, width)] = part.astype(bf16)


class LineGather:
    def __init__(self, at, pieces, sends, recvs):
        self.at, self.pieces, self.sends, self.recvs = at, pieces, sends, recvs
        self.r, self.z = lax.axis_index("rows"), lax.axis_index("chan")
        self.count = lax.axis_size("chan")

    def copy(self, way, step, piece, shard):
        other = self.z + 1 if way == 0 else self.z - 1
        ref = self.at(shard, piece)
        return pltpu.make_async_remote_copy(
            src_ref=ref, dst_ref=ref, send_sem=self.sends.at[way, step, piece], recv_sem=self.recvs.at[way, step, piece],
            device_id=(self.r, other), device_id_type=MESH,
        )

    def has(self, way, step):
        return self.z >= step if way == 0 else self.z + step < self.count

    def open_end(self, way):
        return self.z + 1 < self.count if way == 0 else self.z >= 1

    def shard(self, way, step):
        return self.z - step if way == 0 else self.z + step

    def run(self, step, pieces=None):
        for piece in range(self.pieces) if pieces is None else pieces:
            for way in range(2):
                if step == 0:
                    @pl.when(self.open_end(way))
                    def _():
                        self.copy(way, 0, piece, self.z).start()
                else:
                    @pl.when(self.has(way, step))
                    def _():
                        shard = self.shard(way, step)
                        self.copy(way, step - 1, piece, shard).wait_recv()
                        if step < self.count - 1:
                            @pl.when(self.open_end(way))
                            def _():
                                self.copy(way, step, piece, shard).start()

    def drain(self):
        for step in range(self.count - 1):
            for way in range(2):
                @pl.when(jnp.logical_and(self.has(way, step), self.open_end(way)))
                def _():
                    for piece in range(self.pieces):
                        self.copy(way, step, piece, self.shard(way, step)).wait_send()


class ChanScatter:
    def __init__(self, term, own, out, recv, sends, recvs):
        self.term, self.own, self.out, self.recv, self.sends, self.recvs = term, own, out, recv, sends, recvs
        self.r, self.z = lax.axis_index("rows"), lax.axis_index("chan")
        self.count = lax.axis_size("chan")
        self.line = self.count == 4
        self.tokens = own.shape[0]
        self.half = self.tokens // 2

    def rows(self, piece):
        return pl.ds(piece * self.half, self.half)

    def copy(self, slot, piece, device):
        rows = self.rows(piece)
        return pltpu.make_async_remote_copy(
            src_ref=self.out.at[slot, rows], dst_ref=self.recv.at[slot, rows], send_sem=self.sends.at[slot, piece],
            recv_sem=self.recvs.at[slot, piece], device_id=(self.r, device), device_id_type=MESH,
        )

    def push(self, slot, target, device):
        for piece in range(2):
            rows = self.rows(piece)
            self.out[slot, rows] = self.term(target, rows).astype(bf16)
            self.copy(slot, piece, device).start()

    def start(self):
        z, count = self.z, self.count
        if not self.line:
            for d in range(1, count):
                device = lax.rem(z + d, count)
                self.push(d - 1, device, device)
            self.own[...] = self.term(z, pl.ds(0, self.tokens))
            return
        self.end = jnp.logical_or(z == 0, z == 3)
        self.inner = jnp.logical_not(self.end)
        opposite = lax.rem(z + 2, 4)

        @pl.when(self.end)
        def _():
            self.push(3, 3 - z, 1 + z // 3)
            self.push(0, opposite, opposite)

        @pl.when(z < 3)
        def _():
            self.push(1, z + 1, z + 1)

        @pl.when(z > 0)
        def _():
            self.push(2, z - 1, z - 1)

        @pl.when(self.inner)
        def _():
            for piece in range(2):
                rows = self.rows(piece)
                term = self.term(opposite, rows)
                self.copy(3, piece, opposite).wait_recv()
                self.out[0, rows] = (term + self.recv[3, rows].astype(f32)).astype(bf16)
                self.copy(0, piece, opposite).start()
        self.own[...] = self.term(z, pl.ds(0, self.tokens))

    def finish(self):
        own, z = self.own, self.z

        def add(slot):
            for piece in range(2):
                rows = self.rows(piece)
                self.copy(slot, piece, z).wait_recv()
                own[rows, :] = own[rows, :] + self.recv[slot, rows].astype(f32)

        if not self.line:
            for d in range(1, self.count):
                add(d - 1)
            return

        @pl.when(z > 0)
        def _():
            add(1)

        @pl.when(z < 3)
        def _():
            add(2)
        add(0)

    def drain(self):
        def wait(slot):
            for piece in range(2):
                self.copy(slot, piece, self.z).wait_send()
        if not self.line:
            for d in range(1, self.count):
                wait(d - 1)
            return
        wait(0)

        @pl.when(self.z < 3)
        def _():
            wait(1)

        @pl.when(self.z > 0)
        def _():
            wait(2)

        @pl.when(self.end)
        def _():
            wait(3)


def scatter_scratch(count, tokens, width):
    slots = max(count, 4)
    return [
        vmem((tokens, width), f32), vmem((slots, tokens, width), bf16), vmem((slots, tokens, width), bf16),
        pltpu.SemaphoreType.DMA((slots, 2)), pltpu.SemaphoreType.DMA((slots, 2)),
    ]


def plane(count):
    r = lax.axis_index("rows")
    core = r + 1 - 2 * lax.rem(r, 2)
    x_dev = r + 2 - 4 * lax.rem(r // 2, 2)
    y_dev = r + 4 - 8 * (r // 4)
    return core, x_dev, y_dev, x_dev + y_dev - r


PIECES = 8
VECTORS = 10


def gather_plane(all_ref, count, sends, recvs):
    r, z = lax.axis_index("rows"), lax.axis_index("chan")
    tokens = all_ref.shape[1]
    half = tokens // 2
    core, x_dev, y_dev, diag = plane(count)
    first, second, whole = pl.ds(0, half), pl.ds(half, half), pl.ds(0, tokens)
    pending = []

    def send(i, slab, part, device):
        copy = push(all_ref.at[slab, part], all_ref.at[slab, part], sends.at[i], recvs.at[i], (device, z))
        pending.append(copy)
        return copy

    x1 = send(0, r, first, x_dev)
    y2 = send(1, r, second, y_dev)
    x2 = send(2, r, second, x_dev)
    y1 = send(3, r, first, y_dev)
    waits = [send(4, r, whole, core)]

    def rest():
        x1.wait_recv()
        f1 = send(5, x_dev, first, y_dev)
        waits.append(send(6, x_dev, first, core))
        y2.wait_recv()
        f2 = send(7, y_dev, second, x_dev)
        waits.append(send(8, y_dev, second, core))
        x2.wait_recv()
        waits.append(send(9, x_dev, second, core))
        y1.wait_recv()
        waits.append(send(10, y_dev, first, core))
        f1.wait_recv()
        waits.append(send(11, diag, first, core))
        f2.wait_recv()
        waits.append(send(12, diag, second, core))
        for copy in waits:
            copy.wait_recv()
    return rest, pending


def gather_window(all_ref, count, sends, recvs):
    r, z = lax.axis_index("rows"), lax.axis_index("chan")
    window = all_ref.shape[0]
    own = window // 2 if window < count else r
    pending = []
    for i in range(1, count):
        place = window // 2 - i if i <= window // 2 else window // 2 + count - i
        if window < count and (place < 0 or place >= window):
            continue
        slot = place if window < count else r
        pending.append(push(all_ref.at[own], all_ref.at[slot], sends.at[i], recvs.at[i], (lax.rem(r + i, count), z)))

    def rest():
        for copy in pending:
            copy.wait_recv()
    return rest, pending


def forward_kernel(row_count, chan_count, per_group, entries,
                   offset, x_ref, *refs):
    vec, refs = refs[:VECTORS], refs[VECTORS:]
    (mod, w1, w2, w_att, g_ref, wo_ref,
                   x9_1, x9_2, c1_ref, x1_ref, row_ref, a3_ref, q_ref, all_ref, gall_ref, do_ref,
                   pad1, pad2, own1, out1, recv1, s1, r1, own2, out2, recv2, s2, r2, stat, stat_s, stat_r, halo_s, halo_r,
     a3_s, a3_r, g_s, g_r, kv_s, kv_r) = refs
    rows, cols, width = x_ref.shape
    tokens = rows * cols
    r, z = lax.axis_index("rows"), lax.axis_index("chan")
    greet(row_peers(row_count) + chan_peers(chan_count))
    member, upper, lower = image_masks(offset[0], rows, width, row_count * rows)
    images = len(member)
    up = (lax.rem(r + row_count - 1, row_count), z)
    down = (lax.rem(r + 1, row_count), z)
    pending = []
    gall_ref[z] = g_ref[...]
    third = -(-tokens // 48) * 16
    g_copies = []

    def vector(i):
        return vec[i][...][None]

    def stats(phase, values):
        pieces = []
        for a, b in zip(image_sums(values, member), image_sums(values * values, member)):
            pieces += [a, b]
        copies = share(stat.at[phase], stat_s.at[phase], stat_r.at[phase], row_count, pieces)
        part = pl.ds(phase * third, min(third, tokens - phase * third))
        for d, device in enumerate(chan_peers(chan_count)):
            g_copies.append(push(gall_ref.at[z, part], gall_ref.at[z, part], g_s.at[phase, d], g_r.at[phase, d], device))
        center, scale = norm_rows(share_total(stat.at[phase], copies), member, entries, per_group)
        row_ref[2 * phase] = center
        row_ref[2 * phase + 1] = scale
        return (values - center) * scale

    def rims(phase, pad):
        one = push(pad.at[1], pad.at[rows + 1], halo_s.at[phase, 0], halo_r.at[phase, 0], up)
        two = push(pad.at[rows], pad.at[0], halo_s.at[phase, 1], halo_r.at[phase, 1], down)
        one.wait()
        two.wait()

    def conv(x9, weight, *scratch):
        def term(j, at):
            return jnp.dot(x9[at, :], weight[:, pl.ds(pl.multiple_of(j * width, width), width)], preferred_element_type=f32)
        line = ChanScatter(term, *scratch)
        line.start()
        line.finish()
        return line, scratch[0][...].reshape(rows, cols, width)

    x = x_ref[...].astype(f32)
    n1 = stats(0, x) * vector(0) + vector(1)
    pad1[pl.ds(1, rows)] = (n1 * jax.nn.sigmoid(n1)).astype(bf16)
    rims(0, pad1)
    taps(pad1, upper, lower, x9_1)
    line1, c1 = conv(x9_1, w1, own1, out1, recv1, s1, r1)
    c1 = c1 + vector(2)
    c1_ref[...] = c1
    n2 = stats(1, c1) * vector(3) + vector(4)
    mod_scale = to_rows([mod[i, 0:1, :] for i in range(images)], member)
    mod_shift = to_rows([mod[i, 1:2, :] for i in range(images)], member)
    h2 = n2 * (1.0 + mod_scale) + mod_shift
    pad2[pl.ds(1, rows)] = (h2 * jax.nn.sigmoid(h2)).astype(bf16)
    rims(1, pad2)
    taps(pad2, upper, lower, x9_2)
    line2, c2 = conv(x9_2, w2, own2, out2, recv2, s2, r2)
    x1 = x_ref[...].astype(f32) + (c2 + vector(5))
    x1_ref[...] = x1
    a3 = stats(2, x1) * vector(6) + vector(7)
    a3_ref[z] = a3.astype(bf16).reshape(tokens, width)
    size = tokens // PIECES
    line3 = LineGather(lambda shard, piece: a3_ref.at[shard, pl.ds(piece * size, size)], PIECES, a3_s, a3_r)
    line3.run(0)
    line1.drain()
    line2.drain()
    for step in range(1, chan_count):
        line3.run(step)
    qkv = None
    for i in range(chan_count):
        term = jnp.dot(a3_ref[i], w_att[pl.ds(i * width, width), :], preferred_element_type=f32)
        qkv = term if qkv is None else qkv + term
    window = all_ref.shape[0]
    own = window // 2 if window < row_count else r
    all_ref[own, :, :width] = qkv[:, width : 2 * width].astype(bf16)
    all_ref[own, :, width:] = (qkv[:, 2 * width :] + vec[9][1:2, :]).astype(bf16)
    gather = gather_plane if window == row_count == 8 else gather_window
    rest, copies = gather(all_ref, row_count, kv_s, kv_r)
    q_ref[...] = (qkv[:, :width] + vec[9][0:1, :]).astype(bf16)
    for copy in g_copies:
        copy.wait_recv()
    pending += g_copies
    do = None
    for i in range(chan_count):
        term = lax.dot_general(
            gall_ref[i], wo_ref[:, pl.ds(i * width, width)], (((1,), (1,)), ((), ())), preferred_element_type=f32
        )
        do = term if do is None else do + term
    do_ref[...] = do.astype(bf16)
    rest()
    pending += copies
    line3.drain()
    for copy in pending:
        copy.wait_send()


def forward_block(row_count, chan_count, per_group, entries, window, offset, x, vec, mod, w1, w2, w_att, g, wo):
    rows, cols, width = x.shape
    tokens = rows * cols
    images = row_count * rows // IMG_H
    message = -(-2 * images // 8) * 8
    vm = pl.BlockSpec(memory_space=pltpu.VMEM)
    S = jax.ShapeDtypeStruct
    sem = pltpu.SemaphoreType.DMA
    peers = max(chan_count - 1, 1)
    kv_copies = max(13, row_count)
    return pl.pallas_call(
        functools.partial(forward_kernel, row_count, chan_count, per_group, entries),
        name="forward_block",
        out_shape=(
            S((tokens, 9 * width), bf16),
            S((tokens, 9 * width), bf16),
            S((rows, cols, width), f32),
            S((rows, cols, width), f32),
            S((6, rows, 1, width), f32),
            S((chan_count, tokens, width), bf16),
            S((tokens, width), bf16),
            S((window, tokens, 2 * width), bf16),
            S((chan_count, tokens, width), bf16),
            S((tokens, width), bf16),
        ),
        in_specs=[pl.BlockSpec(memory_space=pltpu.SMEM)] + [vm] * (7 + VECTORS),
        out_specs=(vm,) * 10,
        scratch_shapes=[
            vmem((rows + 2, cols, width), bf16),
            vmem((rows + 2, cols, width), bf16),
            *scatter_scratch(chan_count, tokens, width),
            *scatter_scratch(chan_count, tokens, width),
            vmem((3, row_count, message, width), f32),
            sem((3, row_count - 1)), sem((3, row_count - 1)),
            sem((2, 2)), sem((2, 2)),
            sem((2, peers, PIECES)), sem((2, peers, PIECES)),
            sem((3, peers)), sem((3, peers)),
            sem((kv_copies,)), sem((kv_copies,)),
        ],
        cost_estimate=pl.CostEstimate(flops=2 * 4 * 9 * tokens * width * width * 4, bytes_accessed=16 * 2**20, transcendentals=4 * tokens * width),
        compiler_params=pltpu.CompilerParams(collective_id=0, has_side_effects=True, vmem_limit_bytes=60 * 2**20),
    )(offset, x, *vec, mod, w1, w2, w_att, g, wo)


def contract(a, b, a_dim, b_dim):
    return lax.dot_general(a, b, (((a_dim,), (b_dim,)), ((), ())), preferred_element_type=f32)


class Total:
    def __init__(self, part, out, half, quarters, sends, recvs):
        self.part, self.half, self.quarters, self.out = part, half, quarters, out
        self.sends, self.recvs = sends, recvs
        self.r, self.z = lax.axis_index("rows"), lax.axis_index("chan")
        self.core, self.x, self.y, self.d = plane(8)
        self.n = part.shape[0] // 8
        self.copies = []

    def rows(self, device):
        return pl.ds(pl.multiple_of((lax.rem(device, 2) * 4 + device // 2) * self.n, 16), self.n)

    def half_rows(self, device):
        return pl.ds(pl.multiple_of(lax.rem(device, 2) * 4 * self.n, 16), 4 * self.n)

    def send(self, i, src, dst, device):
        copy = push(src, dst, self.sends.at[i], self.recvs.at[i], (device, self.z))
        self.copies.append(copy)
        return copy

    def one(self):
        self.a = self.send(0, self.part.at[self.half_rows(self.core)], self.half, self.core)

    def two(self):
        self.a.wait_recv()
        mine = self.half_rows(self.r)
        self.half[...] = (self.part[mine, :].astype(f32) + self.half[...].astype(f32)).astype(bf16)
        self.b = []
        for i, device in enumerate((self.d, self.x, self.y)):
            at = pl.ds(pl.multiple_of((device // 2) * self.n, 16), self.n)
            self.b.append(self.send(1 + i, self.half.at[at], self.quarters.at[i], device))

    def three(self):
        at = pl.ds(pl.multiple_of((self.r // 2) * self.n, 16), self.n)
        total = self.half[at, :].astype(f32)
        for i, copy in enumerate(self.b):
            copy.wait_recv()
            total = total + self.quarters[i].astype(f32)
        mine = self.rows(self.r)
        self.out[mine, :] = total.astype(bf16)
        self.c = []
        for i, device in enumerate((self.d, self.x, self.y, self.core)):
            self.c.append(self.send(4 + i, self.out.at[mine], self.out.at[mine], device))

    def four(self):
        self.e = [self.c[3]]
        for i, device in ((1, self.x), (2, self.y), (0, self.d)):
            self.c[i].wait_recv()
            at = self.rows(device)
            self.e.append(self.send(8 + i, self.out.at[at], self.out.at[at], self.core))

    def finish(self):
        for copy in self.e:
            copy.wait_recv()
        for copy in self.copies:
            copy.wait_send()


def total_scratch(n, width):
    return [vmem((n // 2, width), bf16), vmem((3, n // 8, width), bf16), pltpu.SemaphoreType.DMA((11,)), pltpu.SemaphoreType.DMA((11,))]


class Return:
    def __init__(self, parts, cores, out, recv, relay, sends, recvs):
        self.parts, self.cores, self.out, self.recv, self.relay = parts, cores, out, recv, relay
        self.sends, self.recvs = sends, recvs
        self.r, self.z = lax.axis_index("rows"), lax.axis_index("chan")
        self.core, self.x, self.y, self.d = plane(8)
        half = parts.shape[1] // 2
        self.first, self.second, self.whole = pl.ds(0, half), pl.ds(half, half), pl.ds(0, 2 * half)
        self.copies = []

    def send(self, i, src, dst, device):
        copy = push(src, dst, self.sends.at[i], self.recvs.at[i], (device, self.z))
        self.copies.append(copy)
        return copy

    def chip(self, i, device, part):
        return self.parts[device, part].astype(f32) + self.cores[i, part].astype(f32)

    def total(self):
        first, second, out, recv, relay = self.first, self.second, self.out, self.recv, self.relay
        step = self.core - self.r
        to_core = [
            self.send(i, self.parts.at[device + step], self.cores.at[i], self.core)
            for i, device in enumerate((self.d, self.x, self.y, self.r))
        ]
        to_core[0].wait_recv()
        out[0, first] = self.chip(0, self.d, first).astype(bf16)
        relay_x = self.send(4, out.at[0, first], relay.at[0], self.x)
        out[0, second] = self.chip(0, self.d, second).astype(bf16)
        relay_y = self.send(5, out.at[0, second], relay.at[1], self.y)
        to_core[1].wait_recv()
        out[1, first] = self.chip(1, self.x, first).astype(bf16)
        plain_x = self.send(6, out.at[1, first], recv.at[0, first], self.x)
        to_core[2].wait_recv()
        out[2, second] = self.chip(2, self.y, second).astype(bf16)
        plain_y = self.send(7, out.at[2, second], recv.at[1, second], self.y)
        relay_x.wait_recv()
        out[2, first] = (self.chip(2, self.y, first) + relay[0].astype(f32)).astype(bf16)
        merged_y = self.send(8, out.at[2, first], recv.at[1, first], self.y)
        relay_y.wait_recv()
        out[1, second] = (self.chip(1, self.x, second) + relay[1].astype(f32)).astype(bf16)
        merged_x = self.send(9, out.at[1, second], recv.at[0, second], self.x)
        to_core[3].wait_recv()
        own = self.chip(3, self.r, self.whole)
        for copy in (plain_x, plain_y, merged_y, merged_x):
            copy.wait_recv()
        return own + recv[0].astype(f32) + recv[1].astype(f32)

    def drain(self):
        for copy in self.copies:
            copy.wait_send()


def return_scratch(tokens, width):
    return [
        vmem((4, tokens, width), bf16), vmem((3, tokens, width), bf16), vmem((2, tokens, width), bf16),
        vmem((2, tokens // 2, width), bf16), pltpu.SemaphoreType.DMA((10,)), pltpu.SemaphoreType.DMA((10,)),
    ]


class GradRows:
    def __init__(self, pad, up, down, halo_s, halo_r, sends, recvs):
        self.pad, self.up, self.down, self.halo_s, self.halo_r = pad, up, down, halo_s, halo_r
        self.rows = pad.shape[1] - 2
        self.size = self.rows // PIECES
        self.line = LineGather(self.at, PIECES + 2, sends, recvs)

    def at(self, shard, piece):
        if piece < PIECES:
            return self.pad.at[shard, pl.ds(1 + piece * self.size, self.size)]
        return self.pad.at[shard, pl.ds(0 if piece == PIECES else self.rows + 1, 1)]

    def start(self, values):
        pad, rows, z = self.pad, self.rows, lax.axis_index("chan")
        pad[z, pl.ds(1, rows)] = values
        one = push(pad.at[z, 1], pad.at[z, rows + 1], self.halo_s.at[0], self.halo_r.at[0], self.up)
        two = push(pad.at[z, rows], pad.at[z, 0], self.halo_s.at[1], self.halo_r.at[1], self.down)
        self.rims = [one, two]
        self.line.run(0, range(PIECES))
        one.wait_recv()
        two.wait_recv()
        self.line.run(0, (PIECES, PIECES + 1))

    def all(self, start):
        count, _, cols, width = self.pad.shape
        parts = [self.pad[i, pl.ds(start, self.rows)].reshape(self.rows * cols, width) for i in range(count)]
        return jnp.concatenate(parts, axis=1)

    def drain(self):
        for copy in self.rims:
            copy.wait_send()
        self.line.drain()


def conv_back(grad, turned, upper, lower):
    rows, cols, width = grad.rows, grad.pad.shape[2], grad.pad.shape[3]
    tokens = rows * cols
    total = None
    for a, mask in enumerate((lower, None, upper)):
        term = jnp.dot(grad.all(2 - a), turned[a], preferred_element_type=f32)
        if mask is not None:
            wide = jnp.concatenate([mask] * 3, axis=2)
            term = (term.reshape(rows, cols, 3 * width) * wide).reshape(tokens, 3 * width)
        total = term if total is None else total + term
    col = lax.rem(lax.broadcasted_iota(jnp.int32, (tokens, 1), 0), cols)
    before = jnp.where(col == cols - 1, 0.0, pltpu.roll(total[:, :width], tokens - 1, 0))
    after = jnp.where(col == 0, 0.0, pltpu.roll(total[:, 2 * width :], 1, 0))
    return (before + total[:, width : 2 * width] + after).reshape(rows, cols, width)


def silu_slope(values):
    gate = jax.nn.sigmoid(values)
    return gate * (1.0 + values * (1.0 - gate))


def channel_total(values):
    return jnp.sum(jnp.sum(values, axis=1, keepdims=True), axis=0)


def backward_kernel(row_count, chan_count, per_group, entries, fast, offset, x_ref, *refs):
    vec, refs = refs[:VECTORS], refs[VECTORS:]
    (dq_ref, dkv_ref, o_ref, g_all, a3_hbm, x1_ref, c1_hbm, rows_in, mod, x9_1_hbm, x9_2_hbm, w1_hbm, w2_hbm, w_att, wo, dctx,
     result, dfeat, sums, g_conv1, g_conv2, g_att, g_out, g_ctx,
     part1, part2, part_att, part_out, x9_1, x9_2, w1, w2, c1_ref, a3_all, load_s, x9t, turned, d3, dx1_ref,
     gpad, halo_s, halo_r, zh_s, zh_r, stat, stat_s, stat_r) = refs[:47]
    refs = refs[47:]
    da3_line, refs = refs[:5], refs[5:]
    result_line, refs = refs[:5], refs[5:]
    rows, cols, width = x_ref.shape
    tokens = rows * cols
    taps_n = 3 * width
    r, z = lax.axis_index("rows"), lax.axis_index("chan")
    loads = []
    for i, (src, dst) in enumerate(
        ((a3_hbm, a3_all), (c1_hbm, c1_ref), (x9_2_hbm, x9_2), (w2_hbm, w2), (x9_1_hbm, x9_1), (w1_hbm, w1))
    ):
        loads.append(pltpu.make_async_copy(src, dst, load_s.at[i]))
        loads[i].start()
    greet(row_peers(row_count) + chan_peers(chan_count))
    member, upper, lower = image_masks(offset[0], rows, width, row_count * rows)
    images = len(member)
    up = (lax.rem(r + row_count - 1, row_count), z)
    down = (lax.rem(r + 1, row_count), z)

    def vector(i):
        return vec[i][...][None]

    def exchange(phase, pieces):
        buf = stat.at[phase]
        return share_total(buf, share(buf, stat_s.at[phase], stat_r.at[phase], row_count, pieces))

    def norm_pieces(dxh, xhat):
        pieces = []
        for a, b in zip(image_sums(dxh, member), image_sums(dxh * xhat, member)):
            pieces += [a, b]
        return pieces

    def norm_back(total, dxh, xhat, scale):
        grouped = group_sum(total[: 2 * images], per_group) * (1.0 / entries)
        first = to_rows([grouped[2 * i : 2 * i + 1] for i in range(images)], member)
        second = to_rows([grouped[2 * i + 1 : 2 * i + 2] for i in range(images)], member)
        return scale * (dxh - first - xhat * second)

    def turn(x9, weight):
        x9t[...] = x9[...].T
        for a in range(3):
            turned[a] = weight[pl.ds(a * taps_n, taps_n), :].T

    if fast:
        back = Return(dkv_ref, *refs[:6])
        dkv = back.total()
        totals = [
            Total(part, out, *refs[6 + 4 * i : 10 + 4 * i])
            for i, (part, out) in enumerate(((part_att, g_att), (part_out, g_out), (dctx, g_ctx), (part2, g_conv2)))
        ]
        last = [
            Total(part1.at[pl.ds(a * taps_n, taps_n)], g_conv1.at[pl.ds(a * taps_n, taps_n)], *refs[22 + 4 * a : 26 + 4 * a])
            for a in range(3)
        ]
        small, conv2 = totals[:3], totals[3:]
    else:
        dkv = dkv_ref[...]
        small, conv2, last = [], [], []
    dq = dq_ref[...]
    d3[:, :width] = dq.astype(bf16)
    d3[:, width:] = dkv.astype(bf16)
    da3_sum = ChanScatter(
        lambda j, at: contract(d3[at, :], w_att[pl.ds(pl.multiple_of(j * width, width), width), :], 1, 1), *da3_line
    )
    da3_sum.start()
    bias_q = jnp.sum(dq, axis=0, keepdims=True)
    bias_v = jnp.sum(dkv[:, width:], axis=0, keepdims=True)
    loads[0].wait()
    for i in range(chan_count):
        part_att[pl.ds(i * width, width), :] = contract(a3_all[i], d3[...], 0, 0).astype(bf16)
    g_cat = jnp.concatenate([g_all[i] for i in range(chan_count)], axis=1)
    part_out[...] = contract(o_ref[...], g_cat, 0, 0).astype(bf16)
    for stage in (Total.one, Total.two, Total.three, Total.four):
        for t in small:
            stage(t)
    x1 = x1_ref[...]
    g = g_all[z].astype(f32).reshape(rows, cols, width)
    center, scale = rows_in[4], rows_in[5]
    xhat = (x1 - center) * scale
    da3_sum.finish()
    da3 = da3_line[0][...].reshape(rows, cols, width)
    dxh = da3 * vector(6)
    total = exchange(
        0,
        norm_pieces(dxh, xhat) + [channel_total(da3 * xhat), channel_total(da3), bias_q, bias_v, channel_total(g)],
    )
    sums[0:5, :] = total[2 * images : 2 * images + 5]
    dx1 = g + norm_back(total, dxh, xhat, scale)
    grad2 = GradRows(gpad.at[0], up, down, halo_s.at[0], halo_r.at[0], zh_s.at[0], zh_r.at[0])
    grad2.start(dx1.astype(bf16))
    dx1_ref[...] = dx1
    bias_2 = channel_total(dx1)
    for i in (1, 2, 3):
        loads[i].wait()
    grad2.line.run(1)
    turn(x9_2, w2)
    center, scale = rows_in[2], rows_in[3]
    xhat = (c1_ref[...] - center) * scale
    n2 = xhat * vector(3) + vector(4)
    mod_scale = 1.0 + to_rows([mod[i, 0:1, :] for i in range(images)], member)
    mod_shift = to_rows([mod[i, 1:2, :] for i in range(images)], member)
    slope = silu_slope(n2 * mod_scale + mod_shift)
    for step in range(2, chan_count):
        grad2.line.run(step)
    da3_sum.drain()
    for t in small:
        t.finish()
    dh2 = conv_back(grad2, turned, upper, lower) * slope
    dn2 = dh2 * mod_scale
    dxh = dn2 * vector(3)
    dss = []
    for a, b in zip(image_sums(dh2 * n2, member), image_sums(dh2, member)):
        dss += [a, b]
    pieces = norm_pieces(dxh, xhat) + [channel_total(dn2 * xhat), channel_total(dn2), bias_2] + dss
    copies = share(stat.at[1], stat_s.at[1], stat_r.at[1], row_count, pieces)
    grad = grad2.all(1)
    for a in range(3):
        at = pl.ds(a * taps_n, taps_n)
        part2[at, :] = jnp.dot(x9t[at, :], grad, preferred_element_type=f32).astype(bf16)
    for t in conv2:
        t.one()
    total = share_total(stat.at[1], copies)
    sums[5 : 8 + 2 * images, :] = total[2 * images : 4 * images + 3]
    dc1 = norm_back(total, dxh, xhat, scale)
    bias_1 = channel_total(dc1)
    grad1 = GradRows(gpad.at[1], up, down, halo_s.at[1], halo_r.at[1], zh_s.at[1], zh_r.at[1])
    grad1.start(dc1.astype(bf16))
    for t in conv2:
        t.two()
    for i in (4, 5):
        loads[i].wait()
    grad1.line.run(1)
    turn(x9_1, w1)
    center, scale = rows_in[0], rows_in[1]
    xhat = (x_ref[...].astype(f32) - center) * scale
    slope = silu_slope(xhat * vector(0) + vector(1))
    for t in conv2:
        t.three()
    for step in range(2, chan_count - 1):
        grad1.line.run(step)
    for t in conv2:
        t.four()
    grad1.line.run(chan_count - 1)
    result_sum = ChanScatter(
        lambda j, at: jnp.dot(
            o_ref[at, :], wo[:, pl.ds(pl.multiple_of(j * width, width), width)], preferred_element_type=f32
        ),
        *result_line,
    )
    grad = grad1.all(1)
    for a in range(3):
        at = pl.ds(a * taps_n, taps_n)
        part1[at, :] = jnp.dot(x9t[at, :], grad, preferred_element_type=f32).astype(bf16)
        for t in last[a : a + 1]:
            t.one()
    for t in conv2:
        t.finish()
    dn1 = conv_back(grad1, turned, upper, lower) * slope
    dxh = dn1 * vector(0)
    for t in last:
        t.two()
    copies = share(
        stat.at[2], stat_s.at[2], stat_r.at[2], row_count,
        norm_pieces(dxh, xhat) + [channel_total(dn1 * xhat), channel_total(dn1), bias_1],
    )
    result_sum.start()
    for t in last:
        t.three()
    total = share_total(stat.at[2], copies)
    sums[8 + 2 * images : 11 + 2 * images, :] = total[2 * images : 2 * images + 3]
    dfeat[...] = (dx1_ref[...] + norm_back(total, dxh, xhat, scale)).astype(bf16)
    for t in last:
        t.four()
    result_sum.finish()
    result[...] = (x1_ref[...] + result_line[0][...].reshape(rows, cols, width) + vector(8)).astype(bf16)
    for t in last:
        t.finish()
    if fast:
        back.drain()
    else:
        g_conv1[...] = part1[...]
        g_conv2[...] = part2[...]
        g_att[...] = part_att[...]
        g_out[...] = part_out[...]
        g_ctx[...] = dctx[...]
    grad2.drain()
    grad1.drain()
    result_sum.drain()


def backward_block(row_count, chan_count, per_group, entries, fast, offset, x, vec, dq, dkv, o, g_all, a3_all, x1, c1, rows_in,
                   mod, x9_1, x9_2, w1, w2, w_att, wo, dctx):
    rows, cols, width = x.shape
    tokens = rows * cols
    images = row_count * rows // IMG_H
    full = chan_count * width
    taps_n = 9 * width
    message = -(-(4 * images + 5) // 8) * 8
    vm = pl.BlockSpec(memory_space=pltpu.VMEM)
    hbm = pl.BlockSpec(memory_space=pl.ANY)
    S = jax.ShapeDtypeStruct
    sem = pltpu.SemaphoreType.DMA
    peers = max(chan_count - 1, 1)
    ctx_n, ctx_w = dctx.shape
    total_rows = -(-(11 + 2 * images) // 8) * 8
    plane_scratch = [
        *return_scratch(tokens, 2 * width), *total_scratch(full, 3 * width), *total_scratch(width, full),
        *total_scratch(ctx_n, ctx_w), *total_scratch(taps_n, full), *total_scratch(taps_n // 3, full),
        *total_scratch(taps_n // 3, full), *total_scratch(taps_n // 3, full),
    ]
    return pl.pallas_call(
        functools.partial(backward_kernel, row_count, chan_count, per_group, entries, fast),
        name="backward_block",
        out_shape=(
            S((rows, cols, width), bf16), S((rows, cols, width), bf16), S((total_rows, width), f32),
            S((taps_n, full), bf16), S((taps_n, full), bf16), S((full, 3 * width), bf16), S((width, full), bf16),
            S((ctx_n, ctx_w), bf16),
        ),
        in_specs=[pl.BlockSpec(memory_space=pltpu.SMEM)] + [vm] * (5 + VECTORS) + [hbm, vm, hbm, vm, vm, hbm, hbm, hbm, hbm, vm, vm, vm],
        out_specs=(vm,) * 8,
        scratch_shapes=[
            vmem((taps_n, full), bf16), vmem((taps_n, full), bf16), vmem((full, 3 * width), bf16), vmem((width, full), bf16),
            vmem((tokens, taps_n), bf16), vmem((tokens, taps_n), bf16), vmem((taps_n, full), bf16), vmem((taps_n, full), bf16),
            vmem((rows, cols, width), f32), vmem((chan_count, tokens, width), bf16), sem((6,)),
            vmem((taps_n, tokens), bf16), vmem((3, full, taps_n // 3), bf16),
            vmem((tokens, 3 * width), bf16), vmem((rows, cols, width), f32),
            vmem((2, chan_count, rows + 2, cols, width), bf16), sem((2, 2)), sem((2, 2)),
            sem((2, 2, peers, PIECES + 2)), sem((2, 2, peers, PIECES + 2)),
            vmem((3, row_count, message, width), f32), sem((3, row_count - 1)), sem((3, row_count - 1)),
            *scatter_scratch(chan_count, tokens, width), *scatter_scratch(chan_count, tokens, width),
            *(plane_scratch if fast else []),
        ],
        cost_estimate=pl.CostEstimate(flops=2 * 6 * 9 * tokens * width * full, bytes_accessed=24 * 2**20, transcendentals=4 * tokens * width),
        compiler_params=pltpu.CompilerParams(collective_id=1, has_side_effects=True, vmem_limit_bytes=60 * 2**20),
    )(offset, x, *vec, dq, dkv, o, g_all, a3_all, x1, c1, rows_in, mod, x9_1, x9_2, w1, w2, w_att, wo, dctx)


def finish_kernel(images, share_rows, ctx_count, result_in, dfeat_in, sums, g_conv1, g_conv2, g_att, g_out, g_ctx, emb, context,
                  result, dfeat, conv1, conv2, att, out, emb_w, ctx_w, emb_b, att_b, ctx_b, *vectors):
    width = sums.shape[1]
    result[...] = result_in[...]
    dfeat[...] = dfeat_in[...]
    conv1[...] = g_conv1[...].astype(f32)
    conv2[...] = g_conv2[...].astype(f32)
    out[...] = g_out[...].astype(f32)
    for t in range(3):
        att[:, t, :] = g_att[:, pl.ds(t * width, width)].astype(f32)
    block = emb.shape[1]
    for t in range(2):
        rows = jnp.concatenate([sums[8 + 2 * i + t : 9 + 2 * i + t, :] for i in range(images)], axis=0)
        emb_w[pl.ds(t, block, 2), :] = lax.dot_general(
            emb[...].astype(f32), rows, (((0,), (0,)), ((), ())), precision=HIGH, preferred_element_type=f32
        )
    total = None
    for i in range(images):
        term = contract(context[i], g_ctx[pl.ds(i * share_rows, ctx_count), :], 0, 0)
        total = term if total is None else total + term
    for t in range(2):
        ctx_w[pl.ds(t, block, 2), :] = total[:, t * width : (t + 1) * width]

    @pl.when(pl.program_id(0) == 0)
    def _():
        for t in range(2):
            emb_b[t : t + 1, :] = sum(sums[8 + 2 * i + t : 9 + 2 * i + t, :] for i in range(images))
            att_b[t : t + 1, :] = sums[2 + t : 3 + t, :]
            ctx_b[t : t + 1, :] = jnp.sum(g_ctx[:, pl.ds(t * width, width)].astype(f32), axis=0, keepdims=True)
        for ref, i in zip(vectors, (0, 1, 4, 5, 6, 7, 8 + 2 * images, 9 + 2 * images, 10 + 2 * images)):
            ref[...] = sums[i : i + 1, :]


def finish_block(images, share_rows, steps, result, dfeat, sums, g_conv1, g_conv2, g_att, g_out, g_ctx, emb, context):
    width = sums.shape[1]
    depth = emb.shape[1]
    ctx_count = context.shape[1]
    S = jax.ShapeDtypeStruct

    def lead(shape):
        rest = (0,) * (len(shape) - 1)
        return pl.BlockSpec((shape[0] // steps,) + tuple(shape[1:]), lambda s: (s,) + rest)

    def whole(shape):
        return pl.BlockSpec(tuple(shape), lambda s: (0,) * len(shape))

    taps_n, full = g_conv1.shape
    shapes = [
        (result.shape, bf16, lead), (dfeat.shape, bf16, lead), ((taps_n, full), f32, lead), ((taps_n, full), f32, lead),
        ((full, 3, width), f32, lead), ((width, full), f32, lead), ((2 * depth, width), f32, lead),
        ((2 * depth, width), f32, lead), ((2, width), f32, whole), ((2, width), f32, whole), ((2, width), f32, whole),
    ] + [((1, width), f32, whole)] * 9
    return pl.pallas_call(
        functools.partial(finish_kernel, images, share_rows, ctx_count),
        name="finish_block",
        grid=(steps,),
        out_shape=tuple(S(shape, dtype) for shape, dtype, _ in shapes),
        in_specs=[
            lead(result.shape), lead(dfeat.shape), whole(sums.shape), lead(g_conv1.shape), lead(g_conv2.shape), lead(g_att.shape),
            lead(g_out.shape), whole(g_ctx.shape), pl.BlockSpec((images, depth // steps), lambda s: (0, s)),
            pl.BlockSpec((images, ctx_count, depth // steps), lambda s: (0, 0, s)),
        ],
        out_specs=tuple(spec(shape) for shape, _, spec in shapes),
        cost_estimate=pl.CostEstimate(flops=4 * images * ctx_count * depth * width, bytes_accessed=16 * 2**20, transcendentals=0),
        compiler_params=pltpu.CompilerParams(vmem_limit_bytes=48 * 2**20),
    )(result, dfeat, sums, g_conv1, g_conv2, g_att, g_out, g_ctx, emb, context)


def local(
    features,
    embedding,
    context,
    image_offset,
    first_gain,
    first_shift,
    conv_first,
    conv_first_bias,
    embed_weight,
    embed_bias,
    second_gain,
    second_shift,
    conv_second,
    conv_second_bias,
    attend_gain,
    attend_shift,
    attend_weight,
    attend_bias,
    context_weight,
    context_bias,
    output_weight,
    output_bias,
    cotangent,
):
    slab_rows, columns, channels = features.shape
    devices, chan = lax.axis_size("rows"), lax.axis_size("chan")
    total_rows = slab_rows * devices
    images = total_rows // IMG_H
    per_group = C // GROUPS
    entries = IMG_H * columns * per_group
    tokens = slab_rows * columns
    modulate = (
        jnp.einsum("ie,eto->ito", embedding, embed_weight, preferred_element_type=jnp.float32)
        + embed_bias
    )
    context_count = context.shape[1]
    tail = -(-context_count // 256) * 256
    context_proj = (
        jnp.einsum("snc,cto->snto", context, context_weight, preferred_element_type=jnp.float32)
        + context_bias
    )
    context_rows = jnp.pad(
        context_proj.reshape(images, context_count, 2 * channels).astype(bf16), ((0, 0), (0, tail - context_count), (0, 0))
    )
    vectors = [
        vector.reshape(1, channels)
        for vector in (first_gain, first_shift, conv_first_bias, second_gain, second_shift, conv_second_bias, attend_gain,
                       attend_shift, output_bias)
    ] + [attend_bias]
    window = min(devices, 2 * (IMG_H // slab_rows) + 1)
    kernel_one = conv_first.reshape(9 * channels, C)
    kernel_two = conv_second.reshape(9 * channels, C)
    attend_kernels = attend_weight.reshape(C, 3 * channels)
    x9_one, x9_two, middle, inner, row_stats, attend_blocks, queries, kv_all, grad_blocks, grad_attended = forward_block(
        devices, chan, per_group, entries, window, image_offset, features, vectors, modulate, kernel_one, kernel_two,
        attend_kernels, cotangent.reshape(tokens, channels), output_weight,
    )
    share_rows = -(-context_count // 64) * 64
    attended, query_grad, window_grad, context_part = attend(
        devices, slab_rows, image_offset, queries, grad_attended, kv_all.reshape(window * slab_rows, columns, 2 * channels),
        context_rows, total_rows, IMG_H, context_count, images, share_rows,
    )
    fast = devices == 8 and window == devices
    key_value_grad = window_grad.reshape(window, tokens, 2 * channels)
    if not fast:
        pieces, key_value_grad = key_value_grad, jnp.zeros((tokens, 2 * channels), f32)
        for position in range(window):
            shift_by = position - window // 2 if window < devices else None
            piece = pieces[position]
            if shift_by is None:
                piece = jnp.sum(lax.all_to_all(pieces, "rows", 0, 0).astype(f32), axis=0) if position == 0 else 0.0
            elif shift_by != 0:
                piece = from_behind(piece, "rows", shift_by)
            key_value_grad = key_value_grad + (piece if shift_by is None else piece.astype(f32))
    result, features_grad, sums, conv_first_grad, conv_second_grad, attend_grad, output_weight_grad, context_sum = backward_block(
        devices, chan, per_group, entries, fast, image_offset, features, vectors, query_grad, key_value_grad, attended,
        grad_blocks, attend_blocks, inner, middle, row_stats, modulate, x9_one, x9_two, kernel_one, kernel_two, attend_kernels,
        output_weight, context_part,
    )
    if not fast:
        conv_first_grad, conv_second_grad, attend_grad, output_weight_grad, context_sum = lax.psum(
            (conv_first_grad, conv_second_grad, attend_grad, output_weight_grad, context_sum), "rows"
        )
    (result, features_grad, conv_first_grad, conv_second_grad, attend_grad, output_weight_grad, embed_weight_grad,
     context_weight_grad, embed_bias_grad, attend_bias_grad, context_bias_grad, *rest) = finish_block(
        images, share_rows, 8, result, features_grad, sums, conv_first_grad, conv_second_grad, attend_grad,
        output_weight_grad, context_sum, embedding, context,
    )
    (attend_gain_grad, attend_shift_grad, output_bias_grad, second_gain_grad, second_shift_grad, conv_second_bias_grad,
     first_gain_grad, first_shift_grad, conv_first_bias_grad) = [vector.reshape(channels) for vector in rest]
    return (
        result,
        features_grad,
        first_gain_grad,
        first_shift_grad,
        conv_first_grad.reshape(3, 3, channels, C),
        conv_first_bias_grad,
        embed_weight_grad.reshape(-1, 2, channels),
        embed_bias_grad,
        second_gain_grad,
        second_shift_grad,
        conv_second_grad.reshape(3, 3, channels, C),
        conv_second_bias_grad,
        attend_gain_grad,
        attend_shift_grad,
        attend_grad,
        attend_bias_grad,
        context_weight_grad.reshape(-1, 2, channels),
        context_bias_grad,
        output_weight_grad,
        output_bias_grad,
    )


def solution(mesh):
    placed = (
        P("rows", None, "chan"),
        P(),
        P(),
        P(),
        P("chan"),
        P("chan"),
        P(None, None, "chan", None),
        P("chan"),
        P(None, None, "chan"),
        P(None, "chan"),
        P("chan"),
        P("chan"),
        P(None, None, "chan", None),
        P("chan"),
        P("chan"),
        P("chan"),
        P(None, None, "chan"),
        P(None, "chan"),
        P(None, None, "chan"),
        P(None, "chan"),
        P("chan", None),
        P("chan"),
        P("rows", None, "chan"),
    )
    return jax.shard_map(
        local,
        mesh=mesh,
        in_specs=placed,
        out_specs=(
            P("rows", None, "chan"),
            P("rows", None, "chan"),
            P("chan"),
            P("chan"),
            P(None, None, "chan", None),
            P("chan"),
            P(None, None, "chan"),
            P(None, "chan"),
            P("chan"),
            P("chan"),
            P(None, None, "chan", None),
            P("chan"),
            P("chan"),
            P("chan"),
            P(None, None, "chan"),
            P(None, "chan"),
            P(None, None, "chan"),
            P(None, "chan"),
            P("chan", None),
            P("chan"),
        ),
        check_vma=False,
    )
```

```python
import functools

import jax
import jax.numpy as jnp
from jax import lax
from jax.experimental import pallas as pl
from jax.experimental.pallas import tpu as pltpu
from jax.sharding import PartitionSpec as P

C = 512
HEAD_DIM = 64
GROUPS = 32
IMG_H = 64


EPSILON = 1e-05
HIGH = lax.Precision.HIGHEST
NEG = -1e30
bf16, f32 = jnp.bfloat16, jnp.float32


def from_behind(block, axis, distance):
    devices = range(lax.axis_size(axis))
    route = [((i - distance) % len(devices), i) for i in devices]
    return lax.ppermute(block, axis, route)


def dot(a, b, ca, cb):
    return lax.dot_general(a, b, (((ca,), (cb,)), ((), ())), preferred_element_type=f32)


def attend_kernel(tiles, tile_rows, cols, width, image_rows, total_rows, ctx_count, images, window, row_count,
                  offset, q_ref, do_ref, kv_ref, ctx_ref,
                  o_ref, dq_ref, dkv_ref, dctx_ref,
                  kv, kt, vt, qt, do_t, s_buf, p_buf, dk, dv, oacc, qacc, sem):
    slab_rows = tiles * tile_rows
    me = lax.axis_index("rows")
    base = (me - window // 2) * slab_rows if window < row_count else 0
    place = lax.rem(me * slab_rows - offset[0] + total_rows, total_rows)
    image_a = place // image_rows
    split = jnp.minimum(slab_rows, image_rows - lax.rem(place, image_rows))
    image_b = lax.rem(image_a + jnp.where(split < slab_rows, 1, 0), images)
    start_a = lax.rem(offset[0] + image_a * image_rows - base + 2 * total_rows, total_rows)
    start_b = lax.rem(offset[0] + image_b * image_rows - base + 2 * total_rows, total_rows)
    ids = (image_a, image_b)
    tq = tile_rows * cols
    main = image_rows * cols
    tail = kv.shape[1] * cols - main
    heads = width // HEAD_DIM
    straddle = split < slab_rows
    group = 8

    def load(img, start):
        @pl.loop(0, image_rows // group)
        def _(j):
            src = lax.rem(start + j * group, total_rows)
            whole = src + group <= total_rows

            @pl.when(whole)
            def _():
                pltpu.make_async_copy(
                    kv_ref.at[pl.ds(src, group)], kv.at[img, pl.ds(j * group, group)], sem.at[img]
                ).start()

            @pl.when(jnp.logical_not(whole))
            def _():
                @pl.loop(0, group)
                def _(i):
                    pltpu.make_async_copy(
                        kv_ref.at[lax.rem(src + i, total_rows)], kv.at[img, j * group + i], sem.at[img]
                    ).start()

    def finish(img, start):
        pltpu.make_async_copy(kv_ref.at[pl.ds(0, image_rows)], kv.at[img, pl.ds(0, image_rows)], sem.at[img]).wait()
        for i in range(tail // cols):
            kv[img, image_rows + i] = ctx_ref[ids[img], pl.ds(i * cols, cols)]
        step = 256 // cols

        @pl.loop(0, kv.shape[1] // step)
        def _(c):
            at = pl.ds(pl.multiple_of(c * 256, 256), 256)
            rows = kv[img, pl.ds(c * step, step)].reshape(256, 2 * width)
            kt[img, :, at] = rows[:, :width].T
            vt[img, :, at] = rows[:, width:].T
        dk[img] = jnp.zeros(dk.shape[1:], f32)
        dv[img] = jnp.zeros(dv.shape[1:], f32)

    load(0, start_a)

    @pl.when(straddle)
    def _():
        load(1, start_b)
    for t in range(tiles):
        qt[t] = (q_ref[pl.ds(t * tq, tq)] * jnp.asarray(HEAD_DIM ** -0.5, bf16)).T
        do_t[t] = do_ref[pl.ds(t * tq, tq)].T
    finish(0, start_a)

    @pl.when(straddle)
    def _():
        finish(1, start_b)

    count_a = (split + tile_rows - 1) // tile_rows
    first_b = split // tile_rows
    count = count_a + jnp.where(straddle, tiles - first_b, 0)
    feature = lax.broadcasted_iota(jnp.int32, (width, 1), 0) // HEAD_DIM
    lane_row = lax.broadcasted_iota(jnp.int32, (1, tq), 1) // cols
    tail_ok = lax.broadcasted_iota(jnp.int32, (tail, 1), 0) < ctx_count

    @pl.loop(0, count)
    def _(item):
        is_b = (item >= count_a).astype(jnp.int32)
        t = jnp.where(is_b == 1, first_b + item - count_a, item)
        row = t * tile_rows + lane_row
        low = jnp.where(is_b == 1, split, 0)
        high = jnp.where(is_b == 1, slab_rows, split)
        mine = jnp.logical_and(row >= low, row < high)
        q_t = qt[t].astype(f32)
        g_t = do_t[t].astype(f32)
        q_h = [jnp.where(feature == h, q_t, 0.0).astype(bf16) for h in range(heads)]

        def rows_of(at, size, cut):
            return kv[is_b, at].reshape(size, 2 * width)[:, cut]

        parts = (
            (pl.ds(0, image_rows), pl.ds(0, main), main, False), (pl.ds(image_rows, tail // cols), pl.ds(main, tail), tail, True)
        )
        m = [jnp.full((8, tq), NEG, f32) for _ in range(heads)]
        for blocks, at, size, masked in parts:
            keys = rows_of(blocks, size, slice(0, width))
            for h in range(heads):
                s = dot(keys, q_h[h], 1, 0)
                if masked:
                    s = jnp.where(tail_ok, s, NEG)
                s_buf[h, at] = s
                m[h] = jnp.maximum(m[h], jnp.max(s.reshape(size // 8, 8, tq), axis=0))
        m = [jnp.max(v, axis=0, keepdims=True) for v in m]
        l = [jnp.zeros((8, tq), f32) for _ in range(heads)]
        o = [jnp.zeros((HEAD_DIM, tq), f32) for _ in range(heads)]
        for blocks, at, size, masked in parts:
            for h in range(heads):
                p = jnp.exp(s_buf[h, at] - m[h])
                l[h] = l[h] + jnp.sum(p.reshape(size // 8, 8, tq), axis=0)
                p = p.astype(bf16)
                p_buf[at, pl.ds(h * tq, tq)] = p
                o[h] = o[h] + dot(vt[is_b, pl.ds(h * HEAD_DIM, HEAD_DIM), at], p, 1, 0)
        inv = [1.0 / jnp.sum(v, axis=0, keepdims=True) for v in l]
        o_all = jnp.concatenate([o[h] * inv[h] for h in range(heads)], axis=0)
        do_h, delta = [], []
        for h in range(heads):
            scaled = jnp.where(mine, g_t * inv[h], 0.0)
            scaled = jnp.where(feature == h, scaled, 0.0).astype(bf16)
            do_h.append(scaled)
            delta.append(jnp.sum(scaled.astype(f32) * o_all, axis=0, keepdims=True))
        do_cat = jnp.concatenate(do_h, axis=1)
        q_cat = jnp.concatenate(q_h, axis=1)
        dq = [jnp.zeros((HEAD_DIM, tq), f32) for _ in range(heads)]
        for blocks, at, size, masked in parts:
            vals = rows_of(blocks, size, slice(width, 2 * width))
            ps, dss = [], []
            for h in range(heads):
                dp = dot(vals, do_h[h], 1, 0)
                p = p_buf[at, pl.ds(h * tq, tq)]
                ds = (p.astype(f32) * (dp - delta[h])).astype(bf16)
                dq[h] = dq[h] + dot(kt[is_b, pl.ds(h * HEAD_DIM, HEAD_DIM), at], ds, 1, 0)
                ps.append(p)
                dss.append(ds)
            dv[is_b, at] = dv[is_b, at] + dot(jnp.concatenate(ps, axis=1), do_cat, 1, 1)
            dk[is_b, at] = dk[is_b, at] + dot(jnp.concatenate(dss, axis=1), q_cat, 1, 1)
        oacc[t] = jnp.where(mine, o_all, oacc[t])
        qacc[t] = jnp.where(mine, jnp.concatenate(dq, axis=0) * (HEAD_DIM ** -0.5), qacc[t])

    for t in range(tiles):
        o_ref[pl.ds(t * tq, tq)] = oacc[t].T.astype(bf16)
        dq_ref[pl.ds(t * tq, tq)] = qacc[t].T

    dctx_ref[...] = jnp.zeros(dctx_ref.shape, dctx_ref.dtype)
    share_rows = dctx_ref.shape[0] // images
    if images > 1:
        dkv_ref[...] = jnp.zeros(dkv_ref.shape, dkv_ref.dtype)

    def put(img, start):
        @pl.loop(0, image_rows)
        def _(j):
            row = lax.rem(start + j, total_rows)
            at = pl.ds(pl.multiple_of(j * cols, cols), cols)
            dkv_ref[row, :, :width] = dk[img, at].astype(bf16)
            dkv_ref[row, :, width:] = dv[img, at].astype(bf16)
        at = pl.ds(pl.multiple_of(ids[img] * share_rows, 16), share_rows)
        dctx_ref[at, :width] = dk[img, pl.ds(main, share_rows)].astype(bf16)
        dctx_ref[at, width:] = dv[img, pl.ds(main, share_rows)].astype(bf16)
    put(0, start_a)

    @pl.when(straddle)
    def _():
        put(1, start_b)


def attend(row_count, slab, offset, q, do, kv_window, ctx, total_rows, image_rows, ctx_count, images, share_rows, tile_rows=4):
    tokens, width = q.shape
    rows, cols, _ = kv_window.shape
    tiles = tokens // (tile_rows * cols)
    tq = tile_rows * cols
    tail = ctx.shape[1]
    keys = image_rows * cols + tail
    heads = width // HEAD_DIM
    kern = functools.partial(
        attend_kernel, tiles, tile_rows, cols, width, image_rows, total_rows, ctx_count, images, rows // slab, row_count
    )
    vm = pl.BlockSpec(memory_space=pltpu.VMEM)
    return pl.pallas_call(
        kern, name="attend",
        out_shape=(jax.ShapeDtypeStruct((tokens, width), bf16), jax.ShapeDtypeStruct((tokens, width), f32),
                   jax.ShapeDtypeStruct(kv_window.shape, bf16), jax.ShapeDtypeStruct((images * share_rows, 2 * width), bf16)),
        in_specs=[pl.BlockSpec(memory_space=pltpu.SMEM), vm, vm, pl.BlockSpec(memory_space=pl.ANY), vm],
        out_specs=(vm, vm, vm, vm),
        scratch_shapes=[
            pltpu.VMEM((2, keys // cols, cols, 2 * width), bf16),
            pltpu.VMEM((2, width, keys), bf16), pltpu.VMEM((2, width, keys), bf16),
            pltpu.VMEM((tiles, width, tq), bf16), pltpu.VMEM((tiles, width, tq), bf16),
            pltpu.VMEM((heads, keys, tq), f32), pltpu.VMEM((keys, heads * tq), bf16),
            pltpu.VMEM((2, keys, width), f32), pltpu.VMEM((2, keys, width), f32),
            pltpu.VMEM((tiles, width, tq), f32), pltpu.VMEM((tiles, width, tq), f32),
            pltpu.SemaphoreType.DMA((2,)),
        ],
        cost_estimate=pl.CostEstimate(flops=12 * tokens * keys * width, bytes_accessed=8 * 2**20, transcendentals=heads * tokens * keys),
        compiler_params=pltpu.CompilerParams(vmem_limit_bytes=60 * 2**20),
    )(offset, q, do, kv_window, ctx)


MESH = pl.DeviceIdType.MESH
PIECES = 8
SEGMENTS = 4
VECTORS = 10


def vmem(shape, dtype=f32):
    return pltpu.VMEM(shape, dtype)


def greet(devices):
    barrier = pltpu.get_barrier_semaphore()
    for device in devices:
        pl.semaphore_signal(barrier, inc=1, device_id=device, device_id_type=MESH)
    pl.semaphore_wait(barrier, len(devices))


def row_peers(count):
    r, z = lax.axis_index("rows"), lax.axis_index("chan")
    return [(lax.rem(r + d, count), z) for d in range(1, count)]


def chan_peers(count):
    r, z = lax.axis_index("rows"), lax.axis_index("chan")
    return [(r, lax.rem(z + d, count)) for d in range(1, count)]


def push(src, dst, send_sem, recv_sem, device):
    copy = pltpu.make_async_remote_copy(
        src_ref=src, dst_ref=dst, send_sem=send_sem, recv_sem=recv_sem, device_id=device, device_id_type=MESH
    )
    copy.start()
    return copy


def contract(a, b, a_dim, b_dim):
    return lax.dot_general(a, b, (((a_dim,), (b_dim,)), ((), ())), preferred_element_type=f32)


class Locals:
    def __init__(self, sems):
        self.sems, self.copies, self.done = sems, [], set()

    def start(self, src, dst):
        copy = pltpu.make_async_copy(src, dst, self.sems.at[len(self.copies)])
        copy.start()
        self.copies.append(copy)
        return len(self.copies) - 1

    def wait(self, *which):
        for i in which if which else range(len(self.copies)):
            if i not in self.done:
                self.copies[i].wait()
                self.done.add(i)


def share(buf, sends, recvs, count, pieces):
    me = lax.axis_index("rows")
    for index, piece in enumerate(pieces):
        buf[me, pl.ds(index, 1), :] = piece
    return [push(buf.at[me], buf.at[me], sends.at[d], recvs.at[d], device) for d, device in enumerate(row_peers(count))]


def share_total(buf, copies):
    for copy in copies:
        copy.wait()
    total = buf[0]
    for index in range(1, buf.shape[0]):
        total = total + buf[index]
    return total


def image_masks(offset, first, rows, width, total_rows):
    images = total_rows // IMG_H
    row = first - offset + lax.broadcasted_iota(jnp.int32, (rows, 1, width), 0)
    row = jnp.where(row < 0, row + total_rows, row)
    row = jnp.where(row >= total_rows, row - total_rows, row)
    one, zero = jnp.ones((rows, 1, width), f32), jnp.zeros((rows, 1, width), f32)
    member, upper, lower = [], one, one
    for i in range(images):
        inside = jnp.logical_and(row >= i * IMG_H, row < (i + 1) * IMG_H)
        member.append(jnp.where(inside, one, zero))
        upper = jnp.where(row == i * IMG_H, zero, upper)
        lower = jnp.where(row == (i + 1) * IMG_H - 1, zero, lower)
    return member, upper, lower


def group_sum(values, per_group):
    width = values.shape[1]
    one = lax.broadcasted_iota(jnp.int32, (width, width), 0) // per_group
    two = lax.broadcasted_iota(jnp.int32, (width, width), 1) // per_group
    same = (one == two).astype(f32)
    return jnp.dot(values, same, precision=HIGH, preferred_element_type=f32)


def image_sums(values, member):
    by_row = jnp.sum(values, axis=1, keepdims=True)
    return [jnp.sum(by_row * mask, axis=0) for mask in member]


def to_rows(per_image, member):
    total = None
    for mask, value in zip(member, per_image):
        term = mask * value[None]
        total = term if total is None else total + term
    return total


def norm_images(total, images, entries, per_group):
    grouped = group_sum(total, per_group) * (1.0 / entries)
    centers, scales = [], []
    for i in range(images):
        center = grouped[2 * i : 2 * i + 1]
        square = grouped[2 * i + 1 : 2 * i + 2]
        centers.append(center)
        scales.append(lax.rsqrt(square - center * center + EPSILON))
    return centers, scales


def taps(pad, upper, lower, x9):
    rows, cols, width = pad.shape
    rows = rows - 2
    tokens = rows * cols
    col = lax.rem(lax.broadcasted_iota(jnp.int32, (tokens, 1), 0), cols)
    for a in range(3):
        v = pad[pl.ds(a, rows)].astype(f32)
        if a == 0:
            v = v * upper
        if a == 2:
            v = v * lower
        v = v.reshape(tokens, width)
        left = jnp.where(col == 0, 0.0, pltpu.roll(v, 1, 0))
        right = jnp.where(col == cols - 1, 0.0, pltpu.roll(v, tokens - 1, 0))
        for b, part in enumerate((left, v, right)):
            x9[:, pl.ds((3 * a + b) * width, width)] = part.astype(bf16)


class LineGather:
    def __init__(self, at, pieces, sends, recvs):
        self.at, self.pieces, self.sends, self.recvs = at, pieces, sends, recvs
        self.r, self.z = lax.axis_index("rows"), lax.axis_index("chan")
        self.count = lax.axis_size("chan")

    def copy(self, way, step, piece, shard):
        other = self.z + 1 if way == 0 else self.z - 1
        ref = self.at(shard, piece)
        return pltpu.make_async_remote_copy(
            src_ref=ref, dst_ref=ref, send_sem=self.sends.at[way, step, piece], recv_sem=self.recvs.at[way, step, piece],
            device_id=(self.r, other), device_id_type=MESH,
        )

    def has(self, way, step):
        return self.z >= step if way == 0 else self.z + step < self.count

    def open_end(self, way):
        return self.z + 1 < self.count if way == 0 else self.z >= 1

    def shard(self, way, step):
        return self.z - step if way == 0 else self.z + step

    def run(self, step, pieces=None):
        for piece in range(self.pieces) if pieces is None else pieces:
            for way in range(2):
                if step == 0:
                    @pl.when(self.open_end(way))
                    def _():
                        self.copy(way, 0, piece, self.z).start()
                else:
                    @pl.when(self.has(way, step))
                    def _():
                        shard = self.shard(way, step)
                        self.copy(way, step - 1, piece, shard).wait_recv()
                        if step < self.count - 1:
                            @pl.when(self.open_end(way))
                            def _():
                                self.copy(way, step, piece, shard).start()

    def drain(self):
        for step in range(self.count - 1):
            for way in range(2):
                @pl.when(jnp.logical_and(self.has(way, step), self.open_end(way)))
                def _():
                    for piece in range(self.pieces):
                        self.copy(way, step, piece, self.shard(way, step)).wait_send()


class LineScatter:
    def __init__(self, term, own, out, recv, sends, recvs):
        self.term, self.own, self.out, self.recv, self.sends, self.recvs = term, own, out, recv, sends, recvs
        self.r, self.z = lax.axis_index("rows"), lax.axis_index("chan")
        self.pieces = sends.shape[1]
        self.size = own.shape[0] // self.pieces
        self.end = jnp.logical_or(self.z == 0, self.z == 3)
        self.opposite = lax.rem(self.z + 2, 4)

    def rows(self, piece):
        return pl.ds(piece * self.size, self.size)

    def copy(self, slot, piece, device):
        rows = self.rows(piece)
        return pltpu.make_async_remote_copy(
            src_ref=self.out.at[slot, rows], dst_ref=self.recv.at[slot, rows], send_sem=self.sends.at[slot, piece],
            recv_sem=self.recvs.at[slot, piece], device_id=(self.r, device), device_id_type=MESH,
        )

    def push(self, slot, target, device, piece):
        rows = self.rows(piece)
        self.out[slot, rows] = self.term(target, rows).astype(bf16)
        self.copy(slot, piece, device).start()

    def send(self, piece):
        z = self.z

        @pl.when(self.end)
        def _():
            self.push(3, 3 - z, 1 + z // 3, piece)
            self.push(0, self.opposite, self.opposite, piece)

        @pl.when(z < 3)
        def _():
            self.push(1, z + 1, z + 1, piece)

        @pl.when(z > 0)
        def _():
            self.push(2, z - 1, z - 1, piece)

    def merge(self, piece):
        @pl.when(jnp.logical_not(self.end))
        def _():
            rows = self.rows(piece)
            term = self.term(self.opposite, rows)
            self.copy(3, piece, self.opposite).wait_recv()
            self.out[0, rows] = (term + self.recv[3, rows].astype(f32)).astype(bf16)
            self.copy(0, piece, self.opposite).start()

    def keep(self):
        self.own[...] = self.term(self.z, pl.ds(0, self.own.shape[0]))

    def add(self, slot, piece):
        rows = self.rows(piece)
        self.copy(slot, piece, self.z).wait_recv()
        self.own[rows, :] = self.own[rows, :] + self.recv[slot, rows].astype(f32)

    def finish(self):
        for piece in range(self.pieces):
            @pl.when(self.z > 0)
            def _():
                self.add(1, piece)

            @pl.when(self.z < 3)
            def _():
                self.add(2, piece)
            self.add(0, piece)

    def drain(self):
        for piece in range(self.pieces):
            self.copy(0, piece, self.z).wait_send()

            @pl.when(self.z < 3)
            def _():
                self.copy(1, piece, self.z).wait_send()

            @pl.when(self.z > 0)
            def _():
                self.copy(2, piece, self.z).wait_send()

            @pl.when(self.end)
            def _():
                self.copy(3, piece, self.z).wait_send()


def scatter_scratch(tokens, width, pieces):
    return [
        vmem((tokens, width), f32), vmem((4, tokens, width), bf16), vmem((4, tokens, width), bf16),
        pltpu.SemaphoreType.DMA((4, pieces)), pltpu.SemaphoreType.DMA((4, pieces)),
    ]


def plane():
    r = lax.axis_index("rows")
    core = r + 1 - 2 * lax.rem(r, 2)
    x_dev = r + 2 - 4 * lax.rem(r // 2, 2)
    y_dev = r + 4 - 8 * (r // 4)
    return core, x_dev, y_dev, x_dev + y_dev - r


class PlaneGather:
    def __init__(self, all_ref, sends, recvs):
        self.all, self.sends, self.recvs = all_ref, sends, recvs
        self.r, self.z = lax.axis_index("rows"), lax.axis_index("chan")
        self.core, self.x, self.y, self.d = plane()
        self.size = all_ref.shape[1] // SEGMENTS
        self.copies = [{} for _ in range(SEGMENTS)]

    def part(self, segment, which):
        half = self.size // 2
        if which is None:
            return pl.ds(segment * self.size, self.size)
        return pl.ds(segment * self.size + which * half, half)

    def send(self, segment, i, slab, which, device):
        ref = self.all.at[slab, self.part(segment, which)]
        self.copies[segment][i] = push(ref, ref, self.sends.at[segment, i], self.recvs.at[segment, i], (device, self.z))

    def start(self, s):
        self.send(s, 0, self.r, 0, self.x)
        self.send(s, 1, self.r, 1, self.y)
        self.send(s, 2, self.r, 1, self.x)
        self.send(s, 3, self.r, 0, self.y)
        self.send(s, 4, self.r, None, self.core)

    def relay(self, s):
        copies = self.copies[s]
        copies[0].wait_recv()
        self.send(s, 5, self.x, 0, self.y)
        self.send(s, 6, self.x, 0, self.core)
        copies[1].wait_recv()
        self.send(s, 7, self.y, 1, self.x)
        self.send(s, 8, self.y, 1, self.core)
        copies[2].wait_recv()
        self.send(s, 9, self.x, 1, self.core)
        copies[3].wait_recv()
        self.send(s, 10, self.y, 0, self.core)

    def last(self, s):
        copies = self.copies[s]
        copies[5].wait_recv()
        self.send(s, 11, self.d, 0, self.core)
        copies[7].wait_recv()
        self.send(s, 12, self.d, 1, self.core)

    def done(self, s):
        for i in (4, 6, 8, 9, 10, 11, 12):
            self.copies[s][i].wait_recv()

    def drain(self):
        for copies in self.copies:
            for copy in copies.values():
                copy.wait_send()


class WindowGather:
    def __init__(self, all_ref, sends, recvs):
        self.all, self.sends, self.recvs = all_ref, sends, recvs
        self.size = all_ref.shape[1] // SEGMENTS
        self.copies = [[] for _ in range(SEGMENTS)]

    def start(self, s):
        r, z, count = lax.axis_index("rows"), lax.axis_index("chan"), lax.axis_size("rows")
        window = self.all.shape[0]
        own = window // 2 if window < count else r
        part = pl.ds(s * self.size, self.size)
        for i in range(1, count):
            place = window // 2 - i if i <= window // 2 else window // 2 + count - i
            if window < count and (place < 0 or place >= window):
                continue
            slot = place if window < count else r
            device = (lax.rem(r + i, count), z)
            self.copies[s].append(
                push(self.all.at[own, part], self.all.at[slot, part], self.sends.at[s, i], self.recvs.at[s, i], device)
            )

    def relay(self, s):
        pass

    last = relay

    def done(self, s):
        for copy in self.copies[s]:
            copy.wait_recv()

    def drain(self):
        for copies in self.copies:
            for copy in copies:
                copy.wait_send()


def forward_kernel(row_count, chan_count, per_group, entries, fast, offset, x_ref, *refs):
    vec, refs = refs[:VECTORS], refs[VECTORS:]
    (mod, w1_hbm, w2_hbm, att_hbm, g_hbm, wo_hbm,
     x9t_1_hbm, x9t_2_hbm, turn1_hbm, turn2_hbm, c1_hbm, x1_hbm, a3_hbm, all_hbm, gall_hbm, row_ref, q_ref, do_ref,
     w1, w2, w_att, wo, x9t_1, x9t_2, turn1, turn2, x1_ref, a3_ref, all_ref, gall_ref,
     xpad, cpad, pad, x9, own1, out1, recv1, s1, r1, own2, out2, recv2, s2, r2, stat, stat_s, stat_r, halo_s, halo_r,
     a3_s, a3_r, g_s, g_r, kv_s, kv_r, in_s, out_s) = refs
    rows, cols, width = x_ref.shape
    tokens = rows * cols
    r, z = lax.axis_index("rows"), lax.axis_index("chan")
    loads, stores = Locals(in_s), Locals(out_s)
    for src, dst in ((g_hbm, gall_ref.at[z]), (w1_hbm, w1), (w2_hbm, w2), (att_hbm, w_att), (wo_hbm, wo)):
        loads.start(src, dst)
    x = x_ref[...]
    xpad[pl.ds(1, rows)] = x
    greet(row_peers(row_count) + chan_peers(chan_count))
    up = (lax.rem(r + row_count - 1, row_count), z)
    down = (lax.rem(r + 1, row_count), z)

    def rims(phase, ref):
        one = push(ref.at[1], ref.at[rows + 1], halo_s.at[phase, 0], halo_r.at[phase, 0], up)
        two = push(ref.at[rows], ref.at[0], halo_s.at[phase, 1], halo_r.at[phase, 1], down)
        return one, two

    x_rims = rims(0, xpad)
    member, upper, lower = image_masks(offset[0], r * rows - 1, rows + 2, width, row_count * rows)
    images = len(member)
    inner = [mask[1 : rows + 1] for mask in member]
    upper, lower = upper[1 : rows + 1], lower[1 : rows + 1]
    third = -(-tokens // 48) * 16
    g_copies = []
    loads.wait(0)

    def vector(i):
        return vec[i][...][None]

    def stats(phase, values):
        pieces = []
        for a, b in zip(image_sums(values, inner), image_sums(values * values, inner)):
            pieces += [a, b]
        copies = share(stat.at[phase], stat_s.at[phase], stat_r.at[phase], row_count, pieces)
        part = pl.ds(phase * third, min(third, tokens - phase * third))
        for d, device in enumerate(chan_peers(chan_count)):
            g_copies.append(push(gall_ref.at[z, part], gall_ref.at[z, part], g_s.at[phase, d], g_r.at[phase, d], device))
        centers, scales = norm_images(share_total(stat.at[phase], copies), images, entries, per_group)
        row_ref[2 * phase] = to_rows(centers, inner)
        row_ref[2 * phase + 1] = to_rows(scales, inner)
        return centers, scales

    def conv(weight, *scratch):
        def term(j, at):
            return jnp.dot(x9[at, :], weight[:, pl.ds(pl.multiple_of(j * width, width), width)], preferred_element_type=f32)
        line = LineScatter(term, *scratch)
        for piece in range(line.pieces):
            line.send(piece)
        for piece in range(line.pieces):
            line.merge(piece)
        line.keep()
        return line

    def turn(weight, turned):
        for j in range(chan_count):
            for a in range(3):
                turned[j, pl.ds(a * width, width), :] = weight[pl.ds(3 * a * width, 3 * width), pl.ds(j * width, width)].T

    centers, scales = stats(0, x.astype(f32))
    for copy in x_rims:
        copy.wait()
    n1 = (xpad[...].astype(f32) - to_rows(centers, member)) * to_rows(scales, member) * vector(0) + vector(1)
    pad[...] = (n1 * jax.nn.sigmoid(n1)).astype(bf16)
    taps(pad, upper, lower, x9)
    loads.wait(1)
    line1 = conv(w1, own1, out1, recv1, s1, r1)
    x9t_1[...] = x9[...].T
    stores.start(x9t_1, x9t_1_hbm)
    turn(w1, turn1)
    stores.start(turn1, turn1_hbm)
    line1.finish()
    c1 = own1[...].reshape(rows, cols, width) + vector(2)
    cpad[pl.ds(1, rows)] = c1
    c_rims = rims(1, cpad)
    stores.start(cpad.at[pl.ds(1, rows)], c1_hbm)
    centers, scales = stats(1, c1)
    mod_scale = 1.0 + to_rows([mod[i, 0:1, :] for i in range(images)], member)
    mod_shift = to_rows([mod[i, 1:2, :] for i in range(images)], member)
    for copy in c_rims:
        copy.wait()
    n2 = (cpad[...] - to_rows(centers, member)) * to_rows(scales, member) * vector(3) + vector(4)
    h2 = n2 * mod_scale + mod_shift
    pad[...] = (h2 * jax.nn.sigmoid(h2)).astype(bf16)
    taps(pad, upper, lower, x9)
    loads.wait(2)
    line2 = conv(w2, own2, out2, recv2, s2, r2)
    x9t_2[...] = x9[...].T
    stores.start(x9t_2, x9t_2_hbm)
    turn(w2, turn2)
    stores.start(turn2, turn2_hbm)
    line1.drain()
    line2.finish()
    x1 = x.astype(f32) + (own2[...].reshape(rows, cols, width) + vector(5))
    x1_ref[...] = x1
    stores.start(x1_ref, x1_hbm)
    centers, scales = stats(2, x1)
    a3 = (x1 - to_rows(centers, inner)) * to_rows(scales, inner) * vector(6) + vector(7)
    a3_ref[z] = a3.astype(bf16).reshape(tokens, width)

    size, per = tokens // PIECES, PIECES // SEGMENTS
    line = LineGather(lambda shard, piece: a3_ref.at[shard, pl.ds(piece * size, size)], PIECES, a3_s, a3_r)
    window = all_ref.shape[0]
    own = window // 2 if window < row_count else r
    gather = (PlaneGather if fast else WindowGather)(all_ref, kv_s, kv_r)
    loads.wait(3, 4)
    weights = [
        jnp.concatenate([w_att[t, pl.ds(i * width, width), :] for t in range(3)], axis=1) for i in range(chan_count)
    ]

    def run(step, segment):
        line.run(step, range(segment * per, (segment + 1) * per))

    def project(segment):
        at = pl.ds(segment * size * per, size * per)
        qkv = None
        for i in range(chan_count):
            term = jnp.dot(a3_ref[i, at], weights[i], preferred_element_type=f32)
            qkv = term if qkv is None else qkv + term
        all_ref[own, at, :width] = qkv[:, width : 2 * width].astype(bf16)
        all_ref[own, at, width:] = (qkv[:, 2 * width :] + vec[9][1:2, :]).astype(bf16)
        gather.start(segment)
        q_ref[at, :] = (qkv[:, :width] + vec[9][0:1, :]).astype(bf16)

    for step, segment in ((0, 0), (0, 1), (1, 0), (0, 2), (2, 0), (1, 1), (0, 3), (3, 0)):
        run(step, segment)
    project(0)
    for step, segment in ((2, 1), (1, 2), (3, 1)):
        run(step, segment)
    project(1)
    gather.relay(0)
    for step, segment in ((2, 2), (1, 3), (3, 2)):
        run(step, segment)
    project(2)
    gather.relay(1)
    gather.last(0)
    for step, segment in ((2, 3), (3, 3)):
        run(step, segment)
    project(3)
    stores.start(a3_ref, a3_hbm)
    gather.relay(2)
    gather.last(1)
    for copy in g_copies:
        copy.wait_recv()
    stores.start(gall_ref, gall_hbm)
    gather.relay(3)
    do = None
    for i in range(chan_count):
        term = contract(gall_ref[i], wo[:, pl.ds(i * width, width)], 1, 1)
        do = term if do is None else do + term
    do_ref[...] = do.astype(bf16)
    gather.last(2)
    gather.last(3)
    for segment in range(SEGMENTS):
        at = pl.ds(segment * size * per, size * per)
        gather.done(segment)
        stores.start(all_ref.at[:, at], all_hbm.at[:, at])
    line2.drain()
    line.drain()
    gather.drain()
    for copy in g_copies:
        copy.wait_send()
    stores.wait()


def forward_block(row_count, chan_count, per_group, entries, window, fast, offset, x, vec, mod, w1, w2, w_att, g, wo):
    rows, cols, width = x.shape
    tokens = rows * cols
    images = row_count * rows // IMG_H
    message = -(-2 * images // 8) * 8
    vm = pl.BlockSpec(memory_space=pltpu.VMEM)
    hbm = pl.BlockSpec(memory_space=pl.ANY)
    S = jax.ShapeDtypeStruct
    sem = pltpu.SemaphoreType.DMA
    peers = chan_count - 1
    full = chan_count * width
    saved = [
        ((9 * width, tokens), bf16), ((9 * width, tokens), bf16),
        ((chan_count, 3 * width, 3 * width), bf16), ((chan_count, 3 * width, 3 * width), bf16),
        ((rows, cols, width), f32), ((rows, cols, width), f32), ((chan_count, tokens, width), bf16),
        ((window, tokens, 2 * width), bf16), ((chan_count, tokens, width), bf16),
    ]
    small = [((6, rows, 1, width), f32), ((tokens, width), bf16), ((tokens, width), bf16)]
    return pl.pallas_call(
        functools.partial(forward_kernel, row_count, chan_count, per_group, entries, fast),
        name="forward_block",
        out_shape=tuple(S(*item) for item in saved + small),
        in_specs=[pl.BlockSpec(memory_space=pltpu.SMEM)] + [vm] * (2 + VECTORS) + [hbm] * 5,
        out_specs=(hbm,) * len(saved) + (vm,) * len(small),
        scratch_shapes=[
            vmem((9 * width, full), bf16), vmem((9 * width, full), bf16), vmem((3, full, width), bf16), vmem((width, full), bf16),
            *[vmem(*item) for i, item in enumerate(saved) if i != 4],
            vmem((rows + 2, cols, width), bf16),
            vmem((rows + 2, cols, width), f32),
            vmem((rows + 2, cols, width), bf16),
            vmem((tokens, 9 * width), bf16),
            *scatter_scratch(tokens, width, 2),
            *scatter_scratch(tokens, width, 2),
            vmem((3, row_count, message, width), f32),
            sem((3, row_count - 1)), sem((3, row_count - 1)),
            sem((2, 2)), sem((2, 2)),
            sem((2, peers, PIECES)), sem((2, peers, PIECES)),
            sem((3, peers)), sem((3, peers)),
            sem((SEGMENTS, max(13, row_count))), sem((SEGMENTS, max(13, row_count))),
            sem((5,)), sem((8 + SEGMENTS,)),
        ],
        cost_estimate=pl.CostEstimate(flops=8 * 9 * tokens * width * full, bytes_accessed=16 * 2**20, transcendentals=4 * tokens * width),
        compiler_params=pltpu.CompilerParams(collective_id=0, has_side_effects=True, vmem_limit_bytes=60 * 2**20),
    )(offset, x, *vec, mod, w1, w2, w_att, g, wo)


class Total:
    def __init__(self, part, out, half, quarters, sends, recvs):
        self.part, self.half, self.quarters, self.out = part, half, quarters, out
        self.sends, self.recvs = sends, recvs
        self.r, self.z = lax.axis_index("rows"), lax.axis_index("chan")
        self.core, self.x, self.y, self.d = plane()
        self.n = part.shape[0] // 8
        self.copies = []

    def rows(self, device):
        return pl.ds(pl.multiple_of((lax.rem(device, 2) * 4 + device // 2) * self.n, 16), self.n)

    def half_rows(self, device):
        return pl.ds(pl.multiple_of(lax.rem(device, 2) * 4 * self.n, 16), 4 * self.n)

    def send(self, i, src, dst, device):
        copy = push(src, dst, self.sends.at[i], self.recvs.at[i], (device, self.z))
        self.copies.append(copy)
        return copy

    def one(self):
        self.a = self.send(0, self.part.at[self.half_rows(self.core)], self.half, self.core)

    def two(self):
        self.a.wait_recv()
        mine = self.half_rows(self.r)
        self.half[...] = (self.part[mine, :].astype(f32) + self.half[...].astype(f32)).astype(bf16)
        self.b = []
        for i, device in enumerate((self.d, self.x, self.y)):
            at = pl.ds(pl.multiple_of((device // 2) * self.n, 16), self.n)
            self.b.append(self.send(1 + i, self.half.at[at], self.quarters.at[i], device))

    def three(self):
        at = pl.ds(pl.multiple_of((self.r // 2) * self.n, 16), self.n)
        total = self.half[at, :].astype(f32)
        for i, copy in enumerate(self.b):
            copy.wait_recv()
            total = total + self.quarters[i].astype(f32)
        mine = self.rows(self.r)
        self.out[mine, :] = total.astype(bf16)
        self.c = []
        for i, device in enumerate((self.d, self.x, self.y, self.core)):
            self.c.append(self.send(4 + i, self.out.at[mine], self.out.at[mine], device))

    def four(self):
        self.e = [self.c[3]]
        for i, device in ((1, self.x), (2, self.y), (0, self.d)):
            self.c[i].wait_recv()
            at = self.rows(device)
            self.e.append(self.send(8 + i, self.out.at[at], self.out.at[at], self.core))

    def finish(self):
        for copy in self.e:
            copy.wait_recv()
        for copy in self.copies:
            copy.wait_send()


def total_scratch(n, width):
    return [vmem((n // 2, width), bf16), vmem((3, n // 8, width), bf16), pltpu.SemaphoreType.DMA((11,)), pltpu.SemaphoreType.DMA((11,))]


class Return:
    def __init__(self, away, parts, cores, out, recv, relay, sends, recvs):
        self.away, self.parts, self.cores, self.out, self.recv, self.relay = away, parts, cores, out, recv, relay
        self.sends, self.recvs = sends, recvs
        self.r, self.z = lax.axis_index("rows"), lax.axis_index("chan")
        self.core, self.x, self.y, self.d = plane()
        self.size = parts.shape[1] // SEGMENTS
        self.copies = [{} for _ in range(SEGMENTS)]

    def at(self, s, which=None):
        half = self.size // 2
        if which is None:
            return pl.ds(s * self.size, self.size)
        return pl.ds(s * self.size + which * half, half)

    def send(self, s, i, src, dst, device):
        self.copies[s][i] = push(src, dst, self.sends.at[s, i], self.recvs.at[s, i], (device, self.z))

    def start(self):
        for s in range(SEGMENTS):
            at = self.at(s)
            for i, device in enumerate((self.d, self.x, self.y, self.r)):
                self.send(s, i, self.away.at[device + self.core - self.r, at], self.cores.at[i, at], self.core)

    def chip(self, i, at):
        return self.parts[i, at].astype(f32) + self.cores[i, at].astype(f32)

    def one(self, s):
        first, second, out, recv = self.at(s, 0), self.at(s, 1), self.out, self.recv
        self.copies[s][0].wait_recv()
        out[0, first] = self.chip(0, first).astype(bf16)
        self.send(s, 4, out.at[0, first], self.relay.at[0, s], self.x)
        out[0, second] = self.chip(0, second).astype(bf16)
        self.send(s, 5, out.at[0, second], self.relay.at[1, s], self.y)
        self.copies[s][1].wait_recv()
        out[1, first] = self.chip(1, first).astype(bf16)
        self.send(s, 6, out.at[1, first], recv.at[0, first], self.x)
        self.copies[s][2].wait_recv()
        out[2, second] = self.chip(2, second).astype(bf16)
        self.send(s, 7, out.at[2, second], recv.at[1, second], self.y)

    def two(self, s):
        first, second, out, recv = self.at(s, 0), self.at(s, 1), self.out, self.recv
        self.copies[s][4].wait_recv()
        out[2, first] = (self.chip(2, first) + self.relay[0, s].astype(f32)).astype(bf16)
        self.send(s, 8, out.at[2, first], recv.at[1, first], self.y)
        self.copies[s][5].wait_recv()
        out[1, second] = (self.chip(1, second) + self.relay[1, s].astype(f32)).astype(bf16)
        self.send(s, 9, out.at[1, second], recv.at[0, second], self.x)

    def three(self, s):
        at = self.at(s)
        for i in (3, 6, 7, 8, 9):
            self.copies[s][i].wait_recv()
        return self.chip(3, at) + self.recv[0, at].astype(f32) + self.recv[1, at].astype(f32)

    def drain(self):
        for copies in self.copies:
            for copy in copies.values():
                copy.wait_send()


def return_scratch(tokens, width):
    shape = (tokens, width)
    sem = pltpu.SemaphoreType.DMA((SEGMENTS, 10))
    return [
        vmem((4, *shape), bf16), vmem((4, *shape), bf16), vmem((3, *shape), bf16), vmem((2, *shape), bf16),
        vmem((2, SEGMENTS, tokens // (2 * SEGMENTS), width), bf16), sem, sem,
    ]


class ConvBack:
    def __init__(self, pad, acc, x9t, turned, parts, outs, totals, up, down, halo_s, halo_r, sends, recvs, upper, lower):
        self.pad, self.acc, self.x9t, self.turned, self.parts, self.outs = pad, acc, x9t, turned, parts, outs
        self.totals, self.up, self.down, self.halo_s, self.halo_r = totals, up, down, halo_s, halo_r
        self.upper, self.lower = upper, lower
        _, self.rows, self.cols, self.width = pad.shape
        self.rows -= 2
        self.tokens = self.rows * self.cols
        self.size = self.rows // PIECES
        self.line = LineGather(self.at, PIECES + 2, sends, recvs)
        z = lax.axis_index("chan")
        low = z < 2
        self.order = (z, z + 1 - 2 * lax.rem(z, 2), jnp.where(low, 2, 1), jnp.where(low, 3, 0))
        self.later = []

    def at(self, shard, piece):
        if piece < PIECES:
            return self.pad.at[shard, pl.ds(1 + piece * self.size, self.size)]
        return self.pad.at[shard, pl.ds(0 if piece == PIECES else self.rows + 1, 1)]

    def start(self, values):
        pad, rows, z = self.pad, self.rows, lax.axis_index("chan")
        pad[z, pl.ds(1, rows)] = values
        self.rims = [
            push(pad.at[z, 1], pad.at[z, rows + 1], self.halo_s.at[0], self.halo_r.at[0], self.up),
            push(pad.at[z, rows], pad.at[z, 0], self.halo_s.at[1], self.halo_r.at[1], self.down),
        ]
        self.line.run(0, range(PIECES))
        for copy in self.rims:
            copy.wait_recv()
        self.line.run(0, (PIECES, PIECES + 1))

    def block(self, step):
        j, rows, tokens, width = self.order[step], self.rows, self.tokens, self.width
        parts = []
        for a, mask in enumerate((self.lower, None, self.upper)):
            part = self.pad[j, pl.ds(2 - a, rows)]
            if mask is not None:
                part = (part.astype(f32) * mask).astype(bf16)
            parts.append(part.reshape(tokens, width))
        self.parts[step] = jnp.dot(self.x9t[...], parts[1], preferred_element_type=f32).astype(bf16)
        if self.totals:
            self.totals[step].one()
        else:
            self.outs[j] = self.parts[step]
        term = jnp.dot(jnp.concatenate(parts, axis=1), self.turned[j], preferred_element_type=f32)
        self.acc[...] = term if step == 0 else self.acc[...] + term

    def run(self, step):
        self.line.run(step)
        self.block(step)

    def input_grad(self):
        total, width, cols, tokens = self.acc[...], self.width, self.cols, self.tokens
        col = lax.rem(lax.broadcasted_iota(jnp.int32, (tokens, 1), 0), cols)
        before = jnp.where(col == cols - 1, 0.0, pltpu.roll(total[:, :width], tokens - 1, 0))
        after = jnp.where(col == 0, 0.0, pltpu.roll(total[:, 2 * width :], 1, 0))
        return (before + total[:, width : 2 * width] + after).reshape(self.rows, cols, width)

    def drain(self):
        for copy in self.rims:
            copy.wait_send()
        self.line.drain()


def silu_slope(values):
    gate = jax.nn.sigmoid(values)
    return gate * (1.0 + values * (1.0 - gate))


def channel_total(values):
    return jnp.sum(jnp.sum(values, axis=1, keepdims=True), axis=0)


def backward_kernel(row_count, chan_count, per_group, entries, fast, offset, *refs):
    vec, refs = refs[:VECTORS], refs[VECTORS:]
    (rows_in, mod, w_att, wo, dctx,
     dq_hbm, dkv_hbm, o_hbm, gall_hbm, a3_hbm, x1_hbm, c1_hbm, x_hbm, x9t_1_hbm, x9t_2_hbm, turn1_hbm, turn2_hbm,
     result, dfeat, sums, g_conv1, g_conv2, g_att, g_out, g_ctx,
     dq_ref, o_ref, gall, a3_all, x1_ref, c1_ref, x_ref, x9t_1, x9t_2, turn1, turn2, load_s,
     part1, part2, part_att, part_out, d3, dx1_ref, acc, gpad, halo_s, halo_r, zh_s, zh_r, stat, stat_s, stat_r,
     res_out, res_recv, res_s, res_r, own, da3_out, da3_recv, da3_s, da3_r) = refs[:61]
    refs = refs[61:]
    rows, cols, width = x_ref.shape
    tokens = rows * cols
    r, z = lax.axis_index("rows"), lax.axis_index("chan")
    loads = Locals(load_s)
    greet(row_peers(row_count) + chan_peers(chan_count))
    if fast:
        back = Return(dkv_hbm, *refs[:7])
        back.start()
        for i, device in enumerate((back.d, back.x, back.y, r)):
            loads.start(dkv_hbm.at[device], back.parts.at[i])
        pairs = iter(range(7, len(refs), 4))

        def total(part, out):
            i = next(pairs)
            return Total(part, out, *refs[i : i + 4])
        small = [total(part_att, g_att), total(part_out, g_out), total(dctx, g_ctx)]
    else:
        for i in range(4):
            loads.start(dkv_hbm.at[pl.ds(i * (tokens // 4), tokens // 4)], refs[0].at[pl.ds(i * (tokens // 4), tokens // 4)])
        small = []
    for src, dst in (
        (dq_hbm, dq_ref), (o_hbm, o_ref), (gall_hbm, gall), (a3_hbm, a3_all), (x1_hbm, x1_ref), (c1_hbm, c1_ref), (x_hbm, x_ref),
        (x9t_2_hbm, x9t_2), (turn2_hbm, turn2), (x9t_1_hbm, x9t_1), (turn1_hbm, turn1),
    ):
        loads.start(src, dst)
    member, upper, lower = image_masks(offset[0], r * rows, rows, width, row_count * rows)
    images = len(member)
    up = (lax.rem(r + row_count - 1, row_count), z)
    down = (lax.rem(r + 1, row_count), z)
    orders = []
    for index, (x9t, turned, parts, outs) in enumerate(((x9t_2, turn2, part2, g_conv2), (x9t_1, turn1, part1, g_conv1))):
        conv = ConvBack(
            gpad.at[index], acc, x9t, turned, parts, outs, [], up, down, halo_s.at[index], halo_r.at[index],
            zh_s.at[index], zh_r.at[index], upper, lower,
        )
        if fast:
            conv.totals = [total(parts.at[step], outs.at[conv.order[step]]) for step in range(chan_count)]
        orders.append(conv)
    conv2, conv1 = orders
    third = -(-tokens // 48) * 16
    res_copies = []

    def vector(i):
        return vec[i][...][None]

    def exchange(phase, pieces):
        copies = share(stat.at[phase], stat_s.at[phase], stat_r.at[phase], row_count, pieces)
        part = pl.ds(phase * third, min(third, tokens - phase * third))
        for d, device in enumerate(chan_peers(chan_count)):
            res_copies.append(push(res_out.at[d, part], res_recv.at[d, part], res_s.at[phase, d], res_r.at[phase, d], device))
        return copies

    def norm_pieces(dxh, xhat):
        pieces = []
        for a, b in zip(image_sums(dxh, member), image_sums(dxh * xhat, member)):
            pieces += [a, b]
        return pieces

    def norm_back(total, dxh, xhat, scale):
        grouped = group_sum(total[: 2 * images], per_group) * (1.0 / entries)
        first = to_rows([grouped[2 * i : 2 * i + 1] for i in range(images)], member)
        second = to_rows([grouped[2 * i + 1 : 2 * i + 2] for i in range(images)], member)
        return scale * (dxh - first - xhat * second)

    def out_term(j):
        return jnp.dot(o_ref[...], wo[:, pl.ds(pl.multiple_of(j * width, width), width)], preferred_element_type=f32)

    def att_rows(j):
        at = pl.ds(pl.multiple_of(j * width, width), width)
        return jnp.concatenate([w_att[t, at, :] for t in range(3)], axis=1)

    line = LineScatter(lambda j, at: contract(d3[at, :], att_rows(j), 1, 1), own, da3_out, da3_recv, da3_s, da3_r)
    size = tokens // SEGMENTS
    bias_v = jnp.zeros((1, width), f32)
    loads.wait(4)
    if fast:
        loads.wait(0, 1, 2, 3)
        for s in range(SEGMENTS + 2):
            if s < SEGMENTS:
                back.one(s)
            if s == 0:
                loads.wait(5, 6)
                for d, device in enumerate(chan_peers(chan_count)):
                    res_out[d] = out_term(device[1]).astype(bf16)
            if 1 <= s <= SEGMENTS:
                back.two(s - 1)
            if s >= 2:
                at = pl.ds((s - 2) * size, size)
                dkv = back.three(s - 2)
                d3[at, :width] = dq_ref[at, :].astype(bf16)
                d3[at, width:] = dkv.astype(bf16)
                bias_v = bias_v + jnp.sum(dkv[:, width:], axis=0, keepdims=True)
                line.send(s - 2)
            if s >= 3:
                line.merge(s - 3)
        line.merge(SEGMENTS - 1)
    else:
        loads.wait(0, 1, 2, 3, 5, 6)
        for d, device in enumerate(chan_peers(chan_count)):
            res_out[d] = out_term(device[1]).astype(bf16)
        for s in range(SEGMENTS + 1):
            if s < SEGMENTS:
                at = pl.ds(s * size, size)
                dkv = refs[0][at, :]
                d3[at, :width] = dq_ref[at, :].astype(bf16)
                d3[at, width:] = dkv.astype(bf16)
                bias_v = bias_v + jnp.sum(dkv[:, width:], axis=0, keepdims=True)
                line.send(s)
            if s >= 1:
                line.merge(s - 1)
    line.keep()
    bias_q = jnp.sum(dq_ref[...], axis=0, keepdims=True)
    loads.wait(7)
    for i in range(chan_count):
        grad = contract(a3_all[i], d3[...], 0, 0).astype(bf16)
        for t in range(3):
            part_att[pl.ds((t * chan_count + i) * width, width), :] = grad[:, t * width : (t + 1) * width]
    g_cat = jnp.concatenate([gall[i] for i in range(chan_count)], axis=1)
    part_out[...] = contract(o_ref[...], g_cat, 0, 0).astype(bf16)
    for t in small:
        t.one()
    loads.wait(8)
    x1 = x1_ref[...]
    g = gall[z].astype(f32).reshape(rows, cols, width)
    center, scale = rows_in[4], rows_in[5]
    xhat = (x1 - center) * scale
    bias_g = channel_total(g)
    for t in small:
        t.two()
    line.finish()
    da3 = own[...].reshape(rows, cols, width)
    dxh = da3 * vector(6)
    copies = exchange(
        0, norm_pieces(dxh, xhat) + [channel_total(da3 * xhat), channel_total(da3), bias_q, bias_v, bias_g]
    )
    for t in small:
        t.three()
    total = share_total(stat.at[0], copies)
    sums[0:5, :] = total[2 * images : 2 * images + 5]
    dx1 = g + norm_back(total, dxh, xhat, scale)
    conv2.start(dx1.astype(bf16))
    dx1_ref[...] = dx1
    bias_2 = channel_total(dx1)
    loads.wait(9, 11, 12)
    conv2.block(0)
    for t in small:
        t.four()
    center, scale = rows_in[2], rows_in[3]
    xhat = (c1_ref[...] - center) * scale
    n2 = xhat * vector(3) + vector(4)
    mod_scale = 1.0 + to_rows([mod[i, 0:1, :] for i in range(images)], member)
    mod_shift = to_rows([mod[i, 1:2, :] for i in range(images)], member)
    slope = silu_slope(n2 * mod_scale + mod_shift)
    conv2.run(1)
    for t in conv2.totals[0:1]:
        t.two()
    conv2.run(2)
    for t in conv2.totals[1:2]:
        t.two()
    for t in conv2.totals[0:1]:
        t.three()
    conv2.run(3)
    dh2 = conv2.input_grad() * slope
    dn2 = dh2 * mod_scale
    dxh = dn2 * vector(3)
    dss = []
    for a, b in zip(image_sums(dh2 * n2, member), image_sums(dh2, member)):
        dss += [a, b]
    copies = exchange(1, norm_pieces(dxh, xhat) + [channel_total(dn2 * xhat), channel_total(dn2), bias_2] + dss)
    for t in conv2.totals[2:3]:
        t.two()
    for t in small:
        t.finish()
    total = share_total(stat.at[1], copies)
    sums[5 : 8 + 2 * images, :] = total[2 * images : 4 * images + 3]
    dc1 = norm_back(total, dxh, xhat, scale)
    conv1.start(dc1.astype(bf16))
    bias_1 = channel_total(dc1)
    loads.wait(10, 13, 14)
    conv1.block(0)
    for t in conv2.totals[3:4]:
        t.two()
    for t in conv2.totals[1:3]:
        t.three()
    for t in conv2.totals[0:1]:
        t.four()
    center, scale = rows_in[0], rows_in[1]
    xhat = (x_ref[...].astype(f32) - center) * scale
    slope = silu_slope(xhat * vector(0) + vector(1))
    conv1.run(1)
    for t in conv1.totals[0:1]:
        t.two()
    for t in conv2.totals[3:4]:
        t.three()
    for t in conv2.totals[1:3]:
        t.four()
    conv1.run(2)
    for t in conv1.totals[1:2]:
        t.two()
    for t in conv1.totals[0:1]:
        t.three()
    for t in conv2.totals[3:4]:
        t.four()
    conv1.run(3)
    for t in conv1.totals[2:3]:
        t.two()
    for t in conv1.totals[1:2]:
        t.three()
    dn1 = conv1.input_grad() * slope
    for t in conv1.totals[3:4]:
        t.two()
    dxh = dn1 * vector(0)
    copies = exchange(2, norm_pieces(dxh, xhat) + [channel_total(dn1 * xhat), channel_total(dn1), bias_1])
    for t in conv1.totals[0:1]:
        t.four()
    for t in conv1.totals[2:4]:
        t.three()
    for t in conv1.totals[1:2]:
        t.four()
    own[...] = out_term(z)
    total = share_total(stat.at[2], copies)
    sums[8 + 2 * images : 11 + 2 * images, :] = total[2 * images : 2 * images + 3]
    dfeat[...] = (dx1_ref[...] + norm_back(total, dxh, xhat, scale)).astype(bf16)
    for t in conv1.totals[2:4]:
        t.four()
    for copy in res_copies:
        copy.wait()
    value = own[...]
    for d in range(chan_count - 1):
        value = value + res_recv[d].astype(f32)
    result[...] = (x1_ref[...] + value.reshape(rows, cols, width) + vector(8)).astype(bf16)
    for t in conv2.totals + conv1.totals:
        t.finish()
    if fast:
        back.drain()
    else:
        g_att[...] = part_att[...]
        g_out[...] = part_out[...]
        g_ctx[...] = dctx[...]
    line.drain()
    conv2.drain()
    conv1.drain()


def backward_block(row_count, chan_count, per_group, entries, fast, offset, x, vec, dq, dkv, o, gall, a3_all, x1, c1, rows_in,
                   mod, x9t_1, x9t_2, turn1, turn2, w_att, wo, dctx):
    rows, cols, width = x.shape
    tokens = rows * cols
    images = row_count * rows // IMG_H
    full = chan_count * width
    message = -(-(4 * images + 5) // 8) * 8
    vm = pl.BlockSpec(memory_space=pltpu.VMEM)
    hbm = pl.BlockSpec(memory_space=pl.ANY)
    S = jax.ShapeDtypeStruct
    sem = pltpu.SemaphoreType.DMA
    peers = chan_count - 1
    total_rows = -(-(11 + 2 * images) // 8) * 8
    early = [rows_in, mod, w_att, wo, dctx]
    late = [dq, dkv, o, gall, a3_all, x1, c1, x, x9t_1, x9t_2, turn1, turn2]
    kernel_grad = S((chan_count, 9 * width, width), bf16)
    if fast:
        plane_scratch = [
            *return_scratch(tokens, 2 * width), *total_scratch(3 * full, width), *total_scratch(width, full),
            *total_scratch(*dctx.shape),
        ]
        for _ in range(2 * chan_count):
            plane_scratch += total_scratch(9 * width, width)
    else:
        plane_scratch = [vmem(dkv.shape, dkv.dtype)]
    return pl.pallas_call(
        functools.partial(backward_kernel, row_count, chan_count, per_group, entries, fast),
        name="backward_block",
        out_shape=(
            S((rows, cols, width), bf16), S((rows, cols, width), bf16), S((total_rows, width), f32),
            kernel_grad, kernel_grad, S((3 * full, width), bf16), S((width, full), bf16), S(dctx.shape, bf16),
        ),
        in_specs=[pl.BlockSpec(memory_space=pltpu.SMEM)] + [vm] * (VECTORS + len(early)) + [hbm] * len(late),
        out_specs=(vm,) * 8,
        scratch_shapes=[
            *[vmem(item.shape, item.dtype) for item in late if item is not dkv], sem((15,)),
            vmem(kernel_grad.shape, bf16), vmem(kernel_grad.shape, bf16), vmem((3 * full, width), bf16), vmem((width, full), bf16),
            vmem((tokens, 3 * width), bf16), vmem((rows, cols, width), f32), vmem((tokens, 3 * width), f32),
            vmem((2, chan_count, rows + 2, cols, width), bf16), sem((2, 2)), sem((2, 2)),
            sem((2, 2, peers, PIECES + 2)), sem((2, 2, peers, PIECES + 2)),
            vmem((3, row_count, message, width), f32), sem((3, row_count - 1)), sem((3, row_count - 1)),
            vmem((peers, tokens, width), bf16), vmem((peers, tokens, width), bf16), sem((3, peers)), sem((3, peers)),
            *scatter_scratch(tokens, width, SEGMENTS),
            *plane_scratch,
        ],
        cost_estimate=pl.CostEstimate(flops=12 * 9 * tokens * width * full, bytes_accessed=24 * 2**20, transcendentals=4 * tokens * width),
        compiler_params=pltpu.CompilerParams(collective_id=1, has_side_effects=True, vmem_limit_bytes=60 * 2**20),
    )(offset, *vec, *early, *late)


def finish_kernel(images, share_rows, ctx_count, result_in, dfeat_in, sums, g_conv1, g_conv2, g_att, g_out, g_ctx, emb, context,
                  result, dfeat, conv1, conv2, att, out, emb_w, ctx_w, emb_b, att_b, ctx_b, *vectors):
    width = sums.shape[1]
    result[...] = result_in[...]
    dfeat[...] = dfeat_in[...]
    for j in range(g_conv1.shape[0]):
        conv1[:, pl.ds(j * width, width)] = g_conv1[j].astype(f32)
        conv2[:, pl.ds(j * width, width)] = g_conv2[j].astype(f32)
    out[...] = g_out[...].astype(f32)
    att[...] = g_att[...].astype(f32)
    block = emb.shape[1]
    for t in range(2):
        rows = jnp.concatenate([sums[8 + 2 * i + t : 9 + 2 * i + t, :] for i in range(images)], axis=0)
        emb_w[pl.ds(t, block, 2), :] = lax.dot_general(
            emb[...].astype(f32), rows, (((0,), (0,)), ((), ())), precision=HIGH, preferred_element_type=f32
        )
    total = None
    for i in range(images):
        term = contract(context[i], g_ctx[pl.ds(i * share_rows, ctx_count), :], 0, 0)
        total = term if total is None else total + term
    for t in range(2):
        ctx_w[pl.ds(t, block, 2), :] = total[:, t * width : (t + 1) * width]

    @pl.when(pl.program_id(0) == 0)
    def _():
        for t in range(2):
            emb_b[t : t + 1, :] = sum(sums[8 + 2 * i + t : 9 + 2 * i + t, :] for i in range(images))
            att_b[t : t + 1, :] = sums[2 + t : 3 + t, :]
            ctx_b[t : t + 1, :] = jnp.sum(g_ctx[:, pl.ds(t * width, width)].astype(f32), axis=0, keepdims=True)
        for ref, i in zip(vectors, (0, 1, 4, 5, 6, 7, 8 + 2 * images, 9 + 2 * images, 10 + 2 * images)):
            ref[...] = sums[i : i + 1, :]


def finish_block(images, share_rows, steps, result, dfeat, sums, g_conv1, g_conv2, g_att, g_out, g_ctx, emb, context):
    width = sums.shape[1]
    depth = emb.shape[1]
    ctx_count = context.shape[1]
    S = jax.ShapeDtypeStruct

    def lead(shape):
        rest = (0,) * (len(shape) - 1)
        return pl.BlockSpec((shape[0] // steps,) + tuple(shape[1:]), lambda s: (s,) + rest)

    def whole(shape):
        return pl.BlockSpec(tuple(shape), lambda s: (0,) * len(shape))

    chan_count, taps_n, _ = g_conv1.shape
    full = chan_count * width
    conv_spec = pl.BlockSpec((chan_count, taps_n // steps, width), lambda s: (0, s, 0))
    shapes = [
        (result.shape, bf16, lead), (dfeat.shape, bf16, lead), ((taps_n, full), f32, lead), ((taps_n, full), f32, lead),
        ((3 * full, width), f32, lead), ((width, full), f32, lead), ((2 * depth, width), f32, lead),
        ((2 * depth, width), f32, lead), ((2, width), f32, whole), ((2, width), f32, whole), ((2, width), f32, whole),
    ] + [((1, width), f32, whole)] * 9
    return pl.pallas_call(
        functools.partial(finish_kernel, images, share_rows, ctx_count),
        name="finish_block",
        grid=(steps,),
        out_shape=tuple(S(shape, dtype) for shape, dtype, _ in shapes),
        in_specs=[
            lead(result.shape), lead(dfeat.shape), whole(sums.shape), conv_spec, conv_spec, lead(g_att.shape),
            lead(g_out.shape), whole(g_ctx.shape), pl.BlockSpec((images, depth // steps), lambda s: (0, s)),
            pl.BlockSpec((images, ctx_count, depth // steps), lambda s: (0, 0, s)),
        ],
        out_specs=tuple(spec(shape) for shape, _, spec in shapes),
        cost_estimate=pl.CostEstimate(flops=4 * images * ctx_count * depth * width, bytes_accessed=16 * 2**20, transcendentals=0),
        compiler_params=pltpu.CompilerParams(vmem_limit_bytes=60 * 2**20),
    )(result, dfeat, sums, g_conv1, g_conv2, g_att, g_out, g_ctx, emb, context)


def local(
    features,
    embedding,
    context,
    image_offset,
    first_gain,
    first_shift,
    conv_first,
    conv_first_bias,
    embed_weight,
    embed_bias,
    second_gain,
    second_shift,
    conv_second,
    conv_second_bias,
    attend_gain,
    attend_shift,
    attend_weight,
    attend_bias,
    context_weight,
    context_bias,
    output_weight,
    output_bias,
    cotangent,
):
    slab_rows, columns, channels = features.shape
    devices, chan = lax.axis_size("rows"), lax.axis_size("chan")
    total_rows = slab_rows * devices
    images = total_rows // IMG_H
    per_group = C // GROUPS
    entries = IMG_H * columns * per_group
    tokens = slab_rows * columns
    modulate = (
        jnp.einsum("ie,eto->ito", embedding, embed_weight, preferred_element_type=jnp.float32)
        + embed_bias
    )
    context_count = context.shape[1]
    tail = -(-context_count // 256) * 256
    context_proj = (
        jnp.einsum("snc,cto->snto", context, context_weight, preferred_element_type=jnp.float32)
        + context_bias
    )
    context_rows = jnp.pad(
        context_proj.reshape(images, context_count, 2 * channels).astype(bf16), ((0, 0), (0, tail - context_count), (0, 0))
    )
    vectors = [
        vector.reshape(1, channels)
        for vector in (first_gain, first_shift, conv_first_bias, second_gain, second_shift, conv_second_bias, attend_gain,
                       attend_shift, output_bias)
    ] + [attend_bias]
    window = min(devices, 2 * (IMG_H // slab_rows) + 1)
    kernel_one = conv_first.reshape(9 * channels, C)
    kernel_two = conv_second.reshape(9 * channels, C)
    attend_kernels = attend_weight.transpose(1, 0, 2)
    fast = devices == 8 and window == devices
    (x9t_one, x9t_two, turn_one, turn_two, middle, inner, attend_blocks, kv_all, grad_blocks, row_stats, queries,
     grad_attended) = forward_block(
        devices, chan, per_group, entries, window, fast, image_offset, features, vectors, modulate, kernel_one, kernel_two,
        attend_kernels, cotangent.reshape(tokens, channels), output_weight,
    )
    share_rows = -(-context_count // 64) * 64
    attended, query_grad, window_grad, context_part = attend(
        devices, slab_rows, image_offset, queries, grad_attended, kv_all.reshape(window * slab_rows, columns, 2 * channels),
        context_rows, total_rows, IMG_H, context_count, images, share_rows,
    )
    key_value_grad = window_grad.reshape(window, tokens, 2 * channels)
    if not fast:
        pieces, key_value_grad = key_value_grad, jnp.zeros((tokens, 2 * channels), f32)
        for position in range(window):
            shift_by = position - window // 2 if window < devices else None
            piece = pieces[position]
            if shift_by is None:
                piece = jnp.sum(lax.all_to_all(pieces, "rows", 0, 0).astype(f32), axis=0) if position == 0 else 0.0
            elif shift_by != 0:
                piece = from_behind(piece, "rows", shift_by)
            key_value_grad = key_value_grad + (piece if shift_by is None else piece.astype(f32))
    result, features_grad, sums, conv_first_grad, conv_second_grad, attend_grad, output_weight_grad, context_sum = backward_block(
        devices, chan, per_group, entries, fast, image_offset, features, vectors, query_grad, key_value_grad, attended,
        grad_blocks, attend_blocks, inner, middle, row_stats, modulate, x9t_one, x9t_two, turn_one, turn_two, attend_kernels,
        output_weight, context_part,
    )
    if not fast:
        conv_first_grad, conv_second_grad, attend_grad, output_weight_grad, context_sum = lax.psum(
            (conv_first_grad, conv_second_grad, attend_grad, output_weight_grad, context_sum), "rows"
        )
    (result, features_grad, conv_first_grad, conv_second_grad, attend_grad, output_weight_grad, embed_weight_grad,
     context_weight_grad, embed_bias_grad, attend_bias_grad, context_bias_grad, *rest) = finish_block(
        images, share_rows, 8, result, features_grad, sums, conv_first_grad, conv_second_grad, attend_grad,
        output_weight_grad, context_sum, embedding, context,
    )
    (attend_gain_grad, attend_shift_grad, output_bias_grad, second_gain_grad, second_shift_grad, conv_second_bias_grad,
     first_gain_grad, first_shift_grad, conv_first_bias_grad) = [vector.reshape(channels) for vector in rest]
    return (
        result,
        features_grad,
        first_gain_grad,
        first_shift_grad,
        conv_first_grad.reshape(3, 3, channels, C),
        conv_first_bias_grad,
        embed_weight_grad.reshape(-1, 2, channels),
        embed_bias_grad,
        second_gain_grad,
        second_shift_grad,
        conv_second_grad.reshape(3, 3, channels, C),
        conv_second_bias_grad,
        attend_gain_grad,
        attend_shift_grad,
        attend_grad.reshape(3, C, channels).transpose(1, 0, 2),
        attend_bias_grad,
        context_weight_grad.reshape(-1, 2, channels),
        context_bias_grad,
        output_weight_grad,
        output_bias_grad,
    )


def solution(mesh):
    placed = (
        P("rows", None, "chan"),
        P(),
        P(),
        P(),
        P("chan"),
        P("chan"),
        P(None, None, "chan", None),
        P("chan"),
        P(None, None, "chan"),
        P(None, "chan"),
        P("chan"),
        P("chan"),
        P(None, None, "chan", None),
        P("chan"),
        P("chan"),
        P("chan"),
        P(None, None, "chan"),
        P(None, "chan"),
        P(None, None, "chan"),
        P(None, "chan"),
        P("chan", None),
        P("chan"),
        P("rows", None, "chan"),
    )
    return jax.shard_map(
        local,
        mesh=mesh,
        in_specs=placed,
        out_specs=(
            P("rows", None, "chan"),
            P("rows", None, "chan"),
            P("chan"),
            P("chan"),
            P(None, None, "chan", None),
            P("chan"),
            P(None, None, "chan"),
            P(None, "chan"),
            P("chan"),
            P("chan"),
            P(None, None, "chan", None),
            P("chan"),
            P("chan"),
            P("chan"),
            P(None, None, "chan"),
            P(None, "chan"),
            P(None, None, "chan"),
            P(None, "chan"),
            P("chan", None),
            P("chan"),
        ),
        check_vma=False,
    )
```

```python
import functools

import jax
import jax.numpy as jnp
from jax import lax
from jax.experimental import pallas as pl
from jax.experimental.pallas import tpu as pltpu
from jax.sharding import PartitionSpec as P

C = 512
HEAD_DIM = 64
GROUPS = 32
IMG_H = 64


EPSILON = 1e-05
HIGH = lax.Precision.HIGHEST
NEG = -1e30
bf16, f32 = jnp.bfloat16, jnp.float32


def from_behind(block, axis, distance):
    devices = range(lax.axis_size(axis))
    route = [((i - distance) % len(devices), i) for i in devices]
    return lax.ppermute(block, axis, route)


def dot(a, b, ca, cb):
    return lax.dot_general(a, b, (((ca,), (cb,)), ((), ())), preferred_element_type=f32)


def attend_kernel(tiles, tile_rows, cols, width, image_rows, total_rows, ctx_count, images, window, row_count,
                  offset, q_ref, do_ref, kv_ref, ctx_ref,
                  o_ref, dq_ref, dkv_ref, dctx_ref,
                  kv, kt, vt, qt, do_t, s_buf, p_buf, dk, dv, oacc, qacc, sem):
    slab_rows = tiles * tile_rows
    me = lax.axis_index("rows")
    base = (me - window // 2) * slab_rows if window < row_count else 0
    place = lax.rem(me * slab_rows - offset[0] + total_rows, total_rows)
    image_a = place // image_rows
    split = jnp.minimum(slab_rows, image_rows - lax.rem(place, image_rows))
    image_b = lax.rem(image_a + jnp.where(split < slab_rows, 1, 0), images)
    start_a = lax.rem(offset[0] + image_a * image_rows - base + 2 * total_rows, total_rows)
    start_b = lax.rem(offset[0] + image_b * image_rows - base + 2 * total_rows, total_rows)
    ids = (image_a, image_b)
    tq = tile_rows * cols
    main = image_rows * cols
    tail = kv.shape[1] * cols - main
    heads = width // HEAD_DIM
    straddle = split < slab_rows
    group = 8

    def load(img, start):
        @pl.loop(0, image_rows // group)
        def _(j):
            src = lax.rem(start + j * group, total_rows)
            whole = src + group <= total_rows

            @pl.when(whole)
            def _():
                pltpu.make_async_copy(
                    kv_ref.at[pl.ds(src, group)], kv.at[img, pl.ds(j * group, group)], sem.at[img]
                ).start()

            @pl.when(jnp.logical_not(whole))
            def _():
                @pl.loop(0, group)
                def _(i):
                    pltpu.make_async_copy(
                        kv_ref.at[lax.rem(src + i, total_rows)], kv.at[img, j * group + i], sem.at[img]
                    ).start()

    def finish(img, start):
        pltpu.make_async_copy(kv_ref.at[pl.ds(0, image_rows)], kv.at[img, pl.ds(0, image_rows)], sem.at[img]).wait()
        for i in range(tail // cols):
            kv[img, image_rows + i] = ctx_ref[ids[img], pl.ds(i * cols, cols)]
        step = 256 // cols

        @pl.loop(0, kv.shape[1] // step)
        def _(c):
            at = pl.ds(pl.multiple_of(c * 256, 256), 256)
            rows = kv[img, pl.ds(c * step, step)].reshape(256, 2 * width)
            kt[img, :, at] = rows[:, :width].T
            vt[img, :, at] = rows[:, width:].T
        dk[img] = jnp.zeros(dk.shape[1:], f32)
        dv[img] = jnp.zeros(dv.shape[1:], f32)

    load(0, start_a)

    @pl.when(straddle)
    def _():
        load(1, start_b)
    for t in range(tiles):
        qt[t] = (q_ref[pl.ds(t * tq, tq)] * jnp.asarray(HEAD_DIM ** -0.5, bf16)).T
        do_t[t] = do_ref[pl.ds(t * tq, tq)].T
    finish(0, start_a)

    @pl.when(straddle)
    def _():
        finish(1, start_b)

    mixed, cut = split // tile_rows, lax.rem(split, tile_rows)
    count_a = (split + 1) // tile_rows
    first_b = (split + 2) // tile_rows
    count = count_a + jnp.where(straddle, tiles - first_b, 0)
    half_a = jnp.logical_or(cut == 1, cut == 2)
    half_b = jnp.logical_or(cut == 2, cut == 3)
    halves = half_a.astype(jnp.int32) + half_b.astype(jnp.int32)
    first_half = jnp.where(half_a, 0, 1)
    feature = lax.broadcasted_iota(jnp.int32, (width, 1), 0) // HEAD_DIM
    lane_row = lax.broadcasted_iota(jnp.int32, (1, tq), 1) // cols
    tail_ok = lax.broadcasted_iota(jnp.int32, (tail, 1), 0) < ctx_count

    parts = (
        (pl.ds(0, image_rows), pl.ds(0, main), main, False), (pl.ds(image_rows, tail // cols), pl.ds(main, tail), tail, True)
    )

    @pl.loop(0, count)
    def _(item):
        is_b = (item >= count_a).astype(jnp.int32)
        t = jnp.where(is_b == 1, first_b + item - count_a, item)
        row = t * tile_rows + lane_row
        low = jnp.where(is_b == 1, split, 0)
        high = jnp.where(is_b == 1, slab_rows, split)
        mine = jnp.logical_and(row >= low, row < high)
        q_t = qt[t].astype(f32)
        g_t = do_t[t].astype(f32)
        q_h = [jnp.where(feature == h, q_t, 0.0).astype(bf16) for h in range(heads)]

        def rows_of(at, size, cut):
            return kv[is_b, at].reshape(size, 2 * width)[:, cut]

        m = [jnp.full((8, tq), NEG, f32) for _ in range(heads)]
        for blocks, at, size, masked in parts:
            keys = rows_of(blocks, size, slice(0, width))
            for h in range(heads):
                s = dot(keys, q_h[h], 1, 0)
                if masked:
                    s = jnp.where(tail_ok, s, NEG)
                s_buf[h, at] = s
                m[h] = jnp.maximum(m[h], jnp.max(s.reshape(size // 8, 8, tq), axis=0))
        m = [jnp.max(v, axis=0, keepdims=True) for v in m]
        l = [jnp.zeros((8, tq), f32) for _ in range(heads)]
        o = [jnp.zeros((HEAD_DIM, tq), f32) for _ in range(heads)]
        for blocks, at, size, masked in parts:
            for h in range(heads):
                p = jnp.exp(s_buf[h, at] - m[h])
                l[h] = l[h] + jnp.sum(p.reshape(size // 8, 8, tq), axis=0)
                p = p.astype(bf16)
                p_buf[at, pl.ds(h * tq, tq)] = p
                o[h] = o[h] + dot(vt[is_b, pl.ds(h * HEAD_DIM, HEAD_DIM), at], p, 1, 0)
        inv = [1.0 / jnp.sum(v, axis=0, keepdims=True) for v in l]
        o_all = jnp.concatenate([o[h] * inv[h] for h in range(heads)], axis=0)
        do_h, delta = [], []
        for h in range(heads):
            scaled = jnp.where(mine, g_t * inv[h], 0.0)
            scaled = jnp.where(feature == h, scaled, 0.0).astype(bf16)
            do_h.append(scaled)
            delta.append(jnp.sum(scaled.astype(f32) * o_all, axis=0, keepdims=True))
        do_cat = jnp.concatenate(do_h, axis=1)
        q_cat = jnp.concatenate(q_h, axis=1)
        dq = [jnp.zeros((HEAD_DIM, tq), f32) for _ in range(heads)]
        for blocks, at, size, masked in parts:
            vals = rows_of(blocks, size, slice(width, 2 * width))
            ps, dss = [], []
            for h in range(heads):
                dp = dot(vals, do_h[h], 1, 0)
                p = p_buf[at, pl.ds(h * tq, tq)]
                ds = (p.astype(f32) * (dp - delta[h])).astype(bf16)
                dq[h] = dq[h] + dot(kt[is_b, pl.ds(h * HEAD_DIM, HEAD_DIM), at], ds, 1, 0)
                ps.append(p)
                dss.append(ds)
            dv[is_b, at] = dv[is_b, at] + dot(jnp.concatenate(ps, axis=1), do_cat, 1, 1)
            dk[is_b, at] = dk[is_b, at] + dot(jnp.concatenate(dss, axis=1), q_cat, 1, 1)
        oacc[t] = jnp.where(mine, o_all, oacc[t])
        qacc[t] = jnp.where(mine, jnp.concatenate(dq, axis=0) * (HEAD_DIM ** -0.5), qacc[t])

    hq = tq // 2
    lanes = heads * hq
    mine_head = (
        lax.broadcasted_iota(jnp.int32, (width, lanes), 0) // HEAD_DIM == lax.broadcasted_iota(jnp.int32, (width, lanes), 1) // hq
    )
    half_row = lax.rem(lax.broadcasted_iota(jnp.int32, (1, lanes), 1), hq) // cols

    def spread(value):
        return jnp.concatenate([value] * heads, axis=1)

    def diagonal(value):
        return jnp.concatenate(
            [value[h * HEAD_DIM : (h + 1) * HEAD_DIM, h * hq : (h + 1) * hq] for h in range(heads)], axis=0
        )

    @pl.loop(0, halves)
    def _(item):
        is_b = first_half + item
        here = pl.ds(pl.multiple_of(is_b * hq, hq), hq)
        row = mixed * tile_rows + is_b * (tile_rows // 2) + half_row
        low = jnp.where(is_b == 1, split, 0)
        high = jnp.where(is_b == 1, slab_rows, split)
        mine = jnp.logical_and(row >= low, row < high)
        q_b = jnp.where(mine_head, spread(qt[mixed, :, here].astype(f32)), 0.0).astype(bf16)

        def rows_of(at, size, cut):
            return kv[is_b, at].reshape(size, 2 * width)[:, cut]

        m = jnp.full((8, lanes), NEG, f32)
        for blocks, at, size, masked in parts:
            s = dot(rows_of(blocks, size, slice(0, width)), q_b, 1, 0)
            if masked:
                s = jnp.where(tail_ok, s, NEG)
            s_buf[0, at] = s
            m = jnp.maximum(m, jnp.max(s.reshape(size // 8, 8, lanes), axis=0))
        m = jnp.max(m, axis=0, keepdims=True)

        l = jnp.zeros((8, lanes), f32)
        o = None
        for blocks, at, size, masked in parts:
            p = jnp.exp(s_buf[0, at] - m)
            l = l + jnp.sum(p.reshape(size // 8, 8, lanes), axis=0)
            p = p.astype(bf16)
            p_buf[at, pl.ds(0, lanes)] = p
            term = dot(vt[is_b, :, at], p, 1, 0)
            o = term if o is None else o + term
        inv = 1.0 / jnp.sum(l, axis=0, keepdims=True)
        o = o * inv
        do_b = jnp.where(mine_head, spread(do_t[mixed, :, here].astype(f32)), 0.0) * jnp.where(mine, inv, 0.0)
        do_b = do_b.astype(bf16)
        delta = jnp.sum(do_b.astype(f32) * o, axis=0, keepdims=True)

        dq = None
        for blocks, at, size, masked in parts:
            dp = dot(rows_of(blocks, size, slice(width, 2 * width)), do_b, 1, 0)
            p = p_buf[at, pl.ds(0, lanes)]
            ds = (p.astype(f32) * (dp - delta)).astype(bf16)
            term = dot(kt[is_b, :, at], ds, 1, 0)
            dq = term if dq is None else dq + term
            dv[is_b, at] = dv[is_b, at] + dot(p, do_b, 1, 1)
            dk[is_b, at] = dk[is_b, at] + dot(ds, q_b, 1, 1)
        keep = mine[:, :hq]
        oacc[mixed, :, here] = jnp.where(keep, diagonal(o), oacc[mixed, :, here])
        qacc[mixed, :, here] = jnp.where(keep, diagonal(dq) * (HEAD_DIM ** -0.5), qacc[mixed, :, here])

    for t in range(tiles):
        o_ref[pl.ds(t * tq, tq)] = oacc[t].T.astype(bf16)
        dq_ref[pl.ds(t * tq, tq)] = qacc[t].T

    dctx_ref[...] = jnp.zeros(dctx_ref.shape, dctx_ref.dtype)
    share_rows = dctx_ref.shape[0] // images
    if images > 1:
        dkv_ref[...] = jnp.zeros(dkv_ref.shape, dkv_ref.dtype)

    def put(img, start):
        @pl.loop(0, image_rows)
        def _(j):
            row = lax.rem(start + j, total_rows)
            at = pl.ds(pl.multiple_of(j * cols, cols), cols)
            dkv_ref[row, :, :width] = dk[img, at].astype(bf16)
            dkv_ref[row, :, width:] = dv[img, at].astype(bf16)
        at = pl.ds(pl.multiple_of(ids[img] * share_rows, 16), share_rows)
        dctx_ref[at, :width] = dk[img, pl.ds(main, share_rows)].astype(bf16)
        dctx_ref[at, width:] = dv[img, pl.ds(main, share_rows)].astype(bf16)
    put(0, start_a)

    @pl.when(straddle)
    def _():
        put(1, start_b)


def attend(row_count, slab, offset, q, do, kv_window, ctx, total_rows, image_rows, ctx_count, images, share_rows, tile_rows=4):
    tokens, width = q.shape
    rows, cols, _ = kv_window.shape
    tiles = tokens // (tile_rows * cols)
    tq = tile_rows * cols
    tail = ctx.shape[1]
    keys = image_rows * cols + tail
    heads = width // HEAD_DIM
    kern = functools.partial(
        attend_kernel, tiles, tile_rows, cols, width, image_rows, total_rows, ctx_count, images, rows // slab, row_count
    )
    vm = pl.BlockSpec(memory_space=pltpu.VMEM)
    return pl.pallas_call(
        kern, name="attend",
        out_shape=(jax.ShapeDtypeStruct((tokens, width), bf16), jax.ShapeDtypeStruct((tokens, width), f32),
                   jax.ShapeDtypeStruct(kv_window.shape, bf16), jax.ShapeDtypeStruct((images * share_rows, 2 * width), bf16)),
        in_specs=[pl.BlockSpec(memory_space=pltpu.SMEM), vm, vm, pl.BlockSpec(memory_space=pl.ANY), vm],
        out_specs=(vm, vm, vm, vm),
        scratch_shapes=[
            pltpu.VMEM((2, keys // cols, cols, 2 * width), bf16),
            pltpu.VMEM((2, width, keys), bf16), pltpu.VMEM((2, width, keys), bf16),
            pltpu.VMEM((tiles, width, tq), bf16), pltpu.VMEM((tiles, width, tq), bf16),
            pltpu.VMEM((heads, keys, tq), f32), pltpu.VMEM((keys, heads * tq), bf16),
            pltpu.VMEM((2, keys, width), f32), pltpu.VMEM((2, keys, width), f32),
            pltpu.VMEM((tiles, width, tq), f32), pltpu.VMEM((tiles, width, tq), f32),
            pltpu.SemaphoreType.DMA((2,)),
        ],
        cost_estimate=pl.CostEstimate(flops=12 * tokens * keys * width, bytes_accessed=8 * 2**20, transcendentals=heads * tokens * keys),
        compiler_params=pltpu.CompilerParams(vmem_limit_bytes=60 * 2**20),
    )(offset, q, do, kv_window, ctx)


MESH = pl.DeviceIdType.MESH
PIECES = 8
SEGMENTS = 4
VECTORS = 10


def vmem(shape, dtype=f32):
    return pltpu.VMEM(shape, dtype)


def greet(devices):
    barrier = pltpu.get_barrier_semaphore()
    for device in devices:
        pl.semaphore_signal(barrier, inc=1, device_id=device, device_id_type=MESH)
    pl.semaphore_wait(barrier, len(devices))


def row_peers(count):
    r, z = lax.axis_index("rows"), lax.axis_index("chan")
    return [(lax.rem(r + d, count), z) for d in range(1, count)]


def chan_peers(count):
    r, z = lax.axis_index("rows"), lax.axis_index("chan")
    return [(r, lax.rem(z + d, count)) for d in range(1, count)]


def push(src, dst, send_sem, recv_sem, device):
    copy = pltpu.make_async_remote_copy(
        src_ref=src, dst_ref=dst, send_sem=send_sem, recv_sem=recv_sem, device_id=device, device_id_type=MESH
    )
    copy.start()
    return copy


def contract(a, b, a_dim, b_dim):
    return lax.dot_general(a, b, (((a_dim,), (b_dim,)), ((), ())), preferred_element_type=f32)


class Locals:
    def __init__(self, sems):
        self.sems, self.copies, self.done = sems, [], set()

    def start(self, src, dst):
        copy = pltpu.make_async_copy(src, dst, self.sems.at[len(self.copies)])
        copy.start()
        self.copies.append(copy)
        return len(self.copies) - 1

    def wait(self, *which):
        for i in which if which else range(len(self.copies)):
            if i not in self.done:
                self.copies[i].wait()
                self.done.add(i)


def share(buf, sends, recvs, count, pieces):
    me = lax.axis_index("rows")
    for index, piece in enumerate(pieces):
        buf[me, pl.ds(index, 1), :] = piece
    return [push(buf.at[me], buf.at[me], sends.at[d], recvs.at[d], device) for d, device in enumerate(row_peers(count))]


def share_total(buf, copies):
    for copy in copies:
        copy.wait()
    total = buf[0]
    for index in range(1, buf.shape[0]):
        total = total + buf[index]
    return total


def image_masks(offset, first, rows, width, total_rows):
    images = total_rows // IMG_H
    row = first - offset + lax.broadcasted_iota(jnp.int32, (rows, 1, width), 0)
    row = jnp.where(row < 0, row + total_rows, row)
    row = jnp.where(row >= total_rows, row - total_rows, row)
    one, zero = jnp.ones((rows, 1, width), f32), jnp.zeros((rows, 1, width), f32)
    member, upper, lower = [], one, one
    for i in range(images):
        inside = jnp.logical_and(row >= i * IMG_H, row < (i + 1) * IMG_H)
        member.append(jnp.where(inside, one, zero))
        upper = jnp.where(row == i * IMG_H, zero, upper)
        lower = jnp.where(row == (i + 1) * IMG_H - 1, zero, lower)
    return member, upper, lower


def group_sum(values, per_group):
    width = values.shape[1]
    one = lax.broadcasted_iota(jnp.int32, (width, width), 0) // per_group
    two = lax.broadcasted_iota(jnp.int32, (width, width), 1) // per_group
    same = (one == two).astype(f32)
    return jnp.dot(values, same, precision=HIGH, preferred_element_type=f32)


def image_sums(values, member):
    by_row = jnp.sum(values, axis=1, keepdims=True)
    return [jnp.sum(by_row * mask, axis=0) for mask in member]


def to_rows(per_image, member):
    total = None
    for mask, value in zip(member, per_image):
        term = mask * value[None]
        total = term if total is None else total + term
    return total


def norm_images(total, images, entries, per_group):
    grouped = group_sum(total, per_group) * (1.0 / entries)
    centers, scales = [], []
    for i in range(images):
        center = grouped[2 * i : 2 * i + 1]
        square = grouped[2 * i + 1 : 2 * i + 2]
        centers.append(center)
        scales.append(lax.rsqrt(square - center * center + EPSILON))
    return centers, scales


def taps(pad, upper, lower, x9):
    rows, cols, width = pad.shape
    rows = rows - 2
    tokens = rows * cols
    col = lax.rem(lax.broadcasted_iota(jnp.int32, (tokens, 1), 0), cols)
    for a in range(3):
        v = pad[pl.ds(a, rows)].astype(f32)
        if a == 0:
            v = v * upper
        if a == 2:
            v = v * lower
        v = v.reshape(tokens, width)
        left = jnp.where(col == 0, 0.0, pltpu.roll(v, 1, 0))
        right = jnp.where(col == cols - 1, 0.0, pltpu.roll(v, tokens - 1, 0))
        for b, part in enumerate((left, v, right)):
            x9[:, pl.ds((3 * a + b) * width, width)] = part.astype(bf16)


class LineGather:
    def __init__(self, at, pieces, sends, recvs):
        self.at, self.pieces, self.sends, self.recvs = at, pieces, sends, recvs
        self.r, self.z = lax.axis_index("rows"), lax.axis_index("chan")
        self.count = lax.axis_size("chan")

    def copy(self, way, step, piece, shard):
        other = self.z + 1 if way == 0 else self.z - 1
        ref = self.at(shard, piece)
        return pltpu.make_async_remote_copy(
            src_ref=ref, dst_ref=ref, send_sem=self.sends.at[way, step, piece], recv_sem=self.recvs.at[way, step, piece],
            device_id=(self.r, other), device_id_type=MESH,
        )

    def has(self, way, step):
        return self.z >= step if way == 0 else self.z + step < self.count

    def open_end(self, way):
        return self.z + 1 < self.count if way == 0 else self.z >= 1

    def shard(self, way, step):
        return self.z - step if way == 0 else self.z + step

    def run(self, step, pieces=None):
        for piece in range(self.pieces) if pieces is None else pieces:
            for way in range(2):
                if step == 0:
                    @pl.when(self.open_end(way))
                    def _():
                        self.copy(way, 0, piece, self.z).start()
                else:
                    @pl.when(self.has(way, step))
                    def _():
                        shard = self.shard(way, step)
                        self.copy(way, step - 1, piece, shard).wait_recv()
                        if step < self.count - 1:
                            @pl.when(self.open_end(way))
                            def _():
                                self.copy(way, step, piece, shard).start()

    def drain(self):
        for step in range(self.count - 1):
            for way in range(2):
                @pl.when(jnp.logical_and(self.has(way, step), self.open_end(way)))
                def _():
                    for piece in range(self.pieces):
                        self.copy(way, step, piece, self.shard(way, step)).wait_send()


class LineScatter:
    def __init__(self, term, own, out, recv, sends, recvs):
        self.term, self.own, self.out, self.recv, self.sends, self.recvs = term, own, out, recv, sends, recvs
        self.r, self.z = lax.axis_index("rows"), lax.axis_index("chan")
        self.pieces = sends.shape[1]
        self.size = own.shape[0] // self.pieces
        self.end = jnp.logical_or(self.z == 0, self.z == 3)
        self.opposite = lax.rem(self.z + 2, 4)

    def rows(self, piece):
        return pl.ds(piece * self.size, self.size)

    def copy(self, slot, piece, device):
        rows = self.rows(piece)
        return pltpu.make_async_remote_copy(
            src_ref=self.out.at[slot, rows], dst_ref=self.recv.at[slot, rows], send_sem=self.sends.at[slot, piece],
            recv_sem=self.recvs.at[slot, piece], device_id=(self.r, device), device_id_type=MESH,
        )

    def push(self, slot, target, device, piece):
        rows = self.rows(piece)
        self.out[slot, rows] = self.term(target, rows).astype(bf16)
        self.copy(slot, piece, device).start()

    def send(self, piece):
        z = self.z

        @pl.when(self.end)
        def _():
            self.push(3, 3 - z, 1 + z // 3, piece)
            self.push(0, self.opposite, self.opposite, piece)

        @pl.when(z < 3)
        def _():
            self.push(1, z + 1, z + 1, piece)

        @pl.when(z > 0)
        def _():
            self.push(2, z - 1, z - 1, piece)

    def merge(self, piece):
        @pl.when(jnp.logical_not(self.end))
        def _():
            rows = self.rows(piece)
            term = self.term(self.opposite, rows)
            self.copy(3, piece, self.opposite).wait_recv()
            self.out[0, rows] = (term + self.recv[3, rows].astype(f32)).astype(bf16)
            self.copy(0, piece, self.opposite).start()

    def keep(self):
        self.own[...] = self.term(self.z, pl.ds(0, self.own.shape[0]))

    def add(self, slot, piece):
        rows = self.rows(piece)
        self.copy(slot, piece, self.z).wait_recv()
        self.own[rows, :] = self.own[rows, :] + self.recv[slot, rows].astype(f32)

    def finish(self):
        for piece in range(self.pieces):
            @pl.when(self.z > 0)
            def _():
                self.add(1, piece)

            @pl.when(self.z < 3)
            def _():
                self.add(2, piece)
            self.add(0, piece)

    def drain(self):
        for piece in range(self.pieces):
            self.copy(0, piece, self.z).wait_send()

            @pl.when(self.z < 3)
            def _():
                self.copy(1, piece, self.z).wait_send()

            @pl.when(self.z > 0)
            def _():
                self.copy(2, piece, self.z).wait_send()

            @pl.when(self.end)
            def _():
                self.copy(3, piece, self.z).wait_send()


def scatter_scratch(tokens, width, pieces):
    return [
        vmem((tokens, width), f32), vmem((4, tokens, width), bf16), vmem((4, tokens, width), bf16),
        pltpu.SemaphoreType.DMA((4, pieces)), pltpu.SemaphoreType.DMA((4, pieces)),
    ]


def plane():
    r = lax.axis_index("rows")
    core = r + 1 - 2 * lax.rem(r, 2)
    x_dev = r + 2 - 4 * lax.rem(r // 2, 2)
    y_dev = r + 4 - 8 * (r // 4)
    return core, x_dev, y_dev, x_dev + y_dev - r


class PlaneGather:
    def __init__(self, all_ref, sends, recvs):
        self.all, self.sends, self.recvs = all_ref, sends, recvs
        self.r, self.z = lax.axis_index("rows"), lax.axis_index("chan")
        self.core, self.x, self.y, self.d = plane()
        self.size = all_ref.shape[1] // SEGMENTS
        self.copies = [{} for _ in range(SEGMENTS)]

    def part(self, segment, which):
        half = self.size // 2
        if which is None:
            return pl.ds(segment * self.size, self.size)
        return pl.ds(segment * self.size + which * half, half)

    def send(self, segment, i, slab, which, device):
        ref = self.all.at[slab, self.part(segment, which)]
        self.copies[segment][i] = push(ref, ref, self.sends.at[segment, i], self.recvs.at[segment, i], (device, self.z))

    def start(self, s):
        self.send(s, 0, self.r, 0, self.x)
        self.send(s, 1, self.r, 1, self.y)
        self.send(s, 2, self.r, 1, self.x)
        self.send(s, 3, self.r, 0, self.y)
        self.send(s, 4, self.r, None, self.core)

    def relay(self, s):
        copies = self.copies[s]
        copies[0].wait_recv()
        self.send(s, 5, self.x, 0, self.y)
        self.send(s, 6, self.x, 0, self.core)
        copies[1].wait_recv()
        self.send(s, 7, self.y, 1, self.x)
        self.send(s, 8, self.y, 1, self.core)
        copies[2].wait_recv()
        self.send(s, 9, self.x, 1, self.core)
        copies[3].wait_recv()
        self.send(s, 10, self.y, 0, self.core)

    def last(self, s):
        copies = self.copies[s]
        copies[5].wait_recv()
        self.send(s, 11, self.d, 0, self.core)
        copies[7].wait_recv()
        self.send(s, 12, self.d, 1, self.core)

    def done(self, s):
        for i in (4, 6, 8, 9, 10, 11, 12):
            self.copies[s][i].wait_recv()

    def drain(self):
        for copies in self.copies:
            for copy in copies.values():
                copy.wait_send()


class WindowGather:
    def __init__(self, all_ref, sends, recvs):
        self.all, self.sends, self.recvs = all_ref, sends, recvs
        self.size = all_ref.shape[1] // SEGMENTS
        self.copies = [[] for _ in range(SEGMENTS)]

    def start(self, s):
        r, z, count = lax.axis_index("rows"), lax.axis_index("chan"), lax.axis_size("rows")
        window = self.all.shape[0]
        own = window // 2 if window < count else r
        part = pl.ds(s * self.size, self.size)
        for i in range(1, count):
            place = window // 2 - i if i <= window // 2 else window // 2 + count - i
            if window < count and (place < 0 or place >= window):
                continue
            slot = place if window < count else r
            device = (lax.rem(r + i, count), z)
            self.copies[s].append(
                push(self.all.at[own, part], self.all.at[slot, part], self.sends.at[s, i], self.recvs.at[s, i], device)
            )

    def relay(self, s):
        pass

    last = relay

    def done(self, s):
        for copy in self.copies[s]:
            copy.wait_recv()

    def drain(self):
        for copies in self.copies:
            for copy in copies:
                copy.wait_send()


def forward_kernel(row_count, chan_count, per_group, entries, fast, offset, x_ref, *refs):
    vec, refs = refs[:VECTORS], refs[VECTORS:]
    (emb, emb_b, ctx_b, w1_hbm, w2_hbm, att_hbm, g_hbm, wo_hbm, context_hbm, emb_hbm, ctx_hbm,
     x9t_1_hbm, x9t_2_hbm, turn1_hbm, turn2_hbm, c1_hbm, x1_hbm, a3_hbm, all_hbm, gall_hbm, row_ref, q_ref, do_ref,
     mod, ctx_ref,
     w1, w2, w_att, wo, context, emb_w, ctx_w, wide, x9t_1, x9t_2, turn1, turn2, x1_ref, a3_ref, all_ref, gall_ref,
     xpad, cpad, pad, x9, own1, out1, recv1, s1, r1, own2, out2, recv2, s2, r2, stat, stat_s, stat_r, halo_s, halo_r,
     a3_s, a3_r, g_s, g_r, kv_s, kv_r, in_s, out_s) = refs
    rows, cols, width = x_ref.shape
    tokens = rows * cols
    r, z = lax.axis_index("rows"), lax.axis_index("chan")
    loads, stores = Locals(in_s), Locals(out_s)
    for src, dst in ((g_hbm, gall_ref.at[z]), (w1_hbm, w1), (w2_hbm, w2), (att_hbm, w_att), (wo_hbm, wo),
                     (context_hbm, context), (emb_hbm, emb_w), (ctx_hbm, ctx_w)):
        loads.start(src, dst)
    x = x_ref[...]
    xpad[pl.ds(1, rows)] = x
    greet(row_peers(row_count) + chan_peers(chan_count))
    up = (lax.rem(r + row_count - 1, row_count), z)
    down = (lax.rem(r + 1, row_count), z)

    def rims(phase, ref):
        one = push(ref.at[1], ref.at[rows + 1], halo_s.at[phase, 0], halo_r.at[phase, 0], up)
        two = push(ref.at[rows], ref.at[0], halo_s.at[phase, 1], halo_r.at[phase, 1], down)
        return one, two

    x_rims = rims(0, xpad)
    member, upper, lower = image_masks(offset[0], r * rows - 1, rows + 2, width, row_count * rows)
    images = len(member)
    inner = [mask[1 : rows + 1] for mask in member]
    upper, lower = upper[1 : rows + 1], lower[1 : rows + 1]
    third = -(-tokens // 48) * 16
    g_copies = []
    loads.wait(0)

    def vector(i):
        return vec[i][...][None]

    def stats(phase, values):
        pieces = []
        for a, b in zip(image_sums(values, inner), image_sums(values * values, inner)):
            pieces += [a, b]
        copies = share(stat.at[phase], stat_s.at[phase], stat_r.at[phase], row_count, pieces)
        part = pl.ds(phase * third, min(third, tokens - phase * third))
        for d, device in enumerate(chan_peers(chan_count)):
            g_copies.append(push(gall_ref.at[z, part], gall_ref.at[z, part], g_s.at[phase, d], g_r.at[phase, d], device))
        centers, scales = norm_images(share_total(stat.at[phase], copies), images, entries, per_group)
        row_ref[2 * phase] = to_rows(centers, inner)
        row_ref[2 * phase + 1] = to_rows(scales, inner)
        return centers, scales

    def conv(weight, *scratch):
        def term(j, at):
            return jnp.dot(x9[at, :], weight[:, pl.ds(pl.multiple_of(j * width, width), width)], preferred_element_type=f32)
        line = LineScatter(term, *scratch)
        for piece in range(line.pieces):
            line.send(piece)
        for piece in range(line.pieces):
            line.merge(piece)
        line.keep()
        return line

    def turn(weight, turned):
        for j in range(chan_count):
            for a in range(3):
                turned[j, pl.ds(a * width, width), :] = weight[pl.ds(3 * a * width, 3 * width), pl.ds(j * width, width)].T

    def split(weight):
        wide[...] = weight[...].astype(f32)
        return [wide[pl.ds(t, weight.shape[0] // 2, 2), :].astype(bf16) for t in range(2)]

    centers, scales = stats(0, x.astype(f32))
    for copy in x_rims:
        copy.wait()
    n1 = (xpad[...].astype(f32) - to_rows(centers, member)) * to_rows(scales, member) * vector(0) + vector(1)
    pad[...] = (n1 * jax.nn.sigmoid(n1)).astype(bf16)
    taps(pad, upper, lower, x9)
    loads.wait(1)
    line1 = conv(w1, own1, out1, recv1, s1, r1)
    x9t_1[...] = x9[...].T
    stores.start(x9t_1, x9t_1_hbm)
    turn(w1, turn1)
    stores.start(turn1, turn1_hbm)
    loads.wait(5, 6, 7)
    for t, weight in enumerate(split(emb_w)):
        mod[t] = jnp.dot(emb[...], weight, preferred_element_type=f32) + emb_b[t : t + 1, :]
    ctx_ref[...] = jnp.zeros(ctx_ref.shape, bf16)
    for t, weight in enumerate(split(ctx_w)):
        for i in range(images):
            value = jnp.dot(context[i], weight, preferred_element_type=f32) + ctx_b[t : t + 1, :]
            ctx_ref[i, pl.ds(0, context.shape[1]), pl.ds(t * width, width)] = value.astype(bf16)
    line1.finish()
    c1 = own1[...].reshape(rows, cols, width) + vector(2)
    cpad[pl.ds(1, rows)] = c1
    c_rims = rims(1, cpad)
    stores.start(cpad.at[pl.ds(1, rows)], c1_hbm)
    centers, scales = stats(1, c1)
    mod_scale = 1.0 + to_rows([mod[0, i : i + 1, :] for i in range(images)], member)
    mod_shift = to_rows([mod[1, i : i + 1, :] for i in range(images)], member)
    for copy in c_rims:
        copy.wait()
    n2 = (cpad[...] - to_rows(centers, member)) * to_rows(scales, member) * vector(3) + vector(4)
    h2 = n2 * mod_scale + mod_shift
    pad[...] = (h2 * jax.nn.sigmoid(h2)).astype(bf16)
    taps(pad, upper, lower, x9)
    loads.wait(2)
    line2 = conv(w2, own2, out2, recv2, s2, r2)
    x9t_2[...] = x9[...].T
    stores.start(x9t_2, x9t_2_hbm)
    turn(w2, turn2)
    stores.start(turn2, turn2_hbm)
    line1.drain()
    line2.finish()
    x1 = x.astype(f32) + (own2[...].reshape(rows, cols, width) + vector(5))
    x1_ref[...] = x1
    stores.start(x1_ref, x1_hbm)
    centers, scales = stats(2, x1)
    a3 = (x1 - to_rows(centers, inner)) * to_rows(scales, inner) * vector(6) + vector(7)
    a3_ref[z] = a3.astype(bf16).reshape(tokens, width)

    size, per = tokens // PIECES, PIECES // SEGMENTS
    line = LineGather(lambda shard, piece: a3_ref.at[shard, pl.ds(piece * size, size)], PIECES, a3_s, a3_r)
    window = all_ref.shape[0]
    own = window // 2 if window < row_count else r
    gather = (PlaneGather if fast else WindowGather)(all_ref, kv_s, kv_r)
    loads.wait(3, 4)
    weights = [
        jnp.concatenate([w_att[t, pl.ds(i * width, width), :] for t in range(3)], axis=1) for i in range(chan_count)
    ]

    def run(step, segment):
        line.run(step, range(segment * per, (segment + 1) * per))

    def project(segment):
        at = pl.ds(segment * size * per, size * per)
        qkv = None
        for i in range(chan_count):
            term = jnp.dot(a3_ref[i, at], weights[i], preferred_element_type=f32)
            qkv = term if qkv is None else qkv + term
        all_ref[own, at, :width] = qkv[:, width : 2 * width].astype(bf16)
        all_ref[own, at, width:] = (qkv[:, 2 * width :] + vec[9][1:2, :]).astype(bf16)
        gather.start(segment)
        q_ref[at, :] = (qkv[:, :width] + vec[9][0:1, :]).astype(bf16)

    for step, segment in ((0, 0), (0, 1), (1, 0), (0, 2), (2, 0), (1, 1), (0, 3), (3, 0)):
        run(step, segment)
    project(0)
    for step, segment in ((2, 1), (1, 2), (3, 1)):
        run(step, segment)
    project(1)
    gather.relay(0)
    for step, segment in ((2, 2), (1, 3), (3, 2)):
        run(step, segment)
    project(2)
    gather.relay(1)
    gather.last(0)
    for step, segment in ((2, 3), (3, 3)):
        run(step, segment)
    project(3)
    stores.start(a3_ref, a3_hbm)
    gather.relay(2)
    gather.last(1)
    for copy in g_copies:
        copy.wait_recv()
    stores.start(gall_ref, gall_hbm)
    gather.relay(3)
    do = None
    for i in range(chan_count):
        term = contract(gall_ref[i], wo[:, pl.ds(i * width, width)], 1, 1)
        do = term if do is None else do + term
    do_ref[...] = do.astype(bf16)
    gather.last(2)
    gather.last(3)
    for segment in range(SEGMENTS):
        at = pl.ds(segment * size * per, size * per)
        gather.done(segment)
        stores.start(all_ref.at[:, at], all_hbm.at[:, at])
    line2.drain()
    line.drain()
    gather.drain()
    for copy in g_copies:
        copy.wait_send()
    stores.wait()


def forward_block(row_count, chan_count, per_group, entries, window, fast, tail, offset, x, vec, emb, emb_b, ctx_b,
                  w1, w2, w_att, g, wo, context, emb_w, ctx_w):
    rows, cols, width = x.shape
    tokens = rows * cols
    images = row_count * rows // IMG_H
    message = -(-2 * images // 8) * 8
    vm = pl.BlockSpec(memory_space=pltpu.VMEM)
    hbm = pl.BlockSpec(memory_space=pl.ANY)
    S = jax.ShapeDtypeStruct
    sem = pltpu.SemaphoreType.DMA
    peers = chan_count - 1
    full = chan_count * width
    saved = [
        ((9 * width, tokens), bf16), ((9 * width, tokens), bf16),
        ((chan_count, 3 * width, 3 * width), bf16), ((chan_count, 3 * width, 3 * width), bf16),
        ((rows, cols, width), f32), ((rows, cols, width), f32), ((chan_count, tokens, width), bf16),
        ((window, tokens, 2 * width), bf16), ((chan_count, tokens, width), bf16),
    ]
    small = [
        ((6, rows, 1, width), f32), ((tokens, width), bf16), ((tokens, width), bf16), ((2, images, width), f32),
        ((images, tail, 2 * width), bf16),
    ]
    return pl.pallas_call(
        functools.partial(forward_kernel, row_count, chan_count, per_group, entries, fast),
        name="forward_block",
        out_shape=tuple(S(*item) for item in saved + small),
        in_specs=[pl.BlockSpec(memory_space=pltpu.SMEM)] + [vm] * (4 + VECTORS) + [hbm] * 8,
        out_specs=(hbm,) * len(saved) + (vm,) * len(small),
        scratch_shapes=[
            vmem((9 * width, full), bf16), vmem((9 * width, full), bf16), vmem((3, full, width), bf16), vmem((width, full), bf16),
            vmem(context.shape, bf16), vmem(emb_w.shape, bf16), vmem(ctx_w.shape, bf16), vmem(emb_w.shape, f32),
            *[vmem(*item) for i, item in enumerate(saved) if i != 4],
            vmem((rows + 2, cols, width), bf16),
            vmem((rows + 2, cols, width), f32),
            vmem((rows + 2, cols, width), bf16),
            vmem((tokens, 9 * width), bf16),
            *scatter_scratch(tokens, width, 2),
            *scatter_scratch(tokens, width, 2),
            vmem((3, row_count, message, width), f32),
            sem((3, row_count - 1)), sem((3, row_count - 1)),
            sem((2, 2)), sem((2, 2)),
            sem((2, peers, PIECES)), sem((2, peers, PIECES)),
            sem((3, peers)), sem((3, peers)),
            sem((SEGMENTS, max(13, row_count))), sem((SEGMENTS, max(13, row_count))),
            sem((8,)), sem((8 + SEGMENTS,)),
        ],
        cost_estimate=pl.CostEstimate(flops=8 * 9 * tokens * width * full, bytes_accessed=16 * 2**20, transcendentals=4 * tokens * width),
        compiler_params=pltpu.CompilerParams(collective_id=0, has_side_effects=True, vmem_limit_bytes=60 * 2**20),
    )(offset, x, *vec, emb, emb_b, ctx_b, w1, w2, w_att, g, wo, context, emb_w, ctx_w)


class Total:
    def __init__(self, part, out, half, quarters, sends, recvs):
        self.part, self.half, self.quarters, self.out = part, half, quarters, out
        self.sends, self.recvs = sends, recvs
        self.r, self.z = lax.axis_index("rows"), lax.axis_index("chan")
        self.core, self.x, self.y, self.d = plane()
        self.n = part.shape[0] // 8
        self.copies = []

    def rows(self, device):
        return pl.ds(pl.multiple_of((lax.rem(device, 2) * 4 + device // 2) * self.n, 16), self.n)

    def half_rows(self, device):
        return pl.ds(pl.multiple_of(lax.rem(device, 2) * 4 * self.n, 16), 4 * self.n)

    def send(self, i, src, dst, device):
        copy = push(src, dst, self.sends.at[i], self.recvs.at[i], (device, self.z))
        self.copies.append(copy)
        return copy

    def one(self):
        self.a = self.send(0, self.part.at[self.half_rows(self.core)], self.half, self.core)

    def two(self):
        self.a.wait_recv()
        mine = self.half_rows(self.r)
        self.half[...] = (self.part[mine, :].astype(f32) + self.half[...].astype(f32)).astype(bf16)
        self.b = []
        for i, device in enumerate((self.d, self.x, self.y)):
            at = pl.ds(pl.multiple_of((device // 2) * self.n, 16), self.n)
            self.b.append(self.send(1 + i, self.half.at[at], self.quarters.at[i], device))

    def three(self):
        at = pl.ds(pl.multiple_of((self.r // 2) * self.n, 16), self.n)
        total = self.half[at, :].astype(f32)
        for i, copy in enumerate(self.b):
            copy.wait_recv()
            total = total + self.quarters[i].astype(f32)
        mine = self.rows(self.r)
        self.out[mine, :] = total.astype(bf16)
        self.c = []
        for i, device in enumerate((self.d, self.x, self.y, self.core)):
            self.c.append(self.send(4 + i, self.out.at[mine], self.out.at[mine], device))

    def four(self):
        self.e = [self.c[3]]
        for i, device in ((1, self.x), (2, self.y), (0, self.d)):
            self.c[i].wait_recv()
            at = self.rows(device)
            self.e.append(self.send(8 + i, self.out.at[at], self.out.at[at], self.core))

    def finish(self):
        for copy in self.e:
            copy.wait_recv()
        for copy in self.copies:
            copy.wait_send()


def total_scratch(n, width):
    return [vmem((n // 2, width), bf16), vmem((3, n // 8, width), bf16), pltpu.SemaphoreType.DMA((11,)), pltpu.SemaphoreType.DMA((11,))]


class Return:
    def __init__(self, away, parts, cores, out, recv, relay, sends, recvs):
        self.away, self.parts, self.cores, self.out, self.recv, self.relay = away, parts, cores, out, recv, relay
        self.sends, self.recvs = sends, recvs
        self.r, self.z = lax.axis_index("rows"), lax.axis_index("chan")
        self.core, self.x, self.y, self.d = plane()
        self.size = parts.shape[1] // SEGMENTS
        self.copies = [{} for _ in range(SEGMENTS)]

    def at(self, s, which=None):
        half = self.size // 2
        if which is None:
            return pl.ds(s * self.size, self.size)
        return pl.ds(s * self.size + which * half, half)

    def send(self, s, i, src, dst, device):
        self.copies[s][i] = push(src, dst, self.sends.at[s, i], self.recvs.at[s, i], (device, self.z))

    def start(self):
        for s in range(SEGMENTS):
            at = self.at(s)
            for i, device in enumerate((self.d, self.x, self.y, self.r)):
                self.send(s, i, self.away.at[device + self.core - self.r, at], self.cores.at[i, at], self.core)

    def chip(self, i, at):
        return self.parts[i, at].astype(f32) + self.cores[i, at].astype(f32)

    def one(self, s):
        first, second, out, recv = self.at(s, 0), self.at(s, 1), self.out, self.recv
        self.copies[s][0].wait_recv()
        out[0, first] = self.chip(0, first).astype(bf16)
        self.send(s, 4, out.at[0, first], self.relay.at[0, s], self.x)
        out[0, second] = self.chip(0, second).astype(bf16)
        self.send(s, 5, out.at[0, second], self.relay.at[1, s], self.y)
        self.copies[s][1].wait_recv()
        out[1, first] = self.chip(1, first).astype(bf16)
        self.send(s, 6, out.at[1, first], recv.at[0, first], self.x)
        self.copies[s][2].wait_recv()
        out[2, second] = self.chip(2, second).astype(bf16)
        self.send(s, 7, out.at[2, second], recv.at[1, second], self.y)

    def two(self, s):
        first, second, out, recv = self.at(s, 0), self.at(s, 1), self.out, self.recv
        self.copies[s][4].wait_recv()
        out[2, first] = (self.chip(2, first) + self.relay[0, s].astype(f32)).astype(bf16)
        self.send(s, 8, out.at[2, first], recv.at[1, first], self.y)
        self.copies[s][5].wait_recv()
        out[1, second] = (self.chip(1, second) + self.relay[1, s].astype(f32)).astype(bf16)
        self.send(s, 9, out.at[1, second], recv.at[0, second], self.x)

    def three(self, s):
        at = self.at(s)
        for i in (3, 6, 7, 8, 9):
            self.copies[s][i].wait_recv()
        return self.chip(3, at) + self.recv[0, at].astype(f32) + self.recv[1, at].astype(f32)

    def drain(self):
        for copies in self.copies:
            for copy in copies.values():
                copy.wait_send()


def return_scratch(tokens, width):
    shape = (tokens, width)
    sem = pltpu.SemaphoreType.DMA((SEGMENTS, 10))
    return [
        vmem((4, *shape), bf16), vmem((4, *shape), bf16), vmem((3, *shape), bf16), vmem((2, *shape), bf16),
        vmem((2, SEGMENTS, tokens // (2 * SEGMENTS), width), bf16), sem, sem,
    ]


class ConvBack:
    def __init__(self, pad, acc, x9t, turned, parts, outs, totals, up, down, halo_s, halo_r, sends, recvs, upper, lower):
        self.pad, self.acc, self.x9t, self.turned, self.parts, self.outs = pad, acc, x9t, turned, parts, outs
        self.totals, self.up, self.down, self.halo_s, self.halo_r = totals, up, down, halo_s, halo_r
        self.upper, self.lower = upper, lower
        _, self.rows, self.cols, self.width = pad.shape
        self.rows -= 2
        self.tokens = self.rows * self.cols
        self.size = self.rows // PIECES
        self.line = LineGather(self.at, PIECES + 2, sends, recvs)
        z = lax.axis_index("chan")
        low = z < 2
        self.order = (z, z + 1 - 2 * lax.rem(z, 2), jnp.where(low, 2, 1), jnp.where(low, 3, 0))
        self.later = []

    def at(self, shard, piece):
        if piece < PIECES:
            return self.pad.at[shard, pl.ds(1 + piece * self.size, self.size)]
        return self.pad.at[shard, pl.ds(0 if piece == PIECES else self.rows + 1, 1)]

    def start(self, values):
        pad, rows, z = self.pad, self.rows, lax.axis_index("chan")
        pad[z, pl.ds(1, rows)] = values
        self.rims = [
            push(pad.at[z, 1], pad.at[z, rows + 1], self.halo_s.at[0], self.halo_r.at[0], self.up),
            push(pad.at[z, rows], pad.at[z, 0], self.halo_s.at[1], self.halo_r.at[1], self.down),
        ]
        self.line.run(0, range(PIECES))
        for copy in self.rims:
            copy.wait_recv()
        self.line.run(0, (PIECES, PIECES + 1))

    def block(self, step):
        j, rows, tokens, width = self.order[step], self.rows, self.tokens, self.width
        parts = []
        for a, mask in enumerate((self.lower, None, self.upper)):
            part = self.pad[j, pl.ds(2 - a, rows)]
            if mask is not None:
                part = (part.astype(f32) * mask).astype(bf16)
            parts.append(part.reshape(tokens, width))
        self.parts[step] = jnp.dot(self.x9t[...], parts[1], preferred_element_type=f32).astype(bf16)
        if self.totals:
            self.totals[step].one()
        else:
            self.outs[j] = self.parts[step]
        term = jnp.dot(jnp.concatenate(parts, axis=1), self.turned[j], preferred_element_type=f32)
        self.acc[...] = term if step == 0 else self.acc[...] + term

    def run(self, step):
        self.line.run(step)
        self.block(step)

    def input_grad(self):
        total, width, cols, tokens = self.acc[...], self.width, self.cols, self.tokens
        col = lax.rem(lax.broadcasted_iota(jnp.int32, (tokens, 1), 0), cols)
        before = jnp.where(col == cols - 1, 0.0, pltpu.roll(total[:, :width], tokens - 1, 0))
        after = jnp.where(col == 0, 0.0, pltpu.roll(total[:, 2 * width :], 1, 0))
        return (before + total[:, width : 2 * width] + after).reshape(self.rows, cols, width)

    def drain(self):
        for copy in self.rims:
            copy.wait_send()
        self.line.drain()


def silu_slope(values):
    gate = jax.nn.sigmoid(values)
    return gate * (1.0 + values * (1.0 - gate))


def channel_total(values):
    return jnp.sum(jnp.sum(values, axis=1, keepdims=True), axis=0)


def backward_kernel(row_count, chan_count, per_group, entries, fast, offset, *refs):
    vec, refs = refs[:VECTORS], refs[VECTORS:]
    (rows_in, mod, w_att, wo, dctx,
     dq_hbm, dkv_hbm, o_hbm, gall_hbm, a3_hbm, x1_hbm, c1_hbm, x_hbm, x9t_1_hbm, x9t_2_hbm, turn1_hbm, turn2_hbm,
     result, dfeat, sums, g_conv1, g_conv2, g_att, g_out, g_ctx,
     dq_ref, o_ref, gall, a3_all, x1_ref, c1_ref, x_ref, x9t_1, x9t_2, turn1, turn2, load_s,
     part1, part2, part_att, part_out, d3, dx1_ref, acc, gpad, halo_s, halo_r, zh_s, zh_r, stat, stat_s, stat_r,
     res_out, res_recv, res_s, res_r, own, da3_out, da3_recv, da3_s, da3_r) = refs[:61]
    refs = refs[61:]
    rows, cols, width = x_ref.shape
    tokens = rows * cols
    r, z = lax.axis_index("rows"), lax.axis_index("chan")
    loads = Locals(load_s)
    greet(row_peers(row_count) + chan_peers(chan_count))
    if fast:
        back = Return(dkv_hbm, *refs[:7])
        back.start()
        for i, device in enumerate((back.d, back.x, back.y, r)):
            loads.start(dkv_hbm.at[device], back.parts.at[i])
        pairs = iter(range(7, len(refs), 4))

        def total(part, out):
            i = next(pairs)
            return Total(part, out, *refs[i : i + 4])
        small = [total(part_att, g_att), total(part_out, g_out), total(dctx, g_ctx)]
    else:
        for i in range(4):
            loads.start(dkv_hbm.at[pl.ds(i * (tokens // 4), tokens // 4)], refs[0].at[pl.ds(i * (tokens // 4), tokens // 4)])
        small = []
    for src, dst in (
        (dq_hbm, dq_ref), (o_hbm, o_ref), (gall_hbm, gall), (a3_hbm, a3_all), (x1_hbm, x1_ref), (c1_hbm, c1_ref), (x_hbm, x_ref),
        (x9t_2_hbm, x9t_2), (turn2_hbm, turn2), (x9t_1_hbm, x9t_1), (turn1_hbm, turn1),
    ):
        loads.start(src, dst)
    member, upper, lower = image_masks(offset[0], r * rows, rows, width, row_count * rows)
    images = len(member)
    up = (lax.rem(r + row_count - 1, row_count), z)
    down = (lax.rem(r + 1, row_count), z)
    orders = []
    for index, (x9t, turned, parts, outs) in enumerate(((x9t_2, turn2, part2, g_conv2), (x9t_1, turn1, part1, g_conv1))):
        conv = ConvBack(
            gpad.at[index], acc, x9t, turned, parts, outs, [], up, down, halo_s.at[index], halo_r.at[index],
            zh_s.at[index], zh_r.at[index], upper, lower,
        )
        if fast:
            conv.totals = [total(parts.at[step], outs.at[conv.order[step]]) for step in range(chan_count)]
        orders.append(conv)
    conv2, conv1 = orders
    third = -(-tokens // 48) * 16
    res_copies = []

    def vector(i):
        return vec[i][...][None]

    def exchange(phase, pieces):
        copies = share(stat.at[phase], stat_s.at[phase], stat_r.at[phase], row_count, pieces)
        part = pl.ds(phase * third, min(third, tokens - phase * third))
        for d, device in enumerate(chan_peers(chan_count)):
            res_copies.append(push(res_out.at[d, part], res_recv.at[d, part], res_s.at[phase, d], res_r.at[phase, d], device))
        return copies

    def norm_pieces(dxh, xhat):
        pieces = []
        for a, b in zip(image_sums(dxh, member), image_sums(dxh * xhat, member)):
            pieces += [a, b]
        return pieces

    def norm_back(total, dxh, xhat, scale):
        grouped = group_sum(total[: 2 * images], per_group) * (1.0 / entries)
        first = to_rows([grouped[2 * i : 2 * i + 1] for i in range(images)], member)
        second = to_rows([grouped[2 * i + 1 : 2 * i + 2] for i in range(images)], member)
        return scale * (dxh - first - xhat * second)

    def out_term(j):
        return jnp.dot(o_ref[...], wo[:, pl.ds(pl.multiple_of(j * width, width), width)], preferred_element_type=f32)

    def att_rows(j):
        at = pl.ds(pl.multiple_of(j * width, width), width)
        return jnp.concatenate([w_att[t, at, :] for t in range(3)], axis=1)

    line = LineScatter(lambda j, at: contract(d3[at, :], att_rows(j), 1, 1), own, da3_out, da3_recv, da3_s, da3_r)
    size = tokens // SEGMENTS
    bias_v = jnp.zeros((1, width), f32)
    loads.wait(4)
    if fast:
        loads.wait(0, 1, 2, 3)
        for s in range(SEGMENTS + 2):
            if s < SEGMENTS:
                back.one(s)
            if s == 0:
                loads.wait(5, 6)
                for d, device in enumerate(chan_peers(chan_count)):
                    res_out[d] = out_term(device[1]).astype(bf16)
            if 1 <= s <= SEGMENTS:
                back.two(s - 1)
            if s >= 2:
                at = pl.ds((s - 2) * size, size)
                dkv = back.three(s - 2)
                d3[at, :width] = dq_ref[at, :].astype(bf16)
                d3[at, width:] = dkv.astype(bf16)
                bias_v = bias_v + jnp.sum(dkv[:, width:], axis=0, keepdims=True)
                line.send(s - 2)
            if s >= 3:
                line.merge(s - 3)
        line.merge(SEGMENTS - 1)
    else:
        loads.wait(0, 1, 2, 3, 5, 6)
        for d, device in enumerate(chan_peers(chan_count)):
            res_out[d] = out_term(device[1]).astype(bf16)
        for s in range(SEGMENTS + 1):
            if s < SEGMENTS:
                at = pl.ds(s * size, size)
                dkv = refs[0][at, :]
                d3[at, :width] = dq_ref[at, :].astype(bf16)
                d3[at, width:] = dkv.astype(bf16)
                bias_v = bias_v + jnp.sum(dkv[:, width:], axis=0, keepdims=True)
                line.send(s)
            if s >= 1:
                line.merge(s - 1)
    line.keep()
    bias_q = jnp.sum(dq_ref[...], axis=0, keepdims=True)
    loads.wait(7)
    for i in range(chan_count):
        grad = contract(a3_all[i], d3[...], 0, 0).astype(bf16)
        for t in range(3):
            part_att[pl.ds((t * chan_count + i) * width, width), :] = grad[:, t * width : (t + 1) * width]
    g_cat = jnp.concatenate([gall[i] for i in range(chan_count)], axis=1)
    part_out[...] = contract(o_ref[...], g_cat, 0, 0).astype(bf16)
    for t in small:
        t.one()
    loads.wait(8)
    x1 = x1_ref[...]
    g = gall[z].astype(f32).reshape(rows, cols, width)
    center, scale = rows_in[4], rows_in[5]
    xhat = (x1 - center) * scale
    bias_g = channel_total(g)
    for t in small:
        t.two()
    line.finish()
    da3 = own[...].reshape(rows, cols, width)
    dxh = da3 * vector(6)
    copies = exchange(
        0, norm_pieces(dxh, xhat) + [channel_total(da3 * xhat), channel_total(da3), bias_q, bias_v, bias_g]
    )
    for t in small:
        t.three()
    total = share_total(stat.at[0], copies)
    sums[0:5, :] = total[2 * images : 2 * images + 5]
    dx1 = g + norm_back(total, dxh, xhat, scale)
    conv2.start(dx1.astype(bf16))
    dx1_ref[...] = dx1
    bias_2 = channel_total(dx1)
    loads.wait(9, 11, 12)
    conv2.block(0)
    for t in small:
        t.four()
    center, scale = rows_in[2], rows_in[3]
    xhat = (c1_ref[...] - center) * scale
    n2 = xhat * vector(3) + vector(4)
    mod_scale = 1.0 + to_rows([mod[0, i : i + 1, :] for i in range(images)], member)
    mod_shift = to_rows([mod[1, i : i + 1, :] for i in range(images)], member)
    slope = silu_slope(n2 * mod_scale + mod_shift)
    conv2.run(1)
    for t in conv2.totals[0:1]:
        t.two()
    conv2.run(2)
    for t in conv2.totals[1:2]:
        t.two()
    for t in conv2.totals[0:1]:
        t.three()
    conv2.run(3)
    dh2 = conv2.input_grad() * slope
    dn2 = dh2 * mod_scale
    dxh = dn2 * vector(3)
    dss = []
    for a, b in zip(image_sums(dh2 * n2, member), image_sums(dh2, member)):
        dss += [a, b]
    copies = exchange(1, norm_pieces(dxh, xhat) + [channel_total(dn2 * xhat), channel_total(dn2), bias_2] + dss)
    for t in conv2.totals[2:3]:
        t.two()
    for t in small:
        t.finish()
    total = share_total(stat.at[1], copies)
    sums[5 : 8 + 2 * images, :] = total[2 * images : 4 * images + 3]
    dc1 = norm_back(total, dxh, xhat, scale)
    conv1.start(dc1.astype(bf16))
    bias_1 = channel_total(dc1)
    loads.wait(10, 13, 14)
    conv1.block(0)
    for t in conv2.totals[3:4]:
        t.two()
    for t in conv2.totals[1:3]:
        t.three()
    for t in conv2.totals[0:1]:
        t.four()
    center, scale = rows_in[0], rows_in[1]
    xhat = (x_ref[...].astype(f32) - center) * scale
    slope = silu_slope(xhat * vector(0) + vector(1))
    conv1.run(1)
    for t in conv1.totals[0:1]:
        t.two()
    for t in conv2.totals[3:4]:
        t.three()
    for t in conv2.totals[1:3]:
        t.four()
    conv1.run(2)
    for t in conv1.totals[1:2]:
        t.two()
    for t in conv1.totals[0:1]:
        t.three()
    for t in conv2.totals[3:4]:
        t.four()
    conv1.run(3)
    for t in conv1.totals[2:3]:
        t.two()
    for t in conv1.totals[1:2]:
        t.three()
    dn1 = conv1.input_grad() * slope
    for t in conv1.totals[3:4]:
        t.two()
    dxh = dn1 * vector(0)
    copies = exchange(2, norm_pieces(dxh, xhat) + [channel_total(dn1 * xhat), channel_total(dn1), bias_1])
    for t in conv1.totals[0:1]:
        t.four()
    for t in conv1.totals[2:4]:
        t.three()
    for t in conv1.totals[1:2]:
        t.four()
    own[...] = out_term(z)
    total = share_total(stat.at[2], copies)
    sums[8 + 2 * images : 11 + 2 * images, :] = total[2 * images : 2 * images + 3]
    dfeat[...] = (dx1_ref[...] + norm_back(total, dxh, xhat, scale)).astype(bf16)
    for t in conv1.totals[2:4]:
        t.four()
    for copy in res_copies:
        copy.wait()
    value = own[...]
    for d in range(chan_count - 1):
        value = value + res_recv[d].astype(f32)
    result[...] = (x1_ref[...] + value.reshape(rows, cols, width) + vector(8)).astype(bf16)
    for t in conv2.totals + conv1.totals:
        t.finish()
    if fast:
        back.drain()
    else:
        g_att[...] = part_att[...]
        g_out[...] = part_out[...]
        g_ctx[...] = dctx[...]
    line.drain()
    conv2.drain()
    conv1.drain()


def backward_block(row_count, chan_count, per_group, entries, fast, offset, x, vec, dq, dkv, o, gall, a3_all, x1, c1, rows_in,
                   mod, x9t_1, x9t_2, turn1, turn2, w_att, wo, dctx):
    rows, cols, width = x.shape
    tokens = rows * cols
    images = row_count * rows // IMG_H
    full = chan_count * width
    message = -(-(4 * images + 5) // 8) * 8
    vm = pl.BlockSpec(memory_space=pltpu.VMEM)
    hbm = pl.BlockSpec(memory_space=pl.ANY)
    S = jax.ShapeDtypeStruct
    sem = pltpu.SemaphoreType.DMA
    peers = chan_count - 1
    total_rows = -(-(11 + 2 * images) // 8) * 8
    early = [rows_in, mod, w_att, wo, dctx]
    late = [dq, dkv, o, gall, a3_all, x1, c1, x, x9t_1, x9t_2, turn1, turn2]
    kernel_grad = S((chan_count, 9 * width, width), bf16)
    if fast:
        plane_scratch = [
            *return_scratch(tokens, 2 * width), *total_scratch(3 * full, width), *total_scratch(width, full),
            *total_scratch(*dctx.shape),
        ]
        for _ in range(2 * chan_count):
            plane_scratch += total_scratch(9 * width, width)
    else:
        plane_scratch = [vmem(dkv.shape, dkv.dtype)]
    return pl.pallas_call(
        functools.partial(backward_kernel, row_count, chan_count, per_group, entries, fast),
        name="backward_block",
        out_shape=(
            S((rows, cols, width), bf16), S((rows, cols, width), bf16), S((total_rows, width), f32),
            kernel_grad, kernel_grad, S((3 * full, width), bf16), S((width, full), bf16), S(dctx.shape, bf16),
        ),
        in_specs=[pl.BlockSpec(memory_space=pltpu.SMEM)] + [vm] * (VECTORS + len(early)) + [hbm] * len(late),
        out_specs=(vm,) * 8,
        scratch_shapes=[
            *[vmem(item.shape, item.dtype) for item in late if item is not dkv], sem((15,)),
            vmem(kernel_grad.shape, bf16), vmem(kernel_grad.shape, bf16), vmem((3 * full, width), bf16), vmem((width, full), bf16),
            vmem((tokens, 3 * width), bf16), vmem((rows, cols, width), f32), vmem((tokens, 3 * width), f32),
            vmem((2, chan_count, rows + 2, cols, width), bf16), sem((2, 2)), sem((2, 2)),
            sem((2, 2, peers, PIECES + 2)), sem((2, 2, peers, PIECES + 2)),
            vmem((3, row_count, message, width), f32), sem((3, row_count - 1)), sem((3, row_count - 1)),
            vmem((peers, tokens, width), bf16), vmem((peers, tokens, width), bf16), sem((3, peers)), sem((3, peers)),
            *scatter_scratch(tokens, width, SEGMENTS),
            *plane_scratch,
        ],
        cost_estimate=pl.CostEstimate(flops=12 * 9 * tokens * width * full, bytes_accessed=24 * 2**20, transcendentals=4 * tokens * width),
        compiler_params=pltpu.CompilerParams(collective_id=1, has_side_effects=True, vmem_limit_bytes=60 * 2**20),
    )(offset, *vec, *early, *late)


def finish_kernel(images, share_rows, ctx_count, result_in, dfeat_in, sums, g_conv1, g_conv2, g_att, g_out, g_ctx, emb, context,
                  result, dfeat, conv1, conv2, att, out, emb_w, ctx_w, emb_b, att_b, ctx_b, *vectors):
    width = sums.shape[1]
    result[...] = result_in[...]
    dfeat[...] = dfeat_in[...]
    for j in range(g_conv1.shape[0]):
        conv1[:, pl.ds(j * width, width)] = g_conv1[j].astype(f32)
        conv2[:, pl.ds(j * width, width)] = g_conv2[j].astype(f32)
    out[...] = g_out[...].astype(f32)
    att[...] = g_att[...].astype(f32)
    block = emb.shape[1]
    for t in range(2):
        rows = jnp.concatenate([sums[8 + 2 * i + t : 9 + 2 * i + t, :] for i in range(images)], axis=0)
        high = rows.astype(bf16)
        low = (rows - high.astype(f32)).astype(bf16)
        emb_w[pl.ds(t, block, 2), :] = contract(emb[...], high, 0, 0) + contract(emb[...], low, 0, 0)
    total = None
    for i in range(images):
        term = contract(context[i], g_ctx[pl.ds(i * share_rows, ctx_count), :], 0, 0)
        total = term if total is None else total + term
    for t in range(2):
        ctx_w[pl.ds(t, block, 2), :] = total[:, t * width : (t + 1) * width]

    @pl.when(pl.program_id(0) == 0)
    def _():
        for t in range(2):
            emb_b[t : t + 1, :] = sum(sums[8 + 2 * i + t : 9 + 2 * i + t, :] for i in range(images))
            att_b[t : t + 1, :] = sums[2 + t : 3 + t, :]
            ctx_b[t : t + 1, :] = jnp.sum(g_ctx[:, pl.ds(t * width, width)].astype(f32), axis=0, keepdims=True)
        for ref, i in zip(vectors, (0, 1, 4, 5, 6, 7, 8 + 2 * images, 9 + 2 * images, 10 + 2 * images)):
            ref[...] = sums[i : i + 1, :]


def finish_block(images, share_rows, steps, result, dfeat, sums, g_conv1, g_conv2, g_att, g_out, g_ctx, emb, context):
    width = sums.shape[1]
    depth = emb.shape[1]
    ctx_count = context.shape[1]
    S = jax.ShapeDtypeStruct

    def lead(shape):
        rest = (0,) * (len(shape) - 1)
        return pl.BlockSpec((shape[0] // steps,) + tuple(shape[1:]), lambda s: (s,) + rest)

    def whole(shape):
        return pl.BlockSpec(tuple(shape), lambda s: (0,) * len(shape))

    chan_count, taps_n, _ = g_conv1.shape
    full = chan_count * width
    conv_spec = pl.BlockSpec((chan_count, taps_n // steps, width), lambda s: (0, s, 0))
    shapes = [
        (result.shape, bf16, lead), (dfeat.shape, bf16, lead), ((taps_n, full), f32, lead), ((taps_n, full), f32, lead),
        ((3 * full, width), f32, lead), ((width, full), f32, lead), ((2 * depth, width), f32, lead),
        ((2 * depth, width), f32, lead), ((2, width), f32, whole), ((2, width), f32, whole), ((2, width), f32, whole),
    ] + [((1, width), f32, whole)] * 9
    return pl.pallas_call(
        functools.partial(finish_kernel, images, share_rows, ctx_count),
        name="finish_block",
        grid=(steps,),
        out_shape=tuple(S(shape, dtype) for shape, dtype, _ in shapes),
        in_specs=[
            lead(result.shape), lead(dfeat.shape), whole(sums.shape), conv_spec, conv_spec, lead(g_att.shape),
            lead(g_out.shape), whole(g_ctx.shape), pl.BlockSpec((images, depth // steps), lambda s: (0, s)),
            pl.BlockSpec((images, ctx_count, depth // steps), lambda s: (0, 0, s)),
        ],
        out_specs=tuple(spec(shape) for shape, _, spec in shapes),
        cost_estimate=pl.CostEstimate(flops=4 * images * ctx_count * depth * width, bytes_accessed=16 * 2**20, transcendentals=0),
        compiler_params=pltpu.CompilerParams(vmem_limit_bytes=60 * 2**20),
    )(result, dfeat, sums, g_conv1, g_conv2, g_att, g_out, g_ctx, emb, context)


def local(
    features,
    embedding,
    context,
    image_offset,
    first_gain,
    first_shift,
    conv_first,
    conv_first_bias,
    embed_weight,
    embed_bias,
    second_gain,
    second_shift,
    conv_second,
    conv_second_bias,
    attend_gain,
    attend_shift,
    attend_weight,
    attend_bias,
    context_weight,
    context_bias,
    output_weight,
    output_bias,
    cotangent,
):
    slab_rows, columns, channels = features.shape
    devices, chan = lax.axis_size("rows"), lax.axis_size("chan")
    total_rows = slab_rows * devices
    images = total_rows // IMG_H
    per_group = C // GROUPS
    entries = IMG_H * columns * per_group
    tokens = slab_rows * columns
    context_count = context.shape[1]
    tail = -(-context_count // 256) * 256
    vectors = [
        vector.reshape(1, channels)
        for vector in (first_gain, first_shift, conv_first_bias, second_gain, second_shift, conv_second_bias, attend_gain,
                       attend_shift, output_bias)
    ] + [attend_bias]
    window = min(devices, 2 * (IMG_H // slab_rows) + 1)
    kernel_one = conv_first.reshape(9 * channels, C)
    kernel_two = conv_second.reshape(9 * channels, C)
    attend_kernels = attend_weight.transpose(1, 0, 2)
    fast = devices == 8 and window == devices
    (x9t_one, x9t_two, turn_one, turn_two, middle, inner, attend_blocks, kv_all, grad_blocks, row_stats, queries,
     grad_attended, modulate, context_rows) = forward_block(
        devices, chan, per_group, entries, window, fast, tail, image_offset, features, vectors, embedding, embed_bias,
        context_bias, kernel_one, kernel_two, attend_kernels, cotangent.reshape(tokens, channels), output_weight, context,
        embed_weight.reshape(-1, channels), context_weight.reshape(-1, channels),
    )
    share_rows = -(-context_count // 64) * 64
    attended, query_grad, window_grad, context_part = attend(
        devices, slab_rows, image_offset, queries, grad_attended, kv_all.reshape(window * slab_rows, columns, 2 * channels),
        context_rows, total_rows, IMG_H, context_count, images, share_rows,
    )
    key_value_grad = window_grad.reshape(window, tokens, 2 * channels)
    if not fast:
        pieces, key_value_grad = key_value_grad, jnp.zeros((tokens, 2 * channels), f32)
        for position in range(window):
            shift_by = position - window // 2 if window < devices else None
            piece = pieces[position]
            if shift_by is None:
                piece = jnp.sum(lax.all_to_all(pieces, "rows", 0, 0).astype(f32), axis=0) if position == 0 else 0.0
            elif shift_by != 0:
                piece = from_behind(piece, "rows", shift_by)
            key_value_grad = key_value_grad + (piece if shift_by is None else piece.astype(f32))
    result, features_grad, sums, conv_first_grad, conv_second_grad, attend_grad, output_weight_grad, context_sum = backward_block(
        devices, chan, per_group, entries, fast, image_offset, features, vectors, query_grad, key_value_grad, attended,
        grad_blocks, attend_blocks, inner, middle, row_stats, modulate, x9t_one, x9t_two, turn_one, turn_two, attend_kernels,
        output_weight, context_part,
    )
    if not fast:
        conv_first_grad, conv_second_grad, attend_grad, output_weight_grad, context_sum = lax.psum(
            (conv_first_grad, conv_second_grad, attend_grad, output_weight_grad, context_sum), "rows"
        )
    (result, features_grad, conv_first_grad, conv_second_grad, attend_grad, output_weight_grad, embed_weight_grad,
     context_weight_grad, embed_bias_grad, attend_bias_grad, context_bias_grad, *rest) = finish_block(
        images, share_rows, 2, result, features_grad, sums, conv_first_grad, conv_second_grad, attend_grad,
        output_weight_grad, context_sum, embedding, context,
    )
    (attend_gain_grad, attend_shift_grad, output_bias_grad, second_gain_grad, second_shift_grad, conv_second_bias_grad,
     first_gain_grad, first_shift_grad, conv_first_bias_grad) = [vector.reshape(channels) for vector in rest]
    return (
        result,
        features_grad,
        first_gain_grad,
        first_shift_grad,
        conv_first_grad.reshape(3, 3, channels, C),
        conv_first_bias_grad,
        embed_weight_grad.reshape(-1, 2, channels),
        embed_bias_grad,
        second_gain_grad,
        second_shift_grad,
        conv_second_grad.reshape(3, 3, channels, C),
        conv_second_bias_grad,
        attend_gain_grad,
        attend_shift_grad,
        attend_grad.reshape(3, C, channels).transpose(1, 0, 2),
        attend_bias_grad,
        context_weight_grad.reshape(-1, 2, channels),
        context_bias_grad,
        output_weight_grad,
        output_bias_grad,
    )


def solution(mesh):
    placed = (
        P("rows", None, "chan"),
        P(),
        P(),
        P(),
        P("chan"),
        P("chan"),
        P(None, None, "chan", None),
        P("chan"),
        P(None, None, "chan"),
        P(None, "chan"),
        P("chan"),
        P("chan"),
        P(None, None, "chan", None),
        P("chan"),
        P("chan"),
        P("chan"),
        P(None, None, "chan"),
        P(None, "chan"),
        P(None, None, "chan"),
        P(None, "chan"),
        P("chan", None),
        P("chan"),
        P("rows", None, "chan"),
    )
    return jax.shard_map(
        local,
        mesh=mesh,
        in_specs=placed,
        out_specs=(
            P("rows", None, "chan"),
            P("rows", None, "chan"),
            P("chan"),
            P("chan"),
            P(None, None, "chan", None),
            P("chan"),
            P(None, None, "chan"),
            P(None, "chan"),
            P("chan"),
            P("chan"),
            P(None, None, "chan", None),
            P("chan"),
            P("chan"),
            P("chan"),
            P(None, None, "chan"),
            P(None, "chan"),
            P(None, None, "chan"),
            P(None, "chan"),
            P("chan", None),
            P("chan"),
        ),
        check_vma=False,
    )
```

```python
import functools

import jax
import jax.numpy as jnp
from jax import lax
from jax.experimental import pallas as pl
from jax.experimental.pallas import tpu as pltpu
from jax.sharding import PartitionSpec as P

C = 512
HEAD_DIM = 64
GROUPS = 32
IMG_H = 64


EPSILON = 1e-05
HIGH = lax.Precision.HIGHEST
NEG = -1e30
bf16, f32 = jnp.bfloat16, jnp.float32


def from_behind(block, axis, distance):
    devices = range(lax.axis_size(axis))
    route = [((i - distance) % len(devices), i) for i in devices]
    return lax.ppermute(block, axis, route)


def dot(a, b, ca, cb):
    return lax.dot_general(a, b, (((ca,), (cb,)), ((), ())), preferred_element_type=f32)


def attend_kernel(tiles, tile_rows, cols, width, image_rows, total_rows, ctx_count, images, window, row_count,
                  offset, q_ref, do_ref, kv_ref, ctx_ref,
                  o_ref, dq_ref, dkv_ref, dctx_ref,
                  kv, kt, vt, qt, do_t, s_buf, p_buf, dk, dv, oacc, qacc, sem):
    slab_rows = tiles * tile_rows
    me = lax.axis_index("rows")
    base = (me - window // 2) * slab_rows if window < row_count else 0
    place = lax.rem(me * slab_rows - offset[0] + total_rows, total_rows)
    image_a = place // image_rows
    split = jnp.minimum(slab_rows, image_rows - lax.rem(place, image_rows))
    image_b = lax.rem(image_a + jnp.where(split < slab_rows, 1, 0), images)
    start_a = lax.rem(offset[0] + image_a * image_rows - base + 2 * total_rows, total_rows)
    start_b = lax.rem(offset[0] + image_b * image_rows - base + 2 * total_rows, total_rows)
    ids = (image_a, image_b)
    tq = tile_rows * cols
    main = image_rows * cols
    tail = kv.shape[1] * cols - main
    heads = width // HEAD_DIM
    straddle = split < slab_rows
    group = 8

    def load(img, start):
        @pl.loop(0, image_rows // group)
        def _(j):
            src = lax.rem(start + j * group, total_rows)
            whole = src + group <= total_rows

            @pl.when(whole)
            def _():
                pltpu.make_async_copy(
                    kv_ref.at[pl.ds(src, group)], kv.at[img, pl.ds(j * group, group)], sem.at[img]
                ).start()

            @pl.when(jnp.logical_not(whole))
            def _():
                @pl.loop(0, group)
                def _(i):
                    pltpu.make_async_copy(
                        kv_ref.at[lax.rem(src + i, total_rows)], kv.at[img, j * group + i], sem.at[img]
                    ).start()

    def finish(img, start):
        pltpu.make_async_copy(kv_ref.at[pl.ds(0, image_rows)], kv.at[img, pl.ds(0, image_rows)], sem.at[img]).wait()
        for i in range(tail // cols):
            kv[img, image_rows + i] = ctx_ref[ids[img], pl.ds(i * cols, cols)]
        step = 256 // cols

        @pl.loop(0, kv.shape[1] // step)
        def _(c):
            at = pl.ds(pl.multiple_of(c * 256, 256), 256)
            rows = kv[img, pl.ds(c * step, step)].reshape(256, 2 * width)
            kt[img, :, at] = rows[:, :width].T
            vt[img, :, at] = rows[:, width:].T
        dk[img] = jnp.zeros(dk.shape[1:], f32)
        dv[img] = jnp.zeros(dv.shape[1:], f32)

    load(0, start_a)

    @pl.when(straddle)
    def _():
        load(1, start_b)
    for t in range(tiles):
        qt[t] = (q_ref[pl.ds(t * tq, tq)] * jnp.asarray(HEAD_DIM ** -0.5, bf16)).T
        do_t[t] = do_ref[pl.ds(t * tq, tq)].T
    finish(0, start_a)

    @pl.when(straddle)
    def _():
        finish(1, start_b)

    mixed, cut = split // tile_rows, lax.rem(split, tile_rows)
    count_a = (split + 1) // tile_rows
    first_b = (split + 2) // tile_rows
    count = count_a + jnp.where(straddle, tiles - first_b, 0)
    half_a = jnp.logical_or(cut == 1, cut == 2)
    half_b = jnp.logical_or(cut == 2, cut == 3)
    halves = half_a.astype(jnp.int32) + half_b.astype(jnp.int32)
    first_half = jnp.where(half_a, 0, 1)
    feature = lax.broadcasted_iota(jnp.int32, (width, 1), 0) // HEAD_DIM
    lane_row = lax.broadcasted_iota(jnp.int32, (1, tq), 1) // cols
    tail_ok = lax.broadcasted_iota(jnp.int32, (tail, 1), 0) < ctx_count

    parts = (
        (pl.ds(0, image_rows), pl.ds(0, main), main, False), (pl.ds(image_rows, tail // cols), pl.ds(main, tail), tail, True)
    )

    @pl.loop(0, count)
    def _(item):
        is_b = (item >= count_a).astype(jnp.int32)
        t = jnp.where(is_b == 1, first_b + item - count_a, item)
        row = t * tile_rows + lane_row
        low = jnp.where(is_b == 1, split, 0)
        high = jnp.where(is_b == 1, slab_rows, split)
        mine = jnp.logical_and(row >= low, row < high)
        q_t = qt[t].astype(f32)
        g_t = do_t[t].astype(f32)
        q_h = [jnp.where(feature == h, q_t, 0.0).astype(bf16) for h in range(heads)]

        def rows_of(at, size, cut):
            return kv[is_b, at].reshape(size, 2 * width)[:, cut]

        m = [jnp.full((8, tq), NEG, f32) for _ in range(heads)]
        for blocks, at, size, masked in parts:
            keys = rows_of(blocks, size, slice(0, width))
            for h in range(heads):
                s = dot(keys, q_h[h], 1, 0)
                if masked:
                    s = jnp.where(tail_ok, s, NEG)
                s_buf[h, at] = s
                m[h] = jnp.maximum(m[h], jnp.max(s.reshape(size // 8, 8, tq), axis=0))
        m = [jnp.max(v, axis=0, keepdims=True) for v in m]
        l = [jnp.zeros((8, tq), f32) for _ in range(heads)]
        o = [jnp.zeros((HEAD_DIM, tq), f32) for _ in range(heads)]
        for blocks, at, size, masked in parts:
            for h in range(heads):
                p = jnp.exp(s_buf[h, at] - m[h])
                l[h] = l[h] + jnp.sum(p.reshape(size // 8, 8, tq), axis=0)
                p = p.astype(bf16)
                p_buf[at, pl.ds(h * tq, tq)] = p
                o[h] = o[h] + dot(vt[is_b, pl.ds(h * HEAD_DIM, HEAD_DIM), at], p, 1, 0)
        inv = [1.0 / jnp.sum(v, axis=0, keepdims=True) for v in l]
        o_all = jnp.concatenate([o[h] * inv[h] for h in range(heads)], axis=0)
        do_h, delta = [], []
        for h in range(heads):
            scaled = jnp.where(mine, g_t * inv[h], 0.0)
            scaled = jnp.where(feature == h, scaled, 0.0).astype(bf16)
            do_h.append(scaled)
            delta.append(jnp.sum(scaled.astype(f32) * o_all, axis=0, keepdims=True))
        do_cat = jnp.concatenate(do_h, axis=1)
        q_cat = jnp.concatenate(q_h, axis=1)
        dq = [jnp.zeros((HEAD_DIM, tq), f32) for _ in range(heads)]
        for blocks, at, size, masked in parts:
            vals = rows_of(blocks, size, slice(width, 2 * width))
            ps, dss = [], []
            for h in range(heads):
                dp = dot(vals, do_h[h], 1, 0)
                p = p_buf[at, pl.ds(h * tq, tq)]
                ds = (p.astype(f32) * (dp - delta[h])).astype(bf16)
                dq[h] = dq[h] + dot(kt[is_b, pl.ds(h * HEAD_DIM, HEAD_DIM), at], ds, 1, 0)
                ps.append(p)
                dss.append(ds)
            dv[is_b, at] = dv[is_b, at] + dot(jnp.concatenate(ps, axis=1), do_cat, 1, 1)
            dk[is_b, at] = dk[is_b, at] + dot(jnp.concatenate(dss, axis=1), q_cat, 1, 1)
        oacc[t] = jnp.where(mine, o_all, oacc[t])
        qacc[t] = jnp.where(mine, jnp.concatenate(dq, axis=0) * (HEAD_DIM ** -0.5), qacc[t])

    hq = tq // 2
    lanes = heads * hq
    mine_head = (
        lax.broadcasted_iota(jnp.int32, (width, lanes), 0) // HEAD_DIM == lax.broadcasted_iota(jnp.int32, (width, lanes), 1) // hq
    )
    half_row = lax.rem(lax.broadcasted_iota(jnp.int32, (1, lanes), 1), hq) // cols

    def spread(value):
        return jnp.concatenate([value] * heads, axis=1)

    def diagonal(value):
        return jnp.concatenate(
            [value[h * HEAD_DIM : (h + 1) * HEAD_DIM, h * hq : (h + 1) * hq] for h in range(heads)], axis=0
        )

    @pl.loop(0, halves)
    def _(item):
        is_b = first_half + item
        here = pl.ds(pl.multiple_of(is_b * hq, hq), hq)
        row = mixed * tile_rows + is_b * (tile_rows // 2) + half_row
        low = jnp.where(is_b == 1, split, 0)
        high = jnp.where(is_b == 1, slab_rows, split)
        mine = jnp.logical_and(row >= low, row < high)
        q_b = jnp.where(mine_head, spread(qt[mixed, :, here].astype(f32)), 0.0).astype(bf16)

        def rows_of(at, size, cut):
            return kv[is_b, at].reshape(size, 2 * width)[:, cut]

        def chunk(c):
            return pl.ds(c * (2048 // cols), 2048 // cols), pl.ds(pl.multiple_of(c * 2048, 2048), 2048), 2048, False

        def score(part, m):
            blocks, at, size, masked = part
            s = dot(rows_of(blocks, size, slice(0, width)), q_b, 1, 0)
            if masked:
                s = jnp.where(tail_ok, s, NEG)
            s_buf[0, at] = s
            return jnp.maximum(m, jnp.max(s.reshape(size // 8, 8, lanes), axis=0))

        steps = main // 2048
        m = lax.fori_loop(0, steps, lambda c, m: score(chunk(c), m), jnp.full((8, lanes), NEG, f32))
        m = jnp.max(score(parts[1], m), axis=0, keepdims=True)

        def prob(part, carry):
            blocks, at, size, masked = part
            l, o = carry
            p = jnp.exp(s_buf[0, at] - m)
            l = l + jnp.sum(p.reshape(size // 8, 8, lanes), axis=0)
            p = p.astype(bf16)
            p_buf[at, pl.ds(0, lanes)] = p
            return l, o + dot(vt[is_b, :, at], p, 1, 0)

        carry = (jnp.zeros((8, lanes), f32), jnp.zeros((width, lanes), f32))
        l, o = prob(parts[1], lax.fori_loop(0, steps, lambda c, x: prob(chunk(c), x), carry))
        inv = 1.0 / jnp.sum(l, axis=0, keepdims=True)
        o = o * inv
        do_b = jnp.where(mine_head, spread(do_t[mixed, :, here].astype(f32)), 0.0) * jnp.where(mine, inv, 0.0)
        do_b = do_b.astype(bf16)
        delta = jnp.sum(do_b.astype(f32) * o, axis=0, keepdims=True)

        def back(part, dq):
            blocks, at, size, masked = part
            dp = dot(rows_of(blocks, size, slice(width, 2 * width)), do_b, 1, 0)
            p = p_buf[at, pl.ds(0, lanes)]
            ds = (p.astype(f32) * (dp - delta)).astype(bf16)
            dv[is_b, at] = dv[is_b, at] + dot(p, do_b, 1, 1)
            dk[is_b, at] = dk[is_b, at] + dot(ds, q_b, 1, 1)
            return dq + dot(kt[is_b, :, at], ds, 1, 0)

        dq = back(parts[1], lax.fori_loop(0, steps, lambda c, x: back(chunk(c), x), jnp.zeros((width, lanes), f32)))
        keep = mine[:, :hq]
        oacc[mixed, :, here] = jnp.where(keep, diagonal(o), oacc[mixed, :, here])
        qacc[mixed, :, here] = jnp.where(keep, diagonal(dq) * (HEAD_DIM ** -0.5), qacc[mixed, :, here])

    for t in range(tiles):
        o_ref[pl.ds(t * tq, tq)] = oacc[t].T.astype(bf16)
        dq_ref[pl.ds(t * tq, tq)] = qacc[t].T

    dctx_ref[...] = jnp.zeros(dctx_ref.shape, dctx_ref.dtype)
    share_rows = dctx_ref.shape[0] // images
    if images > 1:
        dkv_ref[...] = jnp.zeros(dkv_ref.shape, dkv_ref.dtype)

    def put(img, start):
        @pl.loop(0, image_rows)
        def _(j):
            row = lax.rem(start + j, total_rows)
            at = pl.ds(pl.multiple_of(j * cols, cols), cols)
            dkv_ref[row, :, :width] = dk[img, at].astype(bf16)
            dkv_ref[row, :, width:] = dv[img, at].astype(bf16)
        at = pl.ds(pl.multiple_of(ids[img] * share_rows, 16), share_rows)
        dctx_ref[at, :width] = dk[img, pl.ds(main, share_rows)].astype(bf16)
        dctx_ref[at, width:] = dv[img, pl.ds(main, share_rows)].astype(bf16)
    put(0, start_a)

    @pl.when(straddle)
    def _():
        put(1, start_b)


def attend(row_count, slab, offset, q, do, kv_window, ctx, total_rows, image_rows, ctx_count, images, share_rows, tile_rows=4):
    tokens, width = q.shape
    rows, cols, _ = kv_window.shape
    tiles = tokens // (tile_rows * cols)
    tq = tile_rows * cols
    tail = ctx.shape[1]
    keys = image_rows * cols + tail
    heads = width // HEAD_DIM
    kern = functools.partial(
        attend_kernel, tiles, tile_rows, cols, width, image_rows, total_rows, ctx_count, images, rows // slab, row_count
    )
    vm = pl.BlockSpec(memory_space=pltpu.VMEM)
    return pl.pallas_call(
        kern, name="attend",
        out_shape=(jax.ShapeDtypeStruct((tokens, width), bf16), jax.ShapeDtypeStruct((tokens, width), f32),
                   jax.ShapeDtypeStruct(kv_window.shape, bf16), jax.ShapeDtypeStruct((images * share_rows, 2 * width), bf16)),
        in_specs=[pl.BlockSpec(memory_space=pltpu.SMEM), vm, vm, pl.BlockSpec(memory_space=pl.ANY), vm],
        out_specs=(vm, vm, vm, vm),
        scratch_shapes=[
            pltpu.VMEM((2, keys // cols, cols, 2 * width), bf16),
            pltpu.VMEM((2, width, keys), bf16), pltpu.VMEM((2, width, keys), bf16),
            pltpu.VMEM((tiles, width, tq), bf16), pltpu.VMEM((tiles, width, tq), bf16),
            pltpu.VMEM((heads, keys, tq), f32), pltpu.VMEM((keys, heads * tq), bf16),
            pltpu.VMEM((2, keys, width), f32), pltpu.VMEM((2, keys, width), f32),
            pltpu.VMEM((tiles, width, tq), f32), pltpu.VMEM((tiles, width, tq), f32),
            pltpu.SemaphoreType.DMA((2,)),
        ],
        cost_estimate=pl.CostEstimate(flops=12 * tokens * keys * width, bytes_accessed=8 * 2**20, transcendentals=heads * tokens * keys),
        compiler_params=pltpu.CompilerParams(vmem_limit_bytes=60 * 2**20),
    )(offset, q, do, kv_window, ctx)


MESH = pl.DeviceIdType.MESH
PIECES = 8
SEGMENTS = 4
VECTORS = 10


def vmem(shape, dtype=f32):
    return pltpu.VMEM(shape, dtype)


def greet(devices):
    barrier = pltpu.get_barrier_semaphore()
    for device in devices:
        pl.semaphore_signal(barrier, inc=1, device_id=device, device_id_type=MESH)
    pl.semaphore_wait(barrier, len(devices))


def row_peers(count):
    r, z = lax.axis_index("rows"), lax.axis_index("chan")
    return [(lax.rem(r + d, count), z) for d in range(1, count)]


def chan_peers(count):
    r, z = lax.axis_index("rows"), lax.axis_index("chan")
    return [(r, lax.rem(z + d, count)) for d in range(1, count)]


def push(src, dst, send_sem, recv_sem, device):
    copy = pltpu.make_async_remote_copy(
        src_ref=src, dst_ref=dst, send_sem=send_sem, recv_sem=recv_sem, device_id=device, device_id_type=MESH
    )
    copy.start()
    return copy


def contract(a, b, a_dim, b_dim):
    return lax.dot_general(a, b, (((a_dim,), (b_dim,)), ((), ())), preferred_element_type=f32)


class Locals:
    def __init__(self, sems):
        self.sems, self.copies, self.done = sems, [], set()

    def start(self, src, dst):
        copy = pltpu.make_async_copy(src, dst, self.sems.at[len(self.copies)])
        copy.start()
        self.copies.append(copy)
        return len(self.copies) - 1

    def wait(self, *which):
        for i in which if which else range(len(self.copies)):
            if i not in self.done:
                self.copies[i].wait()
                self.done.add(i)


def share(buf, sends, recvs, count, pieces):
    me = lax.axis_index("rows")
    for index, piece in enumerate(pieces):
        buf[me, pl.ds(index, 1), :] = piece
    return [push(buf.at[me], buf.at[me], sends.at[d], recvs.at[d], device) for d, device in enumerate(row_peers(count))]


def share_total(buf, copies):
    for copy in copies:
        copy.wait()
    total = buf[0]
    for index in range(1, buf.shape[0]):
        total = total + buf[index]
    return total


def image_masks(offset, first, rows, width, total_rows):
    images = total_rows // IMG_H
    row = first - offset + lax.broadcasted_iota(jnp.int32, (rows, 1, width), 0)
    row = jnp.where(row < 0, row + total_rows, row)
    row = jnp.where(row >= total_rows, row - total_rows, row)
    one, zero = jnp.ones((rows, 1, width), f32), jnp.zeros((rows, 1, width), f32)
    member, upper, lower = [], one, one
    for i in range(images):
        inside = jnp.logical_and(row >= i * IMG_H, row < (i + 1) * IMG_H)
        member.append(jnp.where(inside, one, zero))
        upper = jnp.where(row == i * IMG_H, zero, upper)
        lower = jnp.where(row == (i + 1) * IMG_H - 1, zero, lower)
    return member, upper, lower


def group_sum(values, per_group):
    width = values.shape[1]
    one = lax.broadcasted_iota(jnp.int32, (width, width), 0) // per_group
    two = lax.broadcasted_iota(jnp.int32, (width, width), 1) // per_group
    same = (one == two).astype(f32)
    return jnp.dot(values, same, precision=HIGH, preferred_element_type=f32)


def image_sums(values, member):
    by_row = jnp.sum(values, axis=1, keepdims=True)
    return [jnp.sum(by_row * mask, axis=0) for mask in member]


def to_rows(per_image, member):
    total = None
    for mask, value in zip(member, per_image):
        term = mask * value[None]
        total = term if total is None else total + term
    return total


def norm_images(total, images, entries, per_group):
    grouped = group_sum(total, per_group) * (1.0 / entries)
    centers, scales = [], []
    for i in range(images):
        center = grouped[2 * i : 2 * i + 1]
        square = grouped[2 * i + 1 : 2 * i + 2]
        centers.append(center)
        scales.append(lax.rsqrt(square - center * center + EPSILON))
    return centers, scales


def taps(pad, upper, lower, x9):
    rows, cols, width = pad.shape
    rows = rows - 2
    tokens = rows * cols
    col = lax.rem(lax.broadcasted_iota(jnp.int32, (tokens, 1), 0), cols)
    for a in range(3):
        v = pad[pl.ds(a, rows)].astype(f32)
        if a == 0:
            v = v * upper
        if a == 2:
            v = v * lower
        v = v.reshape(tokens, width)
        left = jnp.where(col == 0, 0.0, pltpu.roll(v, 1, 0))
        right = jnp.where(col == cols - 1, 0.0, pltpu.roll(v, tokens - 1, 0))
        for b, part in enumerate((left, v, right)):
            x9[:, pl.ds((3 * a + b) * width, width)] = part.astype(bf16)


class LineGather:
    def __init__(self, at, pieces, sends, recvs):
        self.at, self.pieces, self.sends, self.recvs = at, pieces, sends, recvs
        self.r, self.z = lax.axis_index("rows"), lax.axis_index("chan")
        self.count = lax.axis_size("chan")

    def copy(self, way, step, piece, shard):
        other = self.z + 1 if way == 0 else self.z - 1
        ref = self.at(shard, piece)
        return pltpu.make_async_remote_copy(
            src_ref=ref, dst_ref=ref, send_sem=self.sends.at[way, step, piece], recv_sem=self.recvs.at[way, step, piece],
            device_id=(self.r, other), device_id_type=MESH,
        )

    def has(self, way, step):
        return self.z >= step if way == 0 else self.z + step < self.count

    def open_end(self, way):
        return self.z + 1 < self.count if way == 0 else self.z >= 1

    def shard(self, way, step):
        return self.z - step if way == 0 else self.z + step

    def run(self, step, pieces=None):
        for piece in range(self.pieces) if pieces is None else pieces:
            for way in range(2):
                if step == 0:
                    @pl.when(self.open_end(way))
                    def _():
                        self.copy(way, 0, piece, self.z).start()
                else:
                    @pl.when(self.has(way, step))
                    def _():
                        shard = self.shard(way, step)
                        self.copy(way, step - 1, piece, shard).wait_recv()
                        if step < self.count - 1:
                            @pl.when(self.open_end(way))
                            def _():
                                self.copy(way, step, piece, shard).start()

    def drain(self):
        for step in range(self.count - 1):
            for way in range(2):
                @pl.when(jnp.logical_and(self.has(way, step), self.open_end(way)))
                def _():
                    for piece in range(self.pieces):
                        self.copy(way, step, piece, self.shard(way, step)).wait_send()


class LineScatter:
    def __init__(self, term, own, out, recv, sends, recvs):
        self.term, self.own, self.out, self.recv, self.sends, self.recvs = term, own, out, recv, sends, recvs
        self.r, self.z = lax.axis_index("rows"), lax.axis_index("chan")
        self.pieces = sends.shape[1]
        self.size = own.shape[0] // self.pieces
        self.end = jnp.logical_or(self.z == 0, self.z == 3)
        self.opposite = lax.rem(self.z + 2, 4)

    def rows(self, piece):
        return pl.ds(piece * self.size, self.size)

    def copy(self, slot, piece, device):
        rows = self.rows(piece)
        return pltpu.make_async_remote_copy(
            src_ref=self.out.at[slot, rows], dst_ref=self.recv.at[slot, rows], send_sem=self.sends.at[slot, piece],
            recv_sem=self.recvs.at[slot, piece], device_id=(self.r, device), device_id_type=MESH,
        )

    def push(self, slot, target, device, piece):
        rows = self.rows(piece)
        self.out[slot, rows] = self.term(target, rows).astype(bf16)
        self.copy(slot, piece, device).start()

    def send(self, piece):
        z = self.z

        @pl.when(self.end)
        def _():
            self.push(3, 3 - z, 1 + z // 3, piece)
            self.push(0, self.opposite, self.opposite, piece)

        @pl.when(z < 3)
        def _():
            self.push(1, z + 1, z + 1, piece)

        @pl.when(z > 0)
        def _():
            self.push(2, z - 1, z - 1, piece)

    def merge(self, piece):
        @pl.when(jnp.logical_not(self.end))
        def _():
            rows = self.rows(piece)
            term = self.term(self.opposite, rows)
            self.copy(3, piece, self.opposite).wait_recv()
            self.out[0, rows] = (term + self.recv[3, rows].astype(f32)).astype(bf16)
            self.copy(0, piece, self.opposite).start()

    def keep(self):
        self.own[...] = self.term(self.z, pl.ds(0, self.own.shape[0]))

    def add(self, slot, piece):
        rows = self.rows(piece)
        self.copy(slot, piece, self.z).wait_recv()
        self.own[rows, :] = self.own[rows, :] + self.recv[slot, rows].astype(f32)

    def finish(self):
        for piece in range(self.pieces):
            @pl.when(self.z > 0)
            def _():
                self.add(1, piece)

            @pl.when(self.z < 3)
            def _():
                self.add(2, piece)
            self.add(0, piece)

    def drain(self):
        for piece in range(self.pieces):
            self.copy(0, piece, self.z).wait_send()

            @pl.when(self.z < 3)
            def _():
                self.copy(1, piece, self.z).wait_send()

            @pl.when(self.z > 0)
            def _():
                self.copy(2, piece, self.z).wait_send()

            @pl.when(self.end)
            def _():
                self.copy(3, piece, self.z).wait_send()


def scatter_scratch(tokens, width, pieces):
    return [
        vmem((tokens, width), f32), vmem((4, tokens, width), bf16), vmem((4, tokens, width), bf16),
        pltpu.SemaphoreType.DMA((4, pieces)), pltpu.SemaphoreType.DMA((4, pieces)),
    ]


def plane():
    r = lax.axis_index("rows")
    core = r + 1 - 2 * lax.rem(r, 2)
    x_dev = r + 2 - 4 * lax.rem(r // 2, 2)
    y_dev = r + 4 - 8 * (r // 4)
    return core, x_dev, y_dev, x_dev + y_dev - r


class PlaneGather:
    def __init__(self, all_ref, sends, recvs):
        self.all, self.sends, self.recvs = all_ref, sends, recvs
        self.r, self.z = lax.axis_index("rows"), lax.axis_index("chan")
        self.core, self.x, self.y, self.d = plane()
        self.size = all_ref.shape[1] // SEGMENTS
        self.copies = [{} for _ in range(SEGMENTS)]

    def part(self, segment, which):
        half = self.size // 2
        if which is None:
            return pl.ds(segment * self.size, self.size)
        return pl.ds(segment * self.size + which * half, half)

    def send(self, segment, i, slab, which, device):
        ref = self.all.at[slab, self.part(segment, which)]
        self.copies[segment][i] = push(ref, ref, self.sends.at[segment, i], self.recvs.at[segment, i], (device, self.z))

    def start(self, s):
        self.send(s, 0, self.r, 0, self.x)
        self.send(s, 1, self.r, 1, self.y)
        self.send(s, 2, self.r, 1, self.x)
        self.send(s, 3, self.r, 0, self.y)
        self.send(s, 4, self.r, None, self.core)

    def relay(self, s):
        copies = self.copies[s]
        copies[0].wait_recv()
        self.send(s, 5, self.x, 0, self.y)
        self.send(s, 6, self.x, 0, self.core)
        copies[1].wait_recv()
        self.send(s, 7, self.y, 1, self.x)
        self.send(s, 8, self.y, 1, self.core)
        copies[2].wait_recv()
        self.send(s, 9, self.x, 1, self.core)
        copies[3].wait_recv()
        self.send(s, 10, self.y, 0, self.core)

    def last(self, s):
        copies = self.copies[s]
        copies[5].wait_recv()
        self.send(s, 11, self.d, 0, self.core)
        copies[7].wait_recv()
        self.send(s, 12, self.d, 1, self.core)

    def done(self, s):
        for i in (4, 6, 8, 9, 10, 11, 12):
            self.copies[s][i].wait_recv()

    def drain(self):
        for copies in self.copies:
            for copy in copies.values():
                copy.wait_send()


class WindowGather:
    def __init__(self, all_ref, sends, recvs):
        self.all, self.sends, self.recvs = all_ref, sends, recvs
        self.size = all_ref.shape[1] // SEGMENTS
        self.copies = [[] for _ in range(SEGMENTS)]

    def start(self, s):
        r, z, count = lax.axis_index("rows"), lax.axis_index("chan"), lax.axis_size("rows")
        window = self.all.shape[0]
        own = window // 2 if window < count else r
        part = pl.ds(s * self.size, self.size)
        for i in range(1, count):
            place = window // 2 - i if i <= window // 2 else window // 2 + count - i
            if window < count and (place < 0 or place >= window):
                continue
            slot = place if window < count else r
            device = (lax.rem(r + i, count), z)
            self.copies[s].append(
                push(self.all.at[own, part], self.all.at[slot, part], self.sends.at[s, i], self.recvs.at[s, i], device)
            )

    def relay(self, s):
        pass

    last = relay

    def done(self, s):
        for copy in self.copies[s]:
            copy.wait_recv()

    def drain(self):
        for copies in self.copies:
            for copy in copies:
                copy.wait_send()


def forward_kernel(row_count, chan_count, per_group, entries, fast, offset, x_ref, *refs):
    vec, refs = refs[:VECTORS], refs[VECTORS:]
    (emb, emb_b, ctx_b, w1_hbm, w2_hbm, att_hbm, g_hbm, wo_hbm, context_hbm, emb_hbm, ctx_hbm,
     x9t_1_hbm, x9t_2_hbm, turn1_hbm, turn2_hbm, c1_hbm, x1_hbm, a3_hbm, all_hbm, gall_hbm, ctx_out, row_ref, q_ref, do_ref,
     mod, ctx_ref,
     w1, w2, w_att, wo, raw, flat, emb_w, ctx_w, wide, x9t_1, x9t_2, turn1, turn2, x1_ref, a3_ref, all_ref, gall_ref, context,
     xpad, cpad, pad, x9, own1, out1, recv1, s1, r1, own2, out2, recv2, s2, r2, stat, stat_s, stat_r, halo_s, halo_r,
     a3_s, a3_r, g_s, g_r, kv_s, kv_r, in_s, out_s) = refs
    rows, cols, width = x_ref.shape
    tokens = rows * cols
    r, z = lax.axis_index("rows"), lax.axis_index("chan")
    loads, stores = Locals(in_s), Locals(out_s)
    for src, dst in ((g_hbm, gall_ref.at[z]), (w1_hbm, w1), (w2_hbm, w2), (att_hbm, w_att), (wo_hbm, wo),
                     (context_hbm, raw), (emb_hbm, emb_w), (ctx_hbm, ctx_w)):
        loads.start(src, dst)
    x = x_ref[...]
    xpad[pl.ds(1, rows)] = x
    greet(row_peers(row_count) + chan_peers(chan_count))
    up = (lax.rem(r + row_count - 1, row_count), z)
    down = (lax.rem(r + 1, row_count), z)

    def rims(phase, ref):
        one = push(ref.at[1], ref.at[rows + 1], halo_s.at[phase, 0], halo_r.at[phase, 0], up)
        two = push(ref.at[rows], ref.at[0], halo_s.at[phase, 1], halo_r.at[phase, 1], down)
        return one, two

    x_rims = rims(0, xpad)
    member, upper, lower = image_masks(offset[0], r * rows - 1, rows + 2, width, row_count * rows)
    images = len(member)
    inner = [mask[1 : rows + 1] for mask in member]
    upper, lower = upper[1 : rows + 1], lower[1 : rows + 1]
    third = -(-tokens // 48) * 16
    g_copies = []
    loads.wait(0)

    def vector(i):
        return vec[i][...][None]

    def stats(phase, values):
        pieces = []
        for a, b in zip(image_sums(values, inner), image_sums(values * values, inner)):
            pieces += [a, b]
        copies = share(stat.at[phase], stat_s.at[phase], stat_r.at[phase], row_count, pieces)
        part = pl.ds(phase * third, min(third, tokens - phase * third))
        for d, device in enumerate(chan_peers(chan_count)):
            g_copies.append(push(gall_ref.at[z, part], gall_ref.at[z, part], g_s.at[phase, d], g_r.at[phase, d], device))
        centers, scales = norm_images(share_total(stat.at[phase], copies), images, entries, per_group)
        row_ref[2 * phase] = to_rows(centers, inner)
        row_ref[2 * phase + 1] = to_rows(scales, inner)
        return centers, scales

    def conv(weight, *scratch):
        def term(j, at):
            return jnp.dot(x9[at, :], weight[:, pl.ds(pl.multiple_of(j * width, width), width)], preferred_element_type=f32)
        line = LineScatter(term, *scratch)
        for piece in range(line.pieces):
            line.send(piece)
        for piece in range(line.pieces):
            line.merge(piece)
        line.keep()
        return line

    def turn(weight, turned):
        for j in range(chan_count):
            for a in range(3):
                turned[j, pl.ds(a * width, width), :] = weight[pl.ds(3 * a * width, 3 * width), pl.ds(j * width, width)].T

    def split(weight):
        wide[...] = weight[...].astype(f32)
        return [wide[pl.ds(t, weight.shape[0] // 2, 2), :].astype(bf16) for t in range(2)]

    centers, scales = stats(0, x.astype(f32))
    for copy in x_rims:
        copy.wait()
    n1 = (xpad[...].astype(f32) - to_rows(centers, member)) * to_rows(scales, member) * vector(0) + vector(1)
    pad[...] = (n1 * jax.nn.sigmoid(n1)).astype(bf16)
    taps(pad, upper, lower, x9)
    loads.wait(1)
    line1 = conv(w1, own1, out1, recv1, s1, r1)
    x9t_1[...] = x9[...].T
    stores.start(x9t_1, x9t_1_hbm)
    turn(w1, turn1)
    stores.start(turn1, turn1_hbm)
    loads.wait(5, 6, 7)
    for t, weight in enumerate(split(emb_w)):
        mod[t] = jnp.dot(emb[...], weight, preferred_element_type=f32) + emb_b[t : t + 1, :]
    ctx_ref[...] = jnp.zeros(ctx_ref.shape, bf16)
    for c in range(flat.shape[0]):
        lanes = pl.ds(c * width, width)
        flat[c] = raw[:, :, lanes].astype(f32).reshape(flat.shape[1:])
        for i in range(images):
            context[i, :, lanes] = flat[c, pl.ds(i, context.shape[1], images), :].astype(bf16)
    stores.start(context, ctx_out)
    for t, weight in enumerate(split(ctx_w)):
        for i in range(images):
            value = jnp.dot(context[i], weight, preferred_element_type=f32) + ctx_b[t : t + 1, :]
            ctx_ref[i, pl.ds(0, context.shape[1]), pl.ds(t * width, width)] = value.astype(bf16)
    line1.finish()
    c1 = own1[...].reshape(rows, cols, width) + vector(2)
    cpad[pl.ds(1, rows)] = c1
    c_rims = rims(1, cpad)
    stores.start(cpad.at[pl.ds(1, rows)], c1_hbm)
    centers, scales = stats(1, c1)
    mod_scale = 1.0 + to_rows([mod[0, i : i + 1, :] for i in range(images)], member)
    mod_shift = to_rows([mod[1, i : i + 1, :] for i in range(images)], member)
    for copy in c_rims:
        copy.wait()
    n2 = (cpad[...] - to_rows(centers, member)) * to_rows(scales, member) * vector(3) + vector(4)
    h2 = n2 * mod_scale + mod_shift
    pad[...] = (h2 * jax.nn.sigmoid(h2)).astype(bf16)
    taps(pad, upper, lower, x9)
    loads.wait(2)
    line2 = conv(w2, own2, out2, recv2, s2, r2)
    x9t_2[...] = x9[...].T
    stores.start(x9t_2, x9t_2_hbm)
    turn(w2, turn2)
    stores.start(turn2, turn2_hbm)
    line1.drain()
    line2.finish()
    x1 = x.astype(f32) + (own2[...].reshape(rows, cols, width) + vector(5))
    x1_ref[...] = x1
    stores.start(x1_ref, x1_hbm)
    centers, scales = stats(2, x1)
    a3 = (x1 - to_rows(centers, inner)) * to_rows(scales, inner) * vector(6) + vector(7)
    a3_ref[z] = a3.astype(bf16).reshape(tokens, width)

    size, per = tokens // PIECES, PIECES // SEGMENTS
    line = LineGather(lambda shard, piece: a3_ref.at[shard, pl.ds(piece * size, size)], PIECES, a3_s, a3_r)
    window = all_ref.shape[0]
    own = window // 2 if window < row_count else r
    gather = (PlaneGather if fast else WindowGather)(all_ref, kv_s, kv_r)
    loads.wait(3, 4)
    weights = [
        jnp.concatenate([w_att[t, pl.ds(i * width, width), :] for t in range(3)], axis=1) for i in range(chan_count)
    ]

    def run(step, segment):
        line.run(step, range(segment * per, (segment + 1) * per))

    def project(segment):
        at = pl.ds(segment * size * per, size * per)
        qkv = None
        for i in range(chan_count):
            term = jnp.dot(a3_ref[i, at], weights[i], preferred_element_type=f32)
            qkv = term if qkv is None else qkv + term
        all_ref[own, at, :width] = qkv[:, width : 2 * width].astype(bf16)
        all_ref[own, at, width:] = (qkv[:, 2 * width :] + vec[9][1:2, :]).astype(bf16)
        gather.start(segment)
        q_ref[at, :] = (qkv[:, :width] + vec[9][0:1, :]).astype(bf16)

    for step, segment in ((0, 0), (0, 1), (1, 0), (0, 2), (2, 0), (1, 1), (0, 3), (3, 0)):
        run(step, segment)
    project(0)
    for step, segment in ((2, 1), (1, 2), (3, 1)):
        run(step, segment)
    project(1)
    gather.relay(0)
    for step, segment in ((2, 2), (1, 3), (3, 2)):
        run(step, segment)
    project(2)
    gather.relay(1)
    gather.last(0)
    for step, segment in ((2, 3), (3, 3)):
        run(step, segment)
    project(3)
    stores.start(a3_ref, a3_hbm)
    gather.relay(2)
    gather.last(1)
    for copy in g_copies:
        copy.wait_recv()
    stores.start(gall_ref, gall_hbm)
    gather.relay(3)
    do = None
    for i in range(chan_count):
        term = contract(gall_ref[i], wo[:, pl.ds(i * width, width)], 1, 1)
        do = term if do is None else do + term
    do_ref[...] = do.astype(bf16)
    gather.last(2)
    gather.last(3)
    for segment in range(SEGMENTS):
        at = pl.ds(segment * size * per, size * per)
        gather.done(segment)
        stores.start(all_ref.at[:, at], all_hbm.at[:, at])
    line2.drain()
    line.drain()
    gather.drain()
    for copy in g_copies:
        copy.wait_send()
    stores.wait()


def forward_block(row_count, chan_count, per_group, entries, window, fast, tail, offset, x, vec, emb, emb_b, ctx_b,
                  w1, w2, w_att, g, wo, context, emb_w, ctx_w):
    rows, cols, width = x.shape
    tokens = rows * cols
    images = row_count * rows // IMG_H
    message = -(-2 * images // 8) * 8
    vm = pl.BlockSpec(memory_space=pltpu.VMEM)
    hbm = pl.BlockSpec(memory_space=pl.ANY)
    S = jax.ShapeDtypeStruct
    sem = pltpu.SemaphoreType.DMA
    peers = chan_count - 1
    full = chan_count * width
    saved = [
        ((9 * width, tokens), bf16), ((9 * width, tokens), bf16),
        ((chan_count, 3 * width, 3 * width), bf16), ((chan_count, 3 * width, 3 * width), bf16),
        ((rows, cols, width), f32), ((rows, cols, width), f32), ((chan_count, tokens, width), bf16),
        ((window, tokens, 2 * width), bf16), ((chan_count, tokens, width), bf16),
        ((images, context.shape[0], context.shape[2]), bf16),
    ]
    small = [
        ((6, rows, 1, width), f32), ((tokens, width), bf16), ((tokens, width), bf16), ((2, images, width), f32),
        ((images, tail, 2 * width), bf16),
    ]
    return pl.pallas_call(
        functools.partial(forward_kernel, row_count, chan_count, per_group, entries, fast),
        name="forward_block",
        out_shape=tuple(S(*item) for item in saved + small),
        in_specs=[pl.BlockSpec(memory_space=pltpu.SMEM)] + [vm] * (4 + VECTORS) + [hbm] * 8,
        out_specs=(hbm,) * len(saved) + (vm,) * len(small),
        scratch_shapes=[
            vmem((9 * width, full), bf16), vmem((9 * width, full), bf16), vmem((3, full, width), bf16), vmem((width, full), bf16),
            vmem(context.shape, bf16), vmem((context.shape[2] // width, context.shape[0] * images, width), f32), vmem(emb_w.shape, bf16), vmem(ctx_w.shape, bf16), vmem(emb_w.shape, f32),
            *[vmem(*item) for i, item in enumerate(saved) if i != 4],
            vmem((rows + 2, cols, width), bf16),
            vmem((rows + 2, cols, width), f32),
            vmem((rows + 2, cols, width), bf16),
            vmem((tokens, 9 * width), bf16),
            *scatter_scratch(tokens, width, 2),
            *scatter_scratch(tokens, width, 2),
            vmem((3, row_count, message, width), f32),
            sem((3, row_count - 1)), sem((3, row_count - 1)),
            sem((2, 2)), sem((2, 2)),
            sem((2, peers, PIECES)), sem((2, peers, PIECES)),
            sem((3, peers)), sem((3, peers)),
            sem((SEGMENTS, max(13, row_count))), sem((SEGMENTS, max(13, row_count))),
            sem((8,)), sem((9 + SEGMENTS,)),
        ],
        cost_estimate=pl.CostEstimate(flops=8 * 9 * tokens * width * full, bytes_accessed=16 * 2**20, transcendentals=4 * tokens * width),
        compiler_params=pltpu.CompilerParams(collective_id=0, has_side_effects=True, vmem_limit_bytes=60 * 2**20),
    )(offset, x, *vec, emb, emb_b, ctx_b, w1, w2, w_att, g, wo, context, emb_w, ctx_w)


class Total:
    def __init__(self, part, out, half, quarters, sends, recvs):
        self.part, self.half, self.quarters, self.out = part, half, quarters, out
        self.sends, self.recvs = sends, recvs
        self.r, self.z = lax.axis_index("rows"), lax.axis_index("chan")
        self.core, self.x, self.y, self.d = plane()
        self.n = part.shape[0] // 8
        self.copies = []

    def rows(self, device):
        return pl.ds(pl.multiple_of((lax.rem(device, 2) * 4 + device // 2) * self.n, 16), self.n)

    def half_rows(self, device):
        return pl.ds(pl.multiple_of(lax.rem(device, 2) * 4 * self.n, 16), 4 * self.n)

    def send(self, i, src, dst, device):
        copy = push(src, dst, self.sends.at[i], self.recvs.at[i], (device, self.z))
        self.copies.append(copy)
        return copy

    def one(self):
        self.a = self.send(0, self.part.at[self.half_rows(self.core)], self.half, self.core)

    def two(self):
        self.a.wait_recv()
        mine = self.half_rows(self.r)
        self.half[...] = (self.part[mine, :].astype(f32) + self.half[...].astype(f32)).astype(bf16)
        self.b = []
        for i, device in enumerate((self.d, self.x, self.y)):
            at = pl.ds(pl.multiple_of((device // 2) * self.n, 16), self.n)
            self.b.append(self.send(1 + i, self.half.at[at], self.quarters.at[i], device))

    def three(self):
        at = pl.ds(pl.multiple_of((self.r // 2) * self.n, 16), self.n)
        total = self.half[at, :].astype(f32)
        for i, copy in enumerate(self.b):
            copy.wait_recv()
            total = total + self.quarters[i].astype(f32)
        mine = self.rows(self.r)
        self.out[mine, :] = total.astype(bf16)
        self.c = []
        for i, device in enumerate((self.d, self.x, self.y, self.core)):
            self.c.append(self.send(4 + i, self.out.at[mine], self.out.at[mine], device))

    def four(self):
        self.e = [self.c[3]]
        for i, device in ((1, self.x), (2, self.y), (0, self.d)):
            self.c[i].wait_recv()
            at = self.rows(device)
            self.e.append(self.send(8 + i, self.out.at[at], self.out.at[at], self.core))

    def finish(self):
        for copy in self.e:
            copy.wait_recv()
        for copy in self.copies:
            copy.wait_send()


def total_scratch(n, width):
    return [vmem((n // 2, width), bf16), vmem((3, n // 8, width), bf16), pltpu.SemaphoreType.DMA((11,)), pltpu.SemaphoreType.DMA((11,))]


class Return:
    def __init__(self, away, parts, cores, out, recv, relay, sends, recvs):
        self.away, self.parts, self.cores, self.out, self.recv, self.relay = away, parts, cores, out, recv, relay
        self.sends, self.recvs = sends, recvs
        self.r, self.z = lax.axis_index("rows"), lax.axis_index("chan")
        self.core, self.x, self.y, self.d = plane()
        self.size = parts.shape[1] // SEGMENTS
        self.copies = [{} for _ in range(SEGMENTS)]

    def at(self, s, which=None):
        half = self.size // 2
        if which is None:
            return pl.ds(s * self.size, self.size)
        return pl.ds(s * self.size + which * half, half)

    def send(self, s, i, src, dst, device):
        self.copies[s][i] = push(src, dst, self.sends.at[s, i], self.recvs.at[s, i], (device, self.z))

    def start(self):
        for s in range(SEGMENTS):
            at = self.at(s)
            for i, device in enumerate((self.d, self.x, self.y, self.r)):
                self.send(s, i, self.away.at[device + self.core - self.r, at], self.cores.at[i, at], self.core)

    def chip(self, i, at):
        return self.parts[i, at].astype(f32) + self.cores[i, at].astype(f32)

    def one(self, s):
        first, second, out, recv = self.at(s, 0), self.at(s, 1), self.out, self.recv
        self.copies[s][0].wait_recv()
        out[0, first] = self.chip(0, first).astype(bf16)
        self.send(s, 4, out.at[0, first], self.relay.at[0, s], self.x)
        out[0, second] = self.chip(0, second).astype(bf16)
        self.send(s, 5, out.at[0, second], self.relay.at[1, s], self.y)
        self.copies[s][1].wait_recv()
        out[1, first] = self.chip(1, first).astype(bf16)
        self.send(s, 6, out.at[1, first], recv.at[0, first], self.x)
        self.copies[s][2].wait_recv()
        out[2, second] = self.chip(2, second).astype(bf16)
        self.send(s, 7, out.at[2, second], recv.at[1, second], self.y)

    def two(self, s):
        first, second, out, recv = self.at(s, 0), self.at(s, 1), self.out, self.recv
        self.copies[s][4].wait_recv()
        out[2, first] = (self.chip(2, first) + self.relay[0, s].astype(f32)).astype(bf16)
        self.send(s, 8, out.at[2, first], recv.at[1, first], self.y)
        self.copies[s][5].wait_recv()
        out[1, second] = (self.chip(1, second) + self.relay[1, s].astype(f32)).astype(bf16)
        self.send(s, 9, out.at[1, second], recv.at[0, second], self.x)

    def three(self, s):
        at = self.at(s)
        for i in (3, 6, 7, 8, 9):
            self.copies[s][i].wait_recv()
        return self.chip(3, at) + self.recv[0, at].astype(f32) + self.recv[1, at].astype(f32)

    def drain(self):
        for copies in self.copies:
            for copy in copies.values():
                copy.wait_send()


def return_scratch(tokens, width):
    shape = (tokens, width)
    sem = pltpu.SemaphoreType.DMA((SEGMENTS, 10))
    return [
        vmem((4, *shape), bf16), vmem((4, *shape), bf16), vmem((3, *shape), bf16), vmem((2, *shape), bf16),
        vmem((2, SEGMENTS, tokens // (2 * SEGMENTS), width), bf16), sem, sem,
    ]


class ConvBack:
    def __init__(self, pad, acc, x9t, turned, parts, outs, totals, up, down, halo_s, halo_r, sends, recvs, upper, lower):
        self.pad, self.acc, self.x9t, self.turned, self.parts, self.outs = pad, acc, x9t, turned, parts, outs
        self.totals, self.up, self.down, self.halo_s, self.halo_r = totals, up, down, halo_s, halo_r
        self.upper, self.lower = upper, lower
        _, self.rows, self.cols, self.width = pad.shape
        self.rows -= 2
        self.tokens = self.rows * self.cols
        self.size = self.rows // PIECES
        self.line = LineGather(self.at, PIECES + 2, sends, recvs)
        z = lax.axis_index("chan")
        low = z < 2
        self.order = (z, z + 1 - 2 * lax.rem(z, 2), jnp.where(low, 2, 1), jnp.where(low, 3, 0))
        self.later = []

    def at(self, shard, piece):
        if piece < PIECES:
            return self.pad.at[shard, pl.ds(1 + piece * self.size, self.size)]
        return self.pad.at[shard, pl.ds(0 if piece == PIECES else self.rows + 1, 1)]

    def start(self, values):
        pad, rows, z = self.pad, self.rows, lax.axis_index("chan")
        pad[z, pl.ds(1, rows)] = values
        self.rims = [
            push(pad.at[z, 1], pad.at[z, rows + 1], self.halo_s.at[0], self.halo_r.at[0], self.up),
            push(pad.at[z, rows], pad.at[z, 0], self.halo_s.at[1], self.halo_r.at[1], self.down),
        ]
        self.line.run(0, range(PIECES))
        for copy in self.rims:
            copy.wait_recv()
        self.line.run(0, (PIECES, PIECES + 1))

    def block(self, step):
        j, rows, tokens, width = self.order[step], self.rows, self.tokens, self.width
        parts = []
        for a, mask in enumerate((self.lower, None, self.upper)):
            part = self.pad[j, pl.ds(2 - a, rows)]
            if mask is not None:
                part = (part.astype(f32) * mask).astype(bf16)
            parts.append(part.reshape(tokens, width))
        self.parts[step] = jnp.dot(self.x9t[...], parts[1], preferred_element_type=f32).astype(bf16)
        if self.totals:
            self.totals[step].one()
        else:
            self.outs[j] = self.parts[step]
        term = jnp.dot(jnp.concatenate(parts, axis=1), self.turned[j], preferred_element_type=f32)
        self.acc[...] = term if step == 0 else self.acc[...] + term

    def run(self, step):
        self.line.run(step)
        self.block(step)

    def input_grad(self):
        total, width, cols, tokens = self.acc[...], self.width, self.cols, self.tokens
        col = lax.rem(lax.broadcasted_iota(jnp.int32, (tokens, 1), 0), cols)
        before = jnp.where(col == cols - 1, 0.0, pltpu.roll(total[:, :width], tokens - 1, 0))
        after = jnp.where(col == 0, 0.0, pltpu.roll(total[:, 2 * width :], 1, 0))
        return (before + total[:, width : 2 * width] + after).reshape(self.rows, cols, width)

    def drain(self):
        for copy in self.rims:
            copy.wait_send()
        self.line.drain()


def silu_slope(values):
    gate = jax.nn.sigmoid(values)
    return gate * (1.0 + values * (1.0 - gate))


def channel_total(values):
    return jnp.sum(jnp.sum(values, axis=1, keepdims=True), axis=0)


def backward_kernel(row_count, chan_count, per_group, entries, fast, offset, *refs):
    vec, refs = refs[:VECTORS], refs[VECTORS:]
    (rows_in, mod, w_att, wo, dctx,
     dq_hbm, dkv_hbm, o_hbm, gall_hbm, a3_hbm, x1_hbm, c1_hbm, x_hbm, x9t_1_hbm, x9t_2_hbm, turn1_hbm, turn2_hbm,
     result, dfeat, sums, g_conv1, g_conv2, g_att, g_out, g_ctx,
     dq_ref, o_ref, gall, a3_all, x1_ref, c1_ref, x_ref, x9t_1, x9t_2, turn1, turn2, load_s,
     part1, part2, part_att, part_out, d3, dx1_ref, acc, gpad, halo_s, halo_r, zh_s, zh_r, stat, stat_s, stat_r,
     res_out, res_recv, res_s, res_r, own, da3_out, da3_recv, da3_s, da3_r) = refs[:61]
    refs = refs[61:]
    rows, cols, width = x_ref.shape
    tokens = rows * cols
    r, z = lax.axis_index("rows"), lax.axis_index("chan")
    loads = Locals(load_s)
    greet(row_peers(row_count) + chan_peers(chan_count))
    if fast:
        back = Return(dkv_hbm, *refs[:7])
        back.start()
        for i, device in enumerate((back.d, back.x, back.y, r)):
            loads.start(dkv_hbm.at[device], back.parts.at[i])
        pairs = iter(range(7, len(refs), 4))

        def total(part, out):
            i = next(pairs)
            return Total(part, out, *refs[i : i + 4])
        small = [total(part_att, g_att), total(part_out, g_out), total(dctx, g_ctx)]
    else:
        for i in range(4):
            loads.start(dkv_hbm.at[pl.ds(i * (tokens // 4), tokens // 4)], refs[0].at[pl.ds(i * (tokens // 4), tokens // 4)])
        small = []
    for src, dst in (
        (dq_hbm, dq_ref), (o_hbm, o_ref), (gall_hbm, gall), (a3_hbm, a3_all), (x1_hbm, x1_ref), (c1_hbm, c1_ref), (x_hbm, x_ref),
        (x9t_2_hbm, x9t_2), (turn2_hbm, turn2), (x9t_1_hbm, x9t_1), (turn1_hbm, turn1),
    ):
        loads.start(src, dst)
    member, upper, lower = image_masks(offset[0], r * rows, rows, width, row_count * rows)
    images = len(member)
    up = (lax.rem(r + row_count - 1, row_count), z)
    down = (lax.rem(r + 1, row_count), z)
    orders = []
    for index, (x9t, turned, parts, outs) in enumerate(((x9t_2, turn2, part2, g_conv2), (x9t_1, turn1, part1, g_conv1))):
        conv = ConvBack(
            gpad.at[index], acc, x9t, turned, parts, outs, [], up, down, halo_s.at[index], halo_r.at[index],
            zh_s.at[index], zh_r.at[index], upper, lower,
        )
        if fast:
            conv.totals = [total(parts.at[step], outs.at[conv.order[step]]) for step in range(chan_count)]
        orders.append(conv)
    conv2, conv1 = orders
    third = -(-tokens // 48) * 16
    res_copies = []

    def vector(i):
        return vec[i][...][None]

    def exchange(phase, pieces):
        copies = share(stat.at[phase], stat_s.at[phase], stat_r.at[phase], row_count, pieces)
        part = pl.ds(phase * third, min(third, tokens - phase * third))
        for d, device in enumerate(chan_peers(chan_count)):
            res_copies.append(push(res_out.at[d, part], res_recv.at[d, part], res_s.at[phase, d], res_r.at[phase, d], device))
        return copies

    def norm_pieces(dxh, xhat):
        pieces = []
        for a, b in zip(image_sums(dxh, member), image_sums(dxh * xhat, member)):
            pieces += [a, b]
        return pieces

    def norm_back(total, dxh, xhat, scale):
        grouped = group_sum(total[: 2 * images], per_group) * (1.0 / entries)
        first = to_rows([grouped[2 * i : 2 * i + 1] for i in range(images)], member)
        second = to_rows([grouped[2 * i + 1 : 2 * i + 2] for i in range(images)], member)
        return scale * (dxh - first - xhat * second)

    def out_term(j):
        return jnp.dot(o_ref[...], wo[:, pl.ds(pl.multiple_of(j * width, width), width)], preferred_element_type=f32)

    def att_rows(j):
        at = pl.ds(pl.multiple_of(j * width, width), width)
        return jnp.concatenate([w_att[t, at, :] for t in range(3)], axis=1)

    line = LineScatter(lambda j, at: contract(d3[at, :], att_rows(j), 1, 1), own, da3_out, da3_recv, da3_s, da3_r)
    size = tokens // SEGMENTS
    bias_v = jnp.zeros((1, width), f32)
    loads.wait(4)
    if fast:
        loads.wait(0, 1, 2, 3)
        for s in range(SEGMENTS + 2):
            if s < SEGMENTS:
                back.one(s)
            if s == 0:
                loads.wait(5, 6)
                for d, device in enumerate(chan_peers(chan_count)):
                    res_out[d] = out_term(device[1]).astype(bf16)
            if 1 <= s <= SEGMENTS:
                back.two(s - 1)
            if s >= 2:
                at = pl.ds((s - 2) * size, size)
                dkv = back.three(s - 2)
                d3[at, :width] = dq_ref[at, :].astype(bf16)
                d3[at, width:] = dkv.astype(bf16)
                bias_v = bias_v + jnp.sum(dkv[:, width:], axis=0, keepdims=True)
                line.send(s - 2)
            if s >= 3:
                line.merge(s - 3)
        line.merge(SEGMENTS - 1)
    else:
        loads.wait(0, 1, 2, 3, 5, 6)
        for d, device in enumerate(chan_peers(chan_count)):
            res_out[d] = out_term(device[1]).astype(bf16)
        for s in range(SEGMENTS + 1):
            if s < SEGMENTS:
                at = pl.ds(s * size, size)
                dkv = refs[0][at, :]
                d3[at, :width] = dq_ref[at, :].astype(bf16)
                d3[at, width:] = dkv.astype(bf16)
                bias_v = bias_v + jnp.sum(dkv[:, width:], axis=0, keepdims=True)
                line.send(s)
            if s >= 1:
                line.merge(s - 1)
    line.keep()
    bias_q = jnp.sum(dq_ref[...], axis=0, keepdims=True)
    loads.wait(7)
    for i in range(chan_count):
        grad = contract(a3_all[i], d3[...], 0, 0).astype(bf16)
        for t in range(3):
            part_att[pl.ds((t * chan_count + i) * width, width), :] = grad[:, t * width : (t + 1) * width]
    g_cat = jnp.concatenate([gall[i] for i in range(chan_count)], axis=1)
    part_out[...] = contract(o_ref[...], g_cat, 0, 0).astype(bf16)
    for t in small:
        t.one()
    loads.wait(8)
    x1 = x1_ref[...]
    g = gall[z].astype(f32).reshape(rows, cols, width)
    center, scale = rows_in[4], rows_in[5]
    xhat = (x1 - center) * scale
    bias_g = channel_total(g)
    for t in small:
        t.two()
    line.finish()
    da3 = own[...].reshape(rows, cols, width)
    dxh = da3 * vector(6)
    copies = exchange(
        0, norm_pieces(dxh, xhat) + [channel_total(da3 * xhat), channel_total(da3), bias_q, bias_v, bias_g]
    )
    for t in small:
        t.three()
    total = share_total(stat.at[0], copies)
    sums[0:5, :] = total[2 * images : 2 * images + 5]
    dx1 = g + norm_back(total, dxh, xhat, scale)
    conv2.start(dx1.astype(bf16))
    dx1_ref[...] = dx1
    bias_2 = channel_total(dx1)
    loads.wait(9, 11, 12)
    conv2.block(0)
    for t in small:
        t.four()
    center, scale = rows_in[2], rows_in[3]
    xhat = (c1_ref[...] - center) * scale
    n2 = xhat * vector(3) + vector(4)
    mod_scale = 1.0 + to_rows([mod[0, i : i + 1, :] for i in range(images)], member)
    mod_shift = to_rows([mod[1, i : i + 1, :] for i in range(images)], member)
    slope = silu_slope(n2 * mod_scale + mod_shift)
    conv2.run(1)
    for t in conv2.totals[0:1]:
        t.two()
    conv2.run(2)
    for t in conv2.totals[1:2]:
        t.two()
    for t in conv2.totals[0:1]:
        t.three()
    conv2.run(3)
    dh2 = conv2.input_grad() * slope
    dn2 = dh2 * mod_scale
    dxh = dn2 * vector(3)
    dss = []
    for a, b in zip(image_sums(dh2 * n2, member), image_sums(dh2, member)):
        dss += [a, b]
    copies = exchange(1, norm_pieces(dxh, xhat) + [channel_total(dn2 * xhat), channel_total(dn2), bias_2] + dss)
    for t in conv2.totals[2:3]:
        t.two()
    for t in small:
        t.finish()
    total = share_total(stat.at[1], copies)
    sums[5 : 8 + 2 * images, :] = total[2 * images : 4 * images + 3]
    dc1 = norm_back(total, dxh, xhat, scale)
    conv1.start(dc1.astype(bf16))
    bias_1 = channel_total(dc1)
    loads.wait(10, 13, 14)
    conv1.block(0)
    for t in conv2.totals[3:4]:
        t.two()
    for t in conv2.totals[1:3]:
        t.three()
    for t in conv2.totals[0:1]:
        t.four()
    center, scale = rows_in[0], rows_in[1]
    xhat = (x_ref[...].astype(f32) - center) * scale
    slope = silu_slope(xhat * vector(0) + vector(1))
    conv1.run(1)
    for t in conv1.totals[0:1]:
        t.two()
    for t in conv2.totals[3:4]:
        t.three()
    for t in conv2.totals[1:3]:
        t.four()
    conv1.run(2)
    for t in conv1.totals[1:2]:
        t.two()
    for t in conv1.totals[0:1]:
        t.three()
    for t in conv2.totals[3:4]:
        t.four()
    conv1.run(3)
    for t in conv1.totals[2:3]:
        t.two()
    for t in conv1.totals[1:2]:
        t.three()
    dn1 = conv1.input_grad() * slope
    for t in conv1.totals[3:4]:
        t.two()
    dxh = dn1 * vector(0)
    copies = exchange(2, norm_pieces(dxh, xhat) + [channel_total(dn1 * xhat), channel_total(dn1), bias_1])
    for t in conv1.totals[0:1]:
        t.four()
    for t in conv1.totals[2:4]:
        t.three()
    for t in conv1.totals[1:2]:
        t.four()
    own[...] = out_term(z)
    total = share_total(stat.at[2], copies)
    sums[8 + 2 * images : 11 + 2 * images, :] = total[2 * images : 2 * images + 3]
    dfeat[...] = (dx1_ref[...] + norm_back(total, dxh, xhat, scale)).astype(bf16)
    for t in conv1.totals[2:4]:
        t.four()
    for copy in res_copies:
        copy.wait()
    value = own[...]
    for d in range(chan_count - 1):
        value = value + res_recv[d].astype(f32)
    result[...] = (x1_ref[...] + value.reshape(rows, cols, width) + vector(8)).astype(bf16)
    for t in conv2.totals + conv1.totals:
        t.finish()
    if fast:
        back.drain()
    else:
        g_att[...] = part_att[...]
        g_out[...] = part_out[...]
        g_ctx[...] = dctx[...]
    line.drain()
    conv2.drain()
    conv1.drain()


def backward_block(row_count, chan_count, per_group, entries, fast, offset, x, vec, dq, dkv, o, gall, a3_all, x1, c1, rows_in,
                   mod, x9t_1, x9t_2, turn1, turn2, w_att, wo, dctx):
    rows, cols, width = x.shape
    tokens = rows * cols
    images = row_count * rows // IMG_H
    full = chan_count * width
    message = -(-(4 * images + 5) // 8) * 8
    vm = pl.BlockSpec(memory_space=pltpu.VMEM)
    hbm = pl.BlockSpec(memory_space=pl.ANY)
    S = jax.ShapeDtypeStruct
    sem = pltpu.SemaphoreType.DMA
    peers = chan_count - 1
    total_rows = -(-(11 + 2 * images) // 8) * 8
    early = [rows_in, mod, w_att, wo, dctx]
    late = [dq, dkv, o, gall, a3_all, x1, c1, x, x9t_1, x9t_2, turn1, turn2]
    kernel_grad = S((chan_count, 9 * width, width), bf16)
    if fast:
        plane_scratch = [
            *return_scratch(tokens, 2 * width), *total_scratch(3 * full, width), *total_scratch(width, full),
            *total_scratch(*dctx.shape),
        ]
        for _ in range(2 * chan_count):
            plane_scratch += total_scratch(9 * width, width)
    else:
        plane_scratch = [vmem(dkv.shape, dkv.dtype)]
    return pl.pallas_call(
        functools.partial(backward_kernel, row_count, chan_count, per_group, entries, fast),
        name="backward_block",
        out_shape=(
            S((rows, cols, width), bf16), S((rows, cols, width), bf16), S((total_rows, width), f32),
            kernel_grad, kernel_grad, S((3 * full, width), bf16), S((width, full), bf16), S(dctx.shape, bf16),
        ),
        in_specs=[pl.BlockSpec(memory_space=pltpu.SMEM)] + [vm] * (VECTORS + len(early)) + [hbm] * len(late),
        out_specs=(vm,) * 8,
        scratch_shapes=[
            *[vmem(item.shape, item.dtype) for item in late if item is not dkv], sem((15,)),
            vmem(kernel_grad.shape, bf16), vmem(kernel_grad.shape, bf16), vmem((3 * full, width), bf16), vmem((width, full), bf16),
            vmem((tokens, 3 * width), bf16), vmem((rows, cols, width), f32), vmem((tokens, 3 * width), f32),
            vmem((2, chan_count, rows + 2, cols, width), bf16), sem((2, 2)), sem((2, 2)),
            sem((2, 2, peers, PIECES + 2)), sem((2, 2, peers, PIECES + 2)),
            vmem((3, row_count, message, width), f32), sem((3, row_count - 1)), sem((3, row_count - 1)),
            vmem((peers, tokens, width), bf16), vmem((peers, tokens, width), bf16), sem((3, peers)), sem((3, peers)),
            *scatter_scratch(tokens, width, SEGMENTS),
            *plane_scratch,
        ],
        cost_estimate=pl.CostEstimate(flops=12 * 9 * tokens * width * full, bytes_accessed=24 * 2**20, transcendentals=4 * tokens * width),
        compiler_params=pltpu.CompilerParams(collective_id=1, has_side_effects=True, vmem_limit_bytes=60 * 2**20),
    )(offset, *vec, *early, *late)


def finish_kernel(images, share_rows, ctx_count, result_in, dfeat_in, sums, g_conv1, g_conv2, g_att, g_out, g_ctx, emb, context,
                  result, dfeat, conv1, conv2, att, out, emb_w, ctx_w, emb_b, att_b, ctx_b, *vectors):
    width = sums.shape[1]
    result[...] = result_in[...]
    dfeat[...] = dfeat_in[...]
    for j in range(g_conv1.shape[0]):
        conv1[:, pl.ds(j * width, width)] = g_conv1[j].astype(f32)
        conv2[:, pl.ds(j * width, width)] = g_conv2[j].astype(f32)
    out[...] = g_out[...].astype(f32)
    att[...] = g_att[...].astype(f32)
    block = emb.shape[1]
    for t in range(2):
        rows = jnp.concatenate([sums[8 + 2 * i + t : 9 + 2 * i + t, :] for i in range(images)], axis=0)
        high = rows.astype(bf16)
        low = (rows - high.astype(f32)).astype(bf16)
        emb_w[pl.ds(t, block, 2), :] = contract(emb[...], high, 0, 0) + contract(emb[...], low, 0, 0)
    total = None
    for i in range(images):
        term = contract(context[i], g_ctx[pl.ds(i * share_rows, ctx_count), :], 0, 0)
        total = term if total is None else total + term
    for t in range(2):
        ctx_w[pl.ds(t, block, 2), :] = total[:, t * width : (t + 1) * width]

    @pl.when(pl.program_id(0) == 0)
    def _():
        for t in range(2):
            emb_b[t : t + 1, :] = sum(sums[8 + 2 * i + t : 9 + 2 * i + t, :] for i in range(images))
            att_b[t : t + 1, :] = sums[2 + t : 3 + t, :]
            ctx_b[t : t + 1, :] = jnp.sum(g_ctx[:, pl.ds(t * width, width)].astype(f32), axis=0, keepdims=True)
        for ref, i in zip(vectors, (0, 1, 4, 5, 6, 7, 8 + 2 * images, 9 + 2 * images, 10 + 2 * images)):
            ref[...] = sums[i : i + 1, :]


def finish_block(images, share_rows, steps, result, dfeat, sums, g_conv1, g_conv2, g_att, g_out, g_ctx, emb, context):
    width = sums.shape[1]
    depth = emb.shape[1]
    ctx_count = context.shape[1]
    S = jax.ShapeDtypeStruct

    def lead(shape):
        rest = (0,) * (len(shape) - 1)
        return pl.BlockSpec((shape[0] // steps,) + tuple(shape[1:]), lambda s: (s,) + rest)

    def whole(shape):
        return pl.BlockSpec(tuple(shape), lambda s: (0,) * len(shape))

    chan_count, taps_n, _ = g_conv1.shape
    full = chan_count * width
    conv_spec = pl.BlockSpec((chan_count, taps_n // steps, width), lambda s: (0, s, 0))
    shapes = [
        (result.shape, bf16, lead), (dfeat.shape, bf16, lead), ((taps_n, full), f32, lead), ((taps_n, full), f32, lead),
        ((3 * full, width), f32, lead), ((width, full), f32, lead), ((2 * depth, width), f32, lead),
        ((2 * depth, width), f32, lead), ((2, width), f32, whole), ((2, width), f32, whole), ((2, width), f32, whole),
    ] + [((1, width), f32, whole)] * 9
    return pl.pallas_call(
        functools.partial(finish_kernel, images, share_rows, ctx_count),
        name="finish_block",
        grid=(steps,),
        out_shape=tuple(S(shape, dtype) for shape, dtype, _ in shapes),
        in_specs=[
            lead(result.shape), lead(dfeat.shape), whole(sums.shape), conv_spec, conv_spec, lead(g_att.shape),
            lead(g_out.shape), whole(g_ctx.shape), pl.BlockSpec((images, depth // steps), lambda s: (0, s)),
            pl.BlockSpec((images, ctx_count, depth // steps), lambda s: (0, 0, s)),
        ],
        out_specs=tuple(spec(shape) for shape, _, spec in shapes),
        cost_estimate=pl.CostEstimate(flops=4 * images * ctx_count * depth * width, bytes_accessed=16 * 2**20, transcendentals=0),
        compiler_params=pltpu.CompilerParams(vmem_limit_bytes=60 * 2**20),
    )(result, dfeat, sums, g_conv1, g_conv2, g_att, g_out, g_ctx, emb, context)


def local(
    features,
    embedding,
    context,
    image_offset,
    first_gain,
    first_shift,
    conv_first,
    conv_first_bias,
    embed_weight,
    embed_bias,
    second_gain,
    second_shift,
    conv_second,
    conv_second_bias,
    attend_gain,
    attend_shift,
    attend_weight,
    attend_bias,
    context_weight,
    context_bias,
    output_weight,
    output_bias,
    cotangent,
):
    slab_rows, columns, channels = features.shape
    devices, chan = lax.axis_size("rows"), lax.axis_size("chan")
    total_rows = slab_rows * devices
    images = total_rows // IMG_H
    per_group = C // GROUPS
    entries = IMG_H * columns * per_group
    tokens = slab_rows * columns
    context_count = context.shape[1]
    tail = -(-context_count // 256) * 256
    vectors = [
        vector.reshape(1, channels)
        for vector in (first_gain, first_shift, conv_first_bias, second_gain, second_shift, conv_second_bias, attend_gain,
                       attend_shift, output_bias)
    ] + [attend_bias]
    window = min(devices, 2 * (IMG_H // slab_rows) + 1)
    kernel_one = conv_first.reshape(9 * channels, C)
    kernel_two = conv_second.reshape(9 * channels, C)
    attend_kernels = attend_weight.transpose(1, 0, 2)
    fast = devices == 8 and window == devices
    (x9t_one, x9t_two, turn_one, turn_two, middle, inner, attend_blocks, kv_all, grad_blocks, context_own, row_stats, queries,
     grad_attended, modulate, context_rows) = forward_block(
        devices, chan, per_group, entries, window, fast, tail, image_offset, features, vectors, embedding, embed_bias,
        context_bias, kernel_one, kernel_two, attend_kernels, cotangent.reshape(tokens, channels), output_weight, context.transpose(1, 0, 2),
        embed_weight.reshape(-1, channels), context_weight.reshape(-1, channels),
    )
    share_rows = -(-context_count // 64) * 64
    attended, query_grad, window_grad, context_part = attend(
        devices, slab_rows, image_offset, queries, grad_attended, kv_all.reshape(window * slab_rows, columns, 2 * channels),
        context_rows, total_rows, IMG_H, context_count, images, share_rows,
    )
    key_value_grad = window_grad.reshape(window, tokens, 2 * channels)
    if not fast:
        pieces, key_value_grad = key_value_grad, jnp.zeros((tokens, 2 * channels), f32)
        for position in range(window):
            shift_by = position - window // 2 if window < devices else None
            piece = pieces[position]
            if shift_by is None:
                piece = jnp.sum(lax.all_to_all(pieces, "rows", 0, 0).astype(f32), axis=0) if position == 0 else 0.0
            elif shift_by != 0:
                piece = from_behind(piece, "rows", shift_by)
            key_value_grad = key_value_grad + (piece if shift_by is None else piece.astype(f32))
    result, features_grad, sums, conv_first_grad, conv_second_grad, attend_grad, output_weight_grad, context_sum = backward_block(
        devices, chan, per_group, entries, fast, image_offset, features, vectors, query_grad, key_value_grad, attended,
        grad_blocks, attend_blocks, inner, middle, row_stats, modulate, x9t_one, x9t_two, turn_one, turn_two, attend_kernels,
        output_weight, context_part,
    )
    if not fast:
        conv_first_grad, conv_second_grad, attend_grad, output_weight_grad, context_sum = lax.psum(
            (conv_first_grad, conv_second_grad, attend_grad, output_weight_grad, context_sum), "rows"
        )
    (result, features_grad, conv_first_grad, conv_second_grad, attend_grad, output_weight_grad, embed_weight_grad,
     context_weight_grad, embed_bias_grad, attend_bias_grad, context_bias_grad, *rest) = finish_block(
        images, share_rows, 2, result, features_grad, sums, conv_first_grad, conv_second_grad, attend_grad,
        output_weight_grad, context_sum, embedding, context_own,
    )
    (attend_gain_grad, attend_shift_grad, output_bias_grad, second_gain_grad, second_shift_grad, conv_second_bias_grad,
     first_gain_grad, first_shift_grad, conv_first_bias_grad) = [vector.reshape(channels) for vector in rest]
    return (
        result,
        features_grad,
        first_gain_grad,
        first_shift_grad,
        conv_first_grad.reshape(3, 3, channels, C),
        conv_first_bias_grad,
        embed_weight_grad.reshape(-1, 2, channels),
        embed_bias_grad,
        second_gain_grad,
        second_shift_grad,
        conv_second_grad.reshape(3, 3, channels, C),
        conv_second_bias_grad,
        attend_gain_grad,
        attend_shift_grad,
        attend_grad.reshape(3, C, channels).transpose(1, 0, 2),
        attend_bias_grad,
        context_weight_grad.reshape(-1, 2, channels),
        context_bias_grad,
        output_weight_grad,
        output_bias_grad,
    )


def solution(mesh):
    placed = (
        P("rows", None, "chan"),
        P(),
        P(),
        P(),
        P("chan"),
        P("chan"),
        P(None, None, "chan", None),
        P("chan"),
        P(None, None, "chan"),
        P(None, "chan"),
        P("chan"),
        P("chan"),
        P(None, None, "chan", None),
        P("chan"),
        P("chan"),
        P("chan"),
        P(None, None, "chan"),
        P(None, "chan"),
        P(None, None, "chan"),
        P(None, "chan"),
        P("chan", None),
        P("chan"),
        P("rows", None, "chan"),
    )
    return jax.shard_map(
        local,
        mesh=mesh,
        in_specs=placed,
        out_specs=(
            P("rows", None, "chan"),
            P("rows", None, "chan"),
            P("chan"),
            P("chan"),
            P(None, None, "chan", None),
            P("chan"),
            P(None, None, "chan"),
            P(None, "chan"),
            P("chan"),
            P("chan"),
            P(None, None, "chan", None),
            P("chan"),
            P("chan"),
            P("chan"),
            P(None, None, "chan"),
            P(None, "chan"),
            P(None, None, "chan"),
            P(None, "chan"),
            P("chan", None),
            P("chan"),
        ),
        check_vma=False,
    )
```

```python
import functools

import jax
import jax.numpy as jnp
from jax import lax
from jax.experimental import pallas as pl
from jax.experimental.pallas import tpu as pltpu
from jax.sharding import PartitionSpec as P

C = 512
HEAD_DIM = 64
GROUPS = 32
IMG_H = 64


EPSILON = 1e-05
HIGH = lax.Precision.HIGHEST
NEG = -1e30
bf16, f32 = jnp.bfloat16, jnp.float32


def from_behind(block, axis, distance):
    devices = range(lax.axis_size(axis))
    route = [((i - distance) % len(devices), i) for i in devices]
    return lax.ppermute(block, axis, route)


def dot(a, b, ca, cb):
    return lax.dot_general(a, b, (((ca,), (cb,)), ((), ())), preferred_element_type=f32)


def attend_kernel(tiles, tile_rows, cols, width, image_rows, total_rows, ctx_count, images, window, row_count,
                  offset, q_ref, do_ref, kv_ref, ctx_ref,
                  o_ref, dq_ref, dkv_ref, dctx_ref,
                  kv, kt, vt, qt, do_t, s_buf, p_buf, dk, dv, oacc, qacc, sem):
    slab_rows = tiles * tile_rows
    me = lax.axis_index("rows")
    base = (me - window // 2) * slab_rows if window < row_count else 0
    place = lax.rem(me * slab_rows - offset[0] + total_rows, total_rows)
    image_a = place // image_rows
    split = jnp.minimum(slab_rows, image_rows - lax.rem(place, image_rows))
    image_b = lax.rem(image_a + jnp.where(split < slab_rows, 1, 0), images)
    start_a = lax.rem(offset[0] + image_a * image_rows - base + 2 * total_rows, total_rows)
    start_b = lax.rem(offset[0] + image_b * image_rows - base + 2 * total_rows, total_rows)
    ids = (image_a, image_b)
    tq = tile_rows * cols
    main = image_rows * cols
    tail = kv.shape[1] * cols - main
    heads = width // HEAD_DIM
    straddle = split < slab_rows
    group = 8

    def load(img, start):
        @pl.loop(0, image_rows // group)
        def _(j):
            src = lax.rem(start + j * group, total_rows)
            whole = src + group <= total_rows

            @pl.when(whole)
            def _():
                pltpu.make_async_copy(
                    kv_ref.at[pl.ds(src, group)], kv.at[img, pl.ds(j * group, group)], sem.at[img]
                ).start()

            @pl.when(jnp.logical_not(whole))
            def _():
                @pl.loop(0, group)
                def _(i):
                    pltpu.make_async_copy(
                        kv_ref.at[lax.rem(src + i, total_rows)], kv.at[img, j * group + i], sem.at[img]
                    ).start()

    def finish(img, start):
        pltpu.make_async_copy(kv_ref.at[pl.ds(0, image_rows)], kv.at[img, pl.ds(0, image_rows)], sem.at[img]).wait()
        for i in range(tail // cols):
            kv[img, image_rows + i] = ctx_ref[ids[img], pl.ds(i * cols, cols)]
        step = 256 // cols

        @pl.loop(0, kv.shape[1] // step)
        def _(c):
            at = pl.ds(pl.multiple_of(c * 256, 256), 256)
            rows = kv[img, pl.ds(c * step, step)].reshape(256, 2 * width)
            kt[img, :, at] = rows[:, :width].T
            vt[img, :, at] = rows[:, width:].T
        dk[img] = jnp.zeros(dk.shape[1:], f32)
        dv[img] = jnp.zeros(dv.shape[1:], f32)

    load(0, start_a)

    @pl.when(straddle)
    def _():
        load(1, start_b)
    for t in range(tiles):
        qt[t] = (q_ref[pl.ds(t * tq, tq)] * jnp.asarray(HEAD_DIM ** -0.5, bf16)).T
        do_t[t] = do_ref[pl.ds(t * tq, tq)].T
    finish(0, start_a)

    @pl.when(straddle)
    def _():
        finish(1, start_b)

    mixed, cut = split // tile_rows, lax.rem(split, tile_rows)
    count_a = (split + 1) // tile_rows
    first_b = (split + 2) // tile_rows
    count = count_a + jnp.where(straddle, tiles - first_b, 0)
    half_a = jnp.logical_or(cut == 1, cut == 2)
    half_b = jnp.logical_or(cut == 2, cut == 3)
    halves = half_a.astype(jnp.int32) + half_b.astype(jnp.int32)
    first_half = jnp.where(half_a, 0, 1)
    feature = lax.broadcasted_iota(jnp.int32, (width, 1), 0) // HEAD_DIM
    lane_row = lax.broadcasted_iota(jnp.int32, (1, tq), 1) // cols
    tail_ok = lax.broadcasted_iota(jnp.int32, (tail, 1), 0) < ctx_count

    parts = (
        (pl.ds(0, image_rows), pl.ds(0, main), main, False), (pl.ds(image_rows, tail // cols), pl.ds(main, tail), tail, True)
    )

    @pl.loop(0, count)
    def _(item):
        is_b = (item >= count_a).astype(jnp.int32)
        t = jnp.where(is_b == 1, first_b + item - count_a, item)
        row = t * tile_rows + lane_row
        low = jnp.where(is_b == 1, split, 0)
        high = jnp.where(is_b == 1, slab_rows, split)
        mine = jnp.logical_and(row >= low, row < high)
        q_t = qt[t].astype(f32)
        g_t = do_t[t].astype(f32)
        q_h = [jnp.where(feature == h, q_t, 0.0).astype(bf16) for h in range(heads)]

        def rows_of(at, size, cut):
            return kv[is_b, at].reshape(size, 2 * width)[:, cut]

        m = [jnp.full((8, tq), NEG, f32) for _ in range(heads)]
        for blocks, at, size, masked in parts:
            keys = rows_of(blocks, size, slice(0, width))
            for h in range(heads):
                s = dot(keys, q_h[h], 1, 0)
                if masked:
                    s = jnp.where(tail_ok, s, NEG)
                s_buf[h, at] = s
                m[h] = jnp.maximum(m[h], jnp.max(s.reshape(size // 8, 8, tq), axis=0))
        m = [jnp.max(v, axis=0, keepdims=True) for v in m]
        l = [jnp.zeros((8, tq), f32) for _ in range(heads)]
        o = [jnp.zeros((HEAD_DIM, tq), f32) for _ in range(heads)]
        for blocks, at, size, masked in parts:
            for h in range(heads):
                p = jnp.exp(s_buf[h, at] - m[h])
                l[h] = l[h] + jnp.sum(p.reshape(size // 8, 8, tq), axis=0)
                p = p.astype(bf16)
                p_buf[at, pl.ds(h * tq, tq)] = p
                o[h] = o[h] + dot(vt[is_b, pl.ds(h * HEAD_DIM, HEAD_DIM), at], p, 1, 0)
        inv = [1.0 / jnp.sum(v, axis=0, keepdims=True) for v in l]
        o_all = jnp.concatenate([o[h] * inv[h] for h in range(heads)], axis=0)
        do_h, delta = [], []
        for h in range(heads):
            scaled = jnp.where(mine, g_t * inv[h], 0.0)
            scaled = jnp.where(feature == h, scaled, 0.0).astype(bf16)
            do_h.append(scaled)
            delta.append(jnp.sum(scaled.astype(f32) * o_all, axis=0, keepdims=True))
        do_cat = jnp.concatenate(do_h, axis=1)
        q_cat = jnp.concatenate(q_h, axis=1)
        dq = [jnp.zeros((HEAD_DIM, tq), f32) for _ in range(heads)]
        for blocks, at, size, masked in parts:
            vals = rows_of(blocks, size, slice(width, 2 * width))
            ps, dss = [], []
            for h in range(heads):
                dp = dot(vals, do_h[h], 1, 0)
                p = p_buf[at, pl.ds(h * tq, tq)]
                ds = (p.astype(f32) * (dp - delta[h])).astype(bf16)
                dq[h] = dq[h] + dot(kt[is_b, pl.ds(h * HEAD_DIM, HEAD_DIM), at], ds, 1, 0)
                ps.append(p)
                dss.append(ds)
            dv[is_b, at] = dv[is_b, at] + dot(jnp.concatenate(ps, axis=1), do_cat, 1, 1)
            dk[is_b, at] = dk[is_b, at] + dot(jnp.concatenate(dss, axis=1), q_cat, 1, 1)
        oacc[t] = jnp.where(mine, o_all, oacc[t])
        qacc[t] = jnp.where(mine, jnp.concatenate(dq, axis=0) * (HEAD_DIM ** -0.5), qacc[t])

    hq = tq // 2
    lanes = heads * hq
    mine_head = (
        lax.broadcasted_iota(jnp.int32, (width, lanes), 0) // HEAD_DIM == lax.broadcasted_iota(jnp.int32, (width, lanes), 1) // hq
    )
    half_row = lax.rem(lax.broadcasted_iota(jnp.int32, (1, lanes), 1), hq) // cols

    def spread(value):
        return jnp.concatenate([value] * heads, axis=1)

    def diagonal(value):
        return jnp.concatenate(
            [value[h * HEAD_DIM : (h + 1) * HEAD_DIM, h * hq : (h + 1) * hq] for h in range(heads)], axis=0
        )

    @pl.loop(0, halves)
    def _(item):
        is_b = first_half + item
        here = pl.ds(pl.multiple_of(is_b * hq, hq), hq)
        row = mixed * tile_rows + is_b * (tile_rows // 2) + half_row
        low = jnp.where(is_b == 1, split, 0)
        high = jnp.where(is_b == 1, slab_rows, split)
        mine = jnp.logical_and(row >= low, row < high)
        q_b = jnp.where(mine_head, spread(qt[mixed, :, here].astype(f32)), 0.0).astype(bf16)

        def rows_of(at, size, cut):
            return kv[is_b, at].reshape(size, 2 * width)[:, cut]

        def chunk(c):
            return pl.ds(c * (2048 // cols), 2048 // cols), pl.ds(pl.multiple_of(c * 2048, 2048), 2048), 2048, False

        def score(part, m):
            blocks, at, size, masked = part
            s = dot(rows_of(blocks, size, slice(0, width)), q_b, 1, 0)
            if masked:
                s = jnp.where(tail_ok, s, NEG)
            s_buf[0, at] = s
            return jnp.maximum(m, jnp.max(s.reshape(size // 8, 8, lanes), axis=0))

        steps = main // 2048
        m = lax.fori_loop(0, steps, lambda c, m: score(chunk(c), m), jnp.full((8, lanes), NEG, f32))
        m = jnp.max(score(parts[1], m), axis=0, keepdims=True)

        def prob(part, carry):
            blocks, at, size, masked = part
            l, o = carry
            p = jnp.exp(s_buf[0, at] - m)
            l = l + jnp.sum(p.reshape(size // 8, 8, lanes), axis=0)
            p = p.astype(bf16)
            p_buf[at, pl.ds(0, lanes)] = p
            return l, o + dot(vt[is_b, :, at], p, 1, 0)

        carry = (jnp.zeros((8, lanes), f32), jnp.zeros((width, lanes), f32))
        l, o = prob(parts[1], lax.fori_loop(0, steps, lambda c, x: prob(chunk(c), x), carry))
        inv = 1.0 / jnp.sum(l, axis=0, keepdims=True)
        o = o * inv
        do_b = jnp.where(mine_head, spread(do_t[mixed, :, here].astype(f32)), 0.0) * jnp.where(mine, inv, 0.0)
        do_b = do_b.astype(bf16)
        delta = jnp.sum(do_b.astype(f32) * o, axis=0, keepdims=True)

        def back(part, dq):
            blocks, at, size, masked = part
            dp = dot(rows_of(blocks, size, slice(width, 2 * width)), do_b, 1, 0)
            p = p_buf[at, pl.ds(0, lanes)]
            ds = (p.astype(f32) * (dp - delta)).astype(bf16)
            dv[is_b, at] = dv[is_b, at] + dot(p, do_b, 1, 1)
            dk[is_b, at] = dk[is_b, at] + dot(ds, q_b, 1, 1)
            return dq + dot(kt[is_b, :, at], ds, 1, 0)

        dq = back(parts[1], lax.fori_loop(0, steps, lambda c, x: back(chunk(c), x), jnp.zeros((width, lanes), f32)))
        keep = mine[:, :hq]
        oacc[mixed, :, here] = jnp.where(keep, diagonal(o), oacc[mixed, :, here])
        qacc[mixed, :, here] = jnp.where(keep, diagonal(dq) * (HEAD_DIM ** -0.5), qacc[mixed, :, here])

    for t in range(tiles):
        o_ref[pl.ds(t * tq, tq)] = oacc[t].T.astype(bf16)
        dq_ref[pl.ds(t * tq, tq)] = qacc[t].T

    dctx_ref[...] = jnp.zeros(dctx_ref.shape, dctx_ref.dtype)
    share_rows = dctx_ref.shape[0] // images
    if images > 1:
        dkv_ref[...] = jnp.zeros(dkv_ref.shape, dkv_ref.dtype)

    def put(img, start):
        @pl.loop(0, image_rows)
        def _(j):
            row = lax.rem(start + j, total_rows)
            at = pl.ds(pl.multiple_of(j * cols, cols), cols)
            dkv_ref[row, :, :width] = dk[img, at].astype(bf16)
            dkv_ref[row, :, width:] = dv[img, at].astype(bf16)
        at = pl.ds(pl.multiple_of(ids[img] * share_rows, 16), share_rows)
        dctx_ref[at, :width] = dk[img, pl.ds(main, share_rows)].astype(bf16)
        dctx_ref[at, width:] = dv[img, pl.ds(main, share_rows)].astype(bf16)
    put(0, start_a)

    @pl.when(straddle)
    def _():
        put(1, start_b)


def attend(row_count, slab, offset, q, do, kv_window, ctx, total_rows, image_rows, ctx_count, images, share_rows, tile_rows=4):
    tokens, width = q.shape
    rows, cols, _ = kv_window.shape
    tiles = tokens // (tile_rows * cols)
    tq = tile_rows * cols
    tail = ctx.shape[1]
    keys = image_rows * cols + tail
    heads = width // HEAD_DIM
    kern = functools.partial(
        attend_kernel, tiles, tile_rows, cols, width, image_rows, total_rows, ctx_count, images, rows // slab, row_count
    )
    vm = pl.BlockSpec(memory_space=pltpu.VMEM)
    return pl.pallas_call(
        kern, name="attend",
        out_shape=(jax.ShapeDtypeStruct((tokens, width), bf16), jax.ShapeDtypeStruct((tokens, width), f32),
                   jax.ShapeDtypeStruct(kv_window.shape, bf16), jax.ShapeDtypeStruct((images * share_rows, 2 * width), bf16)),
        in_specs=[pl.BlockSpec(memory_space=pltpu.SMEM), vm, vm, pl.BlockSpec(memory_space=pl.ANY), vm],
        out_specs=(vm, vm, vm, vm),
        scratch_shapes=[
            pltpu.VMEM((2, keys // cols, cols, 2 * width), bf16),
            pltpu.VMEM((2, width, keys), bf16), pltpu.VMEM((2, width, keys), bf16),
            pltpu.VMEM((tiles, width, tq), bf16), pltpu.VMEM((tiles, width, tq), bf16),
            pltpu.VMEM((heads, keys, tq), f32), pltpu.VMEM((keys, heads * tq), bf16),
            pltpu.VMEM((2, keys, width), f32), pltpu.VMEM((2, keys, width), f32),
            pltpu.VMEM((tiles, width, tq), f32), pltpu.VMEM((tiles, width, tq), f32),
            pltpu.SemaphoreType.DMA((2,)),
        ],
        cost_estimate=pl.CostEstimate(flops=12 * tokens * keys * width, bytes_accessed=8 * 2**20, transcendentals=heads * tokens * keys),
        compiler_params=pltpu.CompilerParams(vmem_limit_bytes=60 * 2**20),
    )(offset, q, do, kv_window, ctx)


MESH = pl.DeviceIdType.MESH
PIECES = 4
SEGMENTS = 4
VECTORS = 10


def vmem(shape, dtype=f32):
    return pltpu.VMEM(shape, dtype)


def greet(devices):
    barrier = pltpu.get_barrier_semaphore()
    for device in devices:
        pl.semaphore_signal(barrier, inc=1, device_id=device, device_id_type=MESH)
    pl.semaphore_wait(barrier, len(devices))


def row_peers(count):
    r, z = lax.axis_index("rows"), lax.axis_index("chan")
    return [(lax.rem(r + d, count), z) for d in range(1, count)]


def chan_peers(count):
    r, z = lax.axis_index("rows"), lax.axis_index("chan")
    return [(r, lax.rem(z + d, count)) for d in range(1, count)]


def push(src, dst, send_sem, recv_sem, device):
    copy = pltpu.make_async_remote_copy(
        src_ref=src, dst_ref=dst, send_sem=send_sem, recv_sem=recv_sem, device_id=device, device_id_type=MESH
    )
    copy.start()
    return copy


def contract(a, b, a_dim, b_dim):
    return lax.dot_general(a, b, (((a_dim,), (b_dim,)), ((), ())), preferred_element_type=f32)


class Locals:
    def __init__(self, sems):
        self.sems, self.copies, self.done = sems, [], set()

    def start(self, src, dst):
        copy = pltpu.make_async_copy(src, dst, self.sems.at[len(self.copies)])
        copy.start()
        self.copies.append(copy)
        return len(self.copies) - 1

    def wait(self, *which):
        for i in which if which else range(len(self.copies)):
            if i not in self.done:
                self.copies[i].wait()
                self.done.add(i)


def share(buf, sends, recvs, count, pieces):
    me = lax.axis_index("rows")
    for index, piece in enumerate(pieces):
        buf[me, pl.ds(index, 1), :] = piece
    return [push(buf.at[me], buf.at[me], sends.at[d], recvs.at[d], device) for d, device in enumerate(row_peers(count))]


def share_total(buf, copies):
    for copy in copies:
        copy.wait()
    total = buf[0]
    for index in range(1, buf.shape[0]):
        total = total + buf[index]
    return total


def image_masks(offset, first, rows, width, total_rows):
    images = total_rows // IMG_H
    row = first - offset + lax.broadcasted_iota(jnp.int32, (rows, 1, width), 0)
    row = jnp.where(row < 0, row + total_rows, row)
    row = jnp.where(row >= total_rows, row - total_rows, row)
    one, zero = jnp.ones((rows, 1, width), f32), jnp.zeros((rows, 1, width), f32)
    member, upper, lower = [], one, one
    for i in range(images):
        inside = jnp.logical_and(row >= i * IMG_H, row < (i + 1) * IMG_H)
        member.append(jnp.where(inside, one, zero))
        upper = jnp.where(row == i * IMG_H, zero, upper)
        lower = jnp.where(row == (i + 1) * IMG_H - 1, zero, lower)
    return member, upper, lower


def group_sum(values, per_group):
    width = values.shape[1]
    lane = lax.broadcasted_iota(jnp.int32, values.shape, 1)
    step = 1
    while step < per_group:
        above = lax.rem(lane // step, 2) == 0
        values = values + jnp.where(above, pltpu.roll(values, width - step, 1), pltpu.roll(values, step, 1))
        step *= 2
    return values


def image_sums(values, member):
    rows, cols, width = values.shape
    by_row = jnp.sum(values.reshape(rows, cols // 8, 8, width), axis=1)
    return [jnp.sum(jnp.sum(by_row * mask, axis=0), axis=0, keepdims=True) for mask in member]


def to_rows(per_image, member):
    total = None
    for mask, value in zip(member, per_image):
        term = mask * value[None]
        total = term if total is None else total + term
    return total


def norm_images(total, images, entries, per_group):
    grouped = group_sum(total, per_group) * (1.0 / entries)
    centers, scales = [], []
    for i in range(images):
        center = grouped[2 * i : 2 * i + 1]
        square = grouped[2 * i + 1 : 2 * i + 2]
        centers.append(center)
        scales.append(lax.rsqrt(square - center * center + EPSILON))
    return centers, scales


def taps(pad, upper, lower, x9):
    rows, cols, width = pad.shape
    tokens = rows * cols
    inner = tokens - 2 * cols
    col = lax.rem(lax.broadcasted_iota(jnp.int32, (tokens, 1), 0), cols)
    v = pad[...].astype(f32).reshape(tokens, width)
    left = jnp.where(col == 0, 0.0, pltpu.roll(v, 1, 0))
    right = jnp.where(col == cols - 1, 0.0, pltpu.roll(v, tokens - 1, 0))
    for b, part in enumerate((left, v, right)):
        for a, mask in enumerate((upper, None, lower)):
            band = part[a * cols : a * cols + inner]
            if mask is not None:
                band = (band.reshape(rows - 2, cols, width) * mask).reshape(inner, width)
            x9[:, pl.ds((3 * a + b) * width, width)] = band.astype(bf16)


class LineGather:
    def __init__(self, at, pieces, sends, recvs):
        self.at, self.pieces, self.sends, self.recvs = at, pieces, sends, recvs
        self.r, self.z = lax.axis_index("rows"), lax.axis_index("chan")
        self.count = lax.axis_size("chan")

    def copy(self, way, step, piece, shard):
        other = self.z + 1 if way == 0 else self.z - 1
        ref = self.at(shard, piece)
        return pltpu.make_async_remote_copy(
            src_ref=ref, dst_ref=ref, send_sem=self.sends.at[way, step, piece], recv_sem=self.recvs.at[way, step, piece],
            device_id=(self.r, other), device_id_type=MESH,
        )

    def has(self, way, step):
        return self.z >= step if way == 0 else self.z + step < self.count

    def open_end(self, way):
        return self.z + 1 < self.count if way == 0 else self.z >= 1

    def shard(self, way, step):
        return self.z - step if way == 0 else self.z + step

    def run(self, step, pieces=None):
        for piece in range(self.pieces) if pieces is None else pieces:
            for way in range(2):
                if step == 0:
                    @pl.when(self.open_end(way))
                    def _():
                        self.copy(way, 0, piece, self.z).start()
                else:
                    @pl.when(self.has(way, step))
                    def _():
                        shard = self.shard(way, step)
                        self.copy(way, step - 1, piece, shard).wait_recv()
                        if step < self.count - 1:
                            @pl.when(self.open_end(way))
                            def _():
                                self.copy(way, step, piece, shard).start()

    def drain(self):
        for step in range(self.count - 1):
            for way in range(2):
                @pl.when(jnp.logical_and(self.has(way, step), self.open_end(way)))
                def _():
                    for piece in range(self.pieces):
                        self.copy(way, step, piece, self.shard(way, step)).wait_send()


class LineScatter:
    def __init__(self, term, own, out, recv, sends, recvs):
        self.term, self.own, self.out, self.recv, self.sends, self.recvs = term, own, out, recv, sends, recvs
        self.r, self.z = lax.axis_index("rows"), lax.axis_index("chan")
        self.pieces = sends.shape[1]
        self.size = own.shape[0] // self.pieces
        self.end = jnp.logical_or(self.z == 0, self.z == 3)
        self.opposite = lax.rem(self.z + 2, 4)

    def rows(self, piece):
        return pl.ds(piece * self.size, self.size)

    def copy(self, slot, piece, device):
        rows = self.rows(piece)
        return pltpu.make_async_remote_copy(
            src_ref=self.out.at[slot, rows], dst_ref=self.recv.at[slot, rows], send_sem=self.sends.at[slot, piece],
            recv_sem=self.recvs.at[slot, piece], device_id=(self.r, device), device_id_type=MESH,
        )

    def push(self, slot, target, device, piece):
        rows = self.rows(piece)
        self.out[slot, rows] = self.term(target, rows).astype(bf16)
        self.copy(slot, piece, device).start()

    def send(self, piece):
        z = self.z

        @pl.when(self.end)
        def _():
            self.push(3, 3 - z, 1 + z // 3, piece)
            self.push(0, self.opposite, self.opposite, piece)

        @pl.when(z < 3)
        def _():
            self.push(1, z + 1, z + 1, piece)

        @pl.when(z > 0)
        def _():
            self.push(2, z - 1, z - 1, piece)

    def merge(self, piece):
        @pl.when(jnp.logical_not(self.end))
        def _():
            rows = self.rows(piece)
            term = self.term(self.opposite, rows)
            self.copy(3, piece, self.opposite).wait_recv()
            self.out[0, rows] = (term + self.recv[3, rows].astype(f32)).astype(bf16)
            self.copy(0, piece, self.opposite).start()

    def keep(self):
        self.own[...] = self.term(self.z, pl.ds(0, self.own.shape[0]))

    def add(self, slot, piece):
        rows = self.rows(piece)
        self.copy(slot, piece, self.z).wait_recv()
        self.own[rows, :] = self.own[rows, :] + self.recv[slot, rows].astype(f32)

    def finish(self):
        for piece in range(self.pieces):
            @pl.when(self.z > 0)
            def _():
                self.add(1, piece)

            @pl.when(self.z < 3)
            def _():
                self.add(2, piece)
            self.add(0, piece)

    def drain(self):
        for piece in range(self.pieces):
            self.copy(0, piece, self.z).wait_send()

            @pl.when(self.z < 3)
            def _():
                self.copy(1, piece, self.z).wait_send()

            @pl.when(self.z > 0)
            def _():
                self.copy(2, piece, self.z).wait_send()

            @pl.when(self.end)
            def _():
                self.copy(3, piece, self.z).wait_send()


def scatter_scratch(tokens, width, pieces):
    return [
        vmem((tokens, width), f32), vmem((4, tokens, width), bf16), vmem((4, tokens, width), bf16),
        pltpu.SemaphoreType.DMA((4, pieces)), pltpu.SemaphoreType.DMA((4, pieces)),
    ]


def plane():
    r = lax.axis_index("rows")
    core = r + 1 - 2 * lax.rem(r, 2)
    x_dev = r + 2 - 4 * lax.rem(r // 2, 2)
    y_dev = r + 4 - 8 * (r // 4)
    return core, x_dev, y_dev, x_dev + y_dev - r


class PlaneGather:
    def __init__(self, all_ref, sends, recvs):
        self.all, self.sends, self.recvs = all_ref, sends, recvs
        self.r, self.z = lax.axis_index("rows"), lax.axis_index("chan")
        self.core, self.x, self.y, self.d = plane()
        self.size = all_ref.shape[1] // SEGMENTS
        self.copies = [{} for _ in range(SEGMENTS)]

    def part(self, segment, which):
        half = self.size // 2
        if which is None:
            return pl.ds(segment * self.size, self.size)
        return pl.ds(segment * self.size + which * half, half)

    def send(self, segment, i, slab, which, device):
        ref = self.all.at[slab, self.part(segment, which)]
        self.copies[segment][i] = push(ref, ref, self.sends.at[segment, i], self.recvs.at[segment, i], (device, self.z))

    def start(self, s):
        self.send(s, 0, self.r, 0, self.x)
        self.send(s, 1, self.r, 1, self.y)
        self.send(s, 2, self.r, 1, self.x)
        self.send(s, 3, self.r, 0, self.y)
        self.send(s, 4, self.r, None, self.core)

    def relay(self, s):
        copies = self.copies[s]
        copies[0].wait_recv()
        self.send(s, 5, self.x, 0, self.y)
        self.send(s, 6, self.x, 0, self.core)
        copies[1].wait_recv()
        self.send(s, 7, self.y, 1, self.x)
        self.send(s, 8, self.y, 1, self.core)
        copies[2].wait_recv()
        self.send(s, 9, self.x, 1, self.core)
        copies[3].wait_recv()
        self.send(s, 10, self.y, 0, self.core)

    def last(self, s):
        copies = self.copies[s]
        copies[5].wait_recv()
        self.send(s, 11, self.d, 0, self.core)
        copies[7].wait_recv()
        self.send(s, 12, self.d, 1, self.core)

    def done(self, s):
        for i in (4, 6, 8, 9, 10, 11, 12):
            self.copies[s][i].wait_recv()

    def drain(self):
        for copies in self.copies:
            for copy in copies.values():
                copy.wait_send()


class WindowGather:
    def __init__(self, all_ref, sends, recvs):
        self.all, self.sends, self.recvs = all_ref, sends, recvs
        self.size = all_ref.shape[1] // SEGMENTS
        self.copies = [[] for _ in range(SEGMENTS)]

    def start(self, s):
        r, z, count = lax.axis_index("rows"), lax.axis_index("chan"), lax.axis_size("rows")
        window = self.all.shape[0]
        own = window // 2 if window < count else r
        part = pl.ds(s * self.size, self.size)
        for i in range(1, count):
            place = window // 2 - i if i <= window // 2 else window // 2 + count - i
            if window < count and (place < 0 or place >= window):
                continue
            slot = place if window < count else r
            device = (lax.rem(r + i, count), z)
            self.copies[s].append(
                push(self.all.at[own, part], self.all.at[slot, part], self.sends.at[s, i], self.recvs.at[s, i], device)
            )

    def relay(self, s):
        pass

    last = relay

    def done(self, s):
        for copy in self.copies[s]:
            copy.wait_recv()

    def drain(self):
        for copies in self.copies:
            for copy in copies:
                copy.wait_send()


def forward_kernel(row_count, chan_count, per_group, entries, fast, offset, x_ref, *refs):
    vec, refs = refs[:VECTORS], refs[VECTORS:]
    (emb, emb_b, ctx_b, w1_hbm, w2_hbm, att_hbm, g_hbm, wo_hbm, context_hbm, emb_hbm, ctx_hbm,
     x9t_1_hbm, x9t_2_hbm, turn1_hbm, turn2_hbm, c1_hbm, x1_hbm, a3_hbm, all_hbm, gall_hbm, ctx_out, row_ref, q_ref, do_ref,
     mod, ctx_ref,
     w1, w2, w_att, wo, raw, flat, emb_w, ctx_w, wide, x9t_1, x9t_2, turn1, turn2, x1_ref, a3_ref, all_ref, gall_ref, context,
     xpad, cpad, pad, x9, own1, out1, recv1, s1, r1, own2, out2, recv2, s2, r2, stat, stat_s, stat_r, halo_s, halo_r,
     a3_s, a3_r, g_s, g_r, kv_s, kv_r, in_s, out_s) = refs
    rows, cols, width = x_ref.shape
    tokens = rows * cols
    r, z = lax.axis_index("rows"), lax.axis_index("chan")
    loads, stores = Locals(in_s), Locals(out_s)
    for src, dst in ((g_hbm, gall_ref.at[z]), (w1_hbm, w1), (w2_hbm, w2), (att_hbm, w_att), (wo_hbm, wo),
                     (context_hbm, raw), (emb_hbm, emb_w), (ctx_hbm, ctx_w)):
        loads.start(src, dst)
    x = x_ref[...]
    xpad[pl.ds(1, rows)] = x
    greet(row_peers(row_count) + chan_peers(chan_count))
    up = (lax.rem(r + row_count - 1, row_count), z)
    down = (lax.rem(r + 1, row_count), z)

    def rims(phase, ref):
        one = push(ref.at[1], ref.at[rows + 1], halo_s.at[phase, 0], halo_r.at[phase, 0], up)
        two = push(ref.at[rows], ref.at[0], halo_s.at[phase, 1], halo_r.at[phase, 1], down)
        return one, two

    x_rims = rims(0, xpad)
    member, upper, lower = image_masks(offset[0], r * rows - 1, rows + 2, width, row_count * rows)
    images = len(member)
    inner = [mask[1 : rows + 1] for mask in member]
    upper, lower = upper[1 : rows + 1], lower[1 : rows + 1]
    quarter = tokens // 4
    g_copies = []
    loads.wait(0)

    def vector(i):
        return vec[i][...][None]

    def share_g(phase):
        part = pl.ds(phase * quarter, quarter)
        for d, device in enumerate(chan_peers(chan_count)):
            g_copies.append(push(gall_ref.at[z, part], gall_ref.at[z, part], g_s.at[phase, d], g_r.at[phase, d], device))

    def stats(phase, values):
        pieces = []
        for a, b in zip(image_sums(values, inner), image_sums(values * values, inner)):
            pieces += [a, b]
        copies = share(stat.at[phase], stat_s.at[phase], stat_r.at[phase], row_count, pieces)
        share_g(phase)
        centers, scales = norm_images(share_total(stat.at[phase], copies), images, entries, per_group)
        row_ref[2 * phase] = to_rows(centers, inner)
        row_ref[2 * phase + 1] = to_rows(scales, inner)
        return centers, scales

    def conv(weight, *scratch):
        def term(j, at):
            return jnp.dot(x9[at, :], weight[:, pl.ds(pl.multiple_of(j * width, width), width)], preferred_element_type=f32)
        line = LineScatter(term, *scratch)
        for piece in range(line.pieces):
            line.send(piece)
        for piece in range(line.pieces):
            line.merge(piece)
        line.keep()
        return line

    def turn(weight, turned):
        for j in range(chan_count):
            for a in range(3):
                turned[j, pl.ds(a * width, width), :] = weight[pl.ds(3 * a * width, 3 * width), pl.ds(j * width, width)].T

    def split(weight):
        wide[...] = weight[...].astype(f32)
        return [wide[pl.ds(t, weight.shape[0] // 2, 2), :].astype(bf16) for t in range(2)]

    centers, scales = stats(0, x.astype(f32))
    for copy in x_rims:
        copy.wait()
    n1 = (xpad[...].astype(f32) - to_rows(centers, member)) * to_rows(scales, member) * vector(0) + vector(1)
    pad[...] = (n1 * jax.nn.sigmoid(n1)).astype(bf16)
    taps(pad, upper, lower, x9)
    loads.wait(1)
    line1 = conv(w1, own1, out1, recv1, s1, r1)
    x9t_1[...] = x9[...].T
    stores.start(x9t_1, x9t_1_hbm)
    turn(w1, turn1)
    stores.start(turn1, turn1_hbm)
    loads.wait(5, 6, 7)
    for t, weight in enumerate(split(emb_w)):
        mod[t] = jnp.dot(emb[...], weight, preferred_element_type=f32) + emb_b[t : t + 1, :]
    ctx_ref[...] = jnp.zeros(ctx_ref.shape, bf16)
    for c in range(flat.shape[0]):
        lanes = pl.ds(c * width, width)
        flat[c] = raw[:, :, lanes].astype(f32).reshape(flat.shape[1:])
        for i in range(images):
            context[i, :, lanes] = flat[c, pl.ds(i, context.shape[1], images), :].astype(bf16)
    stores.start(context, ctx_out)
    for t, weight in enumerate(split(ctx_w)):
        for i in range(images):
            value = jnp.dot(context[i], weight, preferred_element_type=f32) + ctx_b[t : t + 1, :]
            ctx_ref[i, pl.ds(0, context.shape[1]), pl.ds(t * width, width)] = value.astype(bf16)
    line1.finish()
    c1 = own1[...].reshape(rows, cols, width) + vector(2)
    cpad[pl.ds(1, rows)] = c1
    c_rims = rims(1, cpad)
    stores.start(cpad.at[pl.ds(1, rows)], c1_hbm)
    centers, scales = stats(1, c1)
    mod_scale = 1.0 + to_rows([mod[0, i : i + 1, :] for i in range(images)], member)
    mod_shift = to_rows([mod[1, i : i + 1, :] for i in range(images)], member)
    for copy in c_rims:
        copy.wait()
    n2 = (cpad[...] - to_rows(centers, member)) * to_rows(scales, member) * vector(3) + vector(4)
    h2 = n2 * mod_scale + mod_shift
    pad[...] = (h2 * jax.nn.sigmoid(h2)).astype(bf16)
    taps(pad, upper, lower, x9)
    loads.wait(2)
    line2 = conv(w2, own2, out2, recv2, s2, r2)
    x9t_2[...] = x9[...].T
    stores.start(x9t_2, x9t_2_hbm)
    turn(w2, turn2)
    stores.start(turn2, turn2_hbm)
    line1.drain()
    line2.finish()
    x1 = x.astype(f32) + (own2[...].reshape(rows, cols, width) + vector(5))
    x1_ref[...] = x1
    stores.start(x1_ref, x1_hbm)
    centers, scales = stats(2, x1)
    a3 = (x1 - to_rows(centers, inner)) * to_rows(scales, inner) * vector(6) + vector(7)
    a3_ref[z] = a3.astype(bf16).reshape(tokens, width)

    size, per = tokens // PIECES, PIECES // SEGMENTS
    line = LineGather(lambda shard, piece: a3_ref.at[shard, pl.ds(piece * size, size)], PIECES, a3_s, a3_r)
    window = all_ref.shape[0]
    own = window // 2 if window < row_count else r
    gather = (PlaneGather if fast else WindowGather)(all_ref, kv_s, kv_r)
    loads.wait(3, 4)
    weights = [
        jnp.concatenate([w_att[t, pl.ds(i * width, width), :] for t in range(3)], axis=1) for i in range(chan_count)
    ]

    def run(step, segment):
        line.run(step, range(segment * per, (segment + 1) * per))

    def project(segment):
        at = pl.ds(segment * size * per, size * per)
        qkv = None
        for i in range(chan_count):
            term = jnp.dot(a3_ref[i, at], weights[i], preferred_element_type=f32)
            qkv = term if qkv is None else qkv + term
        all_ref[own, at, :width] = qkv[:, width : 2 * width].astype(bf16)
        all_ref[own, at, width:] = (qkv[:, 2 * width :] + vec[9][1:2, :]).astype(bf16)
        gather.start(segment)
        q_ref[at, :] = (qkv[:, :width] + vec[9][0:1, :]).astype(bf16)

    for step, segment in ((0, 0), (0, 1), (1, 0), (0, 2), (2, 0), (1, 1), (0, 3), (3, 0)):
        run(step, segment)
    project(0)
    for step, segment in ((2, 1), (1, 2), (3, 1)):
        run(step, segment)
    project(1)
    gather.relay(0)
    for step, segment in ((2, 2), (1, 3), (3, 2)):
        run(step, segment)
    project(2)
    gather.relay(1)
    gather.last(0)
    for step, segment in ((2, 3), (3, 3)):
        run(step, segment)
    share_g(3)
    project(3)
    stores.start(a3_ref, a3_hbm)
    gather.relay(2)
    gather.last(1)
    gather.relay(3)
    gather.last(2)
    for copy in g_copies:
        copy.wait_recv()
    stores.start(gall_ref, gall_hbm)
    do = None
    for i in range(chan_count):
        term = contract(gall_ref[i], wo[:, pl.ds(i * width, width)], 1, 1)
        do = term if do is None else do + term
    do_ref[...] = do.astype(bf16)
    gather.last(3)
    for segment in range(SEGMENTS):
        at = pl.ds(segment * size * per, size * per)
        gather.done(segment)
        stores.start(all_ref.at[:, at], all_hbm.at[:, at])
    line2.drain()
    line.drain()
    gather.drain()
    for copy in g_copies:
        copy.wait_send()
    stores.wait()


def forward_block(row_count, chan_count, per_group, entries, window, fast, tail, offset, x, vec, emb, emb_b, ctx_b,
                  w1, w2, w_att, g, wo, context, emb_w, ctx_w):
    rows, cols, width = x.shape
    tokens = rows * cols
    images = row_count * rows // IMG_H
    message = -(-2 * images // 8) * 8
    vm = pl.BlockSpec(memory_space=pltpu.VMEM)
    hbm = pl.BlockSpec(memory_space=pl.ANY)
    S = jax.ShapeDtypeStruct
    sem = pltpu.SemaphoreType.DMA
    peers = chan_count - 1
    full = chan_count * width
    saved = [
        ((9 * width, tokens), bf16), ((9 * width, tokens), bf16),
        ((chan_count, 3 * width, 3 * width), bf16), ((chan_count, 3 * width, 3 * width), bf16),
        ((rows, cols, width), f32), ((rows, cols, width), f32), ((chan_count, tokens, width), bf16),
        ((window, tokens, 2 * width), bf16), ((chan_count, tokens, width), bf16),
        ((images, context.shape[0], context.shape[2]), bf16),
    ]
    small = [
        ((6, rows, 1, width), f32), ((tokens, width), bf16), ((tokens, width), bf16), ((2, images, width), f32),
        ((images, tail, 2 * width), bf16),
    ]
    return pl.pallas_call(
        functools.partial(forward_kernel, row_count, chan_count, per_group, entries, fast),
        name="forward_block",
        out_shape=tuple(S(*item) for item in saved + small),
        in_specs=[pl.BlockSpec(memory_space=pltpu.SMEM)] + [vm] * (4 + VECTORS) + [hbm] * 8,
        out_specs=(hbm,) * len(saved) + (vm,) * len(small),
        scratch_shapes=[
            vmem((9 * width, full), bf16), vmem((9 * width, full), bf16), vmem((3, full, width), bf16), vmem((width, full), bf16),
            vmem(context.shape, bf16), vmem((context.shape[2] // width, context.shape[0] * images, width), f32), vmem(emb_w.shape, bf16), vmem(ctx_w.shape, bf16), vmem(emb_w.shape, f32),
            *[vmem(*item) for i, item in enumerate(saved) if i != 4],
            vmem((rows + 2, cols, width), bf16),
            vmem((rows + 2, cols, width), f32),
            vmem((rows + 2, cols, width), bf16),
            vmem((tokens, 9 * width), bf16),
            *scatter_scratch(tokens, width, 2),
            *scatter_scratch(tokens, width, 2),
            vmem((3, row_count, message, width), f32),
            sem((3, row_count - 1)), sem((3, row_count - 1)),
            sem((2, 2)), sem((2, 2)),
            sem((2, peers, PIECES)), sem((2, peers, PIECES)),
            sem((4, peers)), sem((4, peers)),
            sem((SEGMENTS, max(13, row_count))), sem((SEGMENTS, max(13, row_count))),
            sem((8,)), sem((9 + SEGMENTS,)),
        ],
        cost_estimate=pl.CostEstimate(flops=8 * 9 * tokens * width * full, bytes_accessed=16 * 2**20, transcendentals=4 * tokens * width),
        compiler_params=pltpu.CompilerParams(collective_id=0, has_side_effects=True, vmem_limit_bytes=60 * 2**20),
    )(offset, x, *vec, emb, emb_b, ctx_b, w1, w2, w_att, g, wo, context, emb_w, ctx_w)


class Total:
    def __init__(self, part, out, half, quarters, sends, recvs):
        self.part, self.half, self.quarters, self.out = part, half, quarters, out
        self.sends, self.recvs = sends, recvs
        self.r, self.z = lax.axis_index("rows"), lax.axis_index("chan")
        self.core, self.x, self.y, self.d = plane()
        self.n = part.shape[0] // 8
        self.copies = []

    def rows(self, device):
        return pl.ds(pl.multiple_of((lax.rem(device, 2) * 4 + device // 2) * self.n, 16), self.n)

    def half_rows(self, device):
        return pl.ds(pl.multiple_of(lax.rem(device, 2) * 4 * self.n, 16), 4 * self.n)

    def send(self, i, src, dst, device):
        copy = push(src, dst, self.sends.at[i], self.recvs.at[i], (device, self.z))
        self.copies.append(copy)
        return copy

    def one(self):
        self.a = self.send(0, self.part.at[self.half_rows(self.core)], self.half, self.core)

    def two(self):
        self.a.wait_recv()
        mine = self.half_rows(self.r)
        self.half[...] = (self.part[mine, :].astype(f32) + self.half[...].astype(f32)).astype(bf16)
        self.b = []
        for i, device in enumerate((self.d, self.x, self.y)):
            at = pl.ds(pl.multiple_of((device // 2) * self.n, 16), self.n)
            self.b.append(self.send(1 + i, self.half.at[at], self.quarters.at[i], device))

    def three(self):
        at = pl.ds(pl.multiple_of((self.r // 2) * self.n, 16), self.n)
        total = self.half[at, :].astype(f32)
        for i, copy in enumerate(self.b):
            copy.wait_recv()
            total = total + self.quarters[i].astype(f32)
        mine = self.rows(self.r)
        self.out[mine, :] = total.astype(bf16)
        self.c = []
        for i, device in enumerate((self.d, self.x, self.y, self.core)):
            self.c.append(self.send(4 + i, self.out.at[mine], self.out.at[mine], device))

    def four(self):
        self.e = [self.c[3]]
        for i, device in ((1, self.x), (2, self.y), (0, self.d)):
            self.c[i].wait_recv()
            at = self.rows(device)
            self.e.append(self.send(8 + i, self.out.at[at], self.out.at[at], self.core))

    def finish(self):
        for copy in self.e:
            copy.wait_recv()
        for copy in self.copies:
            copy.wait_send()


def total_scratch(n, width):
    return [vmem((n // 2, width), bf16), vmem((3, n // 8, width), bf16), pltpu.SemaphoreType.DMA((11,)), pltpu.SemaphoreType.DMA((11,))]


class Return:
    def __init__(self, away, parts, cores, out, recv, relay, sends, recvs):
        self.away, self.parts, self.cores, self.out, self.recv, self.relay = away, parts, cores, out, recv, relay
        self.sends, self.recvs = sends, recvs
        self.r, self.z = lax.axis_index("rows"), lax.axis_index("chan")
        self.core, self.x, self.y, self.d = plane()
        self.size = parts.shape[1] // SEGMENTS
        self.copies = [{} for _ in range(SEGMENTS)]

    def at(self, s, which=None):
        half = self.size // 2
        if which is None:
            return pl.ds(s * self.size, self.size)
        return pl.ds(s * self.size + which * half, half)

    def send(self, s, i, src, dst, device):
        self.copies[s][i] = push(src, dst, self.sends.at[s, i], self.recvs.at[s, i], (device, self.z))

    def start(self):
        for s in range(SEGMENTS):
            at = self.at(s)
            for i, device in enumerate((self.d, self.x, self.y, self.r)):
                self.send(s, i, self.away.at[device + self.core - self.r, at], self.cores.at[i, at], self.core)

    def chip(self, i, at):
        return self.parts[i, at].astype(f32) + self.cores[i, at].astype(f32)

    def one(self, s):
        first, second, out, recv = self.at(s, 0), self.at(s, 1), self.out, self.recv
        self.copies[s][0].wait_recv()
        out[0, first] = self.chip(0, first).astype(bf16)
        self.send(s, 4, out.at[0, first], self.relay.at[0, s], self.x)
        out[0, second] = self.chip(0, second).astype(bf16)
        self.send(s, 5, out.at[0, second], self.relay.at[1, s], self.y)
        self.copies[s][1].wait_recv()
        out[1, first] = self.chip(1, first).astype(bf16)
        self.send(s, 6, out.at[1, first], recv.at[0, first], self.x)
        self.copies[s][2].wait_recv()
        out[2, second] = self.chip(2, second).astype(bf16)
        self.send(s, 7, out.at[2, second], recv.at[1, second], self.y)

    def two(self, s):
        first, second, out, recv = self.at(s, 0), self.at(s, 1), self.out, self.recv
        self.copies[s][4].wait_recv()
        out[2, first] = (self.chip(2, first) + self.relay[0, s].astype(f32)).astype(bf16)
        self.send(s, 8, out.at[2, first], recv.at[1, first], self.y)
        self.copies[s][5].wait_recv()
        out[1, second] = (self.chip(1, second) + self.relay[1, s].astype(f32)).astype(bf16)
        self.send(s, 9, out.at[1, second], recv.at[0, second], self.x)

    def three(self, s):
        at = self.at(s)
        for i in (3, 6, 7, 8, 9):
            self.copies[s][i].wait_recv()
        return self.chip(3, at) + self.recv[0, at].astype(f32) + self.recv[1, at].astype(f32)

    def drain(self):
        for copies in self.copies:
            for copy in copies.values():
                copy.wait_send()


def return_scratch(tokens, width):
    shape = (tokens, width)
    sem = pltpu.SemaphoreType.DMA((SEGMENTS, 10))
    return [
        vmem((4, *shape), bf16), vmem((4, *shape), bf16), vmem((3, *shape), bf16), vmem((2, *shape), bf16),
        vmem((2, SEGMENTS, tokens // (2 * SEGMENTS), width), bf16), sem, sem,
    ]


class ConvBack:
    def __init__(self, pad, acc, x9t, turned, parts, outs, totals, up, down, halo_s, halo_r, sends, recvs, upper, lower):
        self.pad, self.acc, self.x9t, self.turned, self.parts, self.outs = pad, acc, x9t, turned, parts, outs
        self.totals, self.up, self.down, self.halo_s, self.halo_r = totals, up, down, halo_s, halo_r
        self.upper, self.lower = upper, lower
        _, self.rows, self.cols, self.width = pad.shape
        self.rows -= 2
        self.tokens = self.rows * self.cols
        self.size = self.rows // PIECES
        self.line = LineGather(self.at, PIECES + 2, sends, recvs)
        z = lax.axis_index("chan")
        low = z < 2
        self.order = (z, z + 1 - 2 * lax.rem(z, 2), jnp.where(low, 2, 1), jnp.where(low, 3, 0))
        self.later = []

    def at(self, shard, piece):
        if piece < PIECES:
            return self.pad.at[shard, pl.ds(1 + piece * self.size, self.size)]
        return self.pad.at[shard, pl.ds(0 if piece == PIECES else self.rows + 1, 1)]

    def start(self, values):
        pad, rows, z = self.pad, self.rows, lax.axis_index("chan")
        pad[z, pl.ds(1, rows)] = values
        self.rims = [
            push(pad.at[z, 1], pad.at[z, rows + 1], self.halo_s.at[0], self.halo_r.at[0], self.up),
            push(pad.at[z, rows], pad.at[z, 0], self.halo_s.at[1], self.halo_r.at[1], self.down),
        ]
        self.line.run(0, range(PIECES))
        for copy in self.rims:
            copy.wait_recv()
        self.line.run(0, (PIECES, PIECES + 1))

    def block(self, step, kernel=True):
        j, rows, tokens, width = self.order[step], self.rows, self.tokens, self.width
        parts = []
        for a, mask in enumerate((self.lower, None, self.upper)):
            part = self.pad[j, pl.ds(2 - a, rows)]
            if mask is not None:
                part = (part.astype(f32) * mask).astype(bf16)
            parts.append(part.reshape(tokens, width))
        if kernel:
            self.kernel_grad(step)
        term = jnp.dot(jnp.concatenate(parts, axis=1), self.turned[j], preferred_element_type=f32)
        self.acc[...] = term if step == 0 else self.acc[...] + term

    def kernel_grad(self, step):
        j = self.order[step]
        grad = self.pad[j, pl.ds(1, self.rows)].reshape(self.tokens, self.width)
        self.parts[step] = jnp.dot(self.x9t[...], grad, preferred_element_type=f32).astype(bf16)
        if self.totals:
            self.totals[step].one()
        else:
            self.outs[j] = self.parts[step]

    def run(self, step, kernel=True):
        self.line.run(step)
        self.block(step, kernel)

    def input_grad(self):
        total, width, cols, tokens = self.acc[...], self.width, self.cols, self.tokens
        col = lax.rem(lax.broadcasted_iota(jnp.int32, (tokens, 1), 0), cols)
        before = jnp.where(col == cols - 1, 0.0, pltpu.roll(total[:, :width], tokens - 1, 0))
        after = jnp.where(col == 0, 0.0, pltpu.roll(total[:, 2 * width :], 1, 0))
        return (before + total[:, width : 2 * width] + after).reshape(self.rows, cols, width)

    def drain(self):
        for copy in self.rims:
            copy.wait_send()
        self.line.drain()


def silu_slope(values):
    gate = jax.nn.sigmoid(values)
    return gate * (1.0 + values * (1.0 - gate))


def channel_total(values):
    rows, cols, width = values.shape
    return jnp.sum(jnp.sum(values.reshape(rows * cols // 8, 8, width), axis=0), axis=0, keepdims=True)


def backward_kernel(row_count, chan_count, per_group, entries, fast, offset, *refs):
    vec, refs = refs[:VECTORS], refs[VECTORS:]
    (rows_in, mod, w_att, wo, dctx,
     dq_hbm, dkv_hbm, o_hbm, gall_hbm, a3_hbm, x1_hbm, c1_hbm, x_hbm, x9t_1_hbm, x9t_2_hbm, turn1_hbm, turn2_hbm,
     result, dfeat, sums, g_conv1, g_conv2, g_att, g_out, g_ctx,
     dq_ref, o_ref, gall, a3_all, x1_ref, c1_ref, x_ref, x9t_1, x9t_2, turn1, turn2, load_s,
     part1, part2, part_att, part_out, d3, dx1_ref, acc, gpad, halo_s, halo_r, zh_s, zh_r, stat, stat_s, stat_r,
     res_out, res_recv, res_s, res_r, own, da3_out, da3_recv, da3_s, da3_r) = refs[:61]
    refs = refs[61:]
    rows, cols, width = x_ref.shape
    tokens = rows * cols
    r, z = lax.axis_index("rows"), lax.axis_index("chan")
    loads = Locals(load_s)
    if fast:
        back = Return(dkv_hbm, *refs[:7])
        for i, device in enumerate((back.d, back.x, back.y, r)):
            loads.start(dkv_hbm.at[device], back.parts.at[i])
        pairs = iter(range(7, len(refs), 4))

        def total(part, out):
            i = next(pairs)
            return Total(part, out, *refs[i : i + 4])
        small = [total(part_att, g_att), total(part_out, g_out), total(dctx, g_ctx)]
    else:
        for i in range(4):
            loads.start(dkv_hbm.at[pl.ds(i * (tokens // 4), tokens // 4)], refs[0].at[pl.ds(i * (tokens // 4), tokens // 4)])
        small = []
    for src, dst in (
        (dq_hbm, dq_ref), (o_hbm, o_ref), (gall_hbm, gall), (a3_hbm, a3_all), (x1_hbm, x1_ref), (c1_hbm, c1_ref), (x_hbm, x_ref),
        (x9t_2_hbm, x9t_2), (turn2_hbm, turn2), (x9t_1_hbm, x9t_1), (turn1_hbm, turn1),
    ):
        loads.start(src, dst)
    greet(row_peers(row_count) + chan_peers(chan_count))
    if fast:
        back.start()
    member, upper, lower = image_masks(offset[0], r * rows, rows, width, row_count * rows)
    images = len(member)
    up = (lax.rem(r + row_count - 1, row_count), z)
    down = (lax.rem(r + 1, row_count), z)
    orders = []
    for index, (x9t, turned, parts, outs) in enumerate(((x9t_2, turn2, part2, g_conv2), (x9t_1, turn1, part1, g_conv1))):
        conv = ConvBack(
            gpad.at[index], acc, x9t, turned, parts, outs, [], up, down, halo_s.at[index], halo_r.at[index],
            zh_s.at[index], zh_r.at[index], upper, lower,
        )
        if fast:
            conv.totals = [total(parts.at[step], outs.at[conv.order[step]]) for step in range(chan_count)]
        orders.append(conv)
    conv2, conv1 = orders
    cuts = [0, tokens // 2] + [tokens // 2 + -(-tokens * i // 96) * 16 for i in (1, 2)] + [tokens]
    res_copies = []

    def vector(i):
        return vec[i][...][None]

    def share_result(phase):
        part = pl.ds(cuts[phase], cuts[phase + 1] - cuts[phase])
        for d, device in enumerate(chan_peers(chan_count)):
            res_copies.append(push(res_out.at[d, part], res_recv.at[d, part], res_s.at[phase, d], res_r.at[phase, d], device))

    def exchange(phase, pieces):
        copies = share(stat.at[phase], stat_s.at[phase], stat_r.at[phase], row_count, pieces)
        share_result(phase + 1)
        return copies

    def norm_pieces(dxh, xhat):
        pieces = []
        for a, b in zip(image_sums(dxh, member), image_sums(dxh * xhat, member)):
            pieces += [a, b]
        return pieces

    def norm_back(total, dxh, xhat, scale):
        grouped = group_sum(total[: 2 * images], per_group) * (1.0 / entries)
        first = to_rows([grouped[2 * i : 2 * i + 1] for i in range(images)], member)
        second = to_rows([grouped[2 * i + 1 : 2 * i + 2] for i in range(images)], member)
        return scale * (dxh - first - xhat * second)

    def out_term(j):
        return jnp.dot(o_ref[...], wo[:, pl.ds(pl.multiple_of(j * width, width), width)], preferred_element_type=f32)

    def att_rows(j):
        at = pl.ds(pl.multiple_of(j * width, width), width)
        return jnp.concatenate([w_att[t, at, :] for t in range(3)], axis=1)

    line = LineScatter(lambda j, at: contract(d3[at, :], att_rows(j), 1, 1), own, da3_out, da3_recv, da3_s, da3_r)
    size = tokens // SEGMENTS
    bias_v = jnp.zeros((1, width), f32)
    loads.wait(4)
    if fast:
        loads.wait(0, 1, 2, 3)
        for s in range(SEGMENTS + 2):
            if s < SEGMENTS:
                back.one(s)
            if s == 0:
                loads.wait(5, 6)
                for d, device in enumerate(chan_peers(chan_count)):
                    res_out[d] = out_term(device[1]).astype(bf16)
                share_result(0)
            if 1 <= s <= SEGMENTS:
                back.two(s - 1)
            if s >= 2:
                at = pl.ds((s - 2) * size, size)
                dkv = back.three(s - 2)
                d3[at, :width] = dq_ref[at, :].astype(bf16)
                d3[at, width:] = dkv.astype(bf16)
                bias_v = bias_v + jnp.sum(dkv[:, width:], axis=0, keepdims=True)
                line.send(s - 2)
            if s >= 3:
                line.merge(s - 3)
        line.merge(SEGMENTS - 1)
    else:
        loads.wait(0, 1, 2, 3, 5, 6)
        for d, device in enumerate(chan_peers(chan_count)):
            res_out[d] = out_term(device[1]).astype(bf16)
        share_result(0)
        for s in range(SEGMENTS + 1):
            if s < SEGMENTS:
                at = pl.ds(s * size, size)
                dkv = refs[0][at, :]
                d3[at, :width] = dq_ref[at, :].astype(bf16)
                d3[at, width:] = dkv.astype(bf16)
                bias_v = bias_v + jnp.sum(dkv[:, width:], axis=0, keepdims=True)
                line.send(s)
            if s >= 1:
                line.merge(s - 1)
    line.keep()
    bias_q = jnp.sum(dq_ref[...], axis=0, keepdims=True)
    loads.wait(7)
    for i in range(chan_count):
        grad = contract(a3_all[i], d3[...], 0, 0).astype(bf16)
        for t in range(3):
            part_att[pl.ds((t * chan_count + i) * width, width), :] = grad[:, t * width : (t + 1) * width]
    g_cat = jnp.concatenate([gall[i] for i in range(chan_count)], axis=1)
    part_out[...] = contract(o_ref[...], g_cat, 0, 0).astype(bf16)
    for t in small:
        t.one()
    loads.wait(8)
    x1 = x1_ref[...]
    g = gall[z].astype(f32).reshape(rows, cols, width)
    center, scale = rows_in[4], rows_in[5]
    xhat = (x1 - center) * scale
    bias_g = channel_total(g)
    for t in small:
        t.two()
    line.finish()
    da3 = own[...].reshape(rows, cols, width)
    dxh = da3 * vector(6)
    copies = exchange(
        0, norm_pieces(dxh, xhat) + [channel_total(da3 * xhat), channel_total(da3), bias_q, bias_v, bias_g]
    )
    for t in small:
        t.three()
    total = share_total(stat.at[0], copies)
    sums[0:5, :] = total[2 * images : 2 * images + 5]
    dx1 = g + norm_back(total, dxh, xhat, scale)
    conv2.start(dx1.astype(bf16))
    dx1_ref[...] = dx1
    bias_2 = channel_total(dx1)
    loads.wait(9, 11, 12)
    conv2.block(0)
    for t in small:
        t.four()
    center, scale = rows_in[2], rows_in[3]
    xhat = (c1_ref[...] - center) * scale
    n2 = xhat * vector(3) + vector(4)
    mod_scale = 1.0 + to_rows([mod[0, i : i + 1, :] for i in range(images)], member)
    mod_shift = to_rows([mod[1, i : i + 1, :] for i in range(images)], member)
    slope = silu_slope(n2 * mod_scale + mod_shift)
    conv2.run(1)
    for t in conv2.totals[0:1]:
        t.two()
    conv2.run(2)
    for t in conv2.totals[1:2]:
        t.two()
    for t in conv2.totals[0:1]:
        t.three()
    conv2.run(3, False)
    dh2 = conv2.input_grad() * slope
    dn2 = dh2 * mod_scale
    dxh = dn2 * vector(3)
    dss = []
    for a, b in zip(image_sums(dh2 * n2, member), image_sums(dh2, member)):
        dss += [a, b]
    copies = exchange(1, norm_pieces(dxh, xhat) + [channel_total(dn2 * xhat), channel_total(dn2), bias_2] + dss)
    conv2.kernel_grad(3)
    for t in conv2.totals[2:3]:
        t.two()
    for t in small:
        t.finish()
    total = share_total(stat.at[1], copies)
    sums[5 : 8 + 2 * images, :] = total[2 * images : 4 * images + 3]
    dc1 = norm_back(total, dxh, xhat, scale)
    conv1.start(dc1.astype(bf16))
    bias_1 = channel_total(dc1)
    loads.wait(10, 13, 14)
    conv1.block(0)
    for t in conv2.totals[3:4]:
        t.two()
    for t in conv2.totals[1:3]:
        t.three()
    for t in conv2.totals[0:1]:
        t.four()
    center, scale = rows_in[0], rows_in[1]
    xhat = (x_ref[...].astype(f32) - center) * scale
    slope = silu_slope(xhat * vector(0) + vector(1))
    conv1.run(1)
    for t in conv1.totals[0:1]:
        t.two()
    for t in conv2.totals[3:4]:
        t.three()
    for t in conv2.totals[1:3]:
        t.four()
    conv1.run(2)
    for t in conv1.totals[1:2]:
        t.two()
    for t in conv1.totals[0:1]:
        t.three()
    for t in conv2.totals[3:4]:
        t.four()
    conv1.run(3)
    for t in conv1.totals[2:3]:
        t.two()
    for t in conv1.totals[1:2]:
        t.three()
    dn1 = conv1.input_grad() * slope
    for t in conv1.totals[3:4]:
        t.two()
    dxh = dn1 * vector(0)
    copies = exchange(2, norm_pieces(dxh, xhat) + [channel_total(dn1 * xhat), channel_total(dn1), bias_1])
    for t in conv1.totals[0:1]:
        t.four()
    for t in conv1.totals[2:4]:
        t.three()
    for t in conv1.totals[1:2]:
        t.four()
    own[...] = out_term(z)
    total = share_total(stat.at[2], copies)
    sums[8 + 2 * images : 11 + 2 * images, :] = total[2 * images : 2 * images + 3]
    dfeat[...] = (dx1_ref[...] + norm_back(total, dxh, xhat, scale)).astype(bf16)
    for t in conv1.totals[2:4]:
        t.four()
    for copy in res_copies:
        copy.wait()
    value = own[...]
    for d in range(chan_count - 1):
        value = value + res_recv[d].astype(f32)
    result[...] = (x1_ref[...] + value.reshape(rows, cols, width) + vector(8)).astype(bf16)
    for t in conv2.totals + conv1.totals:
        t.finish()
    if fast:
        back.drain()
    else:
        g_att[...] = part_att[...]
        g_out[...] = part_out[...]
        g_ctx[...] = dctx[...]
    line.drain()
    conv2.drain()
    conv1.drain()


def backward_block(row_count, chan_count, per_group, entries, fast, offset, x, vec, dq, dkv, o, gall, a3_all, x1, c1, rows_in,
                   mod, x9t_1, x9t_2, turn1, turn2, w_att, wo, dctx):
    rows, cols, width = x.shape
    tokens = rows * cols
    images = row_count * rows // IMG_H
    full = chan_count * width
    message = -(-(4 * images + 5) // 8) * 8
    vm = pl.BlockSpec(memory_space=pltpu.VMEM)
    hbm = pl.BlockSpec(memory_space=pl.ANY)
    S = jax.ShapeDtypeStruct
    sem = pltpu.SemaphoreType.DMA
    peers = chan_count - 1
    total_rows = -(-(11 + 2 * images) // 8) * 8
    early = [rows_in, mod, w_att, wo, dctx]
    late = [dq, dkv, o, gall, a3_all, x1, c1, x, x9t_1, x9t_2, turn1, turn2]
    kernel_grad = S((chan_count, 9 * width, width), bf16)
    if fast:
        plane_scratch = [
            *return_scratch(tokens, 2 * width), *total_scratch(3 * full, width), *total_scratch(width, full),
            *total_scratch(*dctx.shape),
        ]
        for _ in range(2 * chan_count):
            plane_scratch += total_scratch(9 * width, width)
    else:
        plane_scratch = [vmem(dkv.shape, dkv.dtype)]
    return pl.pallas_call(
        functools.partial(backward_kernel, row_count, chan_count, per_group, entries, fast),
        name="backward_block",
        out_shape=(
            S((rows, cols, width), bf16), S((rows, cols, width), bf16), S((total_rows, width), f32),
            kernel_grad, kernel_grad, S((3 * full, width), bf16), S((width, full), bf16), S(dctx.shape, bf16),
        ),
        in_specs=[pl.BlockSpec(memory_space=pltpu.SMEM)] + [vm] * (VECTORS + len(early)) + [hbm] * len(late),
        out_specs=(vm,) * 8,
        scratch_shapes=[
            *[vmem(item.shape, item.dtype) for item in late if item is not dkv], sem((15,)),
            vmem(kernel_grad.shape, bf16), vmem(kernel_grad.shape, bf16), vmem((3 * full, width), bf16), vmem((width, full), bf16),
            vmem((tokens, 3 * width), bf16), vmem((rows, cols, width), f32), vmem((tokens, 3 * width), f32),
            vmem((2, chan_count, rows + 2, cols, width), bf16), sem((2, 2)), sem((2, 2)),
            sem((2, 2, peers, PIECES + 2)), sem((2, 2, peers, PIECES + 2)),
            vmem((3, row_count, message, width), f32), sem((3, row_count - 1)), sem((3, row_count - 1)),
            vmem((peers, tokens, width), bf16), vmem((peers, tokens, width), bf16), sem((4, peers)), sem((4, peers)),
            *scatter_scratch(tokens, width, SEGMENTS),
            *plane_scratch,
        ],
        cost_estimate=pl.CostEstimate(flops=12 * 9 * tokens * width * full, bytes_accessed=24 * 2**20, transcendentals=4 * tokens * width),
        compiler_params=pltpu.CompilerParams(collective_id=1, has_side_effects=True, vmem_limit_bytes=60 * 2**20),
    )(offset, *vec, *early, *late)


def finish_kernel(images, share_rows, ctx_count, result_in, dfeat_in, sums, g_conv1, g_conv2, g_att, g_out, g_ctx, emb, context,
                  result, dfeat, conv1, conv2, att, out, emb_w, ctx_w, emb_b, att_b, ctx_b, *vectors):
    width = sums.shape[1]
    result[...] = result_in[...]
    dfeat[...] = dfeat_in[...]
    for j in range(g_conv1.shape[0]):
        conv1[:, pl.ds(j * width, width)] = g_conv1[j].astype(f32)
        conv2[:, pl.ds(j * width, width)] = g_conv2[j].astype(f32)
    out[...] = g_out[...].astype(f32)
    att[...] = g_att[...].astype(f32)
    block = emb.shape[1]
    for t in range(2):
        rows = jnp.concatenate([sums[8 + 2 * i + t : 9 + 2 * i + t, :] for i in range(images)], axis=0)
        high = rows.astype(bf16)
        low = (rows - high.astype(f32)).astype(bf16)
        emb_w[pl.ds(t, block, 2), :] = contract(emb[...], high, 0, 0) + contract(emb[...], low, 0, 0)
    total = None
    for i in range(images):
        term = contract(context[i], g_ctx[pl.ds(i * share_rows, ctx_count), :], 0, 0)
        total = term if total is None else total + term
    for t in range(2):
        ctx_w[pl.ds(t, block, 2), :] = total[:, t * width : (t + 1) * width]

    @pl.when(pl.program_id(0) == 0)
    def _():
        for t in range(2):
            emb_b[t : t + 1, :] = sum(sums[8 + 2 * i + t : 9 + 2 * i + t, :] for i in range(images))
            att_b[t : t + 1, :] = sums[2 + t : 3 + t, :]
            ctx_b[t : t + 1, :] = jnp.sum(g_ctx[:, pl.ds(t * width, width)].astype(f32), axis=0, keepdims=True)
        for ref, i in zip(vectors, (0, 1, 4, 5, 6, 7, 8 + 2 * images, 9 + 2 * images, 10 + 2 * images)):
            ref[...] = sums[i : i + 1, :]


def finish_block(images, share_rows, steps, result, dfeat, sums, g_conv1, g_conv2, g_att, g_out, g_ctx, emb, context):
    width = sums.shape[1]
    depth = emb.shape[1]
    ctx_count = context.shape[1]
    S = jax.ShapeDtypeStruct

    def lead(shape):
        rest = (0,) * (len(shape) - 1)
        return pl.BlockSpec((shape[0] // steps,) + tuple(shape[1:]), lambda s: (s,) + rest)

    def whole(shape):
        return pl.BlockSpec(tuple(shape), lambda s: (0,) * len(shape))

    chan_count, taps_n, _ = g_conv1.shape
    full = chan_count * width
    conv_spec = pl.BlockSpec((chan_count, taps_n // steps, width), lambda s: (0, s, 0))
    shapes = [
        (result.shape, bf16, lead), (dfeat.shape, bf16, lead), ((taps_n, full), f32, lead), ((taps_n, full), f32, lead),
        ((3 * full, width), f32, lead), ((width, full), f32, lead), ((2 * depth, width), f32, lead),
        ((2 * depth, width), f32, lead), ((2, width), f32, whole), ((2, width), f32, whole), ((2, width), f32, whole),
    ] + [((1, width), f32, whole)] * 9
    return pl.pallas_call(
        functools.partial(finish_kernel, images, share_rows, ctx_count),
        name="finish_block",
        grid=(steps,),
        out_shape=tuple(S(shape, dtype) for shape, dtype, _ in shapes),
        in_specs=[
            lead(result.shape), lead(dfeat.shape), whole(sums.shape), conv_spec, conv_spec, lead(g_att.shape),
            lead(g_out.shape), whole(g_ctx.shape), pl.BlockSpec((images, depth // steps), lambda s: (0, s)),
            pl.BlockSpec((images, ctx_count, depth // steps), lambda s: (0, 0, s)),
        ],
        out_specs=tuple(spec(shape) for shape, _, spec in shapes),
        cost_estimate=pl.CostEstimate(flops=4 * images * ctx_count * depth * width, bytes_accessed=16 * 2**20, transcendentals=0),
        compiler_params=pltpu.CompilerParams(vmem_limit_bytes=60 * 2**20),
    )(result, dfeat, sums, g_conv1, g_conv2, g_att, g_out, g_ctx, emb, context)


def local(
    features,
    embedding,
    context,
    image_offset,
    first_gain,
    first_shift,
    conv_first,
    conv_first_bias,
    embed_weight,
    embed_bias,
    second_gain,
    second_shift,
    conv_second,
    conv_second_bias,
    attend_gain,
    attend_shift,
    attend_weight,
    attend_bias,
    context_weight,
    context_bias,
    output_weight,
    output_bias,
    cotangent,
):
    slab_rows, columns, channels = features.shape
    devices, chan = lax.axis_size("rows"), lax.axis_size("chan")
    total_rows = slab_rows * devices
    images = total_rows // IMG_H
    per_group = C // GROUPS
    entries = IMG_H * columns * per_group
    tokens = slab_rows * columns
    context_count = context.shape[1]
    tail = -(-context_count // 256) * 256
    vectors = [
        vector.reshape(1, channels)
        for vector in (first_gain, first_shift, conv_first_bias, second_gain, second_shift, conv_second_bias, attend_gain,
                       attend_shift, output_bias)
    ] + [attend_bias]
    window = min(devices, 2 * (IMG_H // slab_rows) + 1)
    kernel_one = conv_first.reshape(9 * channels, C)
    kernel_two = conv_second.reshape(9 * channels, C)
    attend_kernels = attend_weight.transpose(1, 0, 2)
    fast = devices == 8 and window == devices
    (x9t_one, x9t_two, turn_one, turn_two, middle, inner, attend_blocks, kv_all, grad_blocks, context_own, row_stats, queries,
     grad_attended, modulate, context_rows) = forward_block(
        devices, chan, per_group, entries, window, fast, tail, image_offset, features, vectors, embedding, embed_bias,
        context_bias, kernel_one, kernel_two, attend_kernels, cotangent.reshape(tokens, channels), output_weight, context.transpose(1, 0, 2),
        embed_weight.reshape(-1, channels), context_weight.reshape(-1, channels),
    )
    share_rows = -(-context_count // 64) * 64
    attended, query_grad, window_grad, context_part = attend(
        devices, slab_rows, image_offset, queries, grad_attended, kv_all.reshape(window * slab_rows, columns, 2 * channels),
        context_rows, total_rows, IMG_H, context_count, images, share_rows,
    )
    key_value_grad = window_grad.reshape(window, tokens, 2 * channels)
    if not fast:
        pieces, key_value_grad = key_value_grad, jnp.zeros((tokens, 2 * channels), f32)
        for position in range(window):
            shift_by = position - window // 2 if window < devices else None
            piece = pieces[position]
            if shift_by is None:
                piece = jnp.sum(lax.all_to_all(pieces, "rows", 0, 0).astype(f32), axis=0) if position == 0 else 0.0
            elif shift_by != 0:
                piece = from_behind(piece, "rows", shift_by)
            key_value_grad = key_value_grad + (piece if shift_by is None else piece.astype(f32))
    result, features_grad, sums, conv_first_grad, conv_second_grad, attend_grad, output_weight_grad, context_sum = backward_block(
        devices, chan, per_group, entries, fast, image_offset, features, vectors, query_grad, key_value_grad, attended,
        grad_blocks, attend_blocks, inner, middle, row_stats, modulate, x9t_one, x9t_two, turn_one, turn_two, attend_kernels,
        output_weight, context_part,
    )
    if not fast:
        conv_first_grad, conv_second_grad, attend_grad, output_weight_grad, context_sum = lax.psum(
            (conv_first_grad, conv_second_grad, attend_grad, output_weight_grad, context_sum), "rows"
        )
    (result, features_grad, conv_first_grad, conv_second_grad, attend_grad, output_weight_grad, embed_weight_grad,
     context_weight_grad, embed_bias_grad, attend_bias_grad, context_bias_grad, *rest) = finish_block(
        images, share_rows, 2, result, features_grad, sums, conv_first_grad, conv_second_grad, attend_grad,
        output_weight_grad, context_sum, embedding, context_own,
    )
    (attend_gain_grad, attend_shift_grad, output_bias_grad, second_gain_grad, second_shift_grad, conv_second_bias_grad,
     first_gain_grad, first_shift_grad, conv_first_bias_grad) = [vector.reshape(channels) for vector in rest]
    return (
        result,
        features_grad,
        first_gain_grad,
        first_shift_grad,
        conv_first_grad.reshape(3, 3, channels, C),
        conv_first_bias_grad,
        embed_weight_grad.reshape(-1, 2, channels),
        embed_bias_grad,
        second_gain_grad,
        second_shift_grad,
        conv_second_grad.reshape(3, 3, channels, C),
        conv_second_bias_grad,
        attend_gain_grad,
        attend_shift_grad,
        attend_grad.reshape(3, C, channels).transpose(1, 0, 2),
        attend_bias_grad,
        context_weight_grad.reshape(-1, 2, channels),
        context_bias_grad,
        output_weight_grad,
        output_bias_grad,
    )


def solution(mesh):
    placed = (
        P("rows", None, "chan"),
        P(),
        P(),
        P(),
        P("chan"),
        P("chan"),
        P(None, None, "chan", None),
        P("chan"),
        P(None, None, "chan"),
        P(None, "chan"),
        P("chan"),
        P("chan"),
        P(None, None, "chan", None),
        P("chan"),
        P("chan"),
        P("chan"),
        P(None, None, "chan"),
        P(None, "chan"),
        P(None, None, "chan"),
        P(None, "chan"),
        P("chan", None),
        P("chan"),
        P("rows", None, "chan"),
    )
    return jax.shard_map(
        local,
        mesh=mesh,
        in_specs=placed,
        out_specs=(
            P("rows", None, "chan"),
            P("rows", None, "chan"),
            P("chan"),
            P("chan"),
            P(None, None, "chan", None),
            P("chan"),
            P(None, None, "chan"),
            P(None, "chan"),
            P("chan"),
            P("chan"),
            P(None, None, "chan", None),
            P("chan"),
            P("chan"),
            P("chan"),
            P(None, None, "chan"),
            P(None, "chan"),
            P(None, None, "chan"),
            P(None, "chan"),
            P("chan", None),
            P("chan"),
        ),
        check_vma=False,
    )
```

```python
import functools

import jax
import jax.numpy as jnp
from jax import lax
from jax.experimental import pallas as pl
from jax.experimental.pallas import tpu as pltpu
from jax.sharding import PartitionSpec as P

C = 512
HEAD_DIM = 64
GROUPS = 32
IMG_H = 64


EPSILON = 1e-05
HIGH = lax.Precision.HIGHEST
NEG = -1e30
bf16, f32 = jnp.bfloat16, jnp.float32


def from_behind(block, axis, distance):
    devices = range(lax.axis_size(axis))
    route = [((i - distance) % len(devices), i) for i in devices]
    return lax.ppermute(block, axis, route)


def dot(a, b, ca, cb):
    return lax.dot_general(a, b, (((ca,), (cb,)), ((), ())), preferred_element_type=f32)


def attend_kernel(tiles, tile_rows, cols, width, image_rows, total_rows, ctx_count, images, window, row_count,
                  offset, q_ref, do_ref, kv_ref, ctx_ref,
                  o_ref, dq_ref, dkv_ref, dctx_ref,
                  kv, kt, vt, qt, do_t, s_buf, p_buf, dk, dv, oacc, qacc, sem):
    slab_rows = tiles * tile_rows
    me = lax.axis_index("rows")
    base = (me - window // 2) * slab_rows if window < row_count else 0
    place = lax.rem(me * slab_rows - offset[0] + total_rows, total_rows)
    image_a = place // image_rows
    split = jnp.minimum(slab_rows, image_rows - lax.rem(place, image_rows))
    image_b = lax.rem(image_a + jnp.where(split < slab_rows, 1, 0), images)
    start_a = lax.rem(offset[0] + image_a * image_rows - base + 2 * total_rows, total_rows)
    start_b = lax.rem(offset[0] + image_b * image_rows - base + 2 * total_rows, total_rows)
    ids = (image_a, image_b)
    tq = tile_rows * cols
    main = image_rows * cols
    tail = kv.shape[1] * cols - main
    heads = width // HEAD_DIM
    straddle = split < slab_rows
    group = 8
    per_half = image_rows // group // 2

    def load(img, start):
        @pl.loop(0, image_rows // group)
        def _(j):
            src = lax.rem(start + j * group, total_rows)
            whole = src + group <= total_rows

            @pl.when(whole)
            def _():
                pltpu.make_async_copy(
                    kv_ref.at[pl.ds(src, group)], kv.at[img, pl.ds(j * group, group)], sem.at[img, j // per_half]
                ).start()

            @pl.when(jnp.logical_not(whole))
            def _():
                @pl.loop(0, group)
                def _(i):
                    pltpu.make_async_copy(
                        kv_ref.at[lax.rem(src + i, total_rows)], kv.at[img, j * group + i], sem.at[img, j // per_half]
                    ).start()

    def finish(img, start):
        dk[img] = jnp.zeros(dk.shape[1:], f32)
        dv[img] = jnp.zeros(dv.shape[1:], f32)
        for i in range(tail // cols):
            kv[img, image_rows + i] = ctx_ref[ids[img], pl.ds(i * cols, cols)]
        step = 256 // cols

        def turn(c):
            at = pl.ds(pl.multiple_of(c * 256, 256), 256)
            rows = kv[img, pl.ds(c * step, step)].reshape(256, 2 * width)
            kt[img, :, at] = rows[:, :width].T
            vt[img, :, at] = rows[:, width:].T

        pl.loop(image_rows // step, kv.shape[1] // step)(turn)
        half = image_rows // 2
        for part in range(2):
            rows = pl.ds(part * half, half)
            pltpu.make_async_copy(kv_ref.at[pl.ds(0, half)], kv.at[img, rows], sem.at[img, part]).wait()
            pl.loop(part * half // step, (part + 1) * half // step)(turn)

    load(0, start_a)

    @pl.when(straddle)
    def _():
        load(1, start_b)
    for t in range(tiles):
        qt[t] = (q_ref[pl.ds(t * tq, tq)] * jnp.asarray(HEAD_DIM ** -0.5, bf16)).T
        do_t[t] = do_ref[pl.ds(t * tq, tq)].T
    finish(0, start_a)

    @pl.when(straddle)
    def _():
        finish(1, start_b)

    mixed, cut = split // tile_rows, lax.rem(split, tile_rows)
    count_a = (split + 1) // tile_rows
    first_b = (split + 2) // tile_rows
    count = count_a + jnp.where(straddle, tiles - first_b, 0)
    half_a = jnp.logical_or(cut == 1, cut == 2)
    half_b = jnp.logical_or(cut == 2, cut == 3)
    halves = half_a.astype(jnp.int32) + half_b.astype(jnp.int32)
    first_half = jnp.where(half_a, 0, 1)
    feature = lax.broadcasted_iota(jnp.int32, (width, 1), 0) // HEAD_DIM
    lane_row = lax.broadcasted_iota(jnp.int32, (1, tq), 1) // cols
    tail_ok = lax.broadcasted_iota(jnp.int32, (tail, 1), 0) < ctx_count

    parts = (
        (pl.ds(0, image_rows), pl.ds(0, main), main, False), (pl.ds(image_rows, tail // cols), pl.ds(main, tail), tail, True)
    )

    @pl.loop(0, count)
    def _(item):
        is_b = (item >= count_a).astype(jnp.int32)
        t = jnp.where(is_b == 1, first_b + item - count_a, item)
        row = t * tile_rows + lane_row
        low = jnp.where(is_b == 1, split, 0)
        high = jnp.where(is_b == 1, slab_rows, split)
        mine = jnp.logical_and(row >= low, row < high)
        q_t = qt[t].astype(f32)
        g_t = do_t[t].astype(f32)
        q_h = [jnp.where(feature == h, q_t, 0.0).astype(bf16) for h in range(heads)]

        def rows_of(at, size, cut):
            return kv[is_b, at].reshape(size, 2 * width)[:, cut]

        m = [jnp.full((8, tq), NEG, f32) for _ in range(heads)]
        for blocks, at, size, masked in parts:
            keys = rows_of(blocks, size, slice(0, width))
            for h in range(heads):
                s = dot(keys, q_h[h], 1, 0)
                if masked:
                    s = jnp.where(tail_ok, s, NEG)
                s_buf[h, at] = s
                m[h] = jnp.maximum(m[h], jnp.max(s.reshape(size // 8, 8, tq), axis=0))
        m = [jnp.max(v, axis=0, keepdims=True) for v in m]
        l = [jnp.zeros((8, tq), f32) for _ in range(heads)]
        o = [jnp.zeros((HEAD_DIM, tq), f32) for _ in range(heads)]
        for blocks, at, size, masked in parts:
            for h in range(heads):
                p = jnp.exp(s_buf[h, at] - m[h])
                l[h] = l[h] + jnp.sum(p.reshape(size // 8, 8, tq), axis=0)
                p = p.astype(bf16)
                p_buf[at, pl.ds(h * tq, tq)] = p
                o[h] = o[h] + dot(vt[is_b, pl.ds(h * HEAD_DIM, HEAD_DIM), at], p, 1, 0)
        inv = [1.0 / jnp.sum(v, axis=0, keepdims=True) for v in l]
        o_all = jnp.concatenate([o[h] * inv[h] for h in range(heads)], axis=0)
        do_h, delta = [], []
        for h in range(heads):
            scaled = jnp.where(mine, g_t * inv[h], 0.0)
            scaled = jnp.where(feature == h, scaled, 0.0).astype(bf16)
            do_h.append(scaled)
            delta.append(jnp.sum(scaled.astype(f32) * o_all, axis=0, keepdims=True))
        do_cat = jnp.concatenate(do_h, axis=1)
        q_cat = jnp.concatenate(q_h, axis=1)
        dq = [jnp.zeros((HEAD_DIM, tq), f32) for _ in range(heads)]
        for blocks, at, size, masked in parts:
            vals = rows_of(blocks, size, slice(width, 2 * width))
            ps, dss = [], []
            for h in range(heads):
                dp = dot(vals, do_h[h], 1, 0)
                p = p_buf[at, pl.ds(h * tq, tq)]
                ds = (p.astype(f32) * (dp - delta[h])).astype(bf16)
                dq[h] = dq[h] + dot(kt[is_b, pl.ds(h * HEAD_DIM, HEAD_DIM), at], ds, 1, 0)
                ps.append(p)
                dss.append(ds)
            dv[is_b, at] = dv[is_b, at] + dot(jnp.concatenate(ps, axis=1), do_cat, 1, 1)
            dk[is_b, at] = dk[is_b, at] + dot(jnp.concatenate(dss, axis=1), q_cat, 1, 1)
        oacc[t] = jnp.where(mine, o_all, oacc[t])
        qacc[t] = jnp.where(mine, jnp.concatenate(dq, axis=0) * (HEAD_DIM ** -0.5), qacc[t])

    hq = tq // 2
    lanes = heads * hq
    mine_head = (
        lax.broadcasted_iota(jnp.int32, (width, lanes), 0) // HEAD_DIM == lax.broadcasted_iota(jnp.int32, (width, lanes), 1) // hq
    )
    half_row = lax.rem(lax.broadcasted_iota(jnp.int32, (1, lanes), 1), hq) // cols

    def spread(value):
        return jnp.concatenate([value] * heads, axis=1)

    def diagonal(value):
        return jnp.concatenate(
            [value[h * HEAD_DIM : (h + 1) * HEAD_DIM, h * hq : (h + 1) * hq] for h in range(heads)], axis=0
        )

    @pl.loop(0, halves)
    def _(item):
        is_b = first_half + item
        here = pl.ds(pl.multiple_of(is_b * hq, hq), hq)
        row = mixed * tile_rows + is_b * (tile_rows // 2) + half_row
        low = jnp.where(is_b == 1, split, 0)
        high = jnp.where(is_b == 1, slab_rows, split)
        mine = jnp.logical_and(row >= low, row < high)
        q_b = jnp.where(mine_head, spread(qt[mixed, :, here].astype(f32)), 0.0).astype(bf16)

        def rows_of(at, size, cut):
            return kv[is_b, at].reshape(size, 2 * width)[:, cut]

        def chunk(c):
            return pl.ds(c * (2048 // cols), 2048 // cols), pl.ds(pl.multiple_of(c * 2048, 2048), 2048), 2048, False

        def score(part, m):
            blocks, at, size, masked = part
            s = dot(rows_of(blocks, size, slice(0, width)), q_b, 1, 0)
            if masked:
                s = jnp.where(tail_ok, s, NEG)
            s_buf[0, at] = s
            return jnp.maximum(m, jnp.max(s.reshape(size // 8, 8, lanes), axis=0))

        steps = main // 2048
        m = lax.fori_loop(0, steps, lambda c, m: score(chunk(c), m), jnp.full((8, lanes), NEG, f32))
        m = jnp.max(score(parts[1], m), axis=0, keepdims=True)

        def prob(part, carry):
            blocks, at, size, masked = part
            l, o = carry
            p = jnp.exp(s_buf[0, at] - m)
            l = l + jnp.sum(p.reshape(size // 8, 8, lanes), axis=0)
            p = p.astype(bf16)
            p_buf[at, pl.ds(0, lanes)] = p
            return l, o + dot(vt[is_b, :, at], p, 1, 0)

        carry = (jnp.zeros((8, lanes), f32), jnp.zeros((width, lanes), f32))
        l, o = prob(parts[1], lax.fori_loop(0, steps, lambda c, x: prob(chunk(c), x), carry))
        inv = 1.0 / jnp.sum(l, axis=0, keepdims=True)
        o = o * inv
        do_b = jnp.where(mine_head, spread(do_t[mixed, :, here].astype(f32)), 0.0) * jnp.where(mine, inv, 0.0)
        do_b = do_b.astype(bf16)
        delta = jnp.sum(do_b.astype(f32) * o, axis=0, keepdims=True)

        def back(part, dq):
            blocks, at, size, masked = part
            dp = dot(rows_of(blocks, size, slice(width, 2 * width)), do_b, 1, 0)
            p = p_buf[at, pl.ds(0, lanes)]
            ds = (p.astype(f32) * (dp - delta)).astype(bf16)
            dv[is_b, at] = dv[is_b, at] + dot(p, do_b, 1, 1)
            dk[is_b, at] = dk[is_b, at] + dot(ds, q_b, 1, 1)
            return dq + dot(kt[is_b, :, at], ds, 1, 0)

        dq = back(parts[1], lax.fori_loop(0, steps, lambda c, x: back(chunk(c), x), jnp.zeros((width, lanes), f32)))
        keep = mine[:, :hq]
        oacc[mixed, :, here] = jnp.where(keep, diagonal(o), oacc[mixed, :, here])
        qacc[mixed, :, here] = jnp.where(keep, diagonal(dq) * (HEAD_DIM ** -0.5), qacc[mixed, :, here])

    for t in range(tiles):
        o_ref[pl.ds(t * tq, tq)] = oacc[t].T.astype(bf16)
        dq_ref[pl.ds(t * tq, tq)] = qacc[t].T

    dctx_ref[...] = jnp.zeros(dctx_ref.shape, dctx_ref.dtype)
    share_rows = dctx_ref.shape[0] // images
    if images == 2 and window == row_count:
        @pl.when(jnp.logical_not(straddle))
        def _():
            dkv_ref[...] = jnp.zeros(dkv_ref.shape, dkv_ref.dtype)
    else:
        dkv_ref[...] = jnp.zeros(dkv_ref.shape, dkv_ref.dtype)

    def put(img, start):
        @pl.loop(0, image_rows)
        def _(j):
            row = lax.rem(start + j, total_rows)
            at = pl.ds(pl.multiple_of(j * cols, cols), cols)
            dkv_ref[row, :, :width] = dk[img, at].astype(bf16)
            dkv_ref[row, :, width:] = dv[img, at].astype(bf16)
        at = pl.ds(pl.multiple_of(ids[img] * share_rows, 16), share_rows)
        dctx_ref[at, :width] = dk[img, pl.ds(main, share_rows)].astype(bf16)
        dctx_ref[at, width:] = dv[img, pl.ds(main, share_rows)].astype(bf16)
    put(0, start_a)

    @pl.when(straddle)
    def _():
        put(1, start_b)


def attend(row_count, slab, offset, q, do, kv_window, ctx, total_rows, image_rows, ctx_count, images, share_rows, tile_rows=4):
    tokens, width = q.shape
    rows, cols, _ = kv_window.shape
    tiles = tokens // (tile_rows * cols)
    tq = tile_rows * cols
    tail = ctx.shape[1]
    keys = image_rows * cols + tail
    heads = width // HEAD_DIM
    kern = functools.partial(
        attend_kernel, tiles, tile_rows, cols, width, image_rows, total_rows, ctx_count, images, rows // slab, row_count
    )
    vm = pl.BlockSpec(memory_space=pltpu.VMEM)
    return pl.pallas_call(
        kern, name="attend",
        out_shape=(jax.ShapeDtypeStruct((tokens, width), bf16), jax.ShapeDtypeStruct((tokens, width), f32),
                   jax.ShapeDtypeStruct(kv_window.shape, bf16), jax.ShapeDtypeStruct((images * share_rows, 2 * width), bf16)),
        in_specs=[pl.BlockSpec(memory_space=pltpu.SMEM), vm, vm, pl.BlockSpec(memory_space=pl.ANY), vm],
        out_specs=(vm, vm, vm, vm),
        scratch_shapes=[
            pltpu.VMEM((2, keys // cols, cols, 2 * width), bf16),
            pltpu.VMEM((2, width, keys), bf16), pltpu.VMEM((2, width, keys), bf16),
            pltpu.VMEM((tiles, width, tq), bf16), pltpu.VMEM((tiles, width, tq), bf16),
            pltpu.VMEM((heads, keys, tq), f32), pltpu.VMEM((keys, heads * tq), bf16),
            pltpu.VMEM((2, keys, width), f32), pltpu.VMEM((2, keys, width), f32),
            pltpu.VMEM((tiles, width, tq), f32), pltpu.VMEM((tiles, width, tq), f32),
            pltpu.SemaphoreType.DMA((2, 2)),
        ],
        cost_estimate=pl.CostEstimate(flops=12 * tokens * keys * width, bytes_accessed=8 * 2**20, transcendentals=heads * tokens * keys),
        compiler_params=pltpu.CompilerParams(vmem_limit_bytes=60 * 2**20),
    )(offset, q, do, kv_window, ctx)


MESH = pl.DeviceIdType.MESH
PIECES = 4
SEGMENTS = 4
VECTORS = 10


def vmem(shape, dtype=f32):
    return pltpu.VMEM(shape, dtype)


def greet(devices):
    barrier = pltpu.get_barrier_semaphore()
    for device in devices:
        pl.semaphore_signal(barrier, inc=1, device_id=device, device_id_type=MESH)
    pl.semaphore_wait(barrier, len(devices))


def row_peers(count):
    r, z = lax.axis_index("rows"), lax.axis_index("chan")
    return [(lax.rem(r + d, count), z) for d in range(1, count)]


def chan_peers(count):
    r, z = lax.axis_index("rows"), lax.axis_index("chan")
    return [(r, lax.rem(z + d, count)) for d in range(1, count)]


def push(src, dst, send_sem, recv_sem, device):
    copy = pltpu.make_async_remote_copy(
        src_ref=src, dst_ref=dst, send_sem=send_sem, recv_sem=recv_sem, device_id=device, device_id_type=MESH
    )
    copy.start()
    return copy


def contract(a, b, a_dim, b_dim):
    return lax.dot_general(a, b, (((a_dim,), (b_dim,)), ((), ())), preferred_element_type=f32)


class Locals:
    def __init__(self, sems):
        self.sems, self.copies, self.done = sems, [], set()

    def start(self, src, dst):
        copy = pltpu.make_async_copy(src, dst, self.sems.at[len(self.copies)])
        copy.start()
        self.copies.append(copy)
        return len(self.copies) - 1

    def wait(self, *which):
        for i in which if which else range(len(self.copies)):
            if i not in self.done:
                self.copies[i].wait()
                self.done.add(i)


def share(buf, sends, recvs, count, pieces):
    me = lax.axis_index("rows")
    for index, piece in enumerate(pieces):
        buf[me, pl.ds(index, 1), :] = piece
    return [push(buf.at[me], buf.at[me], sends.at[d], recvs.at[d], device) for d, device in enumerate(row_peers(count))]


def share_total(buf, copies):
    for copy in copies:
        copy.wait()
    total = buf[0]
    for index in range(1, buf.shape[0]):
        total = total + buf[index]
    return total


def image_masks(offset, first, rows, width, total_rows):
    images = total_rows // IMG_H
    row = first - offset + lax.broadcasted_iota(jnp.int32, (rows, 1, width), 0)
    row = jnp.where(row < 0, row + total_rows, row)
    row = jnp.where(row >= total_rows, row - total_rows, row)
    one, zero = jnp.ones((rows, 1, width), f32), jnp.zeros((rows, 1, width), f32)
    member, upper, lower = [], one, one
    for i in range(images):
        inside = jnp.logical_and(row >= i * IMG_H, row < (i + 1) * IMG_H)
        member.append(jnp.where(inside, one, zero))
        upper = jnp.where(row == i * IMG_H, zero, upper)
        lower = jnp.where(row == (i + 1) * IMG_H - 1, zero, lower)
    return member, upper, lower


def group_sum(values, per_group):
    width = values.shape[1]
    lane = lax.broadcasted_iota(jnp.int32, values.shape, 1)
    step = 1
    while step < per_group:
        above = lax.rem(lane // step, 2) == 0
        values = values + jnp.where(above, pltpu.roll(values, width - step, 1), pltpu.roll(values, step, 1))
        step *= 2
    return values


def image_sums(values, member):
    rows, cols, width = values.shape
    by_row = jnp.sum(values.reshape(rows, cols // 8, 8, width), axis=1)
    return [jnp.sum(jnp.sum(by_row * mask, axis=0), axis=0, keepdims=True) for mask in member]


def to_rows(per_image, member):
    total = None
    for mask, value in zip(member, per_image):
        term = mask * value[None]
        total = term if total is None else total + term
    return total


def norm_images(total, images, entries, per_group):
    grouped = group_sum(total, per_group) * (1.0 / entries)
    centers, scales = [], []
    for i in range(images):
        center = grouped[2 * i : 2 * i + 1]
        square = grouped[2 * i + 1 : 2 * i + 2]
        centers.append(center)
        scales.append(lax.rsqrt(square - center * center + EPSILON))
    return centers, scales


def taps(pad, upper, lower, x9):
    rows, cols, width = pad.shape
    tokens = rows * cols
    inner = tokens - 2 * cols
    col = lax.rem(lax.broadcasted_iota(jnp.int32, (tokens, 1), 0), cols)
    v = pad[...].astype(f32).reshape(tokens, width)
    left = jnp.where(col == 0, 0.0, pltpu.roll(v, 1, 0))
    right = jnp.where(col == cols - 1, 0.0, pltpu.roll(v, tokens - 1, 0))
    for b, part in enumerate((left, v, right)):
        for a, mask in enumerate((upper, None, lower)):
            band = part[a * cols : a * cols + inner]
            if mask is not None:
                band = (band.reshape(rows - 2, cols, width) * mask).reshape(inner, width)
            x9[:, pl.ds((3 * a + b) * width, width)] = band.astype(bf16)


class LineGather:
    def __init__(self, at, pieces, sends, recvs):
        self.at, self.pieces, self.sends, self.recvs = at, pieces, sends, recvs
        self.r, self.z = lax.axis_index("rows"), lax.axis_index("chan")
        self.count = lax.axis_size("chan")

    def copy(self, way, step, piece, shard):
        other = self.z + 1 if way == 0 else self.z - 1
        ref = self.at(shard, piece)
        return pltpu.make_async_remote_copy(
            src_ref=ref, dst_ref=ref, send_sem=self.sends.at[way, step, piece], recv_sem=self.recvs.at[way, step, piece],
            device_id=(self.r, other), device_id_type=MESH,
        )

    def has(self, way, step):
        return self.z >= step if way == 0 else self.z + step < self.count

    def open_end(self, way):
        return self.z + 1 < self.count if way == 0 else self.z >= 1

    def shard(self, way, step):
        return self.z - step if way == 0 else self.z + step

    def run(self, step, pieces=None):
        for piece in range(self.pieces) if pieces is None else pieces:
            for way in range(2):
                if step == 0:
                    @pl.when(self.open_end(way))
                    def _():
                        self.copy(way, 0, piece, self.z).start()
                else:
                    @pl.when(self.has(way, step))
                    def _():
                        shard = self.shard(way, step)
                        self.copy(way, step - 1, piece, shard).wait_recv()
                        if step < self.count - 1:
                            @pl.when(self.open_end(way))
                            def _():
                                self.copy(way, step, piece, shard).start()

    def drain(self):
        for step in range(self.count - 1):
            for way in range(2):
                @pl.when(jnp.logical_and(self.has(way, step), self.open_end(way)))
                def _():
                    for piece in range(self.pieces):
                        self.copy(way, step, piece, self.shard(way, step)).wait_send()


class LineScatter:
    def __init__(self, term, own, out, recv, sends, recvs):
        self.term, self.own, self.out, self.recv, self.sends, self.recvs = term, own, out, recv, sends, recvs
        self.r, self.z = lax.axis_index("rows"), lax.axis_index("chan")
        self.pieces = sends.shape[1]
        self.size = own.shape[0] // self.pieces
        self.end = jnp.logical_or(self.z == 0, self.z == 3)
        self.opposite = lax.rem(self.z + 2, 4)

    def rows(self, piece):
        return pl.ds(piece * self.size, self.size)

    def copy(self, slot, piece, device):
        rows = self.rows(piece)
        return pltpu.make_async_remote_copy(
            src_ref=self.out.at[slot, rows], dst_ref=self.recv.at[slot, rows], send_sem=self.sends.at[slot, piece],
            recv_sem=self.recvs.at[slot, piece], device_id=(self.r, device), device_id_type=MESH,
        )

    def push(self, slot, target, device, piece):
        rows = self.rows(piece)
        self.out[slot, rows] = self.term(target, rows).astype(bf16)
        self.copy(slot, piece, device).start()

    def send(self, piece):
        z = self.z

        @pl.when(self.end)
        def _():
            self.push(3, 3 - z, 1 + z // 3, piece)
            self.push(0, self.opposite, self.opposite, piece)

        @pl.when(z < 3)
        def _():
            self.push(1, z + 1, z + 1, piece)

        @pl.when(z > 0)
        def _():
            self.push(2, z - 1, z - 1, piece)

    def merge(self, piece):
        @pl.when(jnp.logical_not(self.end))
        def _():
            rows = self.rows(piece)
            term = self.term(self.opposite, rows)
            self.copy(3, piece, self.opposite).wait_recv()
            self.out[0, rows] = (term + self.recv[3, rows].astype(f32)).astype(bf16)
            self.copy(0, piece, self.opposite).start()

    def keep(self):
        self.own[...] = self.term(self.z, pl.ds(0, self.own.shape[0]))

    def add(self, slot, piece):
        rows = self.rows(piece)
        self.copy(slot, piece, self.z).wait_recv()
        self.own[rows, :] = self.own[rows, :] + self.recv[slot, rows].astype(f32)

    def finish(self):
        for piece in range(self.pieces):
            @pl.when(self.z > 0)
            def _():
                self.add(1, piece)

            @pl.when(self.z < 3)
            def _():
                self.add(2, piece)
            self.add(0, piece)

    def drain(self):
        for piece in range(self.pieces):
            self.copy(0, piece, self.z).wait_send()

            @pl.when(self.z < 3)
            def _():
                self.copy(1, piece, self.z).wait_send()

            @pl.when(self.z > 0)
            def _():
                self.copy(2, piece, self.z).wait_send()

            @pl.when(self.end)
            def _():
                self.copy(3, piece, self.z).wait_send()


def scatter_scratch(tokens, width, pieces):
    return [
        vmem((tokens, width), f32), vmem((4, tokens, width), bf16), vmem((4, tokens, width), bf16),
        pltpu.SemaphoreType.DMA((4, pieces)), pltpu.SemaphoreType.DMA((4, pieces)),
    ]


def plane():
    r = lax.axis_index("rows")
    core = r + 1 - 2 * lax.rem(r, 2)
    x_dev = r + 2 - 4 * lax.rem(r // 2, 2)
    y_dev = r + 4 - 8 * (r // 4)
    return core, x_dev, y_dev, x_dev + y_dev - r


class PlaneGather:
    def __init__(self, all_ref, sends, recvs):
        self.all, self.sends, self.recvs = all_ref, sends, recvs
        self.r, self.z = lax.axis_index("rows"), lax.axis_index("chan")
        self.core, self.x, self.y, self.d = plane()
        self.size = all_ref.shape[1] // SEGMENTS
        self.copies = [{} for _ in range(SEGMENTS)]

    def part(self, segment, which):
        half = self.size // 2
        if which is None:
            return pl.ds(segment * self.size, self.size)
        return pl.ds(segment * self.size + which * half, half)

    def send(self, segment, i, slab, which, device):
        ref = self.all.at[slab, self.part(segment, which)]
        self.copies[segment][i] = push(ref, ref, self.sends.at[segment, i], self.recvs.at[segment, i], (device, self.z))

    def start(self, s):
        self.send(s, 0, self.r, 0, self.x)
        self.send(s, 1, self.r, 1, self.y)
        self.send(s, 2, self.r, 1, self.x)
        self.send(s, 3, self.r, 0, self.y)
        self.send(s, 4, self.r, None, self.core)

    def relay(self, s):
        copies = self.copies[s]
        copies[0].wait_recv()
        self.send(s, 5, self.x, 0, self.y)
        self.send(s, 6, self.x, 0, self.core)
        copies[1].wait_recv()
        self.send(s, 7, self.y, 1, self.x)
        self.send(s, 8, self.y, 1, self.core)
        copies[2].wait_recv()
        self.send(s, 9, self.x, 1, self.core)
        copies[3].wait_recv()
        self.send(s, 10, self.y, 0, self.core)

    def last(self, s):
        copies = self.copies[s]
        copies[5].wait_recv()
        self.send(s, 11, self.d, 0, self.core)
        copies[7].wait_recv()
        self.send(s, 12, self.d, 1, self.core)

    def done(self, s):
        for i in (4, 6, 8, 9, 10, 11, 12):
            self.copies[s][i].wait_recv()

    def drain(self):
        for copies in self.copies:
            for copy in copies.values():
                copy.wait_send()


class WindowGather:
    def __init__(self, all_ref, sends, recvs):
        self.all, self.sends, self.recvs = all_ref, sends, recvs
        self.size = all_ref.shape[1] // SEGMENTS
        self.copies = [[] for _ in range(SEGMENTS)]

    def start(self, s):
        r, z, count = lax.axis_index("rows"), lax.axis_index("chan"), lax.axis_size("rows")
        window = self.all.shape[0]
        own = window // 2 if window < count else r
        part = pl.ds(s * self.size, self.size)
        for i in range(1, count):
            place = window // 2 - i if i <= window // 2 else window // 2 + count - i
            if window < count and (place < 0 or place >= window):
                continue
            slot = place if window < count else r
            device = (lax.rem(r + i, count), z)
            self.copies[s].append(
                push(self.all.at[own, part], self.all.at[slot, part], self.sends.at[s, i], self.recvs.at[s, i], device)
            )

    def relay(self, s):
        pass

    last = relay

    def done(self, s):
        for copy in self.copies[s]:
            copy.wait_recv()

    def drain(self):
        for copies in self.copies:
            for copy in copies:
                copy.wait_send()


def forward_kernel(row_count, chan_count, per_group, entries, fast, offset, x_ref, *refs):
    vec, refs = refs[:VECTORS], refs[VECTORS:]
    (emb, emb_b, ctx_b, w1_hbm, w2_hbm, att_hbm, g_hbm, wo_hbm, context_hbm, emb_hbm, ctx_hbm,
     x9t_1_hbm, x9t_2_hbm, turn1_hbm, turn2_hbm, c1_hbm, x1_hbm, a3_hbm, all_hbm, gall_hbm, ctx_out, row_ref, q_ref, do_ref,
     mod, ctx_ref,
     w1, w2, w_att, wo, raw, flat, emb_w, ctx_w, wide, x9t_1, x9t_2, turn1, turn2, x1_ref, a3_ref, all_ref, gall_ref, context,
     xpad, cpad, pad, x9, own1, out1, recv1, s1, r1, own2, out2, recv2, s2, r2, stat, stat_s, stat_r, halo_s, halo_r,
     a3_s, a3_r, g_s, g_r, kv_s, kv_r, in_s, out_s) = refs
    rows, cols, width = x_ref.shape
    tokens = rows * cols
    r, z = lax.axis_index("rows"), lax.axis_index("chan")
    loads, stores = Locals(in_s), Locals(out_s)
    for src, dst in ((g_hbm, gall_ref.at[z]), (w1_hbm, w1), (w2_hbm, w2), (att_hbm, w_att), (wo_hbm, wo),
                     (context_hbm, raw), (emb_hbm, emb_w), (ctx_hbm, ctx_w)):
        loads.start(src, dst)
    x = x_ref[...]
    xpad[pl.ds(1, rows)] = x
    greet(row_peers(row_count) + chan_peers(chan_count))
    up = (lax.rem(r + row_count - 1, row_count), z)
    down = (lax.rem(r + 1, row_count), z)

    def rims(phase, ref):
        one = push(ref.at[1], ref.at[rows + 1], halo_s.at[phase, 0], halo_r.at[phase, 0], up)
        two = push(ref.at[rows], ref.at[0], halo_s.at[phase, 1], halo_r.at[phase, 1], down)
        return one, two

    x_rims = rims(0, xpad)
    member, upper, lower = image_masks(offset[0], r * rows - 1, rows + 2, width, row_count * rows)
    images = len(member)
    inner = [mask[1 : rows + 1] for mask in member]
    upper, lower = upper[1 : rows + 1], lower[1 : rows + 1]
    quarter = tokens // 4
    g_copies = []
    loads.wait(0)

    def vector(i):
        return vec[i][...][None]

    def share_g(phase):
        part = pl.ds(phase * quarter, quarter)
        for d, device in enumerate(chan_peers(chan_count)):
            g_copies.append(push(gall_ref.at[z, part], gall_ref.at[z, part], g_s.at[phase, d], g_r.at[phase, d], device))

    def stats(phase, values):
        pieces = []
        for a, b in zip(image_sums(values, inner), image_sums(values * values, inner)):
            pieces += [a, b]
        copies = share(stat.at[phase], stat_s.at[phase], stat_r.at[phase], row_count, pieces)
        share_g(phase)
        centers, scales = norm_images(share_total(stat.at[phase], copies), images, entries, per_group)
        row_ref[2 * phase] = to_rows(centers, inner)
        row_ref[2 * phase + 1] = to_rows(scales, inner)
        return centers, scales

    def conv(weight, *scratch):
        def term(j, at):
            return jnp.dot(x9[at, :], weight[:, pl.ds(pl.multiple_of(j * width, width), width)], preferred_element_type=f32)
        line = LineScatter(term, *scratch)
        for piece in range(line.pieces):
            line.send(piece)
        for piece in range(line.pieces):
            line.merge(piece)
        line.keep()
        return line

    def turn(weight, turned):
        for j in range(chan_count):
            for a in range(3):
                turned[j, pl.ds(a * width, width), :] = weight[pl.ds(3 * a * width, 3 * width), pl.ds(j * width, width)].T

    def split(weight):
        wide[...] = weight[...].astype(f32)
        return [wide[pl.ds(t, weight.shape[0] // 2, 2), :].astype(bf16) for t in range(2)]

    centers, scales = stats(0, x.astype(f32))
    for copy in x_rims:
        copy.wait()
    n1 = (xpad[...].astype(f32) - to_rows(centers, member)) * to_rows(scales, member) * vector(0) + vector(1)
    pad[...] = (n1 * jax.nn.sigmoid(n1)).astype(bf16)
    taps(pad, upper, lower, x9)
    loads.wait(1)
    line1 = conv(w1, own1, out1, recv1, s1, r1)
    x9t_1[...] = x9[...].T
    stores.start(x9t_1, x9t_1_hbm)
    turn(w1, turn1)
    stores.start(turn1, turn1_hbm)
    loads.wait(5, 6, 7)
    for t, weight in enumerate(split(emb_w)):
        mod[t] = jnp.dot(emb[...], weight, preferred_element_type=f32) + emb_b[t : t + 1, :]
    ctx_ref[...] = jnp.zeros(ctx_ref.shape, bf16)
    for c in range(flat.shape[0]):
        lanes = pl.ds(c * width, width)
        flat[c] = raw[:, :, lanes].astype(f32).reshape(flat.shape[1:])
        for i in range(images):
            context[i, :, lanes] = flat[c, pl.ds(i, context.shape[1], images), :].astype(bf16)
    stores.start(context, ctx_out)
    for t, weight in enumerate(split(ctx_w)):
        for i in range(images):
            value = jnp.dot(context[i], weight, preferred_element_type=f32) + ctx_b[t : t + 1, :]
            ctx_ref[i, pl.ds(0, context.shape[1]), pl.ds(t * width, width)] = value.astype(bf16)
    line1.finish()
    c1 = own1[...].reshape(rows, cols, width) + vector(2)
    cpad[pl.ds(1, rows)] = c1
    c_rims = rims(1, cpad)
    stores.start(cpad.at[pl.ds(1, rows)], c1_hbm)
    centers, scales = stats(1, c1)
    mod_scale = 1.0 + to_rows([mod[0, i : i + 1, :] for i in range(images)], member)
    mod_shift = to_rows([mod[1, i : i + 1, :] for i in range(images)], member)
    for copy in c_rims:
        copy.wait()
    n2 = (cpad[...] - to_rows(centers, member)) * to_rows(scales, member) * vector(3) + vector(4)
    h2 = n2 * mod_scale + mod_shift
    pad[...] = (h2 * jax.nn.sigmoid(h2)).astype(bf16)
    taps(pad, upper, lower, x9)
    loads.wait(2)
    line2 = conv(w2, own2, out2, recv2, s2, r2)
    x9t_2[...] = x9[...].T
    stores.start(x9t_2, x9t_2_hbm)
    turn(w2, turn2)
    stores.start(turn2, turn2_hbm)
    line1.drain()
    line2.finish()
    x1 = x.astype(f32) + (own2[...].reshape(rows, cols, width) + vector(5))
    x1_ref[...] = x1
    stores.start(x1_ref, x1_hbm)
    centers, scales = stats(2, x1)
    a3 = (x1 - to_rows(centers, inner)) * to_rows(scales, inner) * vector(6) + vector(7)
    a3_ref[z] = a3.astype(bf16).reshape(tokens, width)

    size, per = tokens // PIECES, PIECES // SEGMENTS
    line = LineGather(lambda shard, piece: a3_ref.at[shard, pl.ds(piece * size, size)], PIECES, a3_s, a3_r)
    window = all_ref.shape[0]
    own = window // 2 if window < row_count else r
    gather = (PlaneGather if fast else WindowGather)(all_ref, kv_s, kv_r)
    loads.wait(3, 4)
    weights = [
        jnp.concatenate([w_att[t, pl.ds(i * width, width), :] for t in range(3)], axis=1) for i in range(chan_count)
    ]

    def run(step, segment):
        line.run(step, range(segment * per, (segment + 1) * per))

    def project(segment):
        at = pl.ds(segment * size * per, size * per)
        qkv = None
        for i in range(chan_count):
            term = jnp.dot(a3_ref[i, at], weights[i], preferred_element_type=f32)
            qkv = term if qkv is None else qkv + term
        all_ref[own, at, :width] = qkv[:, width : 2 * width].astype(bf16)
        all_ref[own, at, width:] = (qkv[:, 2 * width :] + vec[9][1:2, :]).astype(bf16)
        gather.start(segment)
        q_ref[at, :] = (qkv[:, :width] + vec[9][0:1, :]).astype(bf16)

    for step, segment in ((0, 0), (0, 1), (1, 0), (0, 2), (2, 0), (1, 1), (0, 3), (3, 0)):
        run(step, segment)
    project(0)
    for step, segment in ((2, 1), (1, 2), (3, 1)):
        run(step, segment)
    project(1)
    gather.relay(0)
    for step, segment in ((2, 2), (1, 3), (3, 2)):
        run(step, segment)
    project(2)
    gather.relay(1)
    gather.last(0)
    for step, segment in ((2, 3), (3, 3)):
        run(step, segment)
    share_g(3)
    project(3)
    stores.start(a3_ref, a3_hbm)
    gather.relay(2)
    gather.last(1)
    gather.relay(3)
    gather.last(2)
    for copy in g_copies:
        copy.wait_recv()
    stores.start(gall_ref, gall_hbm)
    do = None
    for i in range(chan_count):
        term = contract(gall_ref[i], wo[:, pl.ds(i * width, width)], 1, 1)
        do = term if do is None else do + term
    do_ref[...] = do.astype(bf16)
    gather.last(3)
    for segment in range(SEGMENTS):
        at = pl.ds(segment * size * per, size * per)
        gather.done(segment)
        stores.start(all_ref.at[:, at], all_hbm.at[:, at])
    line2.drain()
    line.drain()
    gather.drain()
    for copy in g_copies:
        copy.wait_send()
    stores.wait()


def forward_block(row_count, chan_count, per_group, entries, window, fast, tail, offset, x, vec, emb, emb_b, ctx_b,
                  w1, w2, w_att, g, wo, context, emb_w, ctx_w):
    rows, cols, width = x.shape
    tokens = rows * cols
    images = row_count * rows // IMG_H
    message = -(-2 * images // 8) * 8
    vm = pl.BlockSpec(memory_space=pltpu.VMEM)
    hbm = pl.BlockSpec(memory_space=pl.ANY)
    S = jax.ShapeDtypeStruct
    sem = pltpu.SemaphoreType.DMA
    peers = chan_count - 1
    full = chan_count * width
    saved = [
        ((9 * width, tokens), bf16), ((9 * width, tokens), bf16),
        ((chan_count, 3 * width, 3 * width), bf16), ((chan_count, 3 * width, 3 * width), bf16),
        ((rows, cols, width), f32), ((rows, cols, width), f32), ((chan_count, tokens, width), bf16),
        ((window, tokens, 2 * width), bf16), ((chan_count, tokens, width), bf16),
        ((images, context.shape[0], context.shape[2]), bf16),
    ]
    small = [
        ((6, rows, 1, width), f32), ((tokens, width), bf16), ((tokens, width), bf16), ((2, images, width), f32),
        ((images, tail, 2 * width), bf16),
    ]
    return pl.pallas_call(
        functools.partial(forward_kernel, row_count, chan_count, per_group, entries, fast),
        name="forward_block",
        out_shape=tuple(S(*item) for item in saved + small),
        in_specs=[pl.BlockSpec(memory_space=pltpu.SMEM)] + [vm] * (4 + VECTORS) + [hbm] * 8,
        out_specs=(hbm,) * len(saved) + (vm,) * len(small),
        scratch_shapes=[
            vmem((9 * width, full), bf16), vmem((9 * width, full), bf16), vmem((3, full, width), bf16), vmem((width, full), bf16),
            vmem(context.shape, bf16), vmem((context.shape[2] // width, context.shape[0] * images, width), f32), vmem(emb_w.shape, bf16), vmem(ctx_w.shape, bf16), vmem(emb_w.shape, f32),
            *[vmem(*item) for i, item in enumerate(saved) if i != 4],
            vmem((rows + 2, cols, width), bf16),
            vmem((rows + 2, cols, width), f32),
            vmem((rows + 2, cols, width), bf16),
            vmem((tokens, 9 * width), bf16),
            *scatter_scratch(tokens, width, 2),
            *scatter_scratch(tokens, width, 2),
            vmem((3, row_count, message, width), f32),
            sem((3, row_count - 1)), sem((3, row_count - 1)),
            sem((2, 2)), sem((2, 2)),
            sem((2, peers, PIECES)), sem((2, peers, PIECES)),
            sem((4, peers)), sem((4, peers)),
            sem((SEGMENTS, max(13, row_count))), sem((SEGMENTS, max(13, row_count))),
            sem((8,)), sem((9 + SEGMENTS,)),
        ],
        cost_estimate=pl.CostEstimate(flops=8 * 9 * tokens * width * full, bytes_accessed=16 * 2**20, transcendentals=4 * tokens * width),
        compiler_params=pltpu.CompilerParams(collective_id=0, has_side_effects=True, vmem_limit_bytes=60 * 2**20),
    )(offset, x, *vec, emb, emb_b, ctx_b, w1, w2, w_att, g, wo, context, emb_w, ctx_w)


class Total:
    def __init__(self, part, out, half, quarters, sends, recvs):
        self.part, self.half, self.quarters, self.out = part, half, quarters, out
        self.sends, self.recvs = sends, recvs
        self.r, self.z = lax.axis_index("rows"), lax.axis_index("chan")
        self.core, self.x, self.y, self.d = plane()
        self.n = part.shape[0] // 8
        self.copies = []

    def rows(self, device):
        return pl.ds(pl.multiple_of((lax.rem(device, 2) * 4 + device // 2) * self.n, 16), self.n)

    def half_rows(self, device):
        return pl.ds(pl.multiple_of(lax.rem(device, 2) * 4 * self.n, 16), 4 * self.n)

    def send(self, i, src, dst, device):
        copy = push(src, dst, self.sends.at[i], self.recvs.at[i], (device, self.z))
        self.copies.append(copy)
        return copy

    def one(self):
        self.a = self.send(0, self.part.at[self.half_rows(self.core)], self.half, self.core)

    def two(self):
        self.a.wait_recv()
        mine = self.half_rows(self.r)
        self.half[...] = (self.part[mine, :].astype(f32) + self.half[...].astype(f32)).astype(bf16)
        self.b = []
        for i, device in enumerate((self.d, self.x, self.y)):
            at = pl.ds(pl.multiple_of((device // 2) * self.n, 16), self.n)
            self.b.append(self.send(1 + i, self.half.at[at], self.quarters.at[i], device))

    def three(self):
        at = pl.ds(pl.multiple_of((self.r // 2) * self.n, 16), self.n)
        total = self.half[at, :].astype(f32)
        for i, copy in enumerate(self.b):
            copy.wait_recv()
            total = total + self.quarters[i].astype(f32)
        mine = self.rows(self.r)
        self.out[mine, :] = total.astype(bf16)
        self.c = []
        for i, device in enumerate((self.d, self.x, self.y, self.core)):
            self.c.append(self.send(4 + i, self.out.at[mine], self.out.at[mine], device))

    def four(self):
        self.e = [self.c[3]]
        for i, device in ((1, self.x), (2, self.y), (0, self.d)):
            self.c[i].wait_recv()
            at = self.rows(device)
            self.e.append(self.send(8 + i, self.out.at[at], self.out.at[at], self.core))

    def finish(self):
        for copy in self.e:
            copy.wait_recv()
        for copy in self.copies:
            copy.wait_send()


def total_scratch(n, width):
    return [vmem((n // 2, width), bf16), vmem((3, n // 8, width), bf16), pltpu.SemaphoreType.DMA((11,)), pltpu.SemaphoreType.DMA((11,))]


class Return:
    def __init__(self, away, parts, cores, out, recv, relay, sends, recvs):
        self.away, self.parts, self.cores, self.out, self.recv, self.relay = away, parts, cores, out, recv, relay
        self.sends, self.recvs = sends, recvs
        self.r, self.z = lax.axis_index("rows"), lax.axis_index("chan")
        self.core, self.x, self.y, self.d = plane()
        self.size = parts.shape[1] // SEGMENTS
        self.copies = [{} for _ in range(SEGMENTS)]

    def at(self, s, which=None):
        half = self.size // 2
        if which is None:
            return pl.ds(s * self.size, self.size)
        return pl.ds(s * self.size + which * half, half)

    def send(self, s, i, src, dst, device):
        self.copies[s][i] = push(src, dst, self.sends.at[s, i], self.recvs.at[s, i], (device, self.z))

    def start(self):
        for s in range(SEGMENTS):
            at = self.at(s)
            for i, device in enumerate((self.d, self.x, self.y, self.r)):
                self.send(s, i, self.away.at[device + self.core - self.r, at], self.cores.at[i, at], self.core)

    def chip(self, i, at):
        return self.parts[i, at].astype(f32) + self.cores[i, at].astype(f32)

    def one(self, s):
        first, second, out, recv = self.at(s, 0), self.at(s, 1), self.out, self.recv
        self.copies[s][0].wait_recv()
        out[0, first] = self.chip(0, first).astype(bf16)
        self.send(s, 4, out.at[0, first], self.relay.at[0, s], self.x)
        out[0, second] = self.chip(0, second).astype(bf16)
        self.send(s, 5, out.at[0, second], self.relay.at[1, s], self.y)
        self.copies[s][1].wait_recv()
        out[1, first] = self.chip(1, first).astype(bf16)
        self.send(s, 6, out.at[1, first], recv.at[0, first], self.x)
        self.copies[s][2].wait_recv()
        out[2, second] = self.chip(2, second).astype(bf16)
        self.send(s, 7, out.at[2, second], recv.at[1, second], self.y)

    def two(self, s):
        first, second, out, recv = self.at(s, 0), self.at(s, 1), self.out, self.recv
        self.copies[s][4].wait_recv()
        out[2, first] = (self.chip(2, first) + self.relay[0, s].astype(f32)).astype(bf16)
        self.send(s, 8, out.at[2, first], recv.at[1, first], self.y)
        self.copies[s][5].wait_recv()
        out[1, second] = (self.chip(1, second) + self.relay[1, s].astype(f32)).astype(bf16)
        self.send(s, 9, out.at[1, second], recv.at[0, second], self.x)

    def three(self, s):
        at = self.at(s)
        for i in (3, 6, 7, 8, 9):
            self.copies[s][i].wait_recv()
        return self.chip(3, at) + self.recv[0, at].astype(f32) + self.recv[1, at].astype(f32)

    def drain(self):
        for copies in self.copies:
            for copy in copies.values():
                copy.wait_send()


def return_scratch(tokens, width):
    shape = (tokens, width)
    sem = pltpu.SemaphoreType.DMA((SEGMENTS, 10))
    return [
        vmem((4, *shape), bf16), vmem((4, *shape), bf16), vmem((3, *shape), bf16), vmem((2, *shape), bf16),
        vmem((2, SEGMENTS, tokens // (2 * SEGMENTS), width), bf16), sem, sem,
    ]


class ConvBack:
    def __init__(self, pad, acc, x9t, turned, parts, outs, totals, up, down, halo_s, halo_r, sends, recvs, upper, lower):
        self.pad, self.acc, self.x9t, self.turned, self.parts, self.outs = pad, acc, x9t, turned, parts, outs
        self.totals, self.up, self.down, self.halo_s, self.halo_r = totals, up, down, halo_s, halo_r
        self.upper, self.lower = upper, lower
        _, self.rows, self.cols, self.width = pad.shape
        self.rows -= 2
        self.tokens = self.rows * self.cols
        self.size = self.rows // PIECES
        self.line = LineGather(self.at, PIECES + 2, sends, recvs)
        z = lax.axis_index("chan")
        low = z < 2
        self.order = (z, z + 1 - 2 * lax.rem(z, 2), jnp.where(low, 2, 1), jnp.where(low, 3, 0))
        self.later = []

    def at(self, shard, piece):
        if piece < PIECES:
            return self.pad.at[shard, pl.ds(1 + piece * self.size, self.size)]
        return self.pad.at[shard, pl.ds(0 if piece == PIECES else self.rows + 1, 1)]

    def start(self, values):
        pad, rows, z = self.pad, self.rows, lax.axis_index("chan")
        pad[z, pl.ds(1, rows)] = values
        self.rims = [
            push(pad.at[z, 1], pad.at[z, rows + 1], self.halo_s.at[0], self.halo_r.at[0], self.up),
            push(pad.at[z, rows], pad.at[z, 0], self.halo_s.at[1], self.halo_r.at[1], self.down),
        ]
        self.line.run(0, range(PIECES))
        for copy in self.rims:
            copy.wait_recv()
        self.line.run(0, (PIECES, PIECES + 1))

    def block(self, step, kernel=True):
        j, rows, tokens, width = self.order[step], self.rows, self.tokens, self.width
        parts = []
        for a, mask in enumerate((self.lower, None, self.upper)):
            part = self.pad[j, pl.ds(2 - a, rows)]
            if mask is not None:
                part = (part.astype(f32) * mask).astype(bf16)
            parts.append(part.reshape(tokens, width))
        if kernel:
            self.kernel_grad(step)
        term = jnp.dot(jnp.concatenate(parts, axis=1), self.turned[j], preferred_element_type=f32)
        self.acc[...] = term if step == 0 else self.acc[...] + term

    def kernel_grad(self, step):
        j = self.order[step]
        grad = self.pad[j, pl.ds(1, self.rows)].reshape(self.tokens, self.width)
        self.parts[step] = jnp.dot(self.x9t[...], grad, preferred_element_type=f32).astype(bf16)
        if self.totals:
            self.totals[step].one()
        else:
            self.outs[j] = self.parts[step]

    def run(self, step, kernel=True):
        self.line.run(step)
        self.block(step, kernel)

    def input_grad(self):
        total, width, cols, tokens = self.acc[...], self.width, self.cols, self.tokens
        col = lax.rem(lax.broadcasted_iota(jnp.int32, (tokens, 1), 0), cols)
        before = jnp.where(col == cols - 1, 0.0, pltpu.roll(total[:, :width], tokens - 1, 0))
        after = jnp.where(col == 0, 0.0, pltpu.roll(total[:, 2 * width :], 1, 0))
        return (before + total[:, width : 2 * width] + after).reshape(self.rows, cols, width)

    def drain(self):
        for copy in self.rims:
            copy.wait_send()
        self.line.drain()


def silu_slope(values):
    gate = jax.nn.sigmoid(values)
    return gate * (1.0 + values * (1.0 - gate))


def channel_total(values):
    rows, cols, width = values.shape
    return jnp.sum(jnp.sum(values.reshape(rows * cols // 8, 8, width), axis=0), axis=0, keepdims=True)


def backward_kernel(row_count, chan_count, per_group, entries, fast, offset, *refs):
    vec, refs = refs[:VECTORS], refs[VECTORS:]
    (rows_in, mod, w_att, wo, dctx,
     dq_hbm, dkv_hbm, o_hbm, gall_hbm, a3_hbm, x1_hbm, c1_hbm, x_hbm, x9t_1_hbm, x9t_2_hbm, turn1_hbm, turn2_hbm,
     result, dfeat, sums, g_conv1, g_conv2, g_att, g_out, g_ctx,
     dq_ref, o_ref, gall, a3_all, x1_ref, c1_ref, x_ref, x9t_1, x9t_2, turn1, turn2, load_s,
     part1, part2, part_att, part_out, d3, dx1_ref, acc, gpad, halo_s, halo_r, zh_s, zh_r, stat, stat_s, stat_r,
     res_out, res_recv, res_s, res_r, own, da3_out, da3_recv, da3_s, da3_r) = refs[:61]
    refs = refs[61:]
    rows, cols, width = x_ref.shape
    tokens = rows * cols
    r, z = lax.axis_index("rows"), lax.axis_index("chan")
    loads = Locals(load_s)
    if fast:
        back = Return(dkv_hbm, *refs[:7])
        for i, device in enumerate((back.d, back.x, back.y, r)):
            loads.start(dkv_hbm.at[device], back.parts.at[i])
        pairs = iter(range(7, len(refs), 4))

        def total(part, out):
            i = next(pairs)
            return Total(part, out, *refs[i : i + 4])
        small = [total(part_att, g_att), total(part_out, g_out), total(dctx, g_ctx)]
    else:
        for i in range(4):
            loads.start(dkv_hbm.at[pl.ds(i * (tokens // 4), tokens // 4)], refs[0].at[pl.ds(i * (tokens // 4), tokens // 4)])
        small = []
    for src, dst in (
        (dq_hbm, dq_ref), (o_hbm, o_ref), (gall_hbm, gall), (a3_hbm, a3_all), (x1_hbm, x1_ref), (c1_hbm, c1_ref), (x_hbm, x_ref),
        (x9t_2_hbm, x9t_2), (turn2_hbm, turn2), (x9t_1_hbm, x9t_1), (turn1_hbm, turn1),
    ):
        loads.start(src, dst)
    greet(row_peers(row_count) + chan_peers(chan_count))
    if fast:
        back.start()
    member, upper, lower = image_masks(offset[0], r * rows, rows, width, row_count * rows)
    images = len(member)
    up = (lax.rem(r + row_count - 1, row_count), z)
    down = (lax.rem(r + 1, row_count), z)
    orders = []
    for index, (x9t, turned, parts, outs) in enumerate(((x9t_2, turn2, part2, g_conv2), (x9t_1, turn1, part1, g_conv1))):
        conv = ConvBack(
            gpad.at[index], acc, x9t, turned, parts, outs, [], up, down, halo_s.at[index], halo_r.at[index],
            zh_s.at[index], zh_r.at[index], upper, lower,
        )
        if fast:
            conv.totals = [total(parts.at[step], outs.at[conv.order[step]]) for step in range(chan_count)]
        orders.append(conv)
    conv2, conv1 = orders
    cuts = [0, tokens // 2] + [tokens // 2 + -(-tokens * i // 96) * 16 for i in (1, 2)] + [tokens]
    res_copies = []

    def vector(i):
        return vec[i][...][None]

    def share_result(phase):
        part = pl.ds(cuts[phase], cuts[phase + 1] - cuts[phase])
        for d, device in enumerate(chan_peers(chan_count)):
            res_copies.append(push(res_out.at[d, part], res_recv.at[d, part], res_s.at[phase, d], res_r.at[phase, d], device))

    def exchange(phase, pieces):
        copies = share(stat.at[phase], stat_s.at[phase], stat_r.at[phase], row_count, pieces)
        share_result(phase + 1)
        return copies

    def norm_pieces(dxh, xhat):
        pieces = []
        for a, b in zip(image_sums(dxh, member), image_sums(dxh * xhat, member)):
            pieces += [a, b]
        return pieces

    def norm_back(total, dxh, xhat, scale):
        grouped = group_sum(total[: 2 * images], per_group) * (1.0 / entries)
        first = to_rows([grouped[2 * i : 2 * i + 1] for i in range(images)], member)
        second = to_rows([grouped[2 * i + 1 : 2 * i + 2] for i in range(images)], member)
        return scale * (dxh - first - xhat * second)

    def out_term(j):
        return jnp.dot(o_ref[...], wo[:, pl.ds(pl.multiple_of(j * width, width), width)], preferred_element_type=f32)

    def att_rows(j):
        at = pl.ds(pl.multiple_of(j * width, width), width)
        return jnp.concatenate([w_att[t, at, :] for t in range(3)], axis=1)

    line = LineScatter(lambda j, at: contract(d3[at, :], att_rows(j), 1, 1), own, da3_out, da3_recv, da3_s, da3_r)
    size = tokens // SEGMENTS
    bias_v = jnp.zeros((1, width), f32)
    loads.wait(4)
    if fast:
        loads.wait(0, 1, 2, 3)
        for s in range(SEGMENTS + 2):
            if s < SEGMENTS:
                back.one(s)
            if s == 0:
                loads.wait(5, 6)
                for d, device in enumerate(chan_peers(chan_count)):
                    res_out[d] = out_term(device[1]).astype(bf16)
                share_result(0)
            if 1 <= s <= SEGMENTS:
                back.two(s - 1)
            if s >= 2:
                at = pl.ds((s - 2) * size, size)
                dkv = back.three(s - 2)
                d3[at, :width] = dq_ref[at, :].astype(bf16)
                d3[at, width:] = dkv.astype(bf16)
                bias_v = bias_v + jnp.sum(dkv[:, width:], axis=0, keepdims=True)
                line.send(s - 2)
            if s >= 3:
                line.merge(s - 3)
        line.merge(SEGMENTS - 1)
    else:
        loads.wait(0, 1, 2, 3, 5, 6)
        for d, device in enumerate(chan_peers(chan_count)):
            res_out[d] = out_term(device[1]).astype(bf16)
        share_result(0)
        for s in range(SEGMENTS + 1):
            if s < SEGMENTS:
                at = pl.ds(s * size, size)
                dkv = refs[0][at, :]
                d3[at, :width] = dq_ref[at, :].astype(bf16)
                d3[at, width:] = dkv.astype(bf16)
                bias_v = bias_v + jnp.sum(dkv[:, width:], axis=0, keepdims=True)
                line.send(s)
            if s >= 1:
                line.merge(s - 1)
    line.keep()
    bias_q = jnp.sum(dq_ref[...], axis=0, keepdims=True)
    loads.wait(7)
    for i in range(chan_count):
        grad = contract(a3_all[i], d3[...], 0, 0).astype(bf16)
        for t in range(3):
            part_att[pl.ds((t * chan_count + i) * width, width), :] = grad[:, t * width : (t + 1) * width]
    g_cat = jnp.concatenate([gall[i] for i in range(chan_count)], axis=1)
    part_out[...] = contract(o_ref[...], g_cat, 0, 0).astype(bf16)
    for t in small:
        t.one()
    loads.wait(8)
    x1 = x1_ref[...]
    g = gall[z].astype(f32).reshape(rows, cols, width)
    center, scale = rows_in[4], rows_in[5]
    xhat = (x1 - center) * scale
    bias_g = channel_total(g)
    for t in small:
        t.two()
    line.finish()
    da3 = own[...].reshape(rows, cols, width)
    dxh = da3 * vector(6)
    copies = exchange(
        0, norm_pieces(dxh, xhat) + [channel_total(da3 * xhat), channel_total(da3), bias_q, bias_v, bias_g]
    )
    for t in small:
        t.three()
    total = share_total(stat.at[0], copies)
    sums[0:5, :] = total[2 * images : 2 * images + 5]
    dx1 = g + norm_back(total, dxh, xhat, scale)
    conv2.start(dx1.astype(bf16))
    dx1_ref[...] = dx1
    bias_2 = channel_total(dx1)
    loads.wait(9, 11, 12)
    conv2.block(0)
    for t in small:
        t.four()
    center, scale = rows_in[2], rows_in[3]
    xhat = (c1_ref[...] - center) * scale
    n2 = xhat * vector(3) + vector(4)
    mod_scale = 1.0 + to_rows([mod[0, i : i + 1, :] for i in range(images)], member)
    mod_shift = to_rows([mod[1, i : i + 1, :] for i in range(images)], member)
    slope = silu_slope(n2 * mod_scale + mod_shift)
    conv2.run(1)
    for t in conv2.totals[0:1]:
        t.two()
    conv2.run(2)
    for t in conv2.totals[1:2]:
        t.two()
    for t in conv2.totals[0:1]:
        t.three()
    conv2.run(3, False)
    dh2 = conv2.input_grad() * slope
    dn2 = dh2 * mod_scale
    dxh = dn2 * vector(3)
    dss = []
    for a, b in zip(image_sums(dh2 * n2, member), image_sums(dh2, member)):
        dss += [a, b]
    copies = exchange(1, norm_pieces(dxh, xhat) + [channel_total(dn2 * xhat), channel_total(dn2), bias_2] + dss)
    conv2.kernel_grad(3)
    for t in conv2.totals[2:3]:
        t.two()
    for t in small:
        t.finish()
    total = share_total(stat.at[1], copies)
    sums[5 : 8 + 2 * images, :] = total[2 * images : 4 * images + 3]
    dc1 = norm_back(total, dxh, xhat, scale)
    conv1.start(dc1.astype(bf16))
    bias_1 = channel_total(dc1)
    loads.wait(10, 13, 14)
    conv1.block(0)
    for t in conv2.totals[3:4]:
        t.two()
    for t in conv2.totals[1:3]:
        t.three()
    for t in conv2.totals[0:1]:
        t.four()
    center, scale = rows_in[0], rows_in[1]
    xhat = (x_ref[...].astype(f32) - center) * scale
    slope = silu_slope(xhat * vector(0) + vector(1))
    conv1.run(1)
    for t in conv1.totals[0:1]:
        t.two()
    for t in conv2.totals[3:4]:
        t.three()
    for t in conv2.totals[1:3]:
        t.four()
    conv1.run(2)
    for t in conv1.totals[1:2]:
        t.two()
    for t in conv1.totals[0:1]:
        t.three()
    for t in conv2.totals[3:4]:
        t.four()
    conv1.run(3)
    for t in conv1.totals[2:3]:
        t.two()
    for t in conv1.totals[1:2]:
        t.three()
    dn1 = conv1.input_grad() * slope
    for t in conv1.totals[3:4]:
        t.two()
    dxh = dn1 * vector(0)
    copies = exchange(2, norm_pieces(dxh, xhat) + [channel_total(dn1 * xhat), channel_total(dn1), bias_1])
    for t in conv1.totals[0:1]:
        t.four()
    for t in conv1.totals[2:4]:
        t.three()
    for t in conv1.totals[1:2]:
        t.four()
    own[...] = out_term(z)
    total = share_total(stat.at[2], copies)
    sums[8 + 2 * images : 11 + 2 * images, :] = total[2 * images : 2 * images + 3]
    dfeat[...] = (dx1_ref[...] + norm_back(total, dxh, xhat, scale)).astype(bf16)
    for t in conv1.totals[2:4]:
        t.four()
    for copy in res_copies:
        copy.wait()
    value = own[...]
    for d in range(chan_count - 1):
        value = value + res_recv[d].astype(f32)
    result[...] = (x1_ref[...] + value.reshape(rows, cols, width) + vector(8)).astype(bf16)
    for t in conv2.totals + conv1.totals:
        t.finish()
    if fast:
        back.drain()
    else:
        g_att[...] = part_att[...]
        g_out[...] = part_out[...]
        g_ctx[...] = dctx[...]
    line.drain()
    conv2.drain()
    conv1.drain()


def backward_block(row_count, chan_count, per_group, entries, fast, offset, x, vec, dq, dkv, o, gall, a3_all, x1, c1, rows_in,
                   mod, x9t_1, x9t_2, turn1, turn2, w_att, wo, dctx):
    rows, cols, width = x.shape
    tokens = rows * cols
    images = row_count * rows // IMG_H
    full = chan_count * width
    message = -(-(4 * images + 5) // 8) * 8
    vm = pl.BlockSpec(memory_space=pltpu.VMEM)
    hbm = pl.BlockSpec(memory_space=pl.ANY)
    S = jax.ShapeDtypeStruct
    sem = pltpu.SemaphoreType.DMA
    peers = chan_count - 1
    total_rows = -(-(11 + 2 * images) // 8) * 8
    early = [rows_in, mod, w_att, wo, dctx]
    late = [dq, dkv, o, gall, a3_all, x1, c1, x, x9t_1, x9t_2, turn1, turn2]
    kernel_grad = S((chan_count, 9 * width, width), bf16)
    if fast:
        plane_scratch = [
            *return_scratch(tokens, 2 * width), *total_scratch(3 * full, width), *total_scratch(width, full),
            *total_scratch(*dctx.shape),
        ]
        for _ in range(2 * chan_count):
            plane_scratch += total_scratch(9 * width, width)
    else:
        plane_scratch = [vmem(dkv.shape, dkv.dtype)]
    return pl.pallas_call(
        functools.partial(backward_kernel, row_count, chan_count, per_group, entries, fast),
        name="backward_block",
        out_shape=(
            S((rows, cols, width), bf16), S((rows, cols, width), bf16), S((total_rows, width), f32),
            kernel_grad, kernel_grad, S((3 * full, width), bf16), S((width, full), bf16), S(dctx.shape, bf16),
        ),
        in_specs=[pl.BlockSpec(memory_space=pltpu.SMEM)] + [vm] * (VECTORS + len(early)) + [hbm] * len(late),
        out_specs=(vm,) * 8,
        scratch_shapes=[
            *[vmem(item.shape, item.dtype) for item in late if item is not dkv], sem((15,)),
            vmem(kernel_grad.shape, bf16), vmem(kernel_grad.shape, bf16), vmem((3 * full, width), bf16), vmem((width, full), bf16),
            vmem((tokens, 3 * width), bf16), vmem((rows, cols, width), f32), vmem((tokens, 3 * width), f32),
            vmem((2, chan_count, rows + 2, cols, width), bf16), sem((2, 2)), sem((2, 2)),
            sem((2, 2, peers, PIECES + 2)), sem((2, 2, peers, PIECES + 2)),
            vmem((3, row_count, message, width), f32), sem((3, row_count - 1)), sem((3, row_count - 1)),
            vmem((peers, tokens, width), bf16), vmem((peers, tokens, width), bf16), sem((4, peers)), sem((4, peers)),
            *scatter_scratch(tokens, width, SEGMENTS),
            *plane_scratch,
        ],
        cost_estimate=pl.CostEstimate(flops=12 * 9 * tokens * width * full, bytes_accessed=24 * 2**20, transcendentals=4 * tokens * width),
        compiler_params=pltpu.CompilerParams(collective_id=1, has_side_effects=True, vmem_limit_bytes=60 * 2**20),
    )(offset, *vec, *early, *late)


def finish_kernel(images, share_rows, ctx_count, result_in, dfeat_in, sums, g_conv1, g_conv2, g_att, g_out, g_ctx, emb, context,
                  result, dfeat, conv1, conv2, att, out, emb_w, ctx_w, emb_b, att_b, ctx_b, *vectors):
    width = sums.shape[1]
    result[...] = result_in[...]
    dfeat[...] = dfeat_in[...]
    for j in range(g_conv1.shape[0]):
        conv1[:, pl.ds(j * width, width)] = g_conv1[j].astype(f32)
        conv2[:, pl.ds(j * width, width)] = g_conv2[j].astype(f32)
    out[...] = g_out[...].astype(f32)
    att[...] = g_att[...].astype(f32)
    block = emb.shape[1]
    for t in range(2):
        rows = jnp.concatenate([sums[8 + 2 * i + t : 9 + 2 * i + t, :] for i in range(images)], axis=0)
        high = rows.astype(bf16)
        low = (rows - high.astype(f32)).astype(bf16)
        emb_w[pl.ds(t, block, 2), :] = contract(emb[...], high, 0, 0) + contract(emb[...], low, 0, 0)
    total = None
    for i in range(images):
        term = contract(context[i], g_ctx[pl.ds(i * share_rows, ctx_count), :], 0, 0)
        total = term if total is None else total + term
    for t in range(2):
        ctx_w[pl.ds(t, block, 2), :] = total[:, t * width : (t + 1) * width]

    @pl.when(pl.program_id(0) == 0)
    def _():
        for t in range(2):
            emb_b[t : t + 1, :] = sum(sums[8 + 2 * i + t : 9 + 2 * i + t, :] for i in range(images))
            att_b[t : t + 1, :] = sums[2 + t : 3 + t, :]
            ctx_b[t : t + 1, :] = jnp.sum(g_ctx[:, pl.ds(t * width, width)].astype(f32), axis=0, keepdims=True)
        for ref, i in zip(vectors, (0, 1, 4, 5, 6, 7, 8 + 2 * images, 9 + 2 * images, 10 + 2 * images)):
            ref[...] = sums[i : i + 1, :]


def finish_block(images, share_rows, steps, result, dfeat, sums, g_conv1, g_conv2, g_att, g_out, g_ctx, emb, context):
    width = sums.shape[1]
    depth = emb.shape[1]
    ctx_count = context.shape[1]
    S = jax.ShapeDtypeStruct

    def lead(shape):
        rest = (0,) * (len(shape) - 1)
        return pl.BlockSpec((shape[0] // steps,) + tuple(shape[1:]), lambda s: (s,) + rest)

    def whole(shape):
        return pl.BlockSpec(tuple(shape), lambda s: (0,) * len(shape))

    chan_count, taps_n, _ = g_conv1.shape
    full = chan_count * width
    conv_spec = pl.BlockSpec((chan_count, taps_n // steps, width), lambda s: (0, s, 0))
    shapes = [
        (result.shape, bf16, lead), (dfeat.shape, bf16, lead), ((taps_n, full), f32, lead), ((taps_n, full), f32, lead),
        ((3 * full, width), f32, lead), ((width, full), f32, lead), ((2 * depth, width), f32, lead),
        ((2 * depth, width), f32, lead), ((2, width), f32, whole), ((2, width), f32, whole), ((2, width), f32, whole),
    ] + [((1, width), f32, whole)] * 9
    return pl.pallas_call(
        functools.partial(finish_kernel, images, share_rows, ctx_count),
        name="finish_block",
        grid=(steps,),
        out_shape=tuple(S(shape, dtype) for shape, dtype, _ in shapes),
        in_specs=[
            lead(result.shape), lead(dfeat.shape), whole(sums.shape), conv_spec, conv_spec, lead(g_att.shape),
            lead(g_out.shape), whole(g_ctx.shape), pl.BlockSpec((images, depth // steps), lambda s: (0, s)),
            pl.BlockSpec((images, ctx_count, depth // steps), lambda s: (0, 0, s)),
        ],
        out_specs=tuple(spec(shape) for shape, _, spec in shapes),
        cost_estimate=pl.CostEstimate(flops=4 * images * ctx_count * depth * width, bytes_accessed=16 * 2**20, transcendentals=0),
        compiler_params=pltpu.CompilerParams(vmem_limit_bytes=60 * 2**20),
    )(result, dfeat, sums, g_conv1, g_conv2, g_att, g_out, g_ctx, emb, context)


def local(
    features,
    embedding,
    context,
    image_offset,
    first_gain,
    first_shift,
    conv_first,
    conv_first_bias,
    embed_weight,
    embed_bias,
    second_gain,
    second_shift,
    conv_second,
    conv_second_bias,
    attend_gain,
    attend_shift,
    attend_weight,
    attend_bias,
    context_weight,
    context_bias,
    output_weight,
    output_bias,
    cotangent,
):
    slab_rows, columns, channels = features.shape
    devices, chan = lax.axis_size("rows"), lax.axis_size("chan")
    total_rows = slab_rows * devices
    images = total_rows // IMG_H
    per_group = C // GROUPS
    entries = IMG_H * columns * per_group
    tokens = slab_rows * columns
    context_count = context.shape[1]
    tail = -(-context_count // 256) * 256
    vectors = [
        vector.reshape(1, channels)
        for vector in (first_gain, first_shift, conv_first_bias, second_gain, second_shift, conv_second_bias, attend_gain,
                       attend_shift, output_bias)
    ] + [attend_bias]
    window = min(devices, 2 * (IMG_H // slab_rows) + 1)
    kernel_one = conv_first.reshape(9 * channels, C)
    kernel_two = conv_second.reshape(9 * channels, C)
    attend_kernels = attend_weight.transpose(1, 0, 2)
    fast = devices == 8 and window == devices
    (x9t_one, x9t_two, turn_one, turn_two, middle, inner, attend_blocks, kv_all, grad_blocks, context_own, row_stats, queries,
     grad_attended, modulate, context_rows) = forward_block(
        devices, chan, per_group, entries, window, fast, tail, image_offset, features, vectors, embedding, embed_bias,
        context_bias, kernel_one, kernel_two, attend_kernels, cotangent.reshape(tokens, channels), output_weight, context.transpose(1, 0, 2),
        embed_weight.reshape(-1, channels), context_weight.reshape(-1, channels),
    )
    share_rows = -(-context_count // 64) * 64
    attended, query_grad, window_grad, context_part = attend(
        devices, slab_rows, image_offset, queries, grad_attended, kv_all.reshape(window * slab_rows, columns, 2 * channels),
        context_rows, total_rows, IMG_H, context_count, images, share_rows,
    )
    key_value_grad = window_grad.reshape(window, tokens, 2 * channels)
    if not fast:
        pieces, key_value_grad = key_value_grad, jnp.zeros((tokens, 2 * channels), f32)
        for position in range(window):
            shift_by = position - window // 2 if window < devices else None
            piece = pieces[position]
            if shift_by is None:
                piece = jnp.sum(lax.all_to_all(pieces, "rows", 0, 0).astype(f32), axis=0) if position == 0 else 0.0
            elif shift_by != 0:
                piece = from_behind(piece, "rows", shift_by)
            key_value_grad = key_value_grad + (piece if shift_by is None else piece.astype(f32))
    result, features_grad, sums, conv_first_grad, conv_second_grad, attend_grad, output_weight_grad, context_sum = backward_block(
        devices, chan, per_group, entries, fast, image_offset, features, vectors, query_grad, key_value_grad, attended,
        grad_blocks, attend_blocks, inner, middle, row_stats, modulate, x9t_one, x9t_two, turn_one, turn_two, attend_kernels,
        output_weight, context_part,
    )
    if not fast:
        conv_first_grad, conv_second_grad, attend_grad, output_weight_grad, context_sum = lax.psum(
            (conv_first_grad, conv_second_grad, attend_grad, output_weight_grad, context_sum), "rows"
        )
    (result, features_grad, conv_first_grad, conv_second_grad, attend_grad, output_weight_grad, embed_weight_grad,
     context_weight_grad, embed_bias_grad, attend_bias_grad, context_bias_grad, *rest) = finish_block(
        images, share_rows, 2, result, features_grad, sums, conv_first_grad, conv_second_grad, attend_grad,
        output_weight_grad, context_sum, embedding, context_own,
    )
    (attend_gain_grad, attend_shift_grad, output_bias_grad, second_gain_grad, second_shift_grad, conv_second_bias_grad,
     first_gain_grad, first_shift_grad, conv_first_bias_grad) = [vector.reshape(channels) for vector in rest]
    return (
        result,
        features_grad,
        first_gain_grad,
        first_shift_grad,
        conv_first_grad.reshape(3, 3, channels, C),
        conv_first_bias_grad,
        embed_weight_grad.reshape(-1, 2, channels),
        embed_bias_grad,
        second_gain_grad,
        second_shift_grad,
        conv_second_grad.reshape(3, 3, channels, C),
        conv_second_bias_grad,
        attend_gain_grad,
        attend_shift_grad,
        attend_grad.reshape(3, C, channels).transpose(1, 0, 2),
        attend_bias_grad,
        context_weight_grad.reshape(-1, 2, channels),
        context_bias_grad,
        output_weight_grad,
        output_bias_grad,
    )


def solution(mesh):
    placed = (
        P("rows", None, "chan"),
        P(),
        P(),
        P(),
        P("chan"),
        P("chan"),
        P(None, None, "chan", None),
        P("chan"),
        P(None, None, "chan"),
        P(None, "chan"),
        P("chan"),
        P("chan"),
        P(None, None, "chan", None),
        P("chan"),
        P("chan"),
        P("chan"),
        P(None, None, "chan"),
        P(None, "chan"),
        P(None, None, "chan"),
        P(None, "chan"),
        P("chan", None),
        P("chan"),
        P("rows", None, "chan"),
    )
    return jax.shard_map(
        local,
        mesh=mesh,
        in_specs=placed,
        out_specs=(
            P("rows", None, "chan"),
            P("rows", None, "chan"),
            P("chan"),
            P("chan"),
            P(None, None, "chan", None),
            P("chan"),
            P(None, None, "chan"),
            P(None, "chan"),
            P("chan"),
            P("chan"),
            P(None, None, "chan", None),
            P("chan"),
            P("chan"),
            P("chan"),
            P(None, None, "chan"),
            P(None, "chan"),
            P(None, None, "chan"),
            P(None, "chan"),
            P("chan", None),
            P("chan"),
        ),
        check_vma=False,
    )
```
